32 devices in a mesh: rows: 8 (over y, x, core), cols: 4 (over z).
Axes of the slice: x: 2, y: 2, z: 4, core: 2. Of those that a mesh axis runs over, the one named last changes fastest.
Arguments:
- features: bfloat16 [4, 64, 160, 256], P(None, 'rows', 'cols'), may hold values from -6 to 6
- occupancy: int32 [4, 64, 160], P(None, 'rows', 'cols'), may hold values from 0 to 1, as said below
- cotangent: bfloat16 [4, 64, 160, 256], P(None, 'rows', 'cols'), may hold values from -6 to 6
- conv_weights: float32 [2, 589824], replicated, may hold values from -0.125 to 0.125
- conv_first: float32 [2, 589824], P(None, ('rows', 'cols')), may hold values from -128 to 128
- conv_second: float32 [2, 589824], P(None, ('rows', 'cols')), may hold values from 20.48 to 327.68
- norm_scale_bias: float32 [4, 256], replicated, may hold values from 0.5 to 1.5
- norm_first: float32 [4, 256], replicated, may hold values from -128 to 128
- norm_second: float32 [4, 256], replicated, may hold values from 20.48 to 327.68
Outputs:
- block_out: bfloat16 [4, 64, 160, 256], P(None, 'rows', 'cols')
- grad_input: float32 [4, 64, 160, 256], P(None, 'rows', 'cols')
- conv_grads: float32 [2, 589824], P(None, ('rows', 'cols'))
- conv_new: float32 [2, 589824], P(None, ('rows', 'cols'))
- conv_first_new: float32 [2, 589824], P(None, ('rows', 'cols'))
- conv_second_new: float32 [2, 589824], P(None, ('rows', 'cols'))
- norm_grads: float32 [4, 256], replicated
- norm_new: float32 [4, 256], replicated
- norm_first_new: float32 [4, 256], replicated
- norm_second_new: float32 [4, 256], replicated
The draws below stay inside these ranges and needn't reach their ends.
Inputs may be any that keep to these rules, and one draw needn't show every extreme that they name: `occupancy`: 0 or 1; the share of ones differs from one 8 x 40 tile to another, the same in every scene.
All inputs are finite; a program needn't handle non-finite values.
Results may differ from the reference program's by a relative error of at most 0.0033.
The reference program's roundings to bfloat16 on the way count: a program that leaves them out, or rounds other values in their place, can miss the bound.
Values may be sent and summed in bfloat16 or wider, within the bound.
No kernel may reach another device: no remote copies, remote signals or barrier semaphores. Data moves between devices by JAX's collectives and lax.ppermute only.
A program may use at most 64 MiB of HBM per device.

```python
import math
import jax
import jax.numpy as jnp
from jax import lax

C = 256
SCENES = 4
TH = 8
TW = 40
STEP = 5
GRID_H = 64
GRID_W = 160
PIXELS = 40960
KCC = 589824


def draw_occupancy(key, part):
    level_key = jax.random.fold_in(key, 11)
    pixel_key = jax.random.fold_in(key, 23)
    tile_rows = GRID_H // TH
    tile_cols = GRID_W // TW
    levels = jax.random.randint(level_key, (tile_rows, tile_cols), 15, 96)
    levels = jnp.repeat(jnp.repeat(levels, TH, axis=0), TW, axis=1)
    pixels = jax.random.randint(pixel_key, (SCENES, GRID_H, GRID_W), 0, 100)
    return jnp.where(pixels < levels[None], 1, 0).astype(jnp.int32)


def steps_of(stream_key, dims, shards, smallest, top_value):
    loudness, own = 1.0, jax.random.fold_in(stream_key, 6)
    for position, parts in shards:
        steps = jnp.exp(jax.random.uniform(jax.random.fold_in(own, position), (parts,), jnp.float32, smallest / len(shards), top_value / len(shards)))
        loudness = loudness * jnp.repeat(steps, dims[position] // parts).reshape([-1 if axis == position else 1 for axis in range(len(dims))])
    return loudness


def scatter_about(rng, shape, scale, bound, shards=(), dtype=jnp.bfloat16):
    level = steps_of(rng, shape, shards, -0.22, 0.18) if shards else 1.0
    values = jax.random.normal(rng, shape, jnp.float32) * scale * level
    return jnp.minimum(jnp.maximum(values, -bound), bound).astype(dtype)


def setup_inputs(seed: int = 0) -> dict:
    splits = jax.random.split(jax.random.key(seed), 10)
    features = scatter_about(splits[0], (SCENES, GRID_H, GRID_W, C), 1.0, 6.0, ((1, 8), (2, 4)))
    occupancy = draw_occupancy(jax.random.fold_in(splits[9], 71), 0)
    cotangent = scatter_about(splits[2], (SCENES, GRID_H, GRID_W, C), 1.0, 6.0, ((1, 8), (2, 4)))
    conv_weights = scatter_about(splits[3], (2, KCC), (9 * C) ** -0.5, 0.125, (), jnp.float32)
    conv_first = scatter_about(splits[4], (2, KCC), (0.11 * PIXELS ** 0.5), 128.0, ((1, 32),), jnp.float32)
    conv_second = jnp.clip(jnp.exp(math.log(327.68) - 2.7725887 * jax.random.uniform(splits[5], (2, KCC), jnp.float32) ** steps_of(splits[5], (2, KCC), ((1, 32),), -0.2, 0.2)), 20.48, 327.68)
    norm_scale_bias = jnp.clip(1.0 + 0.1 * jax.random.normal(splits[6], (4, C), jnp.float32), 0.5, 1.5)
    norm_first = scatter_about(splits[7], (4, C), (0.11 * PIXELS ** 0.5), 128.0, (), jnp.float32)
    norm_second = jnp.clip(jnp.exp(jax.random.uniform(splits[8], (4, C), jnp.float32, math.log(20.48), math.log(327.68))), 20.48, 327.68)
    return {"features": features, "occupancy": occupancy, "cotangent": cotangent, "conv_weights": conv_weights, "conv_first": conv_first, "conv_second": conv_second, "norm_scale_bias": norm_scale_bias, "norm_first": norm_first, "norm_second": norm_second}


@jax.custom_vjp
def low(v):
    return lax.optimization_barrier(v.astype(jnp.bfloat16)).astype(jnp.float32)

@jax.custom_vjp
def low_back(v):
    return v

def low_keep(v):
    return (low(v), None)

def low_pass(kept, grad):
    return (grad,)

def back_keep(v):
    return (v, None)

def back_low(kept, grad):
    return (low(grad),)
low.defvjp(low_keep, low_pass)
low_back.defvjp(back_keep, back_low)

def convolve(field, flat):
    kernel = flat.reshape(3, 3, C, C)
    return lax.conv_general_dilated(field, kernel, (1, 1), ((1, 1), (1, 1)), dimension_numbers=('NHWC', 'HWIO', 'NHWC'), precision=lax.Precision.HIGHEST)

def batch_norm(field, norm_scale, shift):
    mean = lax.optimization_barrier(jnp.mean(field, axis=(0, 1, 2)))
    var = lax.optimization_barrier(jnp.mean(field * field, axis=(0, 1, 2))) - mean * mean
    return (field - mean) * lax.rsqrt(var + 1e-05) * norm_scale + shift

def adamw(weight, grad, first, second, rate):
    first_new = 0.9 * first + 0.1 * grad
    second_new = 0.999 * second + 0.001 * grad * grad
    first_hat = first_new / (1.0 - 0.9 ** STEP)
    second_hat = second_new / (1.0 - 0.999 ** STEP)
    weight_new = weight - rate * (first_hat / (jnp.sqrt(second_hat) + 1e-08) + 0.01 * weight)
    return (weight_new, first_new, second_new)

def reference(features, occupancy, cotangent, conv_weights, conv_first, conv_second, norm_scale_bias, norm_first, norm_second):
    maskf = occupancy.astype(jnp.float32)[..., None]
    inputs = features.astype(jnp.float32)

    def forward(inputs, weights, params):
        masked = low(inputs * maskf)
        pre1 = low_back(convolve(masked, low(weights[0])))
        normed1 = batch_norm(pre1, params[0], params[1])
        hidden = low(jax.nn.relu(normed1))
        pre2 = low_back(convolve(hidden, low(weights[1])))
        normed2 = batch_norm(pre2, params[2], params[3])
        return masked + normed2
    result, pullback = jax.vjp(forward, inputs, conv_weights, norm_scale_bias)
    grad_input, conv_grads, norm_grads = pullback(cotangent.astype(jnp.float32))
    conv_new, conv_first_new, conv_second_new = adamw(conv_weights, conv_grads, conv_first, conv_second, 0.02)
    norm_new, norm_first_new, norm_second_new = adamw(norm_scale_bias, norm_grads, norm_first, norm_second, 0.75)
    return (result.astype(jnp.bfloat16), grad_input, conv_grads, conv_new, conv_first_new, conv_second_new, norm_grads, norm_new, norm_first_new, norm_second_new)
```

```python
import functools
import math

import jax
import jax.numpy as jnp
from jax import lax
from jax.experimental import pallas as pl
from jax.experimental.pallas import tpu as pltpu
from jax.sharding import PartitionSpec as P

STEP = 5
BOTH = ("rows", "cols")
RIM = 4
F32, BF16 = jnp.float32, jnp.bfloat16


def shape_of(shape, dtype):
    return jax.ShapeDtypeStruct(shape, dtype)


def kernel_call(body, out_shape, flops, smem=(), scratch=(), limit=40):
    def call(*operands):
        specs = [
            pl.BlockSpec(memory_space=pltpu.SMEM if i in smem else pltpu.VMEM)
            for i in range(len(operands))
        ]
        return pl.pallas_call(
            body,
            out_shape=out_shape,
            in_specs=specs,
            out_specs=[pl.BlockSpec(memory_space=pltpu.VMEM)] * len(out_shape),
            scratch_shapes=list(scratch),
            compiler_params=pltpu.CompilerParams(vmem_limit_bytes=limit << 20),
            cost_estimate=pl.CostEstimate(
                flops=int(flops), bytes_accessed=4 << 20, transcendentals=0
            ),
        )(*operands)

    return call


def dot(a, b):
    return jnp.dot(a, b, preferred_element_type=F32)


def dot_nt(a, b):
    return lax.dot_general(a, b, (((1,), (1,)), ((), ())), preferred_element_type=F32)


def total_of(ref):
    count = ref.shape[0]
    total = ref[0]
    for i in range(1, count):
        total = total + ref[i]
    return total


def to_all(ref, parts):
    value = jnp.concatenate(parts, axis=0)
    for i in range(ref.shape[0]):
        ref[i] = value


def store_shifted(ref, start, row):
    width, chans = row.shape
    ref[start : start + width, 0:chans] = pltpu.roll(row, 1, 0).astype(BF16)
    ref[start : start + width, chans : 2 * chans] = row.astype(BF16)
    ref[start : start + width, 2 * chans : 3 * chans] = pltpu.roll(row, width - 1, 0).astype(BF16)


class Geometry:
    def __init__(self, scenes, height, width, chans):
        self.s, self.h, self.w, self.c = scenes, height, width, chans
        self.wp = width + 2 * RIM


def in_grid(row, r, g, lo, hi, edge):
    row = jnp.concatenate([row[: g.w], row[g.w :] * edge], axis=0)
    if r < RIM:
        row = row * lo
    elif r >= RIM + g.h:
        row = row * hi
    return row


def edge_mask(bounds, g):
    place = lax.broadcasted_iota(jnp.int32, (2 * RIM, g.c), 0)
    return jnp.where(place < RIM, bounds[2].astype(F32), bounds[3].astype(F32))


def sum_rows(value):
    rows, chans = value.shape
    return jnp.sum(value.reshape(rows // 8, 8, chans), axis=0)


def prepare_kernel(w_ref, one_ref, two_ref):
    chans = one_ref.shape[1]
    lanes = w_ref.shape[1]
    per = chans // lanes
    taps = one_ref.shape[0] // chans

    def tap(t, carry):
        for k, out in enumerate((one_ref, two_ref)):
            parts = [
                w_ref[pl.ds(t * chans * per * 2 + 2 * half + k, chans, stride=2 * per), :]
                for half in range(per)
            ]
            out[pl.ds(pl.multiple_of(t * chans, chans), chans), :] = jnp.concatenate(
                parts, axis=1
            ).astype(BF16)
        return carry

    lax.fori_loop(0, taps, tap, 0)


def first_conv_kernel(g, chunk, up, top, bottom, down, edges, w, x_ref, z_ref, st_ref):
    half = g.h // 2
    rows_in, rows_out = g.h + 2 * RIM, g.h + 2 * RIM - 2
    s1 = jnp.zeros((8, g.c), F32)
    s2 = jnp.zeros((8, g.c), F32)
    for s in range(g.s):
        for r in range(rows_in):
            source, place = (
                (up, r)
                if r < RIM
                else (top, r - RIM)
                if r < RIM + half
                else (bottom, r - RIM - half)
                if r < RIM + g.h
                else (down, r - RIM - g.h)
            )
            row = jnp.concatenate(
                [source[s, place].astype(F32), edges[s, r].astype(F32)], axis=0
            )
            store_shifted(x_ref, (s * rows_in + r) * g.wp, row)
        for r in range(0, rows_out, chunk):
            base = (s * rows_in + r) * g.wp
            size = chunk * g.wp
            lhs = jnp.concatenate(
                [x_ref[base + a * g.wp : base + a * g.wp + size, :] for a in range(3)], axis=1
            )
            acc = dot(lhs, w[...])
            z_ref[(s * rows_out + r) * g.wp : (s * rows_out + r) * g.wp + size, :] = acc
            for i in range(chunk):
                if RIM <= r + i + 1 < RIM + g.h:
                    own = acc[i * g.wp : i * g.wp + g.w]
                    s1 = s1 + sum_rows(own)
                    s2 = s2 + sum_rows(own * own)
    to_all(st_ref, [jnp.sum(s1, 0, keepdims=True), jnp.sum(s2, 0, keepdims=True)])


def stats_of(total, count):
    mean = total[0:1] / count
    var = total[1:2] / count - mean * mean
    return mean, lax.rsqrt(var + 1e-05)


def second_conv_kernel(
    g, chunk, count, bounds, z1, st, params, w, cot, h_ref, z_ref, st_ref
):
    rows_in, rows_out = g.h + 2 * RIM - 2, g.h + 2 * RIM - 4
    mean, rstd = stats_of(total_of(st), count)
    scale = params[0:1] * rstd
    shift = params[1:2] - mean * scale
    lo, hi = bounds[0].astype(F32), bounds[1].astype(F32)
    edge = edge_mask(bounds, g)
    sums = [jnp.zeros((8, g.c), F32) for _ in range(4)]
    for s in range(g.s):
        for r in range(rows_in):
            start = (s * rows_in + r) * g.wp
            row = jnp.maximum(z1[start : start + g.wp, :] * scale + shift, 0.0)
            store_shifted(h_ref, start, in_grid(row, r + 1, g, lo, hi, edge))
        for r in range(0, rows_out, chunk):
            base = (s * rows_in + r) * g.wp
            size = chunk * g.wp
            lhs = jnp.concatenate(
                [h_ref[base + a * g.wp : base + a * g.wp + size, :] for a in range(3)], axis=1
            )
            acc = dot(lhs, w[...])
            z_ref[(s * rows_out + r) * g.wp : (s * rows_out + r) * g.wp + size, :] = acc
            for i in range(chunk):
                if RIM <= r + i + 2 < RIM + g.h:
                    own = acc[i * g.wp : i * g.wp + g.w]
                    dn = cot[s, r + i + 2 - RIM].astype(F32)
                    for k, v in enumerate((own, own * own, dn, dn * own)):
                        sums[k] = sums[k] + sum_rows(v)
    to_all(st_ref, [jnp.sum(v, 0, keepdims=True) for v in sums])


def kernel_gradient(g, core, field, rows_field, first_row, dt_ref, keep, send):
    chans, half = g.c, g.c // 2
    mine = pl.multiple_of(core * half, half)
    other = pl.multiple_of((1 - core) * half, half)
    span = g.h * g.wp
    for a in range(3):
        acc = None
        for s in range(g.s):
            lanes = slice(s * span, (s + 1) * span)
            lhs = jnp.concatenate(
                [dt_ref[pl.ds(mine, half), lanes], dt_ref[pl.ds(other, half), lanes]], axis=0
            )
            start = (s * rows_field + first_row + a) * g.wp
            term = dot(lhs, field[start : start + span, :])
            acc = term if acc is None else acc + term
        for b in range(3):
            keep[a * 3 + b] = acc[0:half, b * chans : (b + 1) * chans]
            send[a * 3 + b] = acc[half:, b * chans : (b + 1) * chans]


def second_gradient_kernel(
    g, count, bounds, z2, st, params, cot_up, cot, cot_down, cot_edges, x, h,
    out_ref, d_ref, keep, send, dt_ref
):
    rows = g.h + 2 * RIM - 4
    total = total_of(st)
    mean, rstd = stats_of(total, count)
    scale, shift = params[2:3], params[3:4]
    sum_dn = total[2:3]
    sum_dx = rstd * (total[3:4] - mean * sum_dn)
    k0 = scale * rstd
    k1 = k0 * (sum_dn / count)
    k2 = k0 * rstd * (sum_dx / count)
    out_scale = scale * rstd
    lo, hi = bounds[0].astype(F32), bounds[1].astype(F32)
    edge = edge_mask(bounds, g)
    x_rows = g.h + 2 * RIM
    rim = RIM - 2
    for s in range(g.s):
        for i in range(rows):
            r = i + 2
            start = (s * rows + i) * g.wp
            source, place = (
                (cot_up, i)
                if i < rim
                else (cot, i - rim)
                if i < rim + g.h
                else (cot_down, i - rim - g.h)
            )
            dn = jnp.concatenate(
                [source[s, place].astype(F32), cot_edges[s, i].astype(F32)], axis=0
            )
            centred = z2[start : start + g.wp, :] - mean
            d = in_grid(k0 * dn - k1 - centred * k2, r, g, lo, hi, edge)
            store_shifted(d_ref, start, d)
            if RIM <= r < RIM + g.h:
                centre = (s * x_rows + r) * g.wp
                masked = x[centre : centre + g.wp, g.c : 2 * g.c].astype(F32)[: g.w]
                out_ref[s, r - RIM] = (
                    masked + (centred[: g.w] * out_scale + shift)
                ).astype(BF16)
                own = jnp.concatenate(
                    [d[: g.w], jnp.zeros((g.wp - g.w, g.c), F32)], axis=0
                )
                at = (s * g.h + r - RIM) * g.wp
                dt_ref[:, at : at + g.wp] = own.astype(BF16).T if False else own.T.astype(BF16)
    kernel_gradient(g, bounds[4], h, g.h + 2 * RIM - 2, RIM - 2, dt_ref, keep, send)


def transposed_conv(g, d_ref, w, s, rows_in, r, chunk):
    acc = None
    size = chunk * g.wp
    for a in range(3):
        start = (s * rows_in + r + a) * g.wp
        for b in range(3):
            tap = (2 - a) * 3 + (2 - b)
            term = dot_nt(
                d_ref[start : start + size, b * g.c : (b + 1) * g.c],
                w[tap * g.c : (tap + 1) * g.c, :],
            )
            acc = term if acc is None else acc + term
    return acc


def hidden_gradient_kernel(g, chunk, count, d, w, z1, st, params, dn_ref, st_ref):
    rows_in, rows_out, z_rows = g.h + 2 * RIM - 4, g.h + 2 * RIM - 6, g.h + 2 * RIM - 2
    mean, rstd = stats_of(total_of(st), count)
    scale = params[0:1] * rstd
    shift = params[1:2] - mean * scale
    s0 = jnp.zeros((8, g.c), F32)
    s1 = jnp.zeros((8, g.c), F32)
    for s in range(g.s):
        for r in range(0, rows_out, chunk):
            acc = transposed_conv(g, d, w, s, rows_in, r, chunk)
            at = (s * z_rows + r + 2) * g.wp
            z = z1[at : at + chunk * g.wp, :]
            dn = jnp.where(z * scale + shift > 0, acc, 0.0)
            dn_ref[(s * rows_out + r) * g.wp : (s * rows_out + r + chunk) * g.wp, :] = dn
            for i in range(chunk):
                if RIM <= r + i + 3 < RIM + g.h:
                    own = dn[i * g.wp : i * g.wp + g.w]
                    s0 = s0 + sum_rows(own)
                    s1 = s1 + sum_rows(own * (z[i * g.wp : i * g.wp + g.w] - mean))
    to_all(
        st_ref, [jnp.sum(s0, 0, keepdims=True), jnp.sum(s1, 0, keepdims=True) * rstd]
    )


def first_gradient_kernel(
    g, count, bounds, dn_ref, z1, st, st3, params, x, e_ref, keep, send, dt_ref
):
    rows, z_rows = g.h + 2 * RIM - 6, g.h + 2 * RIM - 2
    mean, rstd = stats_of(total_of(st), count)
    total = total_of(st3)
    k0 = params[0:1] * rstd
    k1 = k0 * (total[0:1] / count)
    k2 = k0 * rstd * (total[1:2] / count)
    lo, hi = bounds[0].astype(F32), bounds[1].astype(F32)
    edge = edge_mask(bounds, g)
    for s in range(g.s):
        for i in range(rows):
            r = i + 3
            start = (s * rows + i) * g.wp
            at = (s * z_rows + i + 2) * g.wp
            centred = z1[at : at + g.wp, :] - mean
            d = k0 * dn_ref[start : start + g.wp, :] - k1 - centred * k2
            d = in_grid(d, r, g, lo, hi, edge)
            store_shifted(e_ref, start, d)
            if RIM <= r < RIM + g.h:
                own = jnp.concatenate(
                    [d[: g.w], jnp.zeros((g.wp - g.w, g.c), F32)], axis=0
                )
                place = (s * g.h + r - RIM) * g.wp
                dt_ref[:, place : place + g.wp] = own.T.astype(BF16)
    kernel_gradient(g, bounds[4], x, g.h + 2 * RIM, RIM - 1, dt_ref, keep, send)


def input_gradient_kernel(g, chunk, e, w, cot, mask, out_ref):
    rows_in = g.h + 2 * RIM - 6
    for s in range(g.s):
        for r in range(0, g.h, chunk):
            acc = transposed_conv(g, e, w, s, rows_in, r, chunk)
            for i in range(chunk):
                own = acc[i * g.wp : i * g.wp + g.w]
                out_ref[s, r + i] = (cot[s, r + i].astype(F32) + own) * mask[
                    s, r + i
                ].astype(F32)


def pair_sum_kernel(keep, got, out_ref):
    taps, half, chans = keep.shape
    for t in range(taps):
        total = keep[t] + got[t]
        out_ref[t * chans : (t + 1) * chans, :] = total.T.astype(BF16)


def adamw(weight, grad, first, second, rate):
    first_new = 0.9 * first + 0.1 * grad
    second_new = 0.999 * second + 0.001 * grad * grad
    first_hat = first_new / (1.0 - 0.9**STEP)
    second_hat = second_new / (1.0 - 0.999**STEP)
    weight_new = weight - rate * (first_hat / (jnp.sqrt(second_hat) + 1e-08) + 0.01 * weight)
    return (weight_new, first_new, second_new)


def adamw_kernel(ncols, one, two, w, first, second, grad_ref, w_ref, first_ref, second_ref):
    devices, rows, lanes = one.shape
    for k, part in enumerate((one, two)):
        for half in range(2):
            grad = None
            for source in range(devices):
                if (source // ncols) % 2 == half:
                    term = part[source].astype(F32)
                    grad = term if grad is None else grad + term
            at = pl.ds(2 * half + k, rows, stride=4)
            new = adamw(w[at, :], grad, first[at, :], second[at, :], 0.02)
            grad_ref[at, :] = grad
            w_ref[at, :], first_ref[at, :], second_ref[at, :] = new


def shifted(block, axis, step):
    count = lax.axis_size(axis)
    pairs = [(i, i + step) for i in range(count) if 0 <= i + step < count]
    return lax.ppermute(block, axis, pairs)


def to_chunks(flat):
    return flat.reshape(2, -1, 128).transpose(1, 0, 2).reshape(-1, 128)


def from_chunks(rows):
    return rows.reshape(-1, 2, 128).transpose(1, 0, 2).reshape(2, -1)


def exchange(parts):
    return lax.all_to_all(parts, BOTH, 0, 0, tiled=True)


def body(
    features,
    occupancy,
    cotangent,
    conv_weights,
    conv_first,
    conv_second,
    norm_scale_bias,
    norm_first,
    norm_second,
):
    scenes, height, width, chans = features.shape
    g = Geometry(scenes, height, width, chans)
    wp = g.wp
    nrows, ncols = lax.axis_size("rows"), lax.axis_size("cols")
    devices = nrows * ncols
    count = float(scenes * height * width * devices)
    row, col = lax.axis_index("rows"), lax.axis_index("cols")
    bounds = jnp.stack(
        [row > 0, row < nrows - 1, col < ncols - 1, col > 0, row % 2 == 1]
    ).astype(jnp.int32)
    half = height // 2

    maskb = jnp.broadcast_to(occupancy.astype(BF16)[..., None], features.shape)
    top = features[:, :half] * occupancy[:, :half].astype(BF16)[..., None]
    bottom = features[:, half:] * occupancy[:, half:].astype(BF16)[..., None]
    up = shifted(bottom, "rows", 1)
    down = shifted(top, "rows", -1)
    tall = jnp.concatenate([up, top, bottom, down], axis=1)
    right = shifted(tall[:, :, :RIM], "cols", -1)
    left = shifted(tall[:, :, width - RIM :], "cols", 1)
    edges = jnp.concatenate([right, left], axis=2)

    rim = RIM - 2
    cot_up = shifted(cotangent[:, height - rim :], "rows", 1)
    cot_down = shifted(cotangent[:, :rim], "rows", -1)
    cot_tall = jnp.concatenate([cot_up, cotangent, cot_down], axis=1)
    cot_right = shifted(cot_tall[:, :, :rim], "cols", -1)
    cot_left = shifted(cot_tall[:, :, width - rim :], "cols", 1)
    gap = jnp.zeros((scenes, height + 2 * rim, 2 * RIM - 2 * rim, chans), BF16)
    cot_edges = jnp.concatenate([cot_right, gap, cot_left], axis=2)

    chunked = to_chunks(conv_weights)
    taps = 9 * chans
    w1, w2 = kernel_call(
        prepare_kernel, [shape_of((taps, chans), BF16)] * 2, 0
    )(chunked)

    rows1, rows2, rows3 = height + 2 * RIM - 2, height + 2 * RIM - 4, height + 2 * RIM - 6
    n0, n1, n2, n3 = (
        scenes * wp * r for r in (height + 2 * RIM, rows1, rows2, rows3)
    )

    def conv_flops(n):
        return 2 * n * taps * chans

    x, z1, st = kernel_call(
        functools.partial(first_conv_kernel, g, 7),
        [
            shape_of((n0, 3 * chans), BF16),
            shape_of((n1, chans), F32),
            shape_of((devices, 2, chans), F32),
        ],
        conv_flops(n1),
    )(up, top, bottom, down, edges, w1)
    st1 = exchange(st)
    h, z2, st = kernel_call(
        functools.partial(second_conv_kernel, g, 6, count),
        [
            shape_of((n1, 3 * chans), BF16),
            shape_of((n2, chans), F32),
            shape_of((devices, 4, chans), F32),
        ],
        conv_flops(n2),
        smem=(0,),
    )(bounds, z1, st1, norm_scale_bias, w2, cotangent)
    st2 = exchange(st)
    grad_shape = shape_of((9, chans // 2, chans), F32)
    own_pixels = scenes * height * wp
    block_out, d, keep2, send2 = kernel_call(
        functools.partial(second_gradient_kernel, g, count),
        [
            shape_of(features.shape, BF16),
            shape_of((n2, 3 * chans), BF16),
            grad_shape,
            grad_shape,
        ],
        conv_flops(own_pixels),
        smem=(0,),
        scratch=[pltpu.VMEM((chans, own_pixels), BF16)],
    )(bounds, z2, st2, norm_scale_bias, cot_up, cotangent, cot_down, cot_edges, x, h)
    pairs = [(i, i ^ 1) for i in range(nrows)]
    got2 = lax.ppermute(send2, "rows", pairs)
    dn1, st = kernel_call(
        functools.partial(hidden_gradient_kernel, g, 5, count),
        [shape_of((n3, chans), F32), shape_of((devices, 2, chans), F32)],
        conv_flops(n3),
    )(d, w2, z1, st1, norm_scale_bias)
    st3 = exchange(st)
    add_pair = kernel_call(pair_sum_kernel, [shape_of((taps, chans // 2), BF16)], 0)
    (part2,) = add_pair(keep2, got2)
    share_rows = taps // devices
    parts2 = exchange(part2.reshape(devices, share_rows, chans // 2))
    e, keep1, send1 = kernel_call(
        functools.partial(first_gradient_kernel, g, count),
        [shape_of((n3, 3 * chans), BF16), grad_shape, grad_shape],
        conv_flops(own_pixels),
        smem=(0,),
        scratch=[pltpu.VMEM((chans, own_pixels), BF16)],
    )(bounds, dn1, z1, st1, st3, norm_scale_bias, x)
    got1 = lax.ppermute(send1, "rows", pairs)
    (part1,) = add_pair(keep1, got1)
    parts1 = exchange(part1.reshape(devices, share_rows, chans // 2))
    (grad_input,) = kernel_call(
        functools.partial(input_gradient_kernel, g, 8),
        [shape_of(features.shape, F32)],
        conv_flops(own_pixels),
    )(e, w1, cotangent, maskb)

    share = conv_first.shape[1]
    start = (row * ncols + col) * (share // 64)
    own_weights = lax.dynamic_slice_in_dim(chunked, start, share // 64, 0)
    chunk_shape = shape_of((share // 64, 128), F32)
    updated = kernel_call(
        functools.partial(adamw_kernel, ncols), [chunk_shape] * 4, 0
    )(parts1, parts2, own_weights, to_chunks(conv_first), to_chunks(conv_second))
    conv_grads, conv_new, conv_first_new, conv_second_new = map(from_chunks, updated)

    total2, total3 = jnp.sum(st2, 0), jnp.sum(st3, 0)
    mean2 = total2[0] / count
    rstd2 = lax.rsqrt(total2[1] / count - mean2 * mean2 + 1e-05)
    norm_grads = jnp.stack(
        [total3[1], total3[0], rstd2 * (total2[3] - mean2 * total2[2]), total2[2]]
    )
    norm_new, norm_first_new, norm_second_new = adamw(
        norm_scale_bias, norm_grads, norm_first, norm_second, 0.75
    )
    return (
        block_out,
        grad_input,
        conv_grads,
        conv_new,
        conv_first_new,
        conv_second_new,
        norm_grads,
        norm_new,
        norm_first_new,
        norm_second_new,
    )


def solution(mesh):
    tile = P(None, "rows", "cols", None)
    share = P(None, ("rows", "cols"))
    return jax.shard_map(
        body,
        mesh=mesh,
        in_specs=(tile, P(None, "rows", "cols"), tile, P(), share, share, P(), P(), P()),
        out_specs=(tile, tile, share, share, share, share, P(), P(), P(), P()),
        check_vma=False,
    )
```

```python
import functools
import math

import jax
import jax.numpy as jnp
from jax import lax
from jax.experimental import pallas as pl
from jax.experimental.pallas import tpu as pltpu
from jax.sharding import PartitionSpec as P

STEP = 5
BOTH = ("rows", "cols")
RIM = 4
F32, BF16 = jnp.float32, jnp.bfloat16


def shape_of(shape, dtype):
    return jax.ShapeDtypeStruct(shape, dtype)


def held(shape, dtype):
    return pltpu.VMEM(shape, dtype)


def stored(shape, dtype):
    return pltpu.HBM(shape, dtype)


def kernel_call(body, out_shape, flops, far=(), far_out=(), scratch=(), limit=16, alias=None, size=4 << 20):
    def call(*operands):
        operands = [
            pltpu.with_memory_space_constraint(v, pltpu.HBM if i in far else pltpu.VMEM)
            for i, v in enumerate(operands)
        ]
        specs = [
            pl.BlockSpec(memory_space=pltpu.HBM if i in far else pltpu.VMEM)
            for i in range(len(operands))
        ]
        return pl.pallas_call(
            body,
            out_shape=out_shape,
            in_specs=specs,
            out_specs=[
                pl.BlockSpec(memory_space=pltpu.HBM if i in far_out else pltpu.VMEM)
                for i in range(len(out_shape))
            ],
            scratch_shapes=list(scratch),
            input_output_aliases=alias or {},
            compiler_params=pltpu.CompilerParams(vmem_limit_bytes=limit << 20),
            cost_estimate=pl.CostEstimate(
                flops=int(flops), bytes_accessed=size, transcendentals=0
            ),
        )(*operands)

    return call


def dot(a, b):
    return jnp.dot(a, b, preferred_element_type=F32)


def dot_nt(a, b):
    return lax.dot_general(a, b, (((1,), (1,)), ((), ())), preferred_element_type=F32)


def total_of(ref):
    count = ref.shape[0]
    total = ref[0]
    for i in range(1, count):
        total = total + ref[i]
    return total


def to_all(ref, parts):
    value = jnp.concatenate(parts, axis=0)
    for i in range(ref.shape[0]):
        ref[i] = value


def store_shifted(ref, start, row):
    width, chans = row.shape
    at = pl.ds(start if isinstance(start, int) else pl.multiple_of(start, 16), width)
    ref[at, 0:chans] = pltpu.roll(row, 1, 0).astype(BF16)
    ref[at, chans : 2 * chans] = row.astype(BF16)
    ref[at, 2 * chans : 3 * chans] = pltpu.roll(row, width - 1, 0).astype(BF16)


class Geometry:
    def __init__(self, scenes, height, width, chans):
        self.s, self.h, self.w, self.c = scenes, height, width, chans
        self.wp = width + 2 * RIM
        self.tall = height + 2 * RIM
        self.near = RIM // 2
        self.cot_tall = height + 2 * self.near
        self.side = (RIM + self.near) * height


class Place:
    def __init__(self):
        row, col = lax.axis_index("rows"), lax.axis_index("cols")
        nrows, ncols = lax.axis_size("rows"), lax.axis_size("cols")
        self.above = (row > 0).astype(F32)
        self.below = (row < nrows - 1).astype(F32)
        self.right = (col < ncols - 1).astype(F32)
        self.left = (col > 0).astype(F32)
        self.core = row % 2
        self.odd_row = row % 2 == 1
        self.odd_col = col % 2 == 1
        self.index = row * ncols + col


def wide(ref, *index):
    return ref[index].astype(F32)


def far_row(rb, rb_edge, s, k):
    return jnp.concatenate([wide(rb, s, k), wide(rb_edge, s, k)], axis=0)


def pixel_mask(occ, s):
    return occ[s].astype(F32).T


def in_grid(row, r, g, place, edge):
    row = jnp.concatenate([row[: g.w], row[g.w :] * edge], axis=0)
    if r < RIM:
        row = row * place.above
    elif r >= RIM + g.h:
        row = row * place.below
    return row


def edge_mask(place, g):
    where = lax.broadcasted_iota(jnp.int32, (2 * RIM, g.c), 0)
    return jnp.where(where < RIM, place.right, place.left)


def sum_rows(value):
    rows, chans = value.shape
    return jnp.sum(value.reshape(rows // 8, 8, chans), axis=0)


def pack_kernel(g, features, occ_far, cot, own, c_ref, d_ref, b_ref, given, seen, occ, sems):
    copies = []
    flags = pltpu.make_async_copy(occ_far, occ, sems.at[2, 0])
    flags.start()
    for s in range(g.s):
        copies.append(
            (
                pltpu.make_async_copy(features.at[s], given.at[s], sems.at[0, s]),
                pltpu.make_async_copy(cot.at[s], seen.at[s], sems.at[1, s]),
            )
        )
        for copy in copies[-1]:
            copy.start()
    odd, odd_row = Place().odd_col, Place().odd_row
    flags.wait()

    def put(s, at, rights, lefts):
        right, left = jnp.concatenate(rights, axis=0), jnp.concatenate(lefts, axis=0)
        c_ref[s, at : at + 16] = jnp.where(odd, left, right).astype(BF16)
        d_ref[s, at : at + 16] = jnp.where(odd, right, left).astype(BF16)

    for s in range(g.s):
        mask = pixel_mask(occ, s)
        for copy in copies[s]:
            copy.wait()
        rows = []
        for r in range(g.h):
            row = wide(given, s, r) * mask[:, r : r + 1]
            rows.append(row)
            own[s, r] = row.astype(BF16)
        cots = [wide(seen, s, r) for r in range(g.h)]
        for k in range(RIM):
            b_ref[s, k] = jnp.where(odd_row, rows[g.h - RIM + k], rows[k]).astype(BF16)
        for k in range(g.near):
            b_ref[s, RIM + k] = jnp.where(odd_row, cots[g.h - g.near + k], cots[k]).astype(BF16)
        for width, at, field in ((RIM, 0, rows), (g.near, RIM * g.h, cots)):
            for k in range(0, g.h, 16 // width):
                group = field[k : k + 16 // width]
                put(s, at + width * k, [v[g.w - width :] for v in group], [v[:width] for v in group])


def assemble_kernel(g, own, cot, rc, rd, ext, cot_ext, a_ref, b_edge):
    place = Place()

    def rows_of(source, s, at, width):
        gap = jnp.zeros((2 * RIM - 2 * width, g.c), F32)
        rows = []
        for first in range(0, g.h, 16 // width):
            k = at + width * first
            c, d = wide(rc, s, slice(k, k + 16)), wide(rd, s, slice(k, k + 16))
            right, left = jnp.where(place.odd_col, d, c), jnp.where(place.odd_col, c, d)
            for r in range(first, min(g.h, first + 16 // width)):
                at_row = slice(width * (r - first), width * (r - first + 1))
                parts = [wide(source, s, r), right[at_row], gap, left[at_row]]
                rows.append(jnp.concatenate([p for p in parts if p.shape[0]], axis=0))
        return rows

    odd = place.odd_row
    for s in range(g.s):
        rows = rows_of(own, s, 0, RIM)
        top, bottom = rows[:RIM], rows[g.h - RIM :]
        for r in range(g.h):
            ext[s, r] = rows[r].astype(BF16)
        for k in range(RIM):
            a_ref[s, k] = jnp.where(odd, top[k], bottom[k]).astype(BF16)
            b_edge[s, k] = jnp.where(odd, bottom[k], top[k])[g.w :].astype(BF16)
        rows = rows_of(cot, s, RIM * g.h, g.near)
        for r in range(g.h):
            cot_ext[s, r] = rows[r].astype(BF16)
        for k in range(g.near):
            top, bottom = rows[k], rows[g.h - g.near + k]
            a_ref[s, RIM + k] = jnp.where(odd, top, bottom).astype(BF16)
            b_edge[s, RIM + k] = jnp.where(odd, bottom, top)[g.w :].astype(BF16)


def prepare_kernel(w_ref, one_ref, two_ref, buffer, sems):
    chans = one_ref.shape[1]
    taps, size, lanes = buffer.shape
    per = chans // lanes
    copies = [
        pltpu.make_async_copy(w_ref.at[pl.ds(t * size, size)], buffer.at[t], sems.at[t])
        for t in range(taps)
    ]
    for copy in copies:
        copy.start()
    for t in range(taps):
        copies[t].wait()
        for k, out in enumerate((one_ref, two_ref)):
            parts = [buffer[t, pl.ds(2 * half + k, chans, stride=2 * per), :] for half in range(per)]
            out[t * chans : (t + 1) * chans, :] = jnp.concatenate(parts, axis=1).astype(BF16)


def place_shifted(ref, row_index, row):
    store_shifted(ref, row_index * row.shape[0], row)


def window_rows(g, x_ref, first, count):
    size = count * g.wp
    return jnp.concatenate(
        [x_ref[(first + a) * g.wp : (first + a) * g.wp + size, :] for a in range(3)], axis=1
    )


def own_conv_kernel(g, ext, w, z_ref, st_ref, x_ref):
    count = g.h - 2
    s1 = jnp.zeros((8, g.c), F32)
    s2 = jnp.zeros((8, g.c), F32)
    for s in range(g.s):
        for r in range(g.h):
            place_shifted(x_ref, s * g.h + r, wide(ext, s, r))
        half = count // 2
        for first in range(0, count, half):
            acc = dot(window_rows(g, x_ref, s * g.h + first, half), w[...])
            at = (s * (g.tall - 2) + RIM + first) * g.wp
            z_ref[at : at + half * g.wp, :] = acc
            for i in range(half):
                v = acc[i * g.wp : i * g.wp + g.w]
                s1 = s1 + sum_rows(v)
                s2 = s2 + sum_rows(v * v)
    st_ref[0:8] = s1
    st_ref[8:16] = s2


def rim_conv_kernel(g, ext, ra, rb, rb_edge, w, st_in, z_in, z_ref, st_ref, x_ref):
    del z_in
    odd = Place().odd_row
    s1, s2 = st_in[0:8], st_in[8:16]
    span = RIM + 2
    for s in range(g.s):
        for side in range(2):
            base = span * (2 * s + side)
            for k in range(RIM):
                near, far = wide(ra, s, k), far_row(rb, rb_edge, s, k)
                row = jnp.where(odd, near, far) if side == 0 else jnp.where(odd, far, near)
                place_shifted(x_ref, base + 2 * side + k, row)
            for j in range(2):
                own = wide(ext, s, (g.h - 2) * side + j)
                place_shifted(x_ref, base + RIM * (1 - side) + j, own)
            acc = dot(window_rows(g, x_ref, base, RIM), w[...])
            at = (s * (g.tall - 2) + (g.h + RIM - 2) * side) * g.wp
            z_ref[at : at + RIM * g.wp, :] = acc
            i = 0 if side else RIM - 1
            v = acc[i * g.wp : i * g.wp + g.w]
            s1 = s1 + sum_rows(v)
            s2 = s2 + sum_rows(v * v)
    to_all(st_ref, [jnp.sum(s1, 0, keepdims=True), jnp.sum(s2, 0, keepdims=True)])


def stats_of(total, count):
    mean = total[0:1] / count
    var = total[1:2] / count - mean * mean
    return mean, lax.rsqrt(var + 1e-05)


def second_conv_kernel(g, chunk, count, z1, st, params, w, cot, h_ref, z_ref, st_ref):
    rows_in, rows_out = g.tall - 2, g.tall - 4
    place = Place()
    mean, rstd = stats_of(total_of(st), count)
    scale = params[0:1] * rstd
    shift = params[1:2] - mean * scale
    edge = edge_mask(place, g)
    sums = [jnp.zeros((8, g.c), F32) for _ in range(4)]
    for s in range(g.s):
        for r in range(rows_in):
            start = (s * rows_in + r) * g.wp
            row = jnp.maximum(z1[start : start + g.wp, :] * scale + shift, 0.0)
            store_shifted(h_ref, start, in_grid(row, r + 1, g, place, edge))
        for r in range(0, rows_out, chunk):
            base = (s * rows_in + r) * g.wp
            size = chunk * g.wp
            lhs = jnp.concatenate(
                [h_ref[base + a * g.wp : base + a * g.wp + size, :] for a in range(3)], axis=1
            )
            acc = dot(lhs, w[...])
            z_ref[(s * rows_out + r) * g.wp : (s * rows_out + r) * g.wp + size, :] = acc
            for i in range(chunk):
                if RIM <= r + i + 2 < RIM + g.h:
                    v = acc[i * g.wp : i * g.wp + g.w]
                    dn = wide(cot, s, r + i + 2 - RIM)[: g.w]
                    for k, term in enumerate((v, v * v, dn, dn * v)):
                        sums[k] = sums[k] + sum_rows(term)
    to_all(st_ref, [jnp.sum(v, 0, keepdims=True) for v in sums])


def own_transposed(g, source, first, lane, s, dt_ref):
    span = g.h * g.wp
    block = source[first : first + span, lane : lane + g.c]
    inside = lax.broadcasted_iota(jnp.int32, (span, 1), 0) % g.wp < g.w
    dt_ref[:, s * span : (s + 1) * span] = jnp.where(inside, block, jnp.zeros_like(block)).T


def kernel_gradient(g, core, field, rows_field, first_row, dt_ref, keep, send):
    chans, half = g.c, g.c // 2
    span = g.h * g.wp
    mine = pl.ds(pl.multiple_of(core * half, half), half)
    other = pl.ds(pl.multiple_of((1 - core) * half, half), half)
    lhs = jnp.concatenate([dt_ref[mine, :], dt_ref[other, :]], axis=0)
    for a in range(3):
        starts = [(s * rows_field + first_row + a) * g.wp for s in range(g.s)]
        acc = dot(lhs, jnp.concatenate([field[at : at + span, :] for at in starts], axis=0))
        for b in range(3):
            keep[a * 3 + b] = acc[0:half, b * chans : (b + 1) * chans]
            send[a * 3 + b] = acc[half:, b * chans : (b + 1) * chans]


def second_gradient_kernel(
    g, count, z2, st, params, ext, cot, ra, rb, rb_edge, h, out_ref, d_ref, keep, send, dt_ref
):
    place = Place()
    rows = g.cot_tall
    total = total_of(st)
    mean, rstd = stats_of(total, count)
    sum_dn = total[2:3]
    sum_dx = rstd * (total[3:4] - mean * sum_dn)
    k0 = params[2:3] * rstd
    k1 = k0 * (sum_dn / count)
    k2 = k0 * rstd * (sum_dx / count)
    shift = params[3:4]
    edge = edge_mask(place, g)

    def cotangent(s, i):
        if g.near <= i < g.near + g.h:
            return wide(cot, s, i - g.near)
        k = i if i < g.near else i - g.near - g.h
        k += RIM
        return jnp.where(
            place.odd_row == (i < g.near), wide(ra, s, k), far_row(rb, rb_edge, s, k)
        )

    for s in range(g.s):
        for i in range(rows):
            r = i + RIM - g.near
            start = (s * rows + i) * g.wp
            centred = z2[start : start + g.wp, :] - mean
            d = k0 * cotangent(s, i) - k1 - centred * k2
            store_shifted(d_ref, start, in_grid(d, r, g, place, edge))
            if RIM <= r < RIM + g.h:
                masked = wide(ext, s, r - RIM)[: g.w]
                out_ref[s, r - RIM] = (masked + (centred[: g.w] * k0 + shift)).astype(BF16)
        own_transposed(g, d_ref, (s * rows + g.near) * g.wp, g.c, s, dt_ref)
    kernel_gradient(g, place.core, h, g.tall - 2, RIM - 2, dt_ref, keep, send)


def transposed_conv(g, d_ref, w, s, rows_in, r, chunk):
    acc = None
    size = chunk * g.wp
    for a in range(3):
        start = (s * rows_in + r + a) * g.wp
        for b in range(3):
            tap = (2 - a) * 3 + (2 - b)
            term = dot_nt(
                d_ref[start : start + size, b * g.c : (b + 1) * g.c],
                w[tap * g.c : (tap + 1) * g.c, :],
            )
            acc = term if acc is None else acc + term
    return acc


def hidden_gradient_kernel(g, chunk, count, d, w, z1, st, params, dn_ref, st_ref):
    rows_in, rows_out, z_rows = g.tall - 4, g.tall - 6, g.tall - 2
    mean, rstd = stats_of(total_of(st), count)
    scale = params[0:1] * rstd
    shift = params[1:2] - mean * scale
    s0 = jnp.zeros((8, g.c), F32)
    s1 = jnp.zeros((8, g.c), F32)
    for s in range(g.s):
        for r in range(0, rows_out, chunk):
            acc = transposed_conv(g, d, w, s, rows_in, r, chunk)
            at = (s * z_rows + r + 2) * g.wp
            z = z1[at : at + chunk * g.wp, :]
            dn = jnp.where(z * scale + shift > 0, acc, 0.0)
            dn_ref[(s * rows_out + r) * g.wp : (s * rows_out + r + chunk) * g.wp, :] = dn
            for i in range(chunk):
                if RIM <= r + i + 3 < RIM + g.h:
                    v = dn[i * g.wp : i * g.wp + g.w]
                    s0 = s0 + sum_rows(v)
                    s1 = s1 + sum_rows(v * (z[i * g.wp : i * g.wp + g.w] - mean))
    to_all(st_ref, [jnp.sum(s0, 0, keepdims=True), jnp.sum(s1, 0, keepdims=True) * rstd])


def first_gradient_kernel(
    g, count, dn, z, st, st3, params, ext, ra, rb, rb_edge, e_ref, keep, send, x_ref, dt_ref
):
    place = Place()
    rows = g.tall - 6
    mean, rstd = stats_of(total_of(st), count)
    total = total_of(st3)
    k0 = params[0:1] * rstd
    k1 = k0 * (total[0:1] / count)
    k2 = k0 * rstd * (total[1:2] / count)
    edge = edge_mask(place, g)
    for s in range(g.s):
        for i in range(rows):
            at = (s * rows + i) * g.wp
            z_at = (s * (g.tall - 2) + i + 2) * g.wp
            d = k0 * dn[at : at + g.wp, :] - k1 - (z[z_at : z_at + g.wp, :] - mean) * k2
            e_ref[at : at + g.wp, :] = in_grid(d, i + 3, g, place, edge).astype(BF16)
        own_transposed(g, e_ref, (s * rows + 1) * g.wp, 0, s, dt_ref)
        above = jnp.where(place.odd_row, wide(ra, s, RIM - 1), far_row(rb, rb_edge, s, RIM - 1))
        below = jnp.where(place.odd_row, far_row(rb, rb_edge, s, 0), wide(ra, s, 0))
        for i in range(rows):
            row = above if i == 0 else below if i == rows - 1 else wide(ext, s, i - 1)
            place_shifted(x_ref, s * rows + i, row)
    kernel_gradient(g, place.core, x_ref, rows, 0, dt_ref, keep, send)


def input_gradient_kernel(g, chunk, e, w, cot, occ, master, out_ref, share_ref, e_ref, sem):
    rows_in = g.tall - 6
    start = pl.multiple_of(Place().index * share_ref.shape[0], 8)
    copy = pltpu.make_async_copy(master.at[pl.ds(start, share_ref.shape[0])], share_ref, sem)
    copy.start()
    for s in range(g.s):
        for i in range(rows_in):
            at = (s * rows_in + i) * g.wp
            store_shifted(e_ref, at, wide(e, slice(at, at + g.wp)))
        mask = pixel_mask(occ, s)
        for r in range(0, g.h, chunk):
            acc = transposed_conv(g, e_ref, w, s, rows_in, r, chunk)
            for i in range(chunk):
                v = acc[i * g.wp : i * g.wp + g.w]
                out_ref[s, r + i] = (wide(cot, s, r + i) + v) * mask[:, r + i : r + i + 1]
    copy.wait()


def pair_sum_kernel(keep, got, out_ref):
    taps, half, chans = keep.shape
    for t in range(taps):
        out_ref[t * chans : (t + 1) * chans, :] = (keep[t] + got[t]).astype(BF16).T


def message_kernel(keep, got, second, out_far, out_ref, sems):
    taps, half, chans = keep.shape
    copies = []
    for t in range(taps):
        rows = pl.ds(t * chans, chans)
        total = (keep[t] + got[t]).astype(BF16).T
        out_ref[rows, :] = jnp.concatenate([total, second[rows, :]], axis=1)
        copies.append(pltpu.make_async_copy(out_ref.at[rows], out_far.at[rows], sems.at[t]))
        copies[-1].start()
    for copy in copies:
        copy.wait()


def adamw(weight, grad, first, second, rate):
    first_new = 0.9 * first + 0.1 * grad
    second_new = 0.999 * second + 0.001 * grad * grad
    first_hat = first_new / (1.0 - 0.9**STEP)
    second_hat = second_new / (1.0 - 0.999**STEP)
    weight_new = weight - rate * (first_hat / (jnp.sqrt(second_hat) + 1e-08) + 0.01 * weight)
    return (weight_new, first_new, second_new)


def update_kernel(
    count, parts, w, first, second, st2, st3, params, n_first, n_second,
    grad_out, w_out, first_out, second_out, n_grad, n_out, n_first_out, n_second_out
):
    devices, rows, lanes = parts.shape
    lanes //= 2
    ncols = lax.axis_size("cols")
    total2, total3 = total_of(st2), total_of(st3)
    mean, rstd = stats_of(total2, count)
    sum_dn = total2[2:3]
    grads = jnp.concatenate(
        [total3[1:2], total3[0:1], rstd * (total2[3:4] - mean * sum_dn), sum_dn], axis=0
    )
    n_grad[...] = grads
    n_out[...], n_first_out[...], n_second_out[...] = adamw(
        params[...], grads, n_first[...], n_second[...], 0.75
    )
    grads = []
    for k in range(2):
        for half in range(2):
            grad = None
            for source in range(devices):
                if (source // ncols) % 2 == half:
                    term = wide(parts, source, slice(None), slice(k * lanes, (k + 1) * lanes))
                    grad = term if grad is None else grad + term
            grads.append((pl.ds(2 * half + k, rows, stride=4), grad))
    for at, grad in grads:
        new = adamw(w[at, :], grad, first[at, :], second[at, :], 0.02)
        grad_out[at, :] = grad
        w_out[at, :], first_out[at, :], second_out[at, :] = new


def swapped(block, axis, first):
    count = lax.axis_size(axis)
    pairs = []
    for i in range(first, count - 1, 2):
        pairs += [(i, i + 1), (i + 1, i)]
    return lax.ppermute(block, axis, pairs)


def to_chunks(flat):
    return flat.reshape(2, -1, 128).transpose(1, 0, 2).reshape(-1, 128)


def from_chunks(rows):
    return rows.reshape(-1, 2, 128).transpose(1, 0, 2).reshape(2, -1)


def exchange(parts):
    return lax.all_to_all(parts, BOTH, 0, 0, tiled=True)


def body(
    features,
    occupancy,
    cotangent,
    conv_weights,
    conv_first,
    conv_second,
    norm_scale_bias,
    norm_first,
    norm_second,
):
    scenes, height, width, chans = features.shape
    g = Geometry(scenes, height, width, chans)
    wp = g.wp
    devices = lax.axis_size("rows") * lax.axis_size("cols")
    count = float(scenes * height * width * devices)
    taps = 9 * chans
    n0, n1, n2, n3 = (scenes * wp * (g.tall - 2 * i) for i in range(4))
    own_pixels = scenes * height * wp
    dma = pltpu.SemaphoreType.DMA

    def conv_flops(n):
        return 2 * n * taps * chans

    side = shape_of((scenes, g.side, chans), BF16)
    own, c, d, b = kernel_call(
        functools.partial(pack_kernel, g),
        [
            shape_of(features.shape, BF16),
            side,
            side,
            shape_of((scenes, RIM + g.near, width, chans), BF16),
        ],
        1e8,
        far=(0, 1, 2),
        scratch=[
            pltpu.VMEM(features.shape, BF16),
            pltpu.VMEM(features.shape, BF16),
            pltpu.VMEM(occupancy.shape, jnp.int32),
            dma((3, scenes)),
        ],
    )(features, occupancy, cotangent)
    rb = swapped(b, "rows", 1)
    rc, rd = swapped(c, "cols", 0), swapped(d, "cols", 1)
    chunked = to_chunks(conv_weights)
    share = conv_first.shape[1]
    chunk_shape = shape_of((share // 64, 128), F32)
    weights = (taps, chans)
    w1, w2 = kernel_call(
        prepare_kernel,
        [held(weights, BF16)] * 2,
        0,
        size=1024,
        far=(0,),
        scratch=[pltpu.VMEM((9, chunked.shape[0] // 9, 128), F32), dma((9,))],
    )(chunked)
    rc, w1, w2 = lax.optimization_barrier((rc, w1, w2))

    def wide_rows(rows):
        return shape_of((scenes, rows, wp, chans), BF16)

    ext, cot_ext, a, b_edge = kernel_call(
        functools.partial(assemble_kernel, g),
        [wide_rows(n) for n in (height, height, RIM + g.near)]
        + [shape_of((scenes, RIM + g.near, 2 * RIM, chans), BF16)],
        0,
        size=1024,
    )(own, cotangent, rc, rd)
    z1, st = kernel_call(
        functools.partial(own_conv_kernel, g),
        [held((n1, chans), F32), held((16, chans), F32)],
        0,
        size=1024,
        scratch=[pltpu.VMEM((scenes * height * wp, 3 * chans), BF16)],
    )(ext, w1)
    b_edge, st = lax.optimization_barrier((b_edge, st))
    rb_edge = swapped(b_edge, "rows", 1)
    a, rb, rb_edge = lax.optimization_barrier((a, rb, rb_edge))
    ra = swapped(a, "rows", 0)
    z1, st = kernel_call(
        functools.partial(rim_conv_kernel, g),
        [held((n1, chans), F32), shape_of((devices, 2, chans), F32)],
        0,
        size=1024,
        scratch=[pltpu.VMEM((scenes * 2 * (RIM + 2) * wp, 3 * chans), BF16)],
        alias={6: 0},
    )(ext, ra, rb, rb_edge, w1, st, z1)
    st1 = exchange(st)
    h, z2, st = kernel_call(
        functools.partial(second_conv_kernel, g, 6, count),
        [
            held((n1, 3 * chans), BF16),
            held((n2, chans), F32),
            shape_of((devices, 4, chans), F32),
        ],
        conv_flops(n2),
    )(z1, st1, norm_scale_bias, w2, cot_ext)
    st2 = exchange(st)
    grad_shape = held((9, chans // 2, chans), F32)
    block_out, d, keep2, send2 = kernel_call(
        functools.partial(second_gradient_kernel, g, count),
        [
            shape_of(features.shape, BF16),
            held((n2, 3 * chans), BF16),
            grad_shape,
            grad_shape,
        ],
        conv_flops(own_pixels),
        scratch=[pltpu.VMEM((chans, own_pixels), BF16)],
    )(z2, st2, norm_scale_bias, ext, cot_ext, ra, rb, rb_edge, h)
    got2 = swapped(send2, "rows", 0)
    dn1, st = kernel_call(
        functools.partial(hidden_gradient_kernel, g, 5, count),
        [held((n3, chans), F32), shape_of((devices, 2, chans), F32)],
        conv_flops(n3),
    )(d, w2, z1, st1, norm_scale_bias)
    st, got2 = lax.optimization_barrier((st, got2))
    st3 = exchange(st)
    e, keep1, send1 = kernel_call(
        functools.partial(first_gradient_kernel, g, count),
        [held((n3, chans), BF16), grad_shape, grad_shape],
        conv_flops(own_pixels),
        scratch=[pltpu.VMEM((n3, 3 * chans), BF16), pltpu.VMEM((chans, own_pixels), BF16)],
    )(dn1, z1, st1, st3, norm_scale_bias, ext, ra, rb, rb_edge)
    got1 = swapped(send1, "rows", 0)
    keep2, got2, keep1 = lax.optimization_barrier((keep2, got2, keep1))
    (second,) = kernel_call(pair_sum_kernel, [held((taps, chans // 2), BF16)], 1e9)(keep2, got2)
    (parts,) = kernel_call(
        message_kernel,
        [stored((taps, chans), BF16)],
        1e9,
        far_out=(0,),
        scratch=[pltpu.VMEM((taps, chans), BF16), dma((9,))],
    )(keep1, got1, second)
    parts = exchange(parts.reshape(devices, taps // devices, chans))
    grad_input, own_weights = kernel_call(
        functools.partial(input_gradient_kernel, g, 8),
        [shape_of(features.shape, F32), chunk_shape],
        conv_flops(own_pixels),
        far=(4,),
        scratch=[pltpu.VMEM((n3, 3 * chans), BF16), dma],
    )(e, w1, cotangent, occupancy, chunked)

    norm_shape = shape_of(norm_first.shape, F32)
    updated = kernel_call(
        functools.partial(update_kernel, count),
        [chunk_shape] * 4 + [norm_shape] * 4,
        1e8,
    )(
        parts, own_weights, to_chunks(conv_first), to_chunks(conv_second), st2, st3,
        norm_scale_bias, norm_first, norm_second,
    )
    return (block_out, grad_input, *map(from_chunks, updated[:4]), *updated[4:])


def solution(mesh):
    tile = P(None, "rows", "cols", None)
    share = P(None, ("rows", "cols"))
    return jax.shard_map(
        body,
        mesh=mesh,
        in_specs=(tile, P(None, "rows", "cols"), tile, P(), share, share, P(), P(), P()),
        out_specs=(tile, tile, share, share, share, share, P(), P(), P(), P()),
        check_vma=False,
    )
```

```python
import functools
import math

import jax
import jax.numpy as jnp
from jax import lax
from jax.experimental import pallas as pl
from jax.experimental.pallas import tpu as pltpu
from jax.sharding import PartitionSpec as P

STEP = 5
BOTH = ("rows", "cols")
RIM = 3
COLS = 4
SIDE = 2 * COLS
F32, BF16 = jnp.float32, jnp.bfloat16


def shape_of(shape, dtype):
    return jax.ShapeDtypeStruct(shape, dtype)


def held(shape, dtype):
    return pltpu.VMEM(shape, dtype)


def stored(shape, dtype):
    return pltpu.HBM(shape, dtype)


def kernel_call(body, out_shape, flops, far=(), far_out=(), scratch=(), limit=16, alias=None, size=4 << 20):
    def call(*operands):
        operands = [
            pltpu.with_memory_space_constraint(v, pltpu.HBM if i in far else pltpu.VMEM)
            for i, v in enumerate(operands)
        ]
        specs = [
            pl.BlockSpec(memory_space=pltpu.HBM if i in far else pltpu.VMEM)
            for i in range(len(operands))
        ]
        return pl.pallas_call(
            body,
            out_shape=out_shape,
            in_specs=specs,
            out_specs=[
                pl.BlockSpec(memory_space=pltpu.HBM if i in far_out else pltpu.VMEM)
                for i in range(len(out_shape))
            ],
            scratch_shapes=list(scratch),
            input_output_aliases=alias or {},
            compiler_params=pltpu.CompilerParams(vmem_limit_bytes=limit << 20),
            cost_estimate=pl.CostEstimate(
                flops=int(flops), bytes_accessed=size, transcendentals=0
            ),
        )(*operands)

    return call


def dot(a, b):
    return jnp.dot(a, b, preferred_element_type=F32)


def dot_nt(a, b):
    return lax.dot_general(a, b, (((1,), (1,)), ((), ())), preferred_element_type=F32)


def total_of(ref):
    count = ref.shape[0]
    total = ref[0]
    for i in range(1, count):
        total = total + ref[i]
    return total


def to_all(ref, parts):
    value = jnp.concatenate(parts, axis=0)
    for i in range(ref.shape[0]):
        ref[i] = value


def store_shifted(ref, start, row, offsets=(0, 1, 2)):
    width, chans = row.shape
    for b in offsets:
        moved = row if b == 1 else pltpu.roll(row, 1 if b == 0 else width - 1, 0)
        ref[start : start + width, b * chans : (b + 1) * chans] = moved.astype(BF16)


class Geometry:
    def __init__(self, scenes, height, width, chans):
        self.s, self.h, self.w, self.c = scenes, height, width, chans
        self.wp = width + SIDE
        self.tall = height + 2 * RIM
        self.near = RIM - 2
        self.near_cols = COLS - 2
        self.cot_tall = height + 2 * self.near
        self.side = (COLS + self.near_cols) * height
        self.corner = -(-(COLS * RIM + self.near_cols * self.near) // 16) * 16


class Place:
    def __init__(self):
        row, col = lax.axis_index("rows"), lax.axis_index("cols")
        nrows, ncols = lax.axis_size("rows"), lax.axis_size("cols")
        self.above = (row > 0).astype(F32)
        self.below = (row < nrows - 1).astype(F32)
        self.right = (col < ncols - 1).astype(F32)
        self.left = (col > 0).astype(F32)
        self.core = row % 2
        self.odd_row = row % 2 == 1
        self.odd_col = col % 2 == 1
        self.index = row * ncols + col


def wide(ref, *index):
    return ref[index].astype(F32)


def far_rows(g, place, rb, rb_c, rb_d, s):
    right, left = sides(g, place, rb_c, rb_d, s)
    rows = []
    for k in range(RIM + g.near):
        width = COLS if k < RIM else g.near_cols
        at = COLS * min(k, RIM) + g.near_cols * max(k - RIM, 0)
        rows.append(
            jnp.concatenate([wide(rb, s, k), side_columns(g, right, left, at, width)], axis=0)
        )
    return rows


def pixel_mask(occ, s):
    return occ[s].astype(F32).T


def in_grid(row, r, g, place, edge):
    row = jnp.concatenate([row[: g.w], row[g.w :] * edge], axis=0)
    if r < RIM:
        row = row * place.above
    elif r >= RIM + g.h:
        row = row * place.below
    return row


def edge_mask(place, g):
    where = lax.broadcasted_iota(jnp.int32, (SIDE, g.c), 0)
    return jnp.where(where < SIDE // 2, place.right, place.left)


def sum_rows(value):
    rows, chans = value.shape
    return jnp.sum(value.reshape(rows // 8, 8, chans), axis=0)


def pack_kernel(
    g, features, occ_far, cot, own, c_ref, d_ref, b_ref, bc_ref, bd_ref, given, seen, occ, sems
):
    copies = []
    flags = pltpu.make_async_copy(occ_far, occ, sems.at[2, 0])
    flags.start()
    for s in range(g.s):
        copies.append(
            (
                pltpu.make_async_copy(features.at[s], given.at[s], sems.at[0, s]),
                pltpu.make_async_copy(cot.at[s], seen.at[s], sems.at[1, s]),
            )
        )
        for copy in copies[-1]:
            copy.start()
    odd, odd_row = Place().odd_col, Place().odd_row
    flags.wait()

    for s in range(g.s):
        mask = pixel_mask(occ, s)
        for copy in copies[s]:
            copy.wait()
        rows = []
        for r in range(g.h):
            row = wide(given, s, r) * mask[:, r : r + 1]
            rows.append(row)
            own[s, r] = row.astype(BF16)
        cots = [wide(seen, s, r) for r in range(g.h)]
        ends = []
        for field, count in ((rows, RIM), (cots, g.near)):
            for k in range(count):
                ends.append(jnp.where(odd_row, field[g.h - count + k], field[k]))
                b_ref[s, len(ends) - 1] = ends[-1].astype(BF16)
        spare = jnp.zeros((g.corner - COLS * RIM - g.near_cols * g.near, g.c), F32)
        widths = [COLS] * RIM + [g.near_cols] * g.near
        right = [v[g.w - width :] for v, width in zip(ends, widths, strict=True)]
        left = [v[:width] for v, width in zip(ends, widths, strict=True)]
        right, left = (jnp.concatenate(v + [spare], axis=0) for v in (right, left))
        bc_ref[s] = jnp.where(odd, left, right).astype(BF16)
        bd_ref[s] = jnp.where(odd, right, left).astype(BF16)
        right = jnp.concatenate(
            [v[g.w - COLS :] for v in rows] + [v[g.w - g.near_cols :] for v in cots], axis=0
        )
        left = jnp.concatenate([v[:COLS] for v in rows] + [v[: g.near_cols] for v in cots], axis=0)
        c_ref[s] = jnp.where(odd, left, right).astype(BF16)
        d_ref[s] = jnp.where(odd, right, left).astype(BF16)


def sides(g, place, rc, rd, s):
    c, d = wide(rc, s), wide(rd, s)
    return jnp.where(place.odd_col, d, c), jnp.where(place.odd_col, c, d)


def side_columns(g, right, left, at, width):
    parts = [right[at : at + width], jnp.zeros((SIDE - 2 * width, g.c), F32), left[at : at + width]]
    return jnp.concatenate([part for part in parts if part.shape[0]], axis=0)


def assemble_kernel(g, own, cot, rc, rd, ext, cot_ext, a_ref):
    place = Place()

    odd = place.odd_row
    for s in range(g.s):
        right, left = sides(g, place, rc, rd, s)
        for source, full, at, width, count, first in (
            (own, ext, 0, COLS, RIM, 0),
            (cot, cot_ext, COLS * g.h, g.near_cols, g.near, RIM),
        ):
            rows = []
            for r in range(g.h):
                beyond = side_columns(g, right, left, at + width * r, width)
                rows.append(jnp.concatenate([wide(source, s, r), beyond], axis=0))
                full[s, r] = rows[r].astype(BF16)
            for k in range(count):
                top, bottom = rows[k], rows[g.h - count + k]
                a_ref[s, first + k] = jnp.where(odd, top, bottom).astype(BF16)


def prepare_kernel(w_ref, one_ref, two_ref, buffer, sems):
    chans = one_ref.shape[1]
    taps, size, lanes = buffer.shape
    per = chans // lanes
    copies = [
        pltpu.make_async_copy(w_ref.at[pl.ds(t * size, size)], buffer.at[t], sems.at[t])
        for t in range(taps)
    ]
    for copy in copies:
        copy.start()
    for t in range(taps):
        copies[t].wait()
        for k, out in enumerate((one_ref, two_ref)):
            parts = [buffer[t, pl.ds(2 * half + k, chans, stride=2 * per), :] for half in range(per)]
            out[t * chans : (t + 1) * chans, :] = jnp.concatenate(parts, axis=1).astype(BF16)


def place_shifted(ref, row_index, row):
    store_shifted(ref, row_index * row.shape[0], row)


def window_rows(g, x_ref, first, count):
    size = count * g.wp
    return jnp.concatenate(
        [x_ref[(first + a) * g.wp : (first + a) * g.wp + size, :] for a in range(3)], axis=1
    )


def own_conv_kernel(g, ext, w, z_ref, st_ref, x_ref):
    count = g.h - 2
    s1 = jnp.zeros((8, g.c), F32)
    s2 = jnp.zeros((8, g.c), F32)
    for s in range(g.s):
        for r in range(g.h):
            place_shifted(x_ref, s * (g.h + 2) + 1 + r, wide(ext, s, r))
        half = count // 2
        for first in range(0, count, half):
            acc = dot(window_rows(g, x_ref, s * (g.h + 2) + 1 + first, half), w[...])
            at = (s * (g.tall - 2) + RIM + first) * g.wp
            z_ref[at : at + half * g.wp, :] = acc
            for i in range(half):
                v = acc[i * g.wp : i * g.wp + g.w]
                s1 = s1 + sum_rows(v)
                s2 = s2 + sum_rows(v * v)
    st_ref[0:8] = s1
    st_ref[8:16] = s2


def rim_conv_kernel(
    g, ext, ra, rb, rb_c, rb_d, w, st_in, z_in, x_in, z_ref, st_ref, x_own, cot_ref, x_ref
):
    del z_in, x_in
    place = Place()
    odd = place.odd_row
    s1, s2 = st_in[0:8], st_in[8:16]
    span = RIM + 2
    for s in range(g.s):
        far = far_rows(g, place, rb, rb_c, rb_d, s)
        near = [wide(ra, s, k) for k in range(RIM + g.near)]
        for side in range(2):
            base = span * (2 * s + side)
            beyond = [
                jnp.where(odd, b, a) if side else jnp.where(odd, a, b)
                for a, b in zip(near, far, strict=True)
            ]
            for k in range(RIM):
                place_shifted(x_ref, base + 2 * side + k, beyond[k])
            next_row = beyond[0 if side else RIM - 1]
            place_shifted(x_own, s * (g.h + 2) + (g.h + 1) * side, next_row)
            cot_ref[s, side] = beyond[RIM].astype(BF16)
            source = (s * (g.h + 2) + 1 + (g.h - 2) * side) * g.wp
            target = (base + RIM * (1 - side)) * g.wp
            x_ref[target : target + 2 * g.wp, :] = x_own[source : source + 2 * g.wp, :]
            acc = dot(window_rows(g, x_ref, base, RIM), w[...])
            at = (s * (g.tall - 2) + (g.h + RIM - 2) * side) * g.wp
            z_ref[at : at + RIM * g.wp, :] = acc
            i = 0 if side else RIM - 1
            v = acc[i * g.wp : i * g.wp + g.w]
            s1 = s1 + sum_rows(v)
            s2 = s2 + sum_rows(v * v)
    to_all(st_ref, [jnp.sum(s1, 0, keepdims=True), jnp.sum(s2, 0, keepdims=True)])


def stats_of(total, count):
    mean = total[0:1] / count
    var = total[1:2] / count - mean * mean
    return mean, lax.rsqrt(var + 1e-05)


def second_conv_kernel(g, chunk, count, z1, st, params, w, cot, h_ref, z_ref, st_ref):
    rows_in, rows_out = g.tall - 2, g.tall - 4
    place = Place()
    mean, rstd = stats_of(total_of(st), count)
    scale = params[0:1] * rstd
    shift = params[1:2] - mean * scale
    edge = edge_mask(place, g)
    sums = [jnp.zeros((8, g.c), F32) for _ in range(4)]
    for s in range(g.s):
        for r in range(rows_in):
            start = (s * rows_in + r) * g.wp
            row = jnp.maximum(z1[start : start + g.wp, :] * scale + shift, 0.0)
            store_shifted(h_ref, start, in_grid(row, r + 1, g, place, edge))
        for r in range(0, rows_out, chunk):
            base = (s * rows_in + r) * g.wp
            size = chunk * g.wp
            lhs = jnp.concatenate(
                [h_ref[base + a * g.wp : base + a * g.wp + size, :] for a in range(3)], axis=1
            )
            acc = dot(lhs, w[...])
            z_ref[(s * rows_out + r) * g.wp : (s * rows_out + r) * g.wp + size, :] = acc
            for i in range(chunk):
                if RIM <= r + i + 2 < RIM + g.h:
                    v = acc[i * g.wp : i * g.wp + g.w]
                    dn = wide(cot, s, r + i + 2 - RIM)[: g.w]
                    for k, term in enumerate((v, v * v, dn, dn * v)):
                        sums[k] = sums[k] + sum_rows(term)
    to_all(st_ref, [jnp.sum(v, 0, keepdims=True) for v in sums])


def own_transposed(g, source, first, s, dt_ref):
    span = g.h * g.wp
    block = source[first : first + span, :]
    inside = lax.broadcasted_iota(jnp.int32, (span, 1), 0) % g.wp < g.w
    dt_ref[:, s * span : (s + 1) * span] = jnp.where(inside, block, jnp.zeros_like(block)).T


def kernel_gradient(g, core, field, rows_field, first_row, dt_ref, keep, send):
    chans, half = g.c, g.c // 2
    span = g.h * g.wp
    mine = pl.ds(pl.multiple_of(core * half, half), half)
    other = pl.ds(pl.multiple_of((1 - core) * half, half), half)
    lhs = jnp.concatenate([dt_ref[mine, :], dt_ref[other, :]], axis=0)
    for a in range(3):
        starts = [(s * rows_field + first_row + a) * g.wp for s in range(g.s)]
        acc = dot(lhs, jnp.concatenate([field[at : at + span, :] for at in starts], axis=0))
        for b in range(3):
            keep[a * 3 + b] = acc[0:half, b * chans : (b + 1) * chans]
            send[a * 3 + b] = acc[half:, b * chans : (b + 1) * chans]


def second_gradient_kernel(
    g, count, z2, st, params, cot, cot_next, h, d_ref, keep, send, dt_ref
):
    place = Place()
    rows = g.cot_tall
    total = total_of(st)
    mean, rstd = stats_of(total, count)
    sum_dn = total[2:3]
    sum_dx = rstd * (total[3:4] - mean * sum_dn)
    k0 = params[2:3] * rstd
    k1 = k0 * (sum_dn / count)
    k2 = k0 * rstd * (sum_dx / count)
    edge = edge_mask(place, g)
    for s in range(g.s):
        for i in range(rows):
            rim = not g.near <= i < g.near + g.h
            dn = wide(cot_next, s, 0 if i < g.near else 1) if rim else wide(cot, s, i - g.near)
            start = (s * rows + i) * g.wp
            d = k0 * dn - k1 - (z2[start : start + g.wp, :] - mean) * k2
            d = in_grid(d, i + RIM - g.near, g, place, edge)
            d_ref[start : start + g.wp, :] = d.astype(BF16)
        own_transposed(g, d_ref, (s * rows + g.near) * g.wp, s, dt_ref)
    kernel_gradient(g, place.core, h, g.tall - 2, RIM - 2, dt_ref, keep, send)


def transposed_conv(g, d_ref, w, s, rows_in, r, chunk):
    acc = None
    size = chunk * g.wp
    for a in range(3):
        start = (s * rows_in + r + a) * g.wp
        for b in range(3):
            tap = (2 - a) * 3 + (2 - b)
            term = dot_nt(
                d_ref[start : start + size, b * g.c : (b + 1) * g.c],
                w[tap * g.c : (tap + 1) * g.c, :],
            )
            acc = term if acc is None else acc + term
    return acc


def hidden_gradient_kernel(
    g, chunk, count, d, w, z1, z2, st, st2, params, ext, dn_ref, st_ref, out_ref, d_ref
):
    mean2, rstd2 = stats_of(total_of(st2), count)
    scale2 = params[2:3] * rstd2
    shift2 = params[3:4] - mean2 * scale2
    rows_in, rows_out, z_rows = g.tall - 4, g.tall - 6, g.tall - 2
    mean, rstd = stats_of(total_of(st), count)
    scale = params[0:1] * rstd
    shift = params[1:2] - mean * scale
    s0 = jnp.zeros((8, g.c), F32)
    s1 = jnp.zeros((8, g.c), F32)
    for s in range(g.s):
        for i in range(rows_in):
            at = (s * rows_in + i) * g.wp
            store_shifted(d_ref, at, wide(d, slice(at, at + g.wp)))
        for r in range(g.h):
            at = (s * rows_in + r + g.near) * g.wp
            normed = z2[at : at + g.w, :] * scale2 + shift2
            out_ref[s, r] = (wide(ext, s, r)[: g.w] + normed).astype(BF16)
        for r in range(0, rows_out, chunk):
            acc = transposed_conv(g, d_ref, w, s, rows_in, r, chunk)
            at = (s * z_rows + r + 2) * g.wp
            z = z1[at : at + chunk * g.wp, :]
            dn = jnp.where(z * scale + shift > 0, acc, 0.0)
            dn_ref[(s * rows_out + r) * g.wp : (s * rows_out + r + chunk) * g.wp, :] = dn
            for i in range(chunk):
                if RIM <= r + i + 3 < RIM + g.h:
                    v = dn[i * g.wp : i * g.wp + g.w]
                    s0 = s0 + sum_rows(v)
                    s1 = s1 + sum_rows(v * (z[i * g.wp : i * g.wp + g.w] - mean))
    to_all(st_ref, [jnp.sum(s0, 0, keepdims=True), jnp.sum(s1, 0, keepdims=True) * rstd])


def first_gradient_kernel(
    g, count, dn, z, st, st3, params, x, e_ref, a_ref, b_ref, keep, send, dt_ref
):
    place = Place()
    mean, rstd = stats_of(total_of(st), count)
    total = total_of(st3)
    k0 = params[0:1] * rstd
    k1 = k0 * (total[0:1] / count)
    k2 = k0 * rstd * (total[1:2] / count)
    edge = edge_mask(place, g)
    for s in range(g.s):
        for i in range(g.h):
            at = (s * g.h + i) * g.wp
            z_at = (s * (g.tall - 2) + i + RIM - 1) * g.wp
            d = k0 * dn[at : at + g.wp, :] - k1 - (z[z_at : z_at + g.wp, :] - mean) * k2
            d = in_grid(d, i + RIM, g, place, edge)
            e_ref[at : at + g.wp, :] = d.astype(BF16)
            if i == 0:
                top = d
        a_ref[s, 0] = jnp.where(place.odd_row, top, d).astype(BF16)
        b_ref[s, 0] = jnp.where(place.odd_row, d, top).astype(BF16)
        own_transposed(g, e_ref, s * g.h * g.wp, s, dt_ref)
    kernel_gradient(g, place.core, x, g.h + 2, 0, dt_ref, keep, send)


def input_gradient_kernel(
    g, chunk, e, ra, rb, w_far, cot_far, occ, out_ref, w, cot, e_ref, sems
):
    rows_in = g.h + 2
    place = Place()
    copies = [
        pltpu.make_async_copy(w_far, w, sems.at[0]),
        pltpu.make_async_copy(cot_far, cot, sems.at[1]),
    ]
    for copy in copies:
        copy.start()
    for copy in copies:
        copy.wait()
    for s in range(g.s):
        a, b = wide(ra, s, 0), wide(rb, s, 0)
        rows = [jnp.where(place.odd_row, a, b)]
        for r in range(g.h):
            at = (s * g.h + r) * g.wp
            rows.append(wide(e, slice(at, at + g.wp)))
        rows.append(jnp.where(place.odd_row, b, a))
        for i in range(rows_in):
            place_shifted(e_ref, s * rows_in + i, rows[i])
        mask = pixel_mask(occ, s)
        for r in range(0, g.h, chunk):
            acc = transposed_conv(g, e_ref, w, s, rows_in, r, chunk)
            for i in range(chunk):
                v = acc[i * g.wp : i * g.wp + g.w]
                out_ref[s, r + i] = (wide(cot, s, r + i) + v) * mask[:, r + i : r + i + 1]


def pair_sum_kernel(lane, keep, got, *refs):
    *_, out_far, buffer, sems = refs
    taps, half, chans = keep.shape
    copies = []
    for t in range(taps):
        rows = pl.ds(t * chans, chans)
        buffer[rows, :] = (keep[t] + got[t]).astype(BF16).T
        copies.append(
            pltpu.make_async_copy(buffer.at[rows], out_far.at[rows, pl.ds(lane, half)], sems.at[t])
        )
        copies[-1].start()
    for copy in copies:
        copy.wait()


def adamw(weight, grad, first, second, rate):
    first_new = 0.9 * first + 0.1 * grad
    second_new = 0.999 * second + 0.001 * grad * grad
    first_hat = first_new / (1.0 - 0.9**STEP)
    second_hat = second_new / (1.0 - 0.999**STEP)
    weight_new = weight - rate * (first_hat / (jnp.sqrt(second_hat) + 1e-08) + 0.01 * weight)
    return (weight_new, first_new, second_new)


def update_kernel(
    count, parts, w, first, second, st2, st3, params, n_first, n_second,
    grad_out, w_out, first_out, second_out, n_grad, n_out, n_first_out, n_second_out
):
    devices, rows, lanes = parts.shape
    lanes //= 2
    ncols = lax.axis_size("cols")
    total2, total3 = total_of(st2), total_of(st3)
    mean, rstd = stats_of(total2, count)
    sum_dn = total2[2:3]
    grads = jnp.concatenate(
        [total3[1:2], total3[0:1], rstd * (total2[3:4] - mean * sum_dn), sum_dn], axis=0
    )
    n_grad[...] = grads
    n_out[...], n_first_out[...], n_second_out[...] = adamw(
        params[...], grads, n_first[...], n_second[...], 0.75
    )
    grads = []
    for k in range(2):
        for half in range(2):
            grad = None
            for source in range(devices):
                if (source // ncols) % 2 == half:
                    term = wide(parts, source, slice(None), slice(k * lanes, (k + 1) * lanes))
                    grad = term if grad is None else grad + term
            grads.append((pl.ds(2 * half + k, rows, stride=4), grad))
    for at, grad in grads:
        new = adamw(w[at, :], grad, first[at, :], second[at, :], 0.02)
        grad_out[at, :] = grad
        w_out[at, :], first_out[at, :], second_out[at, :] = new


def swapped(block, axis, first):
    count = lax.axis_size(axis)
    pairs = []
    for i in range(first, count - 1, 2):
        pairs += [(i, i + 1), (i + 1, i)]
    return lax.ppermute(block, axis, pairs)


def swapped_both(block, first_row, first_col):
    nrows, ncols = lax.axis_size("rows"), lax.axis_size("cols")

    def partner(i, first, count):
        j = i + 1 if (i - first) % 2 == 0 else i - 1
        return j if min(i, j) >= first and max(i, j) < count else None

    pairs = []
    for i in range(nrows):
        for j in range(ncols):
            to = partner(i, first_row, nrows), partner(j, first_col, ncols)
            if None not in to:
                pairs.append((i * ncols + j, to[0] * ncols + to[1]))
    return lax.ppermute(block, BOTH, pairs)


def to_chunks(flat):
    return flat.reshape(2, -1, 128).transpose(1, 0, 2).reshape(-1, 128)


def from_chunks(rows):
    return rows.reshape(-1, 2, 128).transpose(1, 0, 2).reshape(2, -1)


def exchange(parts):
    return lax.all_to_all(parts, BOTH, 0, 0, tiled=True)


def body(
    features,
    occupancy,
    cotangent,
    conv_weights,
    conv_first,
    conv_second,
    norm_scale_bias,
    norm_first,
    norm_second,
):
    scenes, height, width, chans = features.shape
    g = Geometry(scenes, height, width, chans)
    wp = g.wp
    devices = lax.axis_size("rows") * lax.axis_size("cols")
    count = float(scenes * height * width * devices)
    taps = 9 * chans
    n0, n1, n2, n3 = (scenes * wp * (g.tall - 2 * i) for i in range(4))
    own_pixels = scenes * height * wp
    dma = pltpu.SemaphoreType.DMA

    def conv_flops(n):
        return 2 * n * taps * chans

    side = shape_of((scenes, g.side, chans), BF16)
    corner = shape_of((scenes, g.corner, chans), BF16)
    own, c, d, b, bc, bd = kernel_call(
        functools.partial(pack_kernel, g),
        [
            shape_of(features.shape, BF16),
            side,
            side,
            shape_of((scenes, RIM + g.near, width, chans), BF16),
            corner,
            corner,
        ],
        1e8,
        far=(0, 1, 2),
        scratch=[
            pltpu.VMEM(features.shape, BF16),
            pltpu.VMEM(features.shape, BF16),
            pltpu.VMEM(occupancy.shape, jnp.int32),
            dma((3, scenes)),
        ],
    )(features, occupancy, cotangent)
    rb = swapped(b, "rows", 1)
    rc, rd = swapped(c, "cols", 0), swapped(d, "cols", 1)
    rb_c, rb_d = swapped_both(bc, 1, 0), swapped_both(bd, 1, 1)
    chunked = to_chunks(conv_weights)
    share = conv_first.shape[1]
    chunk_shape = shape_of((share // 64, 128), F32)
    weights = (taps, chans)
    w1, w2 = kernel_call(
        prepare_kernel,
        [held(weights, BF16)] * 2,
        0,
        size=1024,
        far=(0,),
        scratch=[pltpu.VMEM((9, chunked.shape[0] // 9, 128), F32), dma((9,))],
    )(chunked)

    def wide_rows(rows):
        return shape_of((scenes, rows, wp, chans), BF16)

    ext, cot_ext, a = kernel_call(
        functools.partial(assemble_kernel, g),
        [wide_rows(n) for n in (height, height, RIM + g.near)],
        0,
        size=1024,
    )(own, cotangent, rc, rd)
    rows_x = scenes * (height + 2) * wp
    x_shape = held((rows_x, 3 * chans), BF16)
    z1, st, x = kernel_call(
        functools.partial(own_conv_kernel, g),
        [held((n1, chans), F32), held((16, chans), F32), x_shape],
        0,
        size=1024,
    )(ext, w1)
    a, rb, rb_c, rb_d, w1 = lax.optimization_barrier((a, rb, rb_c, rb_d, w1))
    ra = swapped(a, "rows", 0)
    z1, st, x, cot_next = kernel_call(
        functools.partial(rim_conv_kernel, g),
        [held((n1, chans), F32), shape_of((devices, 2, chans), F32), x_shape, wide_rows(2)],
        0,
        size=1024,
        scratch=[pltpu.VMEM((scenes * 2 * (RIM + 2) * wp, 3 * chans), BF16)],
        alias={7: 0, 8: 2},
    )(ext, ra, rb, rb_c, rb_d, w1, st, z1, x)
    st1 = exchange(st)
    h, z2, st = kernel_call(
        functools.partial(second_conv_kernel, g, 5, count),
        [
            held((n1, 3 * chans), BF16),
            held((n2, chans), F32),
            shape_of((devices, 4, chans), F32),
        ],
        conv_flops(n2),
    )(z1, st1, norm_scale_bias, w2, cot_ext)
    st2 = exchange(st)
    grad_shape = held((9, chans // 2, chans), F32)
    d, keep2, send2 = kernel_call(
        functools.partial(second_gradient_kernel, g, count),
        [held((n2, chans), BF16), grad_shape, grad_shape],
        conv_flops(own_pixels),
        scratch=[pltpu.VMEM((chans, own_pixels), BF16)],
    )(z2, st2, norm_scale_bias, cot_ext, cot_next, h)
    got2 = swapped(send2, "rows", 0)
    dn1, st, block_out = kernel_call(
        functools.partial(hidden_gradient_kernel, g, 8, count),
        [
            held((n3, chans), F32),
            shape_of((devices, 2, chans), F32),
            shape_of(features.shape, BF16),
        ],
        conv_flops(n3),
        scratch=[pltpu.VMEM((n2, 3 * chans), BF16)],
    )(d, w2, z1, z2, st1, st2, norm_scale_bias, ext)
    st, got2 = lax.optimization_barrier((st, got2))
    st3 = exchange(st)
    e, a, b, keep1, send1 = kernel_call(
        functools.partial(first_gradient_kernel, g, count),
        [held((n3, chans), BF16), wide_rows(1), wide_rows(1), grad_shape, grad_shape],
        conv_flops(own_pixels),
        scratch=[pltpu.VMEM((chans, own_pixels), BF16)],
    )(dn1, z1, st1, st3, norm_scale_bias, x)
    got1 = swapped(send1, "rows", 0)
    keep2, got2, keep1 = lax.optimization_barrier((keep2, got2, keep1))

    def add_pair(lane, *operands, **options):
        return kernel_call(
            functools.partial(pair_sum_kernel, lane),
            [stored((taps, chans), BF16)],
            1e9,
            far_out=(0,),
            scratch=[pltpu.VMEM((taps, chans // 2), BF16), dma((9,))],
            **options,
        )(*operands)

    (parts,) = add_pair(chans // 2, keep2, got2)
    (parts,) = add_pair(0, keep1, got1, parts, far=(2,), alias={2: 0})
    parts, chunked = lax.optimization_barrier((parts, chunked))
    parts = exchange(parts.reshape(devices, taps // devices, chans))
    ra, rb = swapped(a, "rows", 0), swapped(b, "rows", 1)
    (grad_input,) = kernel_call(
        functools.partial(input_gradient_kernel, g, 8),
        [shape_of(features.shape, F32)],
        conv_flops(own_pixels),
        far=(3, 4),
        scratch=[
            pltpu.VMEM(weights, BF16),
            pltpu.VMEM(features.shape, BF16),
            pltpu.VMEM((rows_x, 3 * chans), BF16),
            dma((2,)),
        ],
    )(e, ra, rb, w1, cotangent, occupancy)
    own_rows = share // 64
    first_row = (lax.axis_index("rows") * lax.axis_size("cols") + lax.axis_index("cols")) * own_rows
    own_weights = lax.dynamic_slice_in_dim(chunked, first_row, own_rows, 0)

    norm_shape = shape_of(norm_first.shape, F32)
    updated = kernel_call(
        functools.partial(update_kernel, count),
        [chunk_shape] * 4 + [norm_shape] * 4,
        1e8,
    )(
        parts, own_weights, to_chunks(conv_first), to_chunks(conv_second), st2, st3,
        norm_scale_bias, norm_first, norm_second,
    )
    return (block_out, grad_input, *map(from_chunks, updated[:4]), *updated[4:])


def solution(mesh):
    tile = P(None, "rows", "cols", None)
    share = P(None, ("rows", "cols"))
    return jax.shard_map(
        body,
        mesh=mesh,
        in_specs=(tile, P(None, "rows", "cols"), tile, P(), share, share, P(), P(), P()),
        out_specs=(tile, tile, share, share, share, share, P(), P(), P(), P()),
        check_vma=False,
    )
```

```python
import functools
import math

import jax
import jax.numpy as jnp
from jax import lax
from jax.experimental import pallas as pl
from jax.experimental.pallas import tpu as pltpu
from jax.sharding import PartitionSpec as P

STEP = 5
BOTH = ("rows", "cols")
RIM = 3
COLS = 4
SIDE = 2 * COLS
F32, BF16 = jnp.float32, jnp.bfloat16


def shape_of(shape, dtype):
    return jax.ShapeDtypeStruct(shape, dtype)


def held(shape, dtype):
    return pltpu.VMEM(shape, dtype)


def stored(shape, dtype):
    return pltpu.HBM(shape, dtype)


def kernel_call(body, out_shape, flops, far=(), far_out=(), scratch=(), limit=16, alias=None, size=4 << 20):
    def call(*operands):
        operands = [
            pltpu.with_memory_space_constraint(v, pltpu.HBM if i in far else pltpu.VMEM)
            for i, v in enumerate(operands)
        ]
        specs = [
            pl.BlockSpec(memory_space=pltpu.HBM if i in far else pltpu.VMEM)
            for i in range(len(operands))
        ]
        return pl.pallas_call(
            body,
            out_shape=out_shape,
            in_specs=specs,
            out_specs=[
                pl.BlockSpec(memory_space=pltpu.HBM if i in far_out else pltpu.VMEM)
                for i in range(len(out_shape))
            ],
            scratch_shapes=list(scratch),
            input_output_aliases=alias or {},
            compiler_params=pltpu.CompilerParams(vmem_limit_bytes=limit << 20),
            cost_estimate=pl.CostEstimate(
                flops=int(flops), bytes_accessed=size, transcendentals=0
            ),
        )(*operands)

    return call


def dot(a, b):
    return jnp.dot(a, b, preferred_element_type=F32)


def dot_nt(a, b):
    return lax.dot_general(a, b, (((1,), (1,)), ((), ())), preferred_element_type=F32)


def total_of(ref):
    count = ref.shape[0]
    total = ref[0]
    for i in range(1, count):
        total = total + ref[i]
    return total


def to_all(ref, parts):
    value = jnp.concatenate(parts, axis=0)
    for i in range(ref.shape[0]):
        ref[i] = value


def store_shifted(ref, start, row, offsets=(0, 1, 2)):
    width, chans = row.shape
    for b in offsets:
        moved = row if b == 1 else pltpu.roll(row, 1 if b == 0 else width - 1, 0)
        ref[start : start + width, b * chans : (b + 1) * chans] = moved.astype(BF16)


class Geometry:
    def __init__(self, scenes, height, width, chans):
        self.s, self.h, self.w, self.c = scenes, height, width, chans
        self.wp = width + SIDE
        self.tall = height + 2 * RIM
        self.near = RIM - 2
        self.near_cols = COLS - 2
        self.cot_tall = height + 2 * self.near
        self.side = (COLS + self.near_cols) * height
        self.corner = -(-(COLS * RIM + self.near_cols * self.near) // 16) * 16


class Place:
    def __init__(self):
        row, col = lax.axis_index("rows"), lax.axis_index("cols")
        nrows, ncols = lax.axis_size("rows"), lax.axis_size("cols")
        self.above = (row > 0).astype(F32)
        self.below = (row < nrows - 1).astype(F32)
        self.right = (col < ncols - 1).astype(F32)
        self.left = (col > 0).astype(F32)
        self.core = row % 2
        self.second = row // 2 % 2
        self.odd_row = row % 2 == 1
        self.odd_col = col % 2 == 1
        self.index = row * ncols + col


def wide(ref, *index):
    return ref[index].astype(F32)


def far_rows(g, place, rb, rb_c, rb_d, s):
    right, left = sides(g, place, rb_c, rb_d, s)
    rows = []
    for k in range(RIM + g.near):
        width = COLS if k < RIM else g.near_cols
        at = COLS * min(k, RIM) + g.near_cols * max(k - RIM, 0)
        rows.append(
            jnp.concatenate([wide(rb, s, k), side_columns(g, right, left, at, width)], axis=0)
        )
    return rows


def pixel_mask(occ, s):
    return occ[s].astype(F32).T


def in_grid(row, r, g, place, edge):
    row = jnp.concatenate([row[: g.w], row[g.w :] * edge], axis=0)
    if r < RIM:
        row = row * place.above
    elif r >= RIM + g.h:
        row = row * place.below
    return row


def edge_mask(place, g):
    where = lax.broadcasted_iota(jnp.int32, (SIDE, g.c), 0)
    return jnp.where(where < SIDE // 2, place.right, place.left)


def sum_rows(value):
    rows, chans = value.shape
    return jnp.sum(value.reshape(rows // 8, 8, chans), axis=0)


def pack_kernel(
    g, features, occ_far, cot, own, c_ref, d_ref, b_ref, bc_ref, bd_ref, given, seen, occ, sems
):
    copies = []
    flags = pltpu.make_async_copy(occ_far, occ, sems.at[2, 0])
    flags.start()
    for s in range(g.s):
        copies.append(
            (
                pltpu.make_async_copy(features.at[s], given.at[s], sems.at[0, s]),
                pltpu.make_async_copy(cot.at[s], seen.at[s], sems.at[1, s]),
            )
        )
        for copy in copies[-1]:
            copy.start()
    odd, odd_row = Place().odd_col, Place().odd_row
    flags.wait()

    for s in range(g.s):
        mask = pixel_mask(occ, s)
        for copy in copies[s]:
            copy.wait()
        rows = []
        for r in range(g.h):
            row = wide(given, s, r) * mask[:, r : r + 1]
            rows.append(row)
            own[s, r] = row.astype(BF16)
        cots = [wide(seen, s, r) for r in range(g.h)]
        ends = []
        for field, count in ((rows, RIM), (cots, g.near)):
            for k in range(count):
                ends.append(jnp.where(odd_row, field[g.h - count + k], field[k]))
                b_ref[s, len(ends) - 1] = ends[-1].astype(BF16)
        spare = jnp.zeros((g.corner - COLS * RIM - g.near_cols * g.near, g.c), F32)
        widths = [COLS] * RIM + [g.near_cols] * g.near
        right = [v[g.w - width :] for v, width in zip(ends, widths, strict=True)]
        left = [v[:width] for v, width in zip(ends, widths, strict=True)]
        right, left = (jnp.concatenate(v + [spare], axis=0) for v in (right, left))
        bc_ref[s] = jnp.where(odd, left, right).astype(BF16)
        bd_ref[s] = jnp.where(odd, right, left).astype(BF16)
        right = jnp.concatenate(
            [v[g.w - COLS :] for v in rows] + [v[g.w - g.near_cols :] for v in cots], axis=0
        )
        left = jnp.concatenate([v[:COLS] for v in rows] + [v[: g.near_cols] for v in cots], axis=0)
        c_ref[s] = jnp.where(odd, left, right).astype(BF16)
        d_ref[s] = jnp.where(odd, right, left).astype(BF16)


def sides(g, place, rc, rd, s):
    c, d = wide(rc, s), wide(rd, s)
    return jnp.where(place.odd_col, d, c), jnp.where(place.odd_col, c, d)


def side_columns(g, right, left, at, width):
    parts = [right[at : at + width], jnp.zeros((SIDE - 2 * width, g.c), F32), left[at : at + width]]
    return jnp.concatenate([part for part in parts if part.shape[0]], axis=0)


def assemble_kernel(g, own, cot, rc, rd, ext, cot_ext, a_ref):
    place = Place()

    odd = place.odd_row
    for s in range(g.s):
        right, left = sides(g, place, rc, rd, s)
        for source, full, at, width, count, first in (
            (own, ext, 0, COLS, RIM, 0),
            (cot, cot_ext, COLS * g.h, g.near_cols, g.near, RIM),
        ):
            rows = []
            for r in range(g.h):
                beyond = side_columns(g, right, left, at + width * r, width)
                rows.append(jnp.concatenate([wide(source, s, r), beyond], axis=0))
                full[s, r] = rows[r].astype(BF16)
            for k in range(count):
                top, bottom = rows[k], rows[g.h - count + k]
                a_ref[s, first + k] = jnp.where(odd, top, bottom).astype(BF16)


def prepare_kernel(w_ref, one_ref, two_ref, buffer, sems):
    chans = one_ref.shape[1]
    taps, size, lanes = buffer.shape
    per = chans // lanes
    copies = [
        pltpu.make_async_copy(w_ref.at[pl.ds(t * size, size)], buffer.at[t], sems.at[t])
        for t in range(taps)
    ]
    for copy in copies:
        copy.start()
    for t in range(taps):
        copies[t].wait()
        for k, out in enumerate((one_ref, two_ref)):
            parts = [buffer[t, pl.ds(2 * half + k, chans, stride=2 * per), :] for half in range(per)]
            out[t * chans : (t + 1) * chans, :] = jnp.concatenate(parts, axis=1).astype(BF16)


def place_shifted(ref, row_index, row):
    store_shifted(ref, row_index * row.shape[0], row)


def window_rows(g, x_ref, first, count):
    size = count * g.wp
    return jnp.concatenate(
        [x_ref[(first + a) * g.wp : (first + a) * g.wp + size, :] for a in range(3)], axis=1
    )


def own_conv_kernel(g, ext, w, z_ref, st_ref, x_ref):
    count = g.h - 2
    s1 = jnp.zeros((8, g.c), F32)
    s2 = jnp.zeros((8, g.c), F32)
    for s in range(g.s):
        for r in range(g.h):
            place_shifted(x_ref, s * (g.h + 2) + 1 + r, wide(ext, s, r))
        half = count // 2
        for first in range(0, count, half):
            acc = dot(window_rows(g, x_ref, s * (g.h + 2) + 1 + first, half), w[...])
            at = (s * (g.tall - 2) + RIM + first) * g.wp
            z_ref[at : at + half * g.wp, :] = acc
            for i in range(half):
                v = acc[i * g.wp : i * g.wp + g.w]
                s1 = s1 + sum_rows(v)
                s2 = s2 + sum_rows(v * v)
    st_ref[0:8] = s1
    st_ref[8:16] = s2


def rim_conv_kernel(
    g, ext, ra, rb, rb_c, rb_d, w, st_in, z_in, x_in, z_ref, st_ref, x_own, cot_ref, x_ref
):
    del z_in, x_in
    place = Place()
    odd = place.odd_row
    s1, s2 = st_in[0:8], st_in[8:16]
    span = RIM + 2
    for s in range(g.s):
        far = far_rows(g, place, rb, rb_c, rb_d, s)
        near = [wide(ra, s, k) for k in range(RIM + g.near)]
        for side in range(2):
            base = span * (2 * s + side)
            beyond = [
                jnp.where(odd, b, a) if side else jnp.where(odd, a, b)
                for a, b in zip(near, far, strict=True)
            ]
            for k in range(RIM):
                place_shifted(x_ref, base + 2 * side + k, beyond[k])
            next_row = beyond[0 if side else RIM - 1]
            place_shifted(x_own, s * (g.h + 2) + (g.h + 1) * side, next_row)
            cot_ref[s, side] = beyond[RIM].astype(BF16)
            source = (s * (g.h + 2) + 1 + (g.h - 2) * side) * g.wp
            target = (base + RIM * (1 - side)) * g.wp
            x_ref[target : target + 2 * g.wp, :] = x_own[source : source + 2 * g.wp, :]
            acc = dot(window_rows(g, x_ref, base, RIM), w[...])
            at = (s * (g.tall - 2) + (g.h + RIM - 2) * side) * g.wp
            z_ref[at : at + RIM * g.wp, :] = acc
            i = 0 if side else RIM - 1
            v = acc[i * g.wp : i * g.wp + g.w]
            s1 = s1 + sum_rows(v)
            s2 = s2 + sum_rows(v * v)
    to_all(st_ref, [jnp.sum(s1, 0, keepdims=True), jnp.sum(s2, 0, keepdims=True)])


def stats_of(total, count):
    mean = total[0:1] / count
    var = total[1:2] / count - mean * mean
    return mean, lax.rsqrt(var + 1e-05)


def second_conv_kernel(g, chunk, count, z1, st, params, w, cot, h_ref, z_ref, st_ref):
    rows_in, rows_out = g.tall - 2, g.tall - 4
    place = Place()
    mean, rstd = stats_of(total_of(st), count)
    scale = params[0:1] * rstd
    shift = params[1:2] - mean * scale
    edge = edge_mask(place, g)
    sums = [jnp.zeros((8, g.c), F32) for _ in range(4)]
    for s in range(g.s):
        for r in range(rows_in):
            start = (s * rows_in + r) * g.wp
            row = jnp.maximum(z1[start : start + g.wp, :] * scale + shift, 0.0)
            store_shifted(h_ref, start, in_grid(row, r + 1, g, place, edge))
        for r in range(0, rows_out, chunk):
            base = (s * rows_in + r) * g.wp
            size = chunk * g.wp
            lhs = jnp.concatenate(
                [h_ref[base + a * g.wp : base + a * g.wp + size, :] for a in range(3)], axis=1
            )
            acc = dot(lhs, w[...])
            z_ref[(s * rows_out + r) * g.wp : (s * rows_out + r) * g.wp + size, :] = acc
            for i in range(chunk):
                if RIM <= r + i + 2 < RIM + g.h:
                    v = acc[i * g.wp : i * g.wp + g.w]
                    dn = wide(cot, s, r + i + 2 - RIM)[: g.w]
                    for k, term in enumerate((v, v * v, dn, dn * v)):
                        sums[k] = sums[k] + sum_rows(term)
    to_all(st_ref, [jnp.sum(v, 0, keepdims=True) for v in sums])


def own_transposed(g, source, first, s, dt_ref):
    span = g.h * g.wp
    block = source[first : first + span, :]
    inside = lax.broadcasted_iota(jnp.int32, (span, 1), 0) % g.wp < g.w
    dt_ref[:, s * span : (s + 1) * span] = jnp.where(inside, block, jnp.zeros_like(block)).T


def kernel_gradient(g, core, field, rows_field, first_row, dt_ref, keep, send):
    chans, half = g.c, g.c // 2
    span = g.h * g.wp
    mine = pl.ds(pl.multiple_of(core * half, half), half)
    other = pl.ds(pl.multiple_of((1 - core) * half, half), half)
    lhs = jnp.concatenate([dt_ref[mine, :], dt_ref[other, :]], axis=0)
    for a in range(3):
        starts = [(s * rows_field + first_row + a) * g.wp for s in range(g.s)]
        acc = dot(lhs, jnp.concatenate([field[at : at + span, :] for at in starts], axis=0))
        for b in range(3):
            keep[a * 3 + b] = acc[0:half, b * chans : (b + 1) * chans]
            other_half = acc[half:, b * chans : (b + 1) * chans]
            if isinstance(send, tuple):
                send[a][b] = other_half.astype(BF16)
            else:
                send[a * 3 + b] = other_half


def second_gradient_kernel(
    g, count, z2, st, params, cot, cot_next, h, d_ref, keep, send, dt_ref
):
    place = Place()
    rows = g.cot_tall
    total = total_of(st)
    mean, rstd = stats_of(total, count)
    sum_dn = total[2:3]
    sum_dx = rstd * (total[3:4] - mean * sum_dn)
    k0 = params[2:3] * rstd
    k1 = k0 * (sum_dn / count)
    k2 = k0 * rstd * (sum_dx / count)
    edge = edge_mask(place, g)
    for s in range(g.s):
        for i in range(rows):
            rim = not g.near <= i < g.near + g.h
            dn = wide(cot_next, s, 0 if i < g.near else 1) if rim else wide(cot, s, i - g.near)
            start = (s * rows + i) * g.wp
            d = k0 * dn - k1 - (z2[start : start + g.wp, :] - mean) * k2
            d = in_grid(d, i + RIM - g.near, g, place, edge)
            d_ref[start : start + g.wp, :] = d.astype(BF16)
        own_transposed(g, d_ref, (s * rows + g.near) * g.wp, s, dt_ref)
    kernel_gradient(g, place.core, h, g.tall - 2, RIM - 2, dt_ref, keep, send)


def transposed_conv(g, d_ref, w, s, rows_in, r, chunk):
    acc = None
    size = chunk * g.wp
    for a in range(3):
        start = (s * rows_in + r + a) * g.wp
        for b in range(3):
            tap = (2 - a) * 3 + (2 - b)
            term = dot_nt(
                d_ref[start : start + size, b * g.c : (b + 1) * g.c],
                w[tap * g.c : (tap + 1) * g.c, :],
            )
            acc = term if acc is None else acc + term
    return acc


def hidden_gradient_kernel(
    g, chunk, count, d, w, z1, z2, st, st2, params, ext, dn_ref, st_ref, out_ref, d_ref
):
    mean2, rstd2 = stats_of(total_of(st2), count)
    scale2 = params[2:3] * rstd2
    shift2 = params[3:4] - mean2 * scale2
    rows_in, rows_out, z_rows = g.tall - 4, g.tall - 6, g.tall - 2
    mean, rstd = stats_of(total_of(st), count)
    scale = params[0:1] * rstd
    shift = params[1:2] - mean * scale
    s0 = jnp.zeros((8, g.c), F32)
    s1 = jnp.zeros((8, g.c), F32)
    for s in range(g.s):
        for i in range(rows_in):
            at = (s * rows_in + i) * g.wp
            store_shifted(d_ref, at, wide(d, slice(at, at + g.wp)))
        for r in range(g.h):
            at = (s * rows_in + r + g.near) * g.wp
            normed = z2[at : at + g.w, :] * scale2 + shift2
            out_ref[s, r] = (wide(ext, s, r)[: g.w] + normed).astype(BF16)
        for r in range(0, rows_out, chunk):
            acc = transposed_conv(g, d_ref, w, s, rows_in, r, chunk)
            at = (s * z_rows + r + 2) * g.wp
            z = z1[at : at + chunk * g.wp, :]
            dn = jnp.where(z * scale + shift > 0, acc, 0.0)
            dn_ref[(s * rows_out + r) * g.wp : (s * rows_out + r + chunk) * g.wp, :] = dn
            for i in range(chunk):
                if RIM <= r + i + 3 < RIM + g.h:
                    v = dn[i * g.wp : i * g.wp + g.w]
                    s0 = s0 + sum_rows(v)
                    s1 = s1 + sum_rows(v * (z[i * g.wp : i * g.wp + g.w] - mean))
    to_all(st_ref, [jnp.sum(s0, 0, keepdims=True), jnp.sum(s1, 0, keepdims=True) * rstd])


def first_gradient_kernel(
    g, count, dn, z, st, st3, params, x, e_ref, a_ref, b_ref, keep, send0, send1, send2, dt_ref
):
    place = Place()
    mean, rstd = stats_of(total_of(st), count)
    total = total_of(st3)
    k0 = params[0:1] * rstd
    k1 = k0 * (total[0:1] / count)
    k2 = k0 * rstd * (total[1:2] / count)
    edge = edge_mask(place, g)
    for s in range(g.s):
        for i in range(g.h):
            at = (s * g.h + i) * g.wp
            z_at = (s * (g.tall - 2) + i + RIM - 1) * g.wp
            d = k0 * dn[at : at + g.wp, :] - k1 - (z[z_at : z_at + g.wp, :] - mean) * k2
            d = in_grid(d, i + RIM, g, place, edge)
            e_ref[at : at + g.wp, :] = d.astype(BF16)
            if i == 0:
                top = d
        a_ref[s, 0] = jnp.where(place.odd_row, top, d).astype(BF16)
        b_ref[s, 0] = jnp.where(place.odd_row, d, top).astype(BF16)
        own_transposed(g, e_ref, s * g.h * g.wp, s, dt_ref)
    kernel_gradient(g, place.core, x, g.h + 2, 0, dt_ref, keep, (send0, send1, send2))


def input_gradient_kernel(
    g, chunk, e, ra, rb, w_far, cot_far, occ, out_ref, w, cot, e_ref, sems
):
    rows_in = g.h + 2
    place = Place()
    copies = [
        pltpu.make_async_copy(w_far, w, sems.at[0]),
        pltpu.make_async_copy(cot_far, cot, sems.at[1]),
    ]
    for copy in copies:
        copy.start()
    for copy in copies:
        copy.wait()
    for s in range(g.s):
        a, b = wide(ra, s, 0), wide(rb, s, 0)
        rows = [jnp.where(place.odd_row, a, b)]
        for r in range(g.h):
            at = (s * g.h + r) * g.wp
            rows.append(wide(e, slice(at, at + g.wp)))
        rows.append(jnp.where(place.odd_row, b, a))
        for i in range(rows_in):
            place_shifted(e_ref, s * rows_in + i, rows[i])
        mask = pixel_mask(occ, s)
        for r in range(0, g.h, chunk):
            acc = transposed_conv(g, e_ref, w, s, rows_in, r, chunk)
            for i in range(chunk):
                v = acc[i * g.wp : i * g.wp + g.w]
                out_ref[s, r + i] = (wide(cot, s, r + i) + v) * mask[:, r + i : r + i + 1]


def pair_total(keep, got, t):
    other = got[t] if len(got) > 3 else got[t // 3][t % 3].astype(F32)
    return keep[t] + other


def pair_sum_kernel(lane, keep, *refs):
    *got, out_far, buffer, sems = refs
    got = got[0] if len(got) == 1 else got[:3]
    taps, half, chans = keep.shape
    copies = []
    for t in range(taps):
        rows = pl.ds(t * chans, chans)
        buffer[rows, :] = pair_total(keep, got, t).astype(BF16).T
        copies.append(
            pltpu.make_async_copy(buffer.at[rows], out_far.at[rows, pl.ds(lane, half)], sems.at[t])
        )
        copies[-1].start()
    for copy in copies:
        copy.wait()


def half_rows(share):
    return -(-(share // 2) // 8) * 8


def split_kernel(keep, got, kept_ref, sent_ref, buffer):
    taps, half, chans = keep.shape
    devices, rows, _ = kept_ref.shape
    share = taps * chans // devices
    for t in range(taps):
        buffer[t * chans : (t + 1) * chans, :] = pair_total(keep, got, t).T
    second = Place().second
    for i in range(devices):
        mine = pl.multiple_of(i * share + (share - rows) * second, 8)
        other = pl.multiple_of(i * share + (share - rows) * (1 - second), 8)
        kept_ref[i] = buffer[pl.ds(mine, rows), :]
        sent_ref[i] = buffer[pl.ds(other, rows), :].astype(BF16)


def message_kernel(keep, got0, got1, got2, kept, came, out_far, buffer, out_ref, sems):
    taps, half, chans = keep.shape
    devices, rows, _ = kept.shape
    share = taps * chans // devices
    for t in range(taps):
        buffer[t * chans : (t + 1) * chans, :] = pair_total(keep, (got0, got1, got2), t).T
    copies = []
    count = sems.shape[0]
    for part in range(count):
        mine = pl.ds(part * devices // count, devices // count)
        for i in range(part * devices // count, (part + 1) * devices // count):
            first = buffer[i * share : (i + 1) * share, :]
            out_ref[i] = jnp.concatenate([first, kept[i] + wide(came, i)], axis=0).astype(BF16)
        copies.append(pltpu.make_async_copy(out_ref.at[mine], out_far.at[mine], sems.at[part]))
        copies[-1].start()
    for copy in copies:
        copy.wait()


def adamw(weight, grad, first, second, rate):
    first_new = 0.9 * first + 0.1 * grad
    second_new = 0.999 * second + 0.001 * grad * grad
    first_hat = first_new / (1.0 - 0.9**STEP)
    second_hat = second_new / (1.0 - 0.999**STEP)
    weight_new = weight - rate * (first_hat / (jnp.sqrt(second_hat) + 1e-08) + 0.01 * weight)
    return (weight_new, first_new, second_new)


def update_kernel(
    count, parts, w, first_m, second_m, st2, st3, params, n_first, n_second,
    grad_out, w_out, first_out, second_out, n_grad, n_out, n_first_out, n_second_out
):
    devices, ncols = parts.shape[0], lax.axis_size("cols")
    share = w.shape[0] // 4
    total2, total3 = total_of(st2), total_of(st3)
    mean, rstd = stats_of(total2, count)
    sum_dn = total2[2:3]
    grads = jnp.concatenate(
        [total3[1:2], total3[0:1], rstd * (total2[3:4] - mean * sum_dn), sum_dn], axis=0
    )
    n_grad[...] = grads
    n_out[...], n_first_out[...], n_second_out[...] = adamw(
        params[...], grads, n_first[...], n_second[...], 0.75
    )
    def over(chosen, rows, lanes):
        total = None
        for source in range(devices):
            if chosen(source // ncols):
                term = wide(parts, source)[rows, lanes]
                total = term if total is None else total + term
        return total

    grads = []
    every = slice(None)
    for half in range(2):
        if parts.shape[2] == 256:
            for k in range(2):
                lanes = slice(k * 128, (k + 1) * 128)
                grads.append((k, half, over(lambda row: row % 2 == half, every, lanes)))
        else:
            rows = half_rows(share)
            first = over(lambda row: row % 2 == half, slice(0, share), every)
            upper = over(lambda row: row % 4 == half, slice(share, None), every)
            lower = over(lambda row: row % 4 == half + 2, slice(2 * rows, None), every)
            grads += [(0, half, first), (1, half, jnp.concatenate([upper, lower], axis=0))]
    for k, half, grad in grads:
        at = pl.ds(2 * half + k, share, stride=4)
        new = adamw(w[at, :], grad, first_m[at, :], second_m[at, :], 0.02)
        grad_out[at, :] = grad
        w_out[at, :], first_out[at, :], second_out[at, :] = new


def swapped(block, axis, first):
    count = lax.axis_size(axis)
    pairs = []
    for i in range(first, count - 1, 2):
        pairs += [(i, i + 1), (i + 1, i)]
    return lax.ppermute(block, axis, pairs)


def swapped_both(block, first_row, first_col):
    nrows, ncols = lax.axis_size("rows"), lax.axis_size("cols")

    def partner(i, first, count):
        j = i + 1 if (i - first) % 2 == 0 else i - 1
        return j if min(i, j) >= first and max(i, j) < count else None

    pairs = []
    for i in range(nrows):
        for j in range(ncols):
            to = partner(i, first_row, nrows), partner(j, first_col, ncols)
            if None not in to:
                pairs.append((i * ncols + j, to[0] * ncols + to[1]))
    return lax.ppermute(block, BOTH, pairs)


def to_chunks(flat):
    return flat.reshape(2, -1, 128).transpose(1, 0, 2).reshape(-1, 128)


def from_chunks(rows):
    return rows.reshape(-1, 2, 128).transpose(1, 0, 2).reshape(2, -1)


def exchange(parts):
    return lax.all_to_all(parts, BOTH, 0, 0, tiled=True)


def body(
    features,
    occupancy,
    cotangent,
    conv_weights,
    conv_first,
    conv_second,
    norm_scale_bias,
    norm_first,
    norm_second,
):
    scenes, height, width, chans = features.shape
    g = Geometry(scenes, height, width, chans)
    wp = g.wp
    devices = lax.axis_size("rows") * lax.axis_size("cols")
    count = float(scenes * height * width * devices)
    taps = 9 * chans
    n0, n1, n2, n3 = (scenes * wp * (g.tall - 2 * i) for i in range(4))
    own_pixels = scenes * height * wp
    dma = pltpu.SemaphoreType.DMA

    def conv_flops(n):
        return 2 * n * taps * chans

    side = shape_of((scenes, g.side, chans), BF16)
    corner = shape_of((scenes, g.corner, chans), BF16)
    own, c, d, b, bc, bd = kernel_call(
        functools.partial(pack_kernel, g),
        [
            shape_of(features.shape, BF16),
            side,
            side,
            shape_of((scenes, RIM + g.near, width, chans), BF16),
            corner,
            corner,
        ],
        1e8,
        far=(0, 1, 2),
        scratch=[
            pltpu.VMEM(features.shape, BF16),
            pltpu.VMEM(features.shape, BF16),
            pltpu.VMEM(occupancy.shape, jnp.int32),
            dma((3, scenes)),
        ],
    )(features, occupancy, cotangent)
    rb = swapped(b, "rows", 1)
    rc, rd = swapped(c, "cols", 0), swapped(d, "cols", 1)
    rb_c, rb_d = swapped_both(bc, 1, 0), swapped_both(bd, 1, 1)
    chunked = to_chunks(conv_weights)
    share = conv_first.shape[1]
    chunk_shape = shape_of((share // 64, 128), F32)
    weights = (taps, chans)
    w1, w2 = kernel_call(
        prepare_kernel,
        [held(weights, BF16)] * 2,
        0,
        size=1024,
        far=(0,),
        scratch=[pltpu.VMEM((9, chunked.shape[0] // 9, 128), F32), dma((9,))],
    )(chunked)

    def wide_rows(rows):
        return shape_of((scenes, rows, wp, chans), BF16)

    ext, cot_ext, a = kernel_call(
        functools.partial(assemble_kernel, g),
        [wide_rows(n) for n in (height, height, RIM + g.near)],
        0,
        size=1024,
    )(own, cotangent, rc, rd)
    rows_x = scenes * (height + 2) * wp
    x_shape = held((rows_x, 3 * chans), BF16)
    z1, st, x = kernel_call(
        functools.partial(own_conv_kernel, g),
        [held((n1, chans), F32), held((16, chans), F32), x_shape],
        0,
        size=1024,
    )(ext, w1)
    a, rb, rb_c, rb_d, w1 = lax.optimization_barrier((a, rb, rb_c, rb_d, w1))
    ra = swapped(a, "rows", 0)
    z1, st, x, cot_next = kernel_call(
        functools.partial(rim_conv_kernel, g),
        [held((n1, chans), F32), shape_of((devices, 2, chans), F32), x_shape, wide_rows(2)],
        0,
        size=1024,
        scratch=[pltpu.VMEM((scenes * 2 * (RIM + 2) * wp, 3 * chans), BF16)],
        alias={7: 0, 8: 2},
    )(ext, ra, rb, rb_c, rb_d, w1, st, z1, x)
    st1 = exchange(st)
    h, z2, st = kernel_call(
        functools.partial(second_conv_kernel, g, 5, count),
        [
            held((n1, 3 * chans), BF16),
            held((n2, chans), F32),
            shape_of((devices, 4, chans), F32),
        ],
        conv_flops(n2),
    )(z1, st1, norm_scale_bias, w2, cot_ext)
    st2 = exchange(st)
    grad_shape = held((9, chans // 2, chans), F32)
    d, keep2, send2 = kernel_call(
        functools.partial(second_gradient_kernel, g, count),
        [held((n2, chans), BF16), grad_shape, grad_shape],
        conv_flops(own_pixels),
        scratch=[pltpu.VMEM((chans, own_pixels), BF16)],
    )(z2, st2, norm_scale_bias, cot_ext, cot_next, h)
    got2 = swapped(send2, "rows", 0)
    dn1, st, block_out = kernel_call(
        functools.partial(hidden_gradient_kernel, g, 8, count),
        [
            held((n3, chans), F32),
            shape_of((devices, 2, chans), F32),
            held(features.shape, BF16),
        ],
        conv_flops(n3),
        scratch=[pltpu.VMEM((n2, 3 * chans), BF16)],
    )(d, w2, z1, z2, st1, st2, norm_scale_bias, ext)
    nrows = lax.axis_size("rows")
    cut_again = nrows % 4 == 0 and taps // devices % 8 == 0
    if cut_again:
        got2, st = lax.optimization_barrier((got2, st))
        kept_shape = (devices, half_rows(taps // devices), chans // 2)
        kept, sent = kernel_call(
            split_kernel,
            [held(kept_shape, F32), held(kept_shape, BF16)],
            1e8,
            scratch=[pltpu.VMEM((taps, chans // 2), F32)],
        )(keep2, got2)
        st, kept = lax.optimization_barrier((st, kept))
        st3 = exchange(st)
    else:
        st, got2 = lax.optimization_barrier((st, got2))
        st3 = exchange(st)
    cut = held((3, chans // 2, chans), BF16)
    e, a, b, keep1, *send1 = kernel_call(
        functools.partial(first_gradient_kernel, g, count),
        [held((n3, chans), BF16), wide_rows(1), wide_rows(1), grad_shape, cut, cut, cut],
        0,
        size=1024,
        scratch=[pltpu.VMEM((chans, own_pixels), BF16)],
    )(dn1, z1, st1, st3, norm_scale_bias, x)
    got1 = [swapped(part, "rows", 0) for part in send1]
    share_rows = taps // devices
    buffer = pltpu.VMEM((taps, chans // 2), F32)
    if cut_again:
        came = lax.ppermute(sent, "rows", [(i, i ^ 2) for i in range(nrows)])
        rows = share_rows + kept.shape[1]
        (parts,) = kernel_call(
            message_kernel,
            [stored((devices, rows, chans // 2), BF16)],
            1e9,
            far_out=(0,),
            scratch=[buffer, pltpu.VMEM((devices, rows, chans // 2), BF16), dma((4,))],
        )(keep1, *got1, kept, came)
    else:

        def add_pair(lane, *operands, **options):
            return kernel_call(
                functools.partial(pair_sum_kernel, lane),
                [stored((taps, chans), BF16)],
                1e9,
                far_out=(0,),
                scratch=[pltpu.VMEM((taps, chans // 2), BF16), dma((9,))],
                **options,
            )(*operands)

        (parts,) = add_pair(chans // 2, keep2, got2)
        (parts,) = add_pair(0, keep1, *got1, parts, far=(4,), alias={4: 0})
        parts = parts.reshape(devices, share_rows, chans)
    parts, chunked = lax.optimization_barrier((parts, chunked))
    parts = exchange(parts)
    ra, rb = swapped(a, "rows", 0), swapped(b, "rows", 1)
    (grad_input,) = kernel_call(
        functools.partial(input_gradient_kernel, g, 8),
        [shape_of(features.shape, F32)],
        conv_flops(own_pixels),
        far=(3, 4),
        scratch=[
            pltpu.VMEM(weights, BF16),
            pltpu.VMEM(features.shape, BF16),
            pltpu.VMEM((rows_x, 3 * chans), BF16),
            dma((2,)),
        ],
    )(e, ra, rb, w1, cotangent, occupancy)
    own_rows = share // 64
    first_row = (lax.axis_index("rows") * lax.axis_size("cols") + lax.axis_index("cols")) * own_rows
    own_weights = lax.dynamic_slice_in_dim(chunked, first_row, own_rows, 0)

    norm_shape = shape_of(norm_first.shape, F32)
    updated = kernel_call(
        functools.partial(update_kernel, count),
        [chunk_shape] * 4 + [norm_shape] * 4,
        1e8,
    )(
        parts, own_weights, to_chunks(conv_first), to_chunks(conv_second), st2, st3,
        norm_scale_bias, norm_first, norm_second,
    )
    return (block_out, grad_input, *map(from_chunks, updated[:4]), *updated[4:])


def solution(mesh):
    tile = P(None, "rows", "cols", None)
    share = P(None, ("rows", "cols"))
    return jax.shard_map(
        body,
        mesh=mesh,
        in_specs=(tile, P(None, "rows", "cols"), tile, P(), share, share, P(), P(), P()),
        out_specs=(tile, tile, share, share, share, share, P(), P(), P(), P()),
        check_vma=False,
    )
```

```python
import functools
import math

import jax
import jax.numpy as jnp
from jax import lax
from jax.experimental import pallas as pl
from jax.experimental.pallas import tpu as pltpu
from jax.sharding import PartitionSpec as P

STEP = 5
BOTH = ("rows", "cols")
RIM = 3
COLS = 4
SIDE = 2 * COLS
F32, BF16 = jnp.float32, jnp.bfloat16


def shape_of(shape, dtype):
    return jax.ShapeDtypeStruct(shape, dtype)


def held(shape, dtype):
    return pltpu.VMEM(shape, dtype)


def stored(shape, dtype):
    return pltpu.HBM(shape, dtype)


def kernel_call(body, out_shape, flops, far=(), far_out=(), scratch=(), limit=16, alias=None, size=4 << 20):
    def call(*operands):
        operands = [
            pltpu.with_memory_space_constraint(v, pltpu.HBM if i in far else pltpu.VMEM)
            for i, v in enumerate(operands)
        ]
        specs = [
            pl.BlockSpec(memory_space=pltpu.HBM if i in far else pltpu.VMEM)
            for i in range(len(operands))
        ]
        return pl.pallas_call(
            body,
            out_shape=out_shape,
            in_specs=specs,
            out_specs=[
                pl.BlockSpec(memory_space=pltpu.HBM if i in far_out else pltpu.VMEM)
                for i in range(len(out_shape))
            ],
            scratch_shapes=list(scratch),
            input_output_aliases=alias or {},
            compiler_params=pltpu.CompilerParams(vmem_limit_bytes=limit << 20),
            cost_estimate=pl.CostEstimate(
                flops=int(flops), bytes_accessed=size, transcendentals=0
            ),
        )(*operands)

    return call


def dot(a, b):
    return jnp.dot(a, b, preferred_element_type=F32)


def dot_nt(a, b):
    return lax.dot_general(a, b, (((1,), (1,)), ((), ())), preferred_element_type=F32)


def total_of(ref):
    count = ref.shape[0]
    total = ref[0]
    for i in range(1, count):
        total = total + ref[i]
    return total


def to_all(ref, parts):
    value = jnp.concatenate(parts, axis=0)
    for i in range(ref.shape[0]):
        ref[i] = value


def store_shifted(ref, start, row, offsets=(0, 1, 2)):
    width, chans = row.shape
    for b in offsets:
        moved = row if b == 1 else pltpu.roll(row, 1 if b == 0 else width - 1, 0)
        ref[start : start + width, b * chans : (b + 1) * chans] = moved.astype(BF16)


class Geometry:
    def __init__(self, scenes, height, width, chans):
        self.s, self.h, self.w, self.c = scenes, height, width, chans
        self.wp = width + SIDE
        self.tall = height + 2 * RIM
        self.near = RIM - 2
        self.near_cols = COLS - 2
        self.cot_tall = height + 2 * self.near
        self.side = (COLS + self.near_cols) * height
        self.corner = -(-(COLS * RIM + self.near_cols * self.near) // 16) * 16


class Place:
    def __init__(self):
        row, col = lax.axis_index("rows"), lax.axis_index("cols")
        nrows, ncols = lax.axis_size("rows"), lax.axis_size("cols")
        self.above = (row > 0).astype(F32)
        self.below = (row < nrows - 1).astype(F32)
        self.right = (col < ncols - 1).astype(F32)
        self.left = (col > 0).astype(F32)
        self.core = row % 2
        self.second = row // 2 % 2
        self.odd_row = row % 2 == 1
        self.odd_col = col % 2 == 1
        self.index = row * ncols + col


def wide(ref, *index):
    return ref[index].astype(F32)


def far_rows(g, place, rb, rb_c, rb_d, s):
    right, left = sides(g, place, rb_c, rb_d, s)
    rows = []
    for k in range(RIM + g.near):
        width = COLS if k < RIM else g.near_cols
        at = COLS * min(k, RIM) + g.near_cols * max(k - RIM, 0)
        rows.append(
            jnp.concatenate([wide(rb, s, k), side_columns(g, right, left, at, width)], axis=0)
        )
    return rows


def pixel_mask(occ, s):
    return occ[s].astype(F32).T


def in_grid(row, r, g, place, edge):
    row = jnp.concatenate([row[: g.w], row[g.w :] * edge], axis=0)
    if r < RIM:
        row = row * place.above
    elif r >= RIM + g.h:
        row = row * place.below
    return row


def edge_mask(place, g):
    where = lax.broadcasted_iota(jnp.int32, (SIDE, g.c), 0)
    return jnp.where(where < SIDE // 2, place.right, place.left)


def sum_rows(value):
    rows, chans = value.shape
    return jnp.sum(value.reshape(rows // 8, 8, chans), axis=0)


def pack_kernel(
    g, features, occ_far, cot, own, c_ref, d_ref, b_ref, bc_ref, bd_ref, given, seen, occ, sems
):
    copies = []
    flags = pltpu.make_async_copy(occ_far, occ, sems.at[2, 0])
    flags.start()
    for s in range(g.s):
        copies.append(
            (
                pltpu.make_async_copy(features.at[s], given.at[s], sems.at[0, s]),
                pltpu.make_async_copy(cot.at[s], seen.at[s], sems.at[1, s]),
            )
        )
        for copy in copies[-1]:
            copy.start()
    odd, odd_row = Place().odd_col, Place().odd_row
    flags.wait()

    for s in range(g.s):
        mask = pixel_mask(occ, s)
        for copy in copies[s]:
            copy.wait()
        rows = []
        for r in range(g.h):
            row = wide(given, s, r) * mask[:, r : r + 1]
            rows.append(row)
            own[s, r] = row.astype(BF16)
        cots = [wide(seen, s, r) for r in range(g.h)]
        ends = []
        for field, count in ((rows, RIM), (cots, g.near)):
            for k in range(count):
                ends.append(jnp.where(odd_row, field[g.h - count + k], field[k]))
                b_ref[s, len(ends) - 1] = ends[-1].astype(BF16)
        spare = jnp.zeros((g.corner - COLS * RIM - g.near_cols * g.near, g.c), F32)
        widths = [COLS] * RIM + [g.near_cols] * g.near
        right = [v[g.w - width :] for v, width in zip(ends, widths, strict=True)]
        left = [v[:width] for v, width in zip(ends, widths, strict=True)]
        right, left = (jnp.concatenate(v + [spare], axis=0) for v in (right, left))
        bc_ref[s] = jnp.where(odd, left, right).astype(BF16)
        bd_ref[s] = jnp.where(odd, right, left).astype(BF16)
        right = jnp.concatenate(
            [v[g.w - COLS :] for v in rows] + [v[g.w - g.near_cols :] for v in cots], axis=0
        )
        left = jnp.concatenate([v[:COLS] for v in rows] + [v[: g.near_cols] for v in cots], axis=0)
        c_ref[s] = jnp.where(odd, left, right).astype(BF16)
        d_ref[s] = jnp.where(odd, right, left).astype(BF16)


def sides(g, place, rc, rd, s):
    c, d = wide(rc, s), wide(rd, s)
    return jnp.where(place.odd_col, d, c), jnp.where(place.odd_col, c, d)


def side_columns(g, right, left, at, width):
    parts = [right[at : at + width], jnp.zeros((SIDE - 2 * width, g.c), F32), left[at : at + width]]
    return jnp.concatenate([part for part in parts if part.shape[0]], axis=0)


def assemble_kernel(g, own, cot, rc, rd, ext, cot_ext, a_ref):
    place = Place()

    odd = place.odd_row
    for s in range(g.s):
        right, left = sides(g, place, rc, rd, s)
        for source, full, at, width, count, first in (
            (own, ext, 0, COLS, RIM, 0),
            (cot, cot_ext, COLS * g.h, g.near_cols, g.near, RIM),
        ):
            rows = []
            for r in range(g.h):
                beyond = side_columns(g, right, left, at + width * r, width)
                rows.append(jnp.concatenate([wide(source, s, r), beyond], axis=0))
                full[s, r] = rows[r].astype(BF16)
            for k in range(count):
                top, bottom = rows[k], rows[g.h - count + k]
                a_ref[s, first + k] = jnp.where(odd, top, bottom).astype(BF16)


def prepare_kernel(w_ref, one_ref, two_ref, buffer, sems):
    chans = one_ref.shape[1]
    taps, size, lanes = buffer.shape
    per = chans // lanes
    copies = [
        pltpu.make_async_copy(w_ref.at[pl.ds(t * size, size)], buffer.at[t], sems.at[t])
        for t in range(taps)
    ]
    for copy in copies:
        copy.start()
    for t in range(taps):
        copies[t].wait()
        for k, out in enumerate((one_ref, two_ref)):
            parts = [buffer[t, pl.ds(2 * half + k, chans, stride=2 * per), :] for half in range(per)]
            out[t * chans : (t + 1) * chans, :] = jnp.concatenate(parts, axis=1).astype(BF16)


def place_shifted(ref, row_index, row):
    store_shifted(ref, row_index * row.shape[0], row)


def window_rows(g, x_ref, first, count):
    size = count * g.wp
    return jnp.concatenate(
        [x_ref[(first + a) * g.wp : (first + a) * g.wp + size, :] for a in range(3)], axis=1
    )


def own_conv_kernel(g, ext, w, z_ref, st_ref, x_ref):
    count = g.h - 2
    s1 = jnp.zeros((8, g.c), F32)
    s2 = jnp.zeros((8, g.c), F32)
    for s in range(g.s):
        for r in range(g.h):
            place_shifted(x_ref, s * (g.h + 2) + 1 + r, wide(ext, s, r))
        half = count // 2
        for first in range(0, count, half):
            acc = dot(window_rows(g, x_ref, s * (g.h + 2) + 1 + first, half), w[...])
            at = (s * (g.tall - 2) + RIM + first) * g.wp
            z_ref[at : at + half * g.wp, :] = acc
            for i in range(half):
                v = acc[i * g.wp : i * g.wp + g.w]
                s1 = s1 + sum_rows(v)
                s2 = s2 + sum_rows(v * v)
    st_ref[0:8] = s1
    st_ref[8:16] = s2


def rim_conv_kernel(
    g, ext, ra, rb, rb_c, rb_d, w, st_in, z_in, x_in, z_ref, st_ref, x_own, cot_ref, x_ref
):
    del z_in, x_in
    place = Place()
    odd = place.odd_row
    s1, s2 = st_in[0:8], st_in[8:16]
    span = RIM + 2
    for s in range(g.s):
        far = far_rows(g, place, rb, rb_c, rb_d, s)
        near = [wide(ra, s, k) for k in range(RIM + g.near)]
        for side in range(2):
            base = span * (2 * s + side)
            beyond = [
                jnp.where(odd, b, a) if side else jnp.where(odd, a, b)
                for a, b in zip(near, far, strict=True)
            ]
            for k in range(RIM):
                place_shifted(x_ref, base + 2 * side + k, beyond[k])
            next_row = beyond[0 if side else RIM - 1]
            place_shifted(x_own, s * (g.h + 2) + (g.h + 1) * side, next_row)
            cot_ref[s, side] = beyond[RIM].astype(BF16)
            source = (s * (g.h + 2) + 1 + (g.h - 2) * side) * g.wp
            target = (base + RIM * (1 - side)) * g.wp
            x_ref[target : target + 2 * g.wp, :] = x_own[source : source + 2 * g.wp, :]
            acc = dot(window_rows(g, x_ref, base, RIM), w[...])
            at = (s * (g.tall - 2) + (g.h + RIM - 2) * side) * g.wp
            z_ref[at : at + RIM * g.wp, :] = acc
            i = 0 if side else RIM - 1
            v = acc[i * g.wp : i * g.wp + g.w]
            s1 = s1 + sum_rows(v)
            s2 = s2 + sum_rows(v * v)
    to_all(st_ref, [jnp.sum(s1, 0, keepdims=True), jnp.sum(s2, 0, keepdims=True)])


def stats_of(total, count):
    mean = total[0:1] / count
    var = total[1:2] / count - mean * mean
    return mean, lax.rsqrt(var + 1e-05)


def second_conv_kernel(g, chunk, count, z1, st, params, w, cot, h_ref, z_ref, st_ref):
    rows_in, rows_out = g.tall - 2, g.tall - 4
    place = Place()
    mean, rstd = stats_of(total_of(st), count)
    scale = params[0:1] * rstd
    shift = params[1:2] - mean * scale
    edge = edge_mask(place, g)
    sums = [jnp.zeros((8, g.c), F32) for _ in range(4)]
    for s in range(g.s):
        for r in range(rows_in):
            start = (s * rows_in + r) * g.wp
            row = jnp.maximum(z1[start : start + g.wp, :] * scale + shift, 0.0)
            store_shifted(h_ref, start, in_grid(row, r + 1, g, place, edge))
        for r in range(0, rows_out, chunk):
            base = (s * rows_in + r) * g.wp
            size = chunk * g.wp
            lhs = jnp.concatenate(
                [h_ref[base + a * g.wp : base + a * g.wp + size, :] for a in range(3)], axis=1
            )
            acc = dot(lhs, w[...])
            z_ref[(s * rows_out + r) * g.wp : (s * rows_out + r) * g.wp + size, :] = acc
            for i in range(chunk):
                if RIM <= r + i + 2 < RIM + g.h:
                    v = acc[i * g.wp : i * g.wp + g.w]
                    dn = wide(cot, s, r + i + 2 - RIM)[: g.w]
                    for k, term in enumerate((v, v * v, dn, dn * v)):
                        sums[k] = sums[k] + sum_rows(term)
    to_all(st_ref, [jnp.sum(v, 0, keepdims=True) for v in sums])


def own_transposed(g, source, first, s, dt_ref):
    span = g.h * g.wp
    block = source[first : first + span, :]
    inside = lax.broadcasted_iota(jnp.int32, (span, 1), 0) % g.wp < g.w
    dt_ref[:, s * span : (s + 1) * span] = jnp.where(inside, block, jnp.zeros_like(block)).T


def kernel_gradient(g, core, field, rows_field, first_row, dt_ref, keep, send, first, prepare):
    chans, half = g.c, g.c // 2
    span = g.h * g.wp
    mine = pl.ds(pl.multiple_of(core * half, half), half)
    other = pl.ds(pl.multiple_of((1 - core) * half, half), half)
    totals = [None] * 3
    cut = g.s // 2
    groups = (range(cut), range(cut, g.s))
    for s in groups[0]:
        prepare(s)
    for group in groups:
        lanes = slice(group[0] * span, (group[-1] + 1) * span)
        lhs = jnp.concatenate([dt_ref[mine, lanes], dt_ref[other, lanes]], axis=0)
        for a in range(3):
            starts = [(s * rows_field + first_row + a) * g.wp for s in group]
            acc = dot(lhs, jnp.concatenate([field[at : at + span, :] for at in starts], axis=0))
            if group[0] == 0 and a < len(groups[1]):
                prepare(groups[1][a])
            if group[0] == 0:
                for b in range(3):
                    keep[a * 3 + b] = acc[0:half, b * chans : (b + 1) * chans]
                    first[a * 3 + b] = acc[half:, b * chans : (b + 1) * chans]
                continue
            for b in range(3):
                keep[a * 3 + b] += acc[0:half, b * chans : (b + 1) * chans]
                other_half = first[a * 3 + b] + acc[half:, b * chans : (b + 1) * chans]
                if isinstance(send, tuple):
                    send[a][b] = other_half.astype(BF16)
                else:
                    send[a * 3 + b] = other_half


def second_gradient_kernel(
    g, count, z2, st, params, cot, cot_next, h, d_ref, keep, send, dt_ref
):
    place = Place()
    rows = g.cot_tall
    total = total_of(st)
    mean, rstd = stats_of(total, count)
    sum_dn = total[2:3]
    sum_dx = rstd * (total[3:4] - mean * sum_dn)
    k0 = params[2:3] * rstd
    k1 = k0 * (sum_dn / count)
    k2 = k0 * rstd * (sum_dx / count)
    edge = edge_mask(place, g)
    def prepare(s):
        for i in range(rows):
            rim = not g.near <= i < g.near + g.h
            dn = wide(cot_next, s, 0 if i < g.near else 1) if rim else wide(cot, s, i - g.near)
            start = (s * rows + i) * g.wp
            d = k0 * dn - k1 - (z2[start : start + g.wp, :] - mean) * k2
            d = in_grid(d, i + RIM - g.near, g, place, edge)
            d_ref[start : start + g.wp, :] = d.astype(BF16)
        own_transposed(g, d_ref, (s * rows + g.near) * g.wp, s, dt_ref)
    kernel_gradient(g, place.core, h, g.tall - 2, RIM - 2, dt_ref, keep, send, send, prepare)


def transposed_conv(g, d_ref, w, s, rows_in, r, chunk):
    acc = None
    size = chunk * g.wp
    for a in range(3):
        start = (s * rows_in + r + a) * g.wp
        for b in range(3):
            tap = (2 - a) * 3 + (2 - b)
            term = dot_nt(
                d_ref[start : start + size, b * g.c : (b + 1) * g.c],
                w[tap * g.c : (tap + 1) * g.c, :],
            )
            acc = term if acc is None else acc + term
    return acc


def hidden_gradient_kernel(
    g, chunk, count, d, w, z1, z2, st, st2, params, ext, dn_ref, st_ref, out_ref, d_ref
):
    mean2, rstd2 = stats_of(total_of(st2), count)
    scale2 = params[2:3] * rstd2
    shift2 = params[3:4] - mean2 * scale2
    rows_in, rows_out, z_rows = g.tall - 4, g.tall - 6, g.tall - 2
    mean, rstd = stats_of(total_of(st), count)
    scale = params[0:1] * rstd
    shift = params[1:2] - mean * scale
    s0 = jnp.zeros((8, g.c), F32)
    s1 = jnp.zeros((8, g.c), F32)
    for s in range(g.s):
        for i in range(rows_in):
            at = (s * rows_in + i) * g.wp
            store_shifted(d_ref, at, wide(d, slice(at, at + g.wp)))
        for r in range(g.h):
            at = (s * rows_in + r + g.near) * g.wp
            normed = z2[at : at + g.w, :] * scale2 + shift2
            out_ref[s, r] = (wide(ext, s, r)[: g.w] + normed).astype(BF16)
        for r in range(0, rows_out, chunk):
            acc = transposed_conv(g, d_ref, w, s, rows_in, r, chunk)
            at = (s * z_rows + r + 2) * g.wp
            z = z1[at : at + chunk * g.wp, :]
            dn = jnp.where(z * scale + shift > 0, acc, 0.0)
            dn_ref[(s * rows_out + r) * g.wp : (s * rows_out + r + chunk) * g.wp, :] = dn
            for i in range(chunk):
                if RIM <= r + i + 3 < RIM + g.h:
                    v = dn[i * g.wp : i * g.wp + g.w]
                    s0 = s0 + sum_rows(v)
                    s1 = s1 + sum_rows(v * (z[i * g.wp : i * g.wp + g.w] - mean))
    to_all(st_ref, [jnp.sum(s0, 0, keepdims=True), jnp.sum(s1, 0, keepdims=True) * rstd])


def first_gradient_kernel(
    g, count, dn, z, st, st3, params, x, e_ref, a_ref, b_ref, keep, send0, send1, send2, dt_ref, first
):
    place = Place()
    mean, rstd = stats_of(total_of(st), count)
    total = total_of(st3)
    k0 = params[0:1] * rstd
    k1 = k0 * (total[0:1] / count)
    k2 = k0 * rstd * (total[1:2] / count)
    edge = edge_mask(place, g)

    def prepare(s):
        for i in range(g.h):
            at = (s * g.h + i) * g.wp
            z_at = (s * (g.tall - 2) + i + RIM - 1) * g.wp
            d = k0 * dn[at : at + g.wp, :] - k1 - (z[z_at : z_at + g.wp, :] - mean) * k2
            d = in_grid(d, i + RIM, g, place, edge)
            e_ref[at : at + g.wp, :] = d.astype(BF16)
            if i == 0:
                top = d
        a_ref[s, 0] = jnp.where(place.odd_row, top, d).astype(BF16)
        b_ref[s, 0] = jnp.where(place.odd_row, d, top).astype(BF16)
        own_transposed(g, e_ref, s * g.h * g.wp, s, dt_ref)
    send = (send0, send1, send2)
    kernel_gradient(g, place.core, x, g.h + 2, 0, dt_ref, keep, send, first, prepare)


def input_gradient_kernel(
    g, chunk, e, ra, rb, w_far, cot_far, occ, out_ref, w, cot, e_ref, sems
):
    rows_in = g.h + 2
    place = Place()
    copies = [
        pltpu.make_async_copy(w_far, w, sems.at[0]),
        pltpu.make_async_copy(cot_far, cot, sems.at[1]),
    ]
    for copy in copies:
        copy.start()
    for copy in copies:
        copy.wait()
    for s in range(g.s):
        a, b = wide(ra, s, 0), wide(rb, s, 0)
        rows = [jnp.where(place.odd_row, a, b)]
        for r in range(g.h):
            at = (s * g.h + r) * g.wp
            rows.append(wide(e, slice(at, at + g.wp)))
        rows.append(jnp.where(place.odd_row, b, a))
        for i in range(rows_in):
            place_shifted(e_ref, s * rows_in + i, rows[i])
        mask = pixel_mask(occ, s)
        for r in range(0, g.h, chunk):
            acc = transposed_conv(g, e_ref, w, s, rows_in, r, chunk)
            for i in range(chunk):
                v = acc[i * g.wp : i * g.wp + g.w]
                out_ref[s, r + i] = (wide(cot, s, r + i) + v) * mask[:, r + i : r + i + 1]


def pair_total(keep, got, t):
    other = got[t] if len(got) > 3 else got[t // 3][t % 3].astype(F32)
    return keep[t] + other


def pair_sum_kernel(lane, keep, *refs):
    *got, out_far, buffer, sems = refs
    got = got[0] if len(got) == 1 else got[:3]
    taps, half, chans = keep.shape
    copies = []
    for t in range(taps):
        rows = pl.ds(t * chans, chans)
        buffer[rows, :] = pair_total(keep, got, t).astype(BF16).T
        copies.append(
            pltpu.make_async_copy(buffer.at[rows], out_far.at[rows, pl.ds(lane, half)], sems.at[t])
        )
        copies[-1].start()
    for copy in copies:
        copy.wait()


def half_rows(share):
    return -(-(share // 2) // 8) * 8


def split_kernel(keep, got, kept_ref, sent_ref, buffer):
    taps, half, chans = keep.shape
    devices, rows, _ = kept_ref.shape
    share = taps * chans // devices
    for t in range(taps):
        buffer[t * chans : (t + 1) * chans, :] = pair_total(keep, got, t).T
    second = Place().second
    for i in range(devices):
        mine = pl.multiple_of(i * share + (share - rows) * second, 8)
        other = pl.multiple_of(i * share + (share - rows) * (1 - second), 8)
        kept_ref[i] = buffer[pl.ds(mine, rows), :]
        sent_ref[i] = buffer[pl.ds(other, rows), :].astype(BF16)


def message_kernel(keep, got0, got1, got2, kept, came, out_far, buffer, out_ref, sems):
    taps, half, chans = keep.shape
    devices, rows, _ = kept.shape
    share = taps * chans // devices
    for t in range(taps):
        buffer[t * chans : (t + 1) * chans, :] = pair_total(keep, (got0, got1, got2), t).T
    copies = []
    count = sems.shape[0]
    for part in range(count):
        mine = pl.ds(part * devices // count, devices // count)
        for i in range(part * devices // count, (part + 1) * devices // count):
            first = buffer[i * share : (i + 1) * share, :]
            out_ref[i] = jnp.concatenate([first, kept[i] + wide(came, i)], axis=0).astype(BF16)
        copies.append(pltpu.make_async_copy(out_ref.at[mine], out_far.at[mine], sems.at[part]))
        copies[-1].start()
    for copy in copies:
        copy.wait()


def adamw(weight, grad, first, second, rate):
    first_new = 0.9 * first + 0.1 * grad
    second_new = 0.999 * second + 0.001 * grad * grad
    first_hat = first_new / (1.0 - 0.9**STEP)
    second_hat = second_new / (1.0 - 0.999**STEP)
    weight_new = weight - rate * (first_hat / (jnp.sqrt(second_hat) + 1e-08) + 0.01 * weight)
    return (weight_new, first_new, second_new)


def update_kernel(
    count, parts, w, first_m, second_m, st2, st3, params, n_first, n_second,
    grad_out, w_out, first_out, second_out, n_grad, n_out, n_first_out, n_second_out
):
    devices, ncols = parts.shape[0], lax.axis_size("cols")
    share = w.shape[0] // 4
    total2, total3 = total_of(st2), total_of(st3)
    mean, rstd = stats_of(total2, count)
    sum_dn = total2[2:3]
    grads = jnp.concatenate(
        [total3[1:2], total3[0:1], rstd * (total2[3:4] - mean * sum_dn), sum_dn], axis=0
    )
    n_grad[...] = grads
    n_out[...], n_first_out[...], n_second_out[...] = adamw(
        params[...], grads, n_first[...], n_second[...], 0.75
    )
    def over(chosen, rows, lanes):
        total = None
        for source in range(devices):
            if chosen(source // ncols):
                term = wide(parts, source)[rows, lanes]
                total = term if total is None else total + term
        return total

    grads = []
    every = slice(None)
    for half in range(2):
        if parts.shape[2] == 256:
            for k in range(2):
                lanes = slice(k * 128, (k + 1) * 128)
                grads.append((k, half, over(lambda row: row % 2 == half, every, lanes)))
        else:
            rows = half_rows(share)
            first = over(lambda row: row % 2 == half, slice(0, share), every)
            upper = over(lambda row: row % 4 == half, slice(share, None), every)
            lower = over(lambda row: row % 4 == half + 2, slice(2 * rows, None), every)
            grads += [(0, half, first), (1, half, jnp.concatenate([upper, lower], axis=0))]
    for k, half, grad in grads:
        at = pl.ds(2 * half + k, share, stride=4)
        new = adamw(w[at, :], grad, first_m[at, :], second_m[at, :], 0.02)
        grad_out[at, :] = grad
        w_out[at, :], first_out[at, :], second_out[at, :] = new


def swapped(block, axis, first):
    count = lax.axis_size(axis)
    pairs = []
    for i in range(first, count - 1, 2):
        pairs += [(i, i + 1), (i + 1, i)]
    return lax.ppermute(block, axis, pairs)


def swapped_both(block, first_row, first_col):
    nrows, ncols = lax.axis_size("rows"), lax.axis_size("cols")

    def partner(i, first, count):
        j = i + 1 if (i - first) % 2 == 0 else i - 1
        return j if min(i, j) >= first and max(i, j) < count else None

    pairs = []
    for i in range(nrows):
        for j in range(ncols):
            to = partner(i, first_row, nrows), partner(j, first_col, ncols)
            if None not in to:
                pairs.append((i * ncols + j, to[0] * ncols + to[1]))
    return lax.ppermute(block, BOTH, pairs)


def to_chunks(flat):
    return flat.reshape(2, -1, 128).transpose(1, 0, 2).reshape(-1, 128)


def from_chunks(rows):
    return rows.reshape(-1, 2, 128).transpose(1, 0, 2).reshape(2, -1)


def exchange(parts):
    return lax.all_to_all(parts, BOTH, 0, 0, tiled=True)


def body(
    features,
    occupancy,
    cotangent,
    conv_weights,
    conv_first,
    conv_second,
    norm_scale_bias,
    norm_first,
    norm_second,
):
    scenes, height, width, chans = features.shape
    g = Geometry(scenes, height, width, chans)
    wp = g.wp
    devices = lax.axis_size("rows") * lax.axis_size("cols")
    count = float(scenes * height * width * devices)
    taps = 9 * chans
    n0, n1, n2, n3 = (scenes * wp * (g.tall - 2 * i) for i in range(4))
    own_pixels = scenes * height * wp
    dma = pltpu.SemaphoreType.DMA

    def conv_flops(n):
        return 2 * n * taps * chans

    side = shape_of((scenes, g.side, chans), BF16)
    corner = shape_of((scenes, g.corner, chans), BF16)
    own, c, d, b, bc, bd = kernel_call(
        functools.partial(pack_kernel, g),
        [
            shape_of(features.shape, BF16),
            side,
            side,
            shape_of((scenes, RIM + g.near, width, chans), BF16),
            corner,
            corner,
        ],
        1e8,
        far=(0, 1, 2),
        scratch=[
            pltpu.VMEM(features.shape, BF16),
            pltpu.VMEM(features.shape, BF16),
            pltpu.VMEM(occupancy.shape, jnp.int32),
            dma((3, scenes)),
        ],
    )(features, occupancy, cotangent)
    rb = swapped(b, "rows", 1)
    rc, rd = swapped(c, "cols", 0), swapped(d, "cols", 1)
    rb_c, rb_d = swapped_both(bc, 1, 0), swapped_both(bd, 1, 1)
    chunked = to_chunks(conv_weights)
    share = conv_first.shape[1]
    chunk_shape = shape_of((share // 64, 128), F32)
    weights = (taps, chans)
    w1, w2 = kernel_call(
        prepare_kernel,
        [held(weights, BF16)] * 2,
        0,
        size=1024,
        far=(0,),
        scratch=[pltpu.VMEM((9, chunked.shape[0] // 9, 128), F32), dma((9,))],
    )(chunked)

    def wide_rows(rows):
        return shape_of((scenes, rows, wp, chans), BF16)

    ext, cot_ext, a = kernel_call(
        functools.partial(assemble_kernel, g),
        [wide_rows(n) for n in (height, height, RIM + g.near)],
        0,
        size=1024,
    )(own, cotangent, rc, rd)
    rows_x = scenes * (height + 2) * wp
    x_shape = held((rows_x, 3 * chans), BF16)
    z1, st, x = kernel_call(
        functools.partial(own_conv_kernel, g),
        [held((n1, chans), F32), held((16, chans), F32), x_shape],
        0,
        size=1024,
    )(ext, w1)
    a, rb, rb_c, rb_d, w1 = lax.optimization_barrier((a, rb, rb_c, rb_d, w1))
    ra = swapped(a, "rows", 0)
    z1, st, x, cot_next = kernel_call(
        functools.partial(rim_conv_kernel, g),
        [held((n1, chans), F32), shape_of((devices, 2, chans), F32), x_shape, wide_rows(2)],
        0,
        size=1024,
        scratch=[pltpu.VMEM((scenes * 2 * (RIM + 2) * wp, 3 * chans), BF16)],
        alias={7: 0, 8: 2},
    )(ext, ra, rb, rb_c, rb_d, w1, st, z1, x)
    st1 = exchange(st)
    h, z2, st = kernel_call(
        functools.partial(second_conv_kernel, g, 5, count),
        [
            held((n1, 3 * chans), BF16),
            held((n2, chans), F32),
            shape_of((devices, 4, chans), F32),
        ],
        conv_flops(n2),
    )(z1, st1, norm_scale_bias, w2, cot_ext)
    st2 = exchange(st)
    grad_shape = held((9, chans // 2, chans), F32)
    d, keep2, send2 = kernel_call(
        functools.partial(second_gradient_kernel, g, count),
        [held((n2, chans), BF16), grad_shape, grad_shape],
        conv_flops(own_pixels),
        scratch=[pltpu.VMEM((chans, own_pixels), BF16)],
    )(z2, st2, norm_scale_bias, cot_ext, cot_next, h)
    got2 = swapped(send2, "rows", 0)
    dn1, st, block_out = kernel_call(
        functools.partial(hidden_gradient_kernel, g, 8, count),
        [
            held((n3, chans), F32),
            shape_of((devices, 2, chans), F32),
            held(features.shape, BF16),
        ],
        conv_flops(n3),
        scratch=[pltpu.VMEM((n2, 3 * chans), BF16)],
    )(d, w2, z1, z2, st1, st2, norm_scale_bias, ext)
    nrows = lax.axis_size("rows")
    cut_again = nrows % 4 == 0 and taps // devices % 8 == 0
    if cut_again:
        got2, st = lax.optimization_barrier((got2, st))
        kept_shape = (devices, half_rows(taps // devices), chans // 2)
        kept, sent = kernel_call(
            split_kernel,
            [held(kept_shape, F32), held(kept_shape, BF16)],
            1e8,
            scratch=[pltpu.VMEM((taps, chans // 2), F32)],
        )(keep2, got2)
        st, kept = lax.optimization_barrier((st, kept))
        st3 = exchange(st)
    else:
        st, got2 = lax.optimization_barrier((st, got2))
        st3 = exchange(st)
    cut = held((3, chans // 2, chans), BF16)
    e, a, b, keep1, *send1 = kernel_call(
        functools.partial(first_gradient_kernel, g, count),
        [held((n3, chans), BF16), wide_rows(1), wide_rows(1), grad_shape, cut, cut, cut],
        0,
        size=1024,
        scratch=[pltpu.VMEM((chans, own_pixels), BF16), pltpu.VMEM(grad_shape.shape, F32)],
    )(dn1, z1, st1, st3, norm_scale_bias, x)
    got1 = [swapped(part, "rows", 0) for part in send1]
    share_rows = taps // devices
    buffer = pltpu.VMEM((taps, chans // 2), F32)
    if cut_again:
        came = lax.ppermute(sent, "rows", [(i, i ^ 2) for i in range(nrows)])
        rows = share_rows + kept.shape[1]
        (parts,) = kernel_call(
            message_kernel,
            [stored((devices, rows, chans // 2), BF16)],
            1e9,
            far_out=(0,),
            scratch=[buffer, pltpu.VMEM((devices, rows, chans // 2), BF16), dma((4,))],
        )(keep1, *got1, kept, came)
    else:

        def add_pair(lane, *operands, **options):
            return kernel_call(
                functools.partial(pair_sum_kernel, lane),
                [stored((taps, chans), BF16)],
                1e9,
                far_out=(0,),
                scratch=[pltpu.VMEM((taps, chans // 2), BF16), dma((9,))],
                **options,
            )(*operands)

        (parts,) = add_pair(chans // 2, keep2, got2)
        (parts,) = add_pair(0, keep1, *got1, parts, far=(4,), alias={4: 0})
        parts = parts.reshape(devices, share_rows, chans)
    parts, chunked = lax.optimization_barrier((parts, chunked))
    parts = exchange(parts)
    ra, rb = swapped(a, "rows", 0), swapped(b, "rows", 1)
    (grad_input,) = kernel_call(
        functools.partial(input_gradient_kernel, g, 8),
        [shape_of(features.shape, F32)],
        conv_flops(own_pixels),
        far=(3, 4),
        scratch=[
            pltpu.VMEM(weights, BF16),
            pltpu.VMEM(features.shape, BF16),
            pltpu.VMEM((rows_x, 3 * chans), BF16),
            dma((2,)),
        ],
    )(e, ra, rb, w1, cotangent, occupancy)
    own_rows = share // 64
    first_row = (lax.axis_index("rows") * lax.axis_size("cols") + lax.axis_index("cols")) * own_rows
    own_weights = lax.dynamic_slice_in_dim(chunked, first_row, own_rows, 0)

    norm_shape = shape_of(norm_first.shape, F32)
    updated = kernel_call(
        functools.partial(update_kernel, count),
        [chunk_shape] * 4 + [norm_shape] * 4,
        1e8,
    )(
        parts, own_weights, to_chunks(conv_first), to_chunks(conv_second), st2, st3,
        norm_scale_bias, norm_first, norm_second,
    )
    return (block_out, grad_input, *map(from_chunks, updated[:4]), *updated[4:])


def solution(mesh):
    tile = P(None, "rows", "cols", None)
    share = P(None, ("rows", "cols"))
    return jax.shard_map(
        body,
        mesh=mesh,
        in_specs=(tile, P(None, "rows", "cols"), tile, P(), share, share, P(), P(), P()),
        out_specs=(tile, tile, share, share, share, share, P(), P(), P(), P()),
        check_vma=False,
    )
```

```python
import functools
import math

import jax
import jax.numpy as jnp
from jax import lax
from jax.experimental import pallas as pl
from jax.experimental.pallas import tpu as pltpu
from jax.sharding import PartitionSpec as P

STEP = 5
BOTH = ("rows", "cols")
RIM = 3
COLS = 4
SIDE = 2 * COLS
F32, BF16 = jnp.float32, jnp.bfloat16


def shape_of(shape, dtype):
    return jax.ShapeDtypeStruct(shape, dtype)


def held(shape, dtype):
    return pltpu.VMEM(shape, dtype)


def stored(shape, dtype):
    return pltpu.HBM(shape, dtype)


def kernel_call(body, out_shape, flops, far=(), far_out=(), scratch=(), limit=16, alias=None, size=4 << 20):
    def call(*operands):
        operands = [
            pltpu.with_memory_space_constraint(v, pltpu.HBM if i in far else pltpu.VMEM)
            for i, v in enumerate(operands)
        ]
        specs = [
            pl.BlockSpec(memory_space=pltpu.HBM if i in far else pltpu.VMEM)
            for i in range(len(operands))
        ]
        return pl.pallas_call(
            body,
            out_shape=out_shape,
            in_specs=specs,
            out_specs=[
                pl.BlockSpec(memory_space=pltpu.HBM if i in far_out else pltpu.VMEM)
                for i in range(len(out_shape))
            ],
            scratch_shapes=list(scratch),
            input_output_aliases=alias or {},
            compiler_params=pltpu.CompilerParams(vmem_limit_bytes=limit << 20),
            cost_estimate=pl.CostEstimate(
                flops=int(flops), bytes_accessed=size, transcendentals=0
            ),
        )(*operands)

    return call


def dot(a, b):
    return jnp.dot(a, b, preferred_element_type=F32)


def dot_nt(a, b):
    return lax.dot_general(a, b, (((1,), (1,)), ((), ())), preferred_element_type=F32)


def total_of(ref):
    count = ref.shape[0]
    total = ref[0]
    for i in range(1, count):
        total = total + ref[i]
    return total


def to_all(ref, parts):
    value = jnp.concatenate(parts, axis=0)
    for i in range(ref.shape[0]):
        ref[i] = value


def store_shifted(ref, start, row, offsets=(0, 1, 2)):
    width, chans = row.shape
    for b in offsets:
        moved = row if b == 1 else pltpu.roll(row, 1 if b == 0 else width - 1, 0)
        ref[start : start + width, b * chans : (b + 1) * chans] = moved.astype(BF16)


class Geometry:
    def __init__(self, scenes, height, width, chans):
        self.s, self.h, self.w, self.c = scenes, height, width, chans
        self.wp = width + SIDE
        self.tall = height + 2 * RIM
        self.near = RIM - 2
        self.near_cols = COLS - 2
        self.cot_tall = height + 2 * self.near
        self.side = (COLS + self.near_cols) * height
        self.corner = -(-(COLS * RIM + self.near_cols * self.near) // 16) * 16


class Place:
    def __init__(self):
        row, col = lax.axis_index("rows"), lax.axis_index("cols")
        nrows, ncols = lax.axis_size("rows"), lax.axis_size("cols")
        self.above = (row > 0).astype(F32)
        self.below = (row < nrows - 1).astype(F32)
        self.right = (col < ncols - 1).astype(F32)
        self.left = (col > 0).astype(F32)
        self.core = row % 2
        self.second = row // 2 % 2
        self.odd_row = row % 2 == 1
        self.odd_col = col % 2 == 1
        self.index = row * ncols + col


def wide(ref, *index):
    return ref[index].astype(F32)


def far_rows(g, place, rb, rb_c, rb_d, s):
    right, left = sides(g, place, rb_c, rb_d, s)
    rows = []
    for k in range(RIM + g.near):
        width = COLS if k < RIM else g.near_cols
        at = COLS * min(k, RIM) + g.near_cols * max(k - RIM, 0)
        rows.append(
            jnp.concatenate([wide(rb, s, k), side_columns(g, right, left, at, width)], axis=0)
        )
    return rows


def pixel_mask(occ, s):
    return occ[s].astype(F32).T


def in_grid(row, r, g, place, edge):
    row = jnp.concatenate([row[: g.w], row[g.w :] * edge], axis=0)
    if r < RIM:
        row = row * place.above
    elif r >= RIM + g.h:
        row = row * place.below
    return row


def edge_mask(place, g):
    where = lax.broadcasted_iota(jnp.int32, (SIDE, g.c), 0)
    return jnp.where(where < SIDE // 2, place.right, place.left)


def sum_rows(value):
    rows, chans = value.shape
    return jnp.sum(value.reshape(rows // 8, 8, chans), axis=0)


def pack_kernel(
    g, features, occ_far, cot, own, c_ref, d_ref, b_ref, bc_ref, bd_ref, given, seen, occ, sems
):
    copies = []
    flags = pltpu.make_async_copy(occ_far, occ, sems.at[2, 0])
    flags.start()
    for s in range(g.s):
        copies.append(
            (
                pltpu.make_async_copy(features.at[s], given.at[s], sems.at[0, s]),
                pltpu.make_async_copy(cot.at[s], seen.at[s], sems.at[1, s]),
            )
        )
        for copy in copies[-1]:
            copy.start()
    odd, odd_row = Place().odd_col, Place().odd_row
    flags.wait()

    for s in range(g.s):
        mask = pixel_mask(occ, s)
        for copy in copies[s]:
            copy.wait()
        rows = []
        for r in range(g.h):
            row = wide(given, s, r) * mask[:, r : r + 1]
            rows.append(row)
            own[s, r] = row.astype(BF16)
        cots = [wide(seen, s, r) for r in range(g.h)]
        ends = []
        for field, count in ((rows, RIM), (cots, g.near)):
            for k in range(count):
                ends.append(jnp.where(odd_row, field[g.h - count + k], field[k]))
                b_ref[s, len(ends) - 1] = ends[-1].astype(BF16)
        spare = jnp.zeros((g.corner - COLS * RIM - g.near_cols * g.near, g.c), F32)
        widths = [COLS] * RIM + [g.near_cols] * g.near
        right = [v[g.w - width :] for v, width in zip(ends, widths, strict=True)]
        left = [v[:width] for v, width in zip(ends, widths, strict=True)]
        right, left = (jnp.concatenate(v + [spare], axis=0) for v in (right, left))
        bc_ref[s] = jnp.where(odd, left, right).astype(BF16)
        bd_ref[s] = jnp.where(odd, right, left).astype(BF16)
        right = jnp.concatenate(
            [v[g.w - COLS :] for v in rows] + [v[g.w - g.near_cols :] for v in cots], axis=0
        )
        left = jnp.concatenate([v[:COLS] for v in rows] + [v[: g.near_cols] for v in cots], axis=0)
        c_ref[s] = jnp.where(odd, left, right).astype(BF16)
        d_ref[s] = jnp.where(odd, right, left).astype(BF16)


def sides(g, place, rc, rd, s):
    c, d = wide(rc, s), wide(rd, s)
    return jnp.where(place.odd_col, d, c), jnp.where(place.odd_col, c, d)


def side_columns(g, right, left, at, width):
    parts = [right[at : at + width], jnp.zeros((SIDE - 2 * width, g.c), F32), left[at : at + width]]
    return jnp.concatenate([part for part in parts if part.shape[0]], axis=0)


def assemble_kernel(g, own, cot, rc, rd, ext, cot_ext, a_ref):
    place = Place()

    odd = place.odd_row
    for s in range(g.s):
        right, left = sides(g, place, rc, rd, s)
        for source, full, at, width, count, first in (
            (own, ext, 0, COLS, RIM, 0),
            (cot, cot_ext, COLS * g.h, g.near_cols, g.near, RIM),
        ):
            rows = []
            for r in range(g.h):
                beyond = side_columns(g, right, left, at + width * r, width)
                rows.append(jnp.concatenate([wide(source, s, r), beyond], axis=0))
                full[s, r] = rows[r].astype(BF16)
            for k in range(count):
                top, bottom = rows[k], rows[g.h - count + k]
                a_ref[s, first + k] = jnp.where(odd, top, bottom).astype(BF16)


def prepare_kernel(w_ref, one_ref, two_ref, buffer, sems):
    chans = one_ref.shape[1]
    taps, size, lanes = buffer.shape
    per = chans // lanes
    copies = [
        pltpu.make_async_copy(w_ref.at[pl.ds(t * size, size)], buffer.at[t], sems.at[t])
        for t in range(taps)
    ]
    for copy in copies:
        copy.start()
    for t in range(taps):
        copies[t].wait()
        for k, out in enumerate((one_ref, two_ref)):
            parts = [buffer[t, pl.ds(2 * half + k, chans, stride=2 * per), :] for half in range(per)]
            out[t * chans : (t + 1) * chans, :] = jnp.concatenate(parts, axis=1).astype(BF16)


def place_shifted(ref, row_index, row):
    store_shifted(ref, row_index * row.shape[0], row)


def window_rows(g, x_ref, first, count):
    size = count * g.wp
    return jnp.concatenate(
        [x_ref[(first + a) * g.wp : (first + a) * g.wp + size, :] for a in range(3)], axis=1
    )


def own_conv_kernel(g, ext, w, z_ref, st_ref, x_ref):
    count = g.h - 2
    s1 = jnp.zeros((8, g.c), F32)
    s2 = jnp.zeros((8, g.c), F32)
    for s in range(g.s):
        for r in range(g.h):
            place_shifted(x_ref, s * (g.h + 2) + 1 + r, wide(ext, s, r))
        half = count // 2
        for first in range(0, count, half):
            acc = dot(window_rows(g, x_ref, s * (g.h + 2) + 1 + first, half), w[...])
            at = (s * (g.tall - 2) + RIM + first) * g.wp
            z_ref[at : at + half * g.wp, :] = acc
            for i in range(half):
                v = acc[i * g.wp : i * g.wp + g.w]
                s1 = s1 + sum_rows(v)
                s2 = s2 + sum_rows(v * v)
    st_ref[0:8] = s1
    st_ref[8:16] = s2


def rim_conv_kernel(
    g, ext, ra, rb, rb_c, rb_d, w, st_in, z_in, x_in, z_ref, st_ref, x_own, cot_ref, x_ref
):
    del z_in, x_in
    place = Place()
    odd = place.odd_row
    s1, s2 = st_in[0:8], st_in[8:16]
    span = RIM + 2
    for s in range(g.s):
        far = far_rows(g, place, rb, rb_c, rb_d, s)
        near = [wide(ra, s, k) for k in range(RIM + g.near)]
        for side in range(2):
            base = span * (2 * s + side)
            beyond = [
                jnp.where(odd, b, a) if side else jnp.where(odd, a, b)
                for a, b in zip(near, far, strict=True)
            ]
            for k in range(RIM):
                place_shifted(x_ref, base + 2 * side + k, beyond[k])
            next_row = beyond[0 if side else RIM - 1]
            place_shifted(x_own, s * (g.h + 2) + (g.h + 1) * side, next_row)
            cot_ref[s, side] = beyond[RIM].astype(BF16)
            source = (s * (g.h + 2) + 1 + (g.h - 2) * side) * g.wp
            target = (base + RIM * (1 - side)) * g.wp
            x_ref[target : target + 2 * g.wp, :] = x_own[source : source + 2 * g.wp, :]
            acc = dot(window_rows(g, x_ref, base, RIM), w[...])
            at = (s * (g.tall - 2) + (g.h + RIM - 2) * side) * g.wp
            z_ref[at : at + RIM * g.wp, :] = acc
            i = 0 if side else RIM - 1
            v = acc[i * g.wp : i * g.wp + g.w]
            s1 = s1 + sum_rows(v)
            s2 = s2 + sum_rows(v * v)
    to_all(st_ref, [jnp.sum(s1, 0, keepdims=True), jnp.sum(s2, 0, keepdims=True)])


def stats_of(total, count):
    mean = total[0:1] / count
    var = total[1:2] / count - mean * mean
    return mean, lax.rsqrt(var + 1e-05)


def second_conv_kernel(g, chunk, count, z1, st, params, w, cot, h_ref, z_ref, st_ref):
    rows_in, rows_out = g.tall - 2, g.tall - 4
    place = Place()
    mean, rstd = stats_of(total_of(st), count)
    scale = params[0:1] * rstd
    shift = params[1:2] - mean * scale
    edge = edge_mask(place, g)
    sums = [jnp.zeros((8, g.c), F32) for _ in range(4)]
    for s in range(g.s):
        for r in range(rows_in):
            start = (s * rows_in + r) * g.wp
            row = jnp.maximum(z1[start : start + g.wp, :] * scale + shift, 0.0)
            store_shifted(h_ref, start, in_grid(row, r + 1, g, place, edge))
        for r in range(0, rows_out, chunk):
            base = (s * rows_in + r) * g.wp
            size = chunk * g.wp
            lhs = jnp.concatenate(
                [h_ref[base + a * g.wp : base + a * g.wp + size, :] for a in range(3)], axis=1
            )
            acc = dot(lhs, w[...])
            z_ref[(s * rows_out + r) * g.wp : (s * rows_out + r) * g.wp + size, :] = acc
            for i in range(chunk):
                if RIM <= r + i + 2 < RIM + g.h:
                    v = acc[i * g.wp : i * g.wp + g.w]
                    dn = wide(cot, s, r + i + 2 - RIM)[: g.w]
                    for k, term in enumerate((v, v * v, dn, dn * v)):
                        sums[k] = sums[k] + sum_rows(term)
    to_all(st_ref, [jnp.sum(v, 0, keepdims=True) for v in sums])


def own_transposed(g, source, first, s, dt_ref):
    span = g.h * g.wp
    block = source[first : first + span, :]
    inside = lax.broadcasted_iota(jnp.int32, (span, 1), 0) % g.wp < g.w
    dt_ref[:, s * span : (s + 1) * span] = jnp.where(inside, block, jnp.zeros_like(block)).T


def kernel_gradient(g, core, field, rows_field, first_row, dt_ref, keep, send, first, prepare):
    chans, half = g.c, g.c // 2
    span = g.h * g.wp
    mine = pl.ds(pl.multiple_of(core * half, half), half)
    other = pl.ds(pl.multiple_of((1 - core) * half, half), half)
    totals = [None] * 3
    cut = g.s // 2
    groups = (range(cut), range(cut, g.s))
    for s in groups[0]:
        prepare(s)
    for group in groups:
        lanes = slice(group[0] * span, (group[-1] + 1) * span)
        lhs = jnp.concatenate([dt_ref[mine, lanes], dt_ref[other, lanes]], axis=0)
        for a in range(3):
            starts = [(s * rows_field + first_row + a) * g.wp for s in group]
            acc = dot(lhs, jnp.concatenate([field[at : at + span, :] for at in starts], axis=0))
            if group[0] == 0 and a < len(groups[1]):
                prepare(groups[1][a])
            if group[0] == 0:
                for b in range(3):
                    keep[a * 3 + b] = acc[0:half, b * chans : (b + 1) * chans]
                    first[a * 3 + b] = acc[half:, b * chans : (b + 1) * chans]
                continue
            for b in range(3):
                keep[a * 3 + b] += acc[0:half, b * chans : (b + 1) * chans]
                other_half = first[a * 3 + b] + acc[half:, b * chans : (b + 1) * chans]
                send[a * 3 + b] = other_half


def second_gradient_kernel(
    g, count, z2, st, params, cot, cot_next, h, d_ref, keep, send, dt_ref
):
    place = Place()
    rows = g.cot_tall
    total = total_of(st)
    mean, rstd = stats_of(total, count)
    sum_dn = total[2:3]
    sum_dx = rstd * (total[3:4] - mean * sum_dn)
    k0 = params[2:3] * rstd
    k1 = k0 * (sum_dn / count)
    k2 = k0 * rstd * (sum_dx / count)
    edge = edge_mask(place, g)
    def prepare(s):
        for i in range(rows):
            rim = not g.near <= i < g.near + g.h
            dn = wide(cot_next, s, 0 if i < g.near else 1) if rim else wide(cot, s, i - g.near)
            start = (s * rows + i) * g.wp
            d = k0 * dn - k1 - (z2[start : start + g.wp, :] - mean) * k2
            d = in_grid(d, i + RIM - g.near, g, place, edge)
            d_ref[start : start + g.wp, :] = d.astype(BF16)
        own_transposed(g, d_ref, (s * rows + g.near) * g.wp, s, dt_ref)
    kernel_gradient(g, place.core, h, g.tall - 2, RIM - 2, dt_ref, keep, send, send, prepare)


def transposed_conv(g, d_ref, w, s, rows_in, r, chunk):
    acc = None
    size = chunk * g.wp
    for a in range(3):
        start = (s * rows_in + r + a) * g.wp
        for b in range(3):
            tap = (2 - a) * 3 + (2 - b)
            term = dot_nt(
                d_ref[start : start + size, b * g.c : (b + 1) * g.c],
                w[tap * g.c : (tap + 1) * g.c, :],
            )
            acc = term if acc is None else acc + term
    return acc


def hidden_gradient_kernel(
    g, chunk, count, d, w, z1, z2, st, st2, params, ext, dn_ref, st_ref, out_ref, d_ref
):
    mean2, rstd2 = stats_of(total_of(st2), count)
    scale2 = params[2:3] * rstd2
    shift2 = params[3:4] - mean2 * scale2
    rows_in, rows_out, z_rows = g.tall - 4, g.tall - 6, g.tall - 2
    mean, rstd = stats_of(total_of(st), count)
    scale = params[0:1] * rstd
    shift = params[1:2] - mean * scale
    s0 = jnp.zeros((8, g.c), F32)
    s1 = jnp.zeros((8, g.c), F32)
    for s in range(g.s):
        for i in range(rows_in):
            at = (s * rows_in + i) * g.wp
            store_shifted(d_ref, at, wide(d, slice(at, at + g.wp)))
        for r in range(g.h):
            at = (s * rows_in + r + g.near) * g.wp
            normed = z2[at : at + g.w, :] * scale2 + shift2
            out_ref[s, r] = (wide(ext, s, r)[: g.w] + normed).astype(BF16)
        for r in range(0, rows_out, chunk):
            acc = transposed_conv(g, d_ref, w, s, rows_in, r, chunk)
            at = (s * z_rows + r + 2) * g.wp
            z = z1[at : at + chunk * g.wp, :]
            dn = jnp.where(z * scale + shift > 0, acc, 0.0)
            dn_ref[(s * rows_out + r) * g.wp : (s * rows_out + r + chunk) * g.wp, :] = dn
            for i in range(chunk):
                if RIM <= r + i + 3 < RIM + g.h:
                    v = dn[i * g.wp : i * g.wp + g.w]
                    s0 = s0 + sum_rows(v)
                    s1 = s1 + sum_rows(v * (z[i * g.wp : i * g.wp + g.w] - mean))
    to_all(st_ref, [jnp.sum(s0, 0, keepdims=True), jnp.sum(s1, 0, keepdims=True) * rstd])


def half_gradient(g, which, field, rows_field, first_row, dt_ref, out_ref, sums, prepare=None):
    chans, half = g.c, g.c // 2
    span = g.h * g.wp
    channels = pl.ds(pl.multiple_of(which * half, half), half)
    cut = g.s // 2
    groups = range(cut), range(cut, g.s)
    if prepare is not None:
        for s in groups[0]:
            prepare(s)
    for group in groups:
        lhs = dt_ref[channels, group[0] * span : (group[-1] + 1) * span]
        for a in range(3):
            starts = [(s * rows_field + first_row + a) * g.wp for s in group]
            acc = dot(lhs, jnp.concatenate([field[at : at + span, :] for at in starts], axis=0))
            if group[0] == 0 and prepare is not None and a < len(groups[1]):
                prepare(groups[1][a])
            for b in range(3):
                part = acc[:, b * chans : (b + 1) * chans]
                if group[0] == 0:
                    sums[a * 3 + b] = part
                else:
                    rows = slice((a * 3 + b) * chans, (a * 3 + b + 1) * chans)
                    out_ref[rows, :] = (sums[a * 3 + b] + part).T.astype(out_ref.dtype)


def first_gradient_kernel(
    g, count, dn, z, st, st3, params, x, e_ref, a_ref, b_ref, send, dt_ref, first
):
    place = Place()
    mean, rstd = stats_of(total_of(st), count)
    total = total_of(st3)
    k0 = params[0:1] * rstd
    k1 = k0 * (total[0:1] / count)
    k2 = k0 * rstd * (total[1:2] / count)
    edge = edge_mask(place, g)

    def prepare(s):
        for i in range(g.h):
            at = (s * g.h + i) * g.wp
            z_at = (s * (g.tall - 2) + i + RIM - 1) * g.wp
            d = k0 * dn[at : at + g.wp, :] - k1 - (z[z_at : z_at + g.wp, :] - mean) * k2
            d = in_grid(d, i + RIM, g, place, edge)
            e_ref[at : at + g.wp, :] = d.astype(BF16)
            if i == 0:
                top = d
        a_ref[s, 0] = jnp.where(place.odd_row, top, d).astype(BF16)
        b_ref[s, 0] = jnp.where(place.odd_row, d, top).astype(BF16)
        own_transposed(g, e_ref, s * g.h * g.wp, s, dt_ref)
    half_gradient(g, 1 - place.core, x, g.h + 2, 0, dt_ref, send, first, prepare)


def first_own_kernel(g, x, dt_ref, keep, first):
    half_gradient(g, Place().core, x, g.h + 2, 0, dt_ref, keep, first)


def input_gradient_kernel(
    g, chunk, e, ra, rb, w_far, cot_far, occ, out_ref, w, cot, e_ref, sems
):
    rows_in = g.h + 2
    place = Place()
    copies = [
        pltpu.make_async_copy(w_far, w, sems.at[0]),
        pltpu.make_async_copy(cot_far, cot, sems.at[1]),
    ]
    for copy in copies:
        copy.start()
    for copy in copies:
        copy.wait()
    for s in range(g.s):
        a, b = wide(ra, s, 0), wide(rb, s, 0)
        rows = [jnp.where(place.odd_row, a, b)]
        for r in range(g.h):
            at = (s * g.h + r) * g.wp
            rows.append(wide(e, slice(at, at + g.wp)))
        rows.append(jnp.where(place.odd_row, b, a))
        for i in range(rows_in):
            place_shifted(e_ref, s * rows_in + i, rows[i])
        mask = pixel_mask(occ, s)
        for r in range(0, g.h, chunk):
            acc = transposed_conv(g, e_ref, w, s, rows_in, r, chunk)
            for i in range(chunk):
                v = acc[i * g.wp : i * g.wp + g.w]
                out_ref[s, r + i] = (wide(cot, s, r + i) + v) * mask[:, r + i : r + i + 1]


def pair_total(keep, got, t):
    if keep.ndim == 3:
        return (keep[t] + wide(got, t)).T
    chans = 2 * keep.shape[1]
    rows = slice(t * chans, (t + 1) * chans)
    return keep[rows, :] + wide(got, rows)


def pair_sum_kernel(lane, keep, got, *refs):
    *_, out_far, buffer, sems = refs
    half = buffer.shape[1]
    chans = 2 * half
    taps = buffer.shape[0] // chans
    copies = []
    for t in range(taps):
        rows = pl.ds(t * chans, chans)
        buffer[rows, :] = pair_total(keep, got, t).astype(BF16)
        copies.append(
            pltpu.make_async_copy(buffer.at[rows], out_far.at[rows, pl.ds(lane, half)], sems.at[t])
        )
        copies[-1].start()
    for copy in copies:
        copy.wait()


def half_rows(share):
    return -(-(share // 2) // 8) * 8


def split_kernel(keep, got, kept_ref, sent_ref, buffer):
    taps, half, chans = keep.shape
    devices, rows, _ = kept_ref.shape
    share = taps * chans // devices
    for t in range(taps):
        buffer[t * chans : (t + 1) * chans, :] = pair_total(keep, got, t)
    second = Place().second
    for i in range(devices):
        mine = pl.multiple_of(i * share + (share - rows) * second, 8)
        other = pl.multiple_of(i * share + (share - rows) * (1 - second), 8)
        kept_ref[i] = buffer[pl.ds(mine, rows), :]
        sent_ref[i] = buffer[pl.ds(other, rows), :].astype(BF16)


def join_kernel(kept, came, out_ref):
    for i in range(kept.shape[0]):
        out_ref[i] = kept[i] + wide(came, i)


def message_kernel(keep, got, kept, out_far, out_ref, sems):
    devices = kept.shape[0]
    share = keep.shape[0] // devices
    copies = []
    count = sems.shape[0]
    for part in range(count):
        mine = pl.ds(part * devices // count, devices // count)
        for i in range(part * devices // count, (part + 1) * devices // count):
            rows = slice(i * share, (i + 1) * share)
            first = keep[rows, :] + wide(got, rows)
            out_ref[i] = jnp.concatenate([first, kept[i]], axis=0).astype(BF16)
        copies.append(pltpu.make_async_copy(out_ref.at[mine], out_far.at[mine], sems.at[part]))
        copies[-1].start()
    for copy in copies:
        copy.wait()


def adamw(weight, grad, first, second, rate):
    first_new = 0.9 * first + 0.1 * grad
    second_new = 0.999 * second + 0.001 * grad * grad
    first_hat = first_new / (1.0 - 0.9**STEP)
    second_hat = second_new / (1.0 - 0.999**STEP)
    weight_new = weight - rate * (first_hat / (jnp.sqrt(second_hat) + 1e-08) + 0.01 * weight)
    return (weight_new, first_new, second_new)


def update_kernel(
    count, parts, w, first_m, second_m, st2, st3, params, n_first, n_second,
    grad_out, w_out, first_out, second_out, n_grad, n_out, n_first_out, n_second_out
):
    devices, ncols = parts.shape[0], lax.axis_size("cols")
    share = w.shape[0] // 4
    total2, total3 = total_of(st2), total_of(st3)
    mean, rstd = stats_of(total2, count)
    sum_dn = total2[2:3]
    grads = jnp.concatenate(
        [total3[1:2], total3[0:1], rstd * (total2[3:4] - mean * sum_dn), sum_dn], axis=0
    )
    n_grad[...] = grads
    n_out[...], n_first_out[...], n_second_out[...] = adamw(
        params[...], grads, n_first[...], n_second[...], 0.75
    )
    def over(chosen, rows, lanes):
        total = None
        for source in range(devices):
            if chosen(source // ncols):
                term = wide(parts, source)[rows, lanes]
                total = term if total is None else total + term
        return total

    grads = []
    every = slice(None)
    for half in range(2):
        if parts.shape[2] == 256:
            for k in range(2):
                lanes = slice(k * 128, (k + 1) * 128)
                grads.append((k, half, over(lambda row: row % 2 == half, every, lanes)))
        else:
            rows = half_rows(share)
            first = over(lambda row: row % 2 == half, slice(0, share), every)
            upper = over(lambda row: row % 4 == half, slice(share, None), every)
            lower = over(lambda row: row % 4 == half + 2, slice(2 * rows, None), every)
            grads += [(0, half, first), (1, half, jnp.concatenate([upper, lower], axis=0))]
    for k, half, grad in grads:
        at = pl.ds(2 * half + k, share, stride=4)
        new = adamw(w[at, :], grad, first_m[at, :], second_m[at, :], 0.02)
        grad_out[at, :] = grad
        w_out[at, :], first_out[at, :], second_out[at, :] = new


def swapped(block, axis, first):
    count = lax.axis_size(axis)
    pairs = []
    for i in range(first, count - 1, 2):
        pairs += [(i, i + 1), (i + 1, i)]
    return lax.ppermute(block, axis, pairs)


def swapped_both(block, first_row, first_col):
    nrows, ncols = lax.axis_size("rows"), lax.axis_size("cols")

    def partner(i, first, count):
        j = i + 1 if (i - first) % 2 == 0 else i - 1
        return j if min(i, j) >= first and max(i, j) < count else None

    pairs = []
    for i in range(nrows):
        for j in range(ncols):
            to = partner(i, first_row, nrows), partner(j, first_col, ncols)
            if None not in to:
                pairs.append((i * ncols + j, to[0] * ncols + to[1]))
    return lax.ppermute(block, BOTH, pairs)


def to_chunks(flat):
    return flat.reshape(2, -1, 128).transpose(1, 0, 2).reshape(-1, 128)


def from_chunks(rows):
    return rows.reshape(-1, 2, 128).transpose(1, 0, 2).reshape(2, -1)


def exchange(parts):
    return lax.all_to_all(parts, BOTH, 0, 0, tiled=True)


def body(
    features,
    occupancy,
    cotangent,
    conv_weights,
    conv_first,
    conv_second,
    norm_scale_bias,
    norm_first,
    norm_second,
):
    scenes, height, width, chans = features.shape
    g = Geometry(scenes, height, width, chans)
    wp = g.wp
    devices = lax.axis_size("rows") * lax.axis_size("cols")
    count = float(scenes * height * width * devices)
    taps = 9 * chans
    n0, n1, n2, n3 = (scenes * wp * (g.tall - 2 * i) for i in range(4))
    own_pixels = scenes * height * wp
    dma = pltpu.SemaphoreType.DMA

    def conv_flops(n):
        return 2 * n * taps * chans

    side = shape_of((scenes, g.side, chans), BF16)
    corner = shape_of((scenes, g.corner, chans), BF16)
    own, c, d, b, bc, bd = kernel_call(
        functools.partial(pack_kernel, g),
        [
            shape_of(features.shape, BF16),
            side,
            side,
            shape_of((scenes, RIM + g.near, width, chans), BF16),
            corner,
            corner,
        ],
        1e8,
        far=(0, 1, 2),
        scratch=[
            pltpu.VMEM(features.shape, BF16),
            pltpu.VMEM(features.shape, BF16),
            pltpu.VMEM(occupancy.shape, jnp.int32),
            dma((3, scenes)),
        ],
    )(features, occupancy, cotangent)
    rb = swapped(b, "rows", 1)
    rc, rd = swapped(c, "cols", 0), swapped(d, "cols", 1)
    rb_c, rb_d = swapped_both(bc, 1, 0), swapped_both(bd, 1, 1)
    chunked = to_chunks(conv_weights)
    share = conv_first.shape[1]
    chunk_shape = shape_of((share // 64, 128), F32)
    weights = (taps, chans)
    w1, w2 = kernel_call(
        prepare_kernel,
        [held(weights, BF16)] * 2,
        0,
        size=1024,
        far=(0,),
        scratch=[pltpu.VMEM((9, chunked.shape[0] // 9, 128), F32), dma((9,))],
    )(chunked)

    def wide_rows(rows):
        return shape_of((scenes, rows, wp, chans), BF16)

    ext, cot_ext, a = kernel_call(
        functools.partial(assemble_kernel, g),
        [wide_rows(n) for n in (height, height, RIM + g.near)],
        0,
        size=1024,
    )(own, cotangent, rc, rd)
    rows_x = scenes * (height + 2) * wp
    x_shape = held((rows_x, 3 * chans), BF16)
    z1, st, x = kernel_call(
        functools.partial(own_conv_kernel, g),
        [held((n1, chans), F32), held((16, chans), F32), x_shape],
        0,
        size=1024,
    )(ext, w1)
    a, rb, rb_c, rb_d, w1 = lax.optimization_barrier((a, rb, rb_c, rb_d, w1))
    ra = swapped(a, "rows", 0)
    z1, st, x, cot_next = kernel_call(
        functools.partial(rim_conv_kernel, g),
        [held((n1, chans), F32), shape_of((devices, 2, chans), F32), x_shape, wide_rows(2)],
        0,
        size=1024,
        scratch=[pltpu.VMEM((scenes * 2 * (RIM + 2) * wp, 3 * chans), BF16)],
        alias={7: 0, 8: 2},
    )(ext, ra, rb, rb_c, rb_d, w1, st, z1, x)
    st1 = exchange(st)
    h, z2, st = kernel_call(
        functools.partial(second_conv_kernel, g, 5, count),
        [
            held((n1, 3 * chans), BF16),
            held((n2, chans), F32),
            shape_of((devices, 4, chans), F32),
        ],
        conv_flops(n2),
    )(z1, st1, norm_scale_bias, w2, cot_ext)
    st2 = exchange(st)
    grad_shape = held((9, chans // 2, chans), F32)
    d, keep2, send2 = kernel_call(
        functools.partial(second_gradient_kernel, g, count),
        [held((n2, chans), BF16), grad_shape, grad_shape],
        conv_flops(own_pixels),
        scratch=[pltpu.VMEM((chans, own_pixels), BF16)],
    )(z2, st2, norm_scale_bias, cot_ext, cot_next, h)
    got2 = swapped(send2, "rows", 0)
    dn1, st, block_out = kernel_call(
        functools.partial(hidden_gradient_kernel, g, 8, count),
        [
            held((n3, chans), F32),
            shape_of((devices, 2, chans), F32),
            held(features.shape, BF16),
        ],
        conv_flops(n3),
        scratch=[pltpu.VMEM((n2, 3 * chans), BF16)],
    )(d, w2, z1, z2, st1, st2, norm_scale_bias, ext)
    nrows = lax.axis_size("rows")
    cut_again = nrows % 4 == 0 and taps // devices % 8 == 0
    if cut_again:
        got2, st = lax.optimization_barrier((got2, st))
        kept_shape = (devices, half_rows(taps // devices), chans // 2)
        kept, sent = kernel_call(
            split_kernel,
            [held(kept_shape, F32), held(kept_shape, BF16)],
            1e8,
            scratch=[pltpu.VMEM((taps, chans // 2), F32)],
        )(keep2, got2)
        st, kept = lax.optimization_barrier((st, kept))
        came = lax.ppermute(sent, "rows", [(i, i ^ 2) for i in range(nrows)])
        st3 = exchange(st)
    else:
        st, got2 = lax.optimization_barrier((st, got2))
        st3 = exchange(st)
    if cut_again:
        kept, st3 = lax.optimization_barrier((kept, st3))
        (kept,) = kernel_call(join_kernel, [held(kept_shape, F32)], 0, size=1024)(kept, came)
        dn1, kept = lax.optimization_barrier((dn1, kept))
    sent_shape = held((taps, chans // 2), BF16)
    part = pltpu.VMEM(grad_shape.shape, F32)
    e, a, b, send1, dt = kernel_call(
        functools.partial(first_gradient_kernel, g, count),
        [
            held((n3, chans), BF16),
            wide_rows(1),
            wide_rows(1),
            sent_shape,
            held((chans, own_pixels), BF16),
        ],
        0,
        size=1024,
        scratch=[part],
    )(dn1, z1, st1, st3, norm_scale_bias, x)
    (keep1,) = kernel_call(
        functools.partial(first_own_kernel, g), [held((taps, chans // 2), F32)], 0, size=1024, scratch=[part]
    )(x, dt)
    got1 = swapped(send1, "rows", 0)
    share_rows = taps // devices
    if cut_again:
        rows = share_rows + kept.shape[1]
        (parts,) = kernel_call(
            message_kernel,
            [stored((devices, rows, chans // 2), BF16)],
            1e9,
            far_out=(0,),
            scratch=[pltpu.VMEM((devices, rows, chans // 2), BF16), dma((4,))],
        )(keep1, got1, kept)
    else:

        def add_pair(lane, *operands, **options):
            return kernel_call(
                functools.partial(pair_sum_kernel, lane),
                [stored((taps, chans), BF16)],
                1e9,
                far_out=(0,),
                scratch=[pltpu.VMEM((taps, chans // 2), BF16), dma((9,))],
                **options,
            )(*operands)

        (parts,) = add_pair(chans // 2, keep2, got2)
        (parts,) = add_pair(0, keep1, got1, parts, far=(2,), alias={2: 0})
        parts = parts.reshape(devices, share_rows, chans)
    parts, chunked = lax.optimization_barrier((parts, chunked))
    parts = exchange(parts)
    ra, rb = swapped(a, "rows", 0), swapped(b, "rows", 1)
    (grad_input,) = kernel_call(
        functools.partial(input_gradient_kernel, g, 8),
        [shape_of(features.shape, F32)],
        conv_flops(own_pixels),
        far=(3, 4),
        scratch=[
            pltpu.VMEM(weights, BF16),
            pltpu.VMEM(features.shape, BF16),
            pltpu.VMEM((rows_x, 3 * chans), BF16),
            dma((2,)),
        ],
    )(e, ra, rb, w1, cotangent, occupancy)
    own_rows = share // 64
    first_row = (lax.axis_index("rows") * lax.axis_size("cols") + lax.axis_index("cols")) * own_rows
    own_weights = lax.dynamic_slice_in_dim(chunked, first_row, own_rows, 0)

    norm_shape = shape_of(norm_first.shape, F32)
    updated = kernel_call(
        functools.partial(update_kernel, count),
        [chunk_shape] * 4 + [norm_shape] * 4,
        1e8,
    )(
        parts, own_weights, to_chunks(conv_first), to_chunks(conv_second), st2, st3,
        norm_scale_bias, norm_first, norm_second,
    )
    return (block_out, grad_input, *map(from_chunks, updated[:4]), *updated[4:])


def solution(mesh):
    tile = P(None, "rows", "cols", None)
    share = P(None, ("rows", "cols"))
    return jax.shard_map(
        body,
        mesh=mesh,
        in_specs=(tile, P(None, "rows", "cols"), tile, P(), share, share, P(), P(), P()),
        out_specs=(tile, tile, share, share, share, share, P(), P(), P(), P()),
        check_vma=False,
    )
```

```python
import functools
import math

import jax
import jax.numpy as jnp
from jax import lax
from jax.experimental import pallas as pl
from jax.experimental.pallas import tpu as pltpu
from jax.sharding import PartitionSpec as P

STEP = 5
BOTH = ("rows", "cols")
RIM = 3
COLS = 4
SIDE = 2 * COLS
F32, BF16 = jnp.float32, jnp.bfloat16


def shape_of(shape, dtype):
    return jax.ShapeDtypeStruct(shape, dtype)


def held(shape, dtype):
    return pltpu.VMEM(shape, dtype)


def stored(shape, dtype):
    return pltpu.HBM(shape, dtype)


def kernel_call(body, out_shape, flops, far=(), far_out=(), scratch=(), limit=16, alias=None, size=4 << 20):
    def call(*operands):
        operands = [
            pltpu.with_memory_space_constraint(v, pltpu.HBM if i in far else pltpu.VMEM)
            for i, v in enumerate(operands)
        ]
        specs = [
            pl.BlockSpec(memory_space=pltpu.HBM if i in far else pltpu.VMEM)
            for i in range(len(operands))
        ]
        return pl.pallas_call(
            body,
            out_shape=out_shape,
            in_specs=specs,
            out_specs=[
                pl.BlockSpec(memory_space=pltpu.HBM if i in far_out else pltpu.VMEM)
                for i in range(len(out_shape))
            ],
            scratch_shapes=list(scratch),
            input_output_aliases=alias or {},
            compiler_params=pltpu.CompilerParams(vmem_limit_bytes=limit << 20),
            cost_estimate=pl.CostEstimate(
                flops=int(flops), bytes_accessed=size, transcendentals=0
            ),
        )(*operands)

    return call


def dot(a, b):
    return jnp.dot(a, b, preferred_element_type=F32)


def dot_nt(a, b):
    return lax.dot_general(a, b, (((1,), (1,)), ((), ())), preferred_element_type=F32)


def total_of(ref):
    count = ref.shape[0]
    total = ref[0]
    for i in range(1, count):
        total = total + ref[i]
    return total


def to_all(ref, parts):
    value = jnp.concatenate(parts, axis=0)
    for i in range(ref.shape[0]):
        ref[i] = value


def store_shifted(ref, start, row, offsets=(0, 1, 2)):
    width, chans = row.shape
    for b in offsets:
        moved = row if b == 1 else pltpu.roll(row, 1 if b == 0 else width - 1, 0)
        ref[start : start + width, b * chans : (b + 1) * chans] = moved.astype(BF16)


class Geometry:
    def __init__(self, scenes, height, width, chans):
        self.s, self.h, self.w, self.c = scenes, height, width, chans
        self.wp = width + SIDE
        self.tall = height + 2 * RIM
        self.near = RIM - 2
        self.near_cols = COLS - 2
        self.cot_tall = height + 2 * self.near
        self.side = (COLS + self.near_cols) * height
        self.corner = -(-(COLS * RIM + self.near_cols * self.near) // 16) * 16


class Place:
    def __init__(self):
        row, col = lax.axis_index("rows"), lax.axis_index("cols")
        nrows, ncols = lax.axis_size("rows"), lax.axis_size("cols")
        self.above = (row > 0).astype(F32)
        self.below = (row < nrows - 1).astype(F32)
        self.right = (col < ncols - 1).astype(F32)
        self.left = (col > 0).astype(F32)
        self.core = row % 2
        self.second = row // 2 % 2
        self.odd_row = row % 2 == 1
        self.odd_col = col % 2 == 1
        self.index = row * ncols + col


def wide(ref, *index):
    return ref[index].astype(F32)


def far_rows(g, place, rb, rb_c, rb_d, s):
    right, left = sides(g, place, rb_c, rb_d, s)
    rows = []
    for k in range(RIM + g.near):
        width = COLS if k < RIM else g.near_cols
        at = COLS * min(k, RIM) + g.near_cols * max(k - RIM, 0)
        rows.append(
            jnp.concatenate([wide(rb, s, k), side_columns(g, right, left, at, width)], axis=0)
        )
    return rows


def pixel_mask(occ, s):
    return occ[s].astype(F32).T


def in_grid(row, r, g, place, edge):
    row = jnp.concatenate([row[: g.w], row[g.w :] * edge], axis=0)
    if r < RIM:
        row = row * place.above
    elif r >= RIM + g.h:
        row = row * place.below
    return row


def edge_mask(place, g):
    where = lax.broadcasted_iota(jnp.int32, (SIDE, g.c), 0)
    return jnp.where(where < SIDE // 2, place.right, place.left)


def sum_rows(value):
    rows, chans = value.shape
    return jnp.sum(value.reshape(rows // 8, 8, chans), axis=0)


def pack_kernel(
    g, features, occ_far, cot, own, c_ref, d_ref, b_ref, bc_ref, bd_ref, given, seen, occ, sems
):
    copies = []
    flags = pltpu.make_async_copy(occ_far, occ, sems.at[2, 0])
    flags.start()
    for s in range(g.s):
        copies.append(
            (
                pltpu.make_async_copy(features.at[s], given.at[s], sems.at[0, s]),
                pltpu.make_async_copy(cot.at[s], seen.at[s], sems.at[1, s]),
            )
        )
        for copy in copies[-1]:
            copy.start()
    odd, odd_row = Place().odd_col, Place().odd_row
    flags.wait()

    for s in range(g.s):
        mask = pixel_mask(occ, s)
        for copy in copies[s]:
            copy.wait()
        rows = []
        for r in range(g.h):
            row = wide(given, s, r) * mask[:, r : r + 1]
            rows.append(row)
            own[s, r] = row.astype(BF16)
        cots = [wide(seen, s, r) for r in range(g.h)]
        ends = []
        for field, count in ((rows, RIM), (cots, g.near)):
            for k in range(count):
                ends.append(jnp.where(odd_row, field[g.h - count + k], field[k]))
                b_ref[s, len(ends) - 1] = ends[-1].astype(BF16)
        spare = jnp.zeros((g.corner - COLS * RIM - g.near_cols * g.near, g.c), F32)
        widths = [COLS] * RIM + [g.near_cols] * g.near
        right = [v[g.w - width :] for v, width in zip(ends, widths, strict=True)]
        left = [v[:width] for v, width in zip(ends, widths, strict=True)]
        right, left = (jnp.concatenate(v + [spare], axis=0) for v in (right, left))
        bc_ref[s] = jnp.where(odd, left, right).astype(BF16)
        bd_ref[s] = jnp.where(odd, right, left).astype(BF16)
        right = jnp.concatenate(
            [v[g.w - COLS :] for v in rows] + [v[g.w - g.near_cols :] for v in cots], axis=0
        )
        left = jnp.concatenate([v[:COLS] for v in rows] + [v[: g.near_cols] for v in cots], axis=0)
        c_ref[s] = jnp.where(odd, left, right).astype(BF16)
        d_ref[s] = jnp.where(odd, right, left).astype(BF16)


def sides(g, place, rc, rd, s):
    c, d = wide(rc, s), wide(rd, s)
    return jnp.where(place.odd_col, d, c), jnp.where(place.odd_col, c, d)


def side_columns(g, right, left, at, width):
    parts = [right[at : at + width], jnp.zeros((SIDE - 2 * width, g.c), F32), left[at : at + width]]
    return jnp.concatenate([part for part in parts if part.shape[0]], axis=0)


def assemble_kernel(g, own, cot, rc, rd, ext, cot_ext, a_ref):
    place = Place()

    odd = place.odd_row
    for s in range(g.s):
        right, left = sides(g, place, rc, rd, s)
        for source, full, at, width, count, first in (
            (own, ext, 0, COLS, RIM, 0),
            (cot, cot_ext, COLS * g.h, g.near_cols, g.near, RIM),
        ):
            rows = []
            for r in range(g.h):
                beyond = side_columns(g, right, left, at + width * r, width)
                rows.append(jnp.concatenate([wide(source, s, r), beyond], axis=0))
                full[s, r] = rows[r].astype(BF16)
            for k in range(count):
                top, bottom = rows[k], rows[g.h - count + k]
                a_ref[s, first + k] = jnp.where(odd, top, bottom).astype(BF16)


def prepare_kernel(w_ref, one_ref, two_ref, buffer, sems):
    chans = one_ref.shape[1]
    taps, size, lanes = buffer.shape
    per = chans // lanes
    copies = [
        pltpu.make_async_copy(w_ref.at[pl.ds(t * size, size)], buffer.at[t], sems.at[t])
        for t in range(taps)
    ]
    for copy in copies:
        copy.start()
    for t in range(taps):
        copies[t].wait()
        for k, out in enumerate((one_ref, two_ref)):
            parts = [buffer[t, pl.ds(2 * half + k, chans, stride=2 * per), :] for half in range(per)]
            out[t * chans : (t + 1) * chans, :] = jnp.concatenate(parts, axis=1).astype(BF16)


def place_shifted(ref, row_index, row):
    store_shifted(ref, row_index * row.shape[0], row)


def window_rows(g, x_ref, first, count):
    size = count * g.wp
    return jnp.concatenate(
        [x_ref[(first + a) * g.wp : (first + a) * g.wp + size, :] for a in range(3)], axis=1
    )


def own_conv_kernel(g, ext, w, z_ref, st_ref, x_ref):
    count = g.h - 2
    s1 = jnp.zeros((8, g.c), F32)
    s2 = jnp.zeros((8, g.c), F32)
    for s in range(g.s):
        for r in range(g.h):
            place_shifted(x_ref, s * (g.h + 2) + 1 + r, wide(ext, s, r))
        half = count // 2
        for first in range(0, count, half):
            acc = dot(window_rows(g, x_ref, s * (g.h + 2) + 1 + first, half), w[...])
            at = (s * (g.tall - 2) + RIM + first) * g.wp
            z_ref[at : at + half * g.wp, :] = acc
            for i in range(half):
                v = acc[i * g.wp : i * g.wp + g.w]
                s1 = s1 + sum_rows(v)
                s2 = s2 + sum_rows(v * v)
    st_ref[0:8] = s1
    st_ref[8:16] = s2


def rim_conv_kernel(
    g, ext, ra, rb, rb_c, rb_d, w, st_in, z_in, x_in, z_ref, st_ref, x_own, cot_ref, x_ref
):
    del z_in, x_in
    place = Place()
    odd = place.odd_row
    s1, s2 = st_in[0:8], st_in[8:16]
    span = RIM + 2
    for s in range(g.s):
        far = far_rows(g, place, rb, rb_c, rb_d, s)
        near = [wide(ra, s, k) for k in range(RIM + g.near)]
        for side in range(2):
            base = span * (2 * s + side)
            beyond = [
                jnp.where(odd, b, a) if side else jnp.where(odd, a, b)
                for a, b in zip(near, far, strict=True)
            ]
            for k in range(RIM):
                place_shifted(x_ref, base + 2 * side + k, beyond[k])
            next_row = beyond[0 if side else RIM - 1]
            place_shifted(x_own, s * (g.h + 2) + (g.h + 1) * side, next_row)
            cot_ref[s, side] = beyond[RIM].astype(BF16)
            source = (s * (g.h + 2) + 1 + (g.h - 2) * side) * g.wp
            target = (base + RIM * (1 - side)) * g.wp
            x_ref[target : target + 2 * g.wp, :] = x_own[source : source + 2 * g.wp, :]
            acc = dot(window_rows(g, x_ref, base, RIM), w[...])
            at = (s * (g.tall - 2) + (g.h + RIM - 2) * side) * g.wp
            z_ref[at : at + RIM * g.wp, :] = acc
            i = 0 if side else RIM - 1
            v = acc[i * g.wp : i * g.wp + g.w]
            s1 = s1 + sum_rows(v)
            s2 = s2 + sum_rows(v * v)
    to_all(st_ref, [jnp.sum(s1, 0, keepdims=True), jnp.sum(s2, 0, keepdims=True)])


def typical_hidden(params):
    scale, shift = params[0:1], params[1:2]
    return 0.5 * (shift + jnp.sqrt(shift * shift + 0.64 * scale * scale))


def stats_of(total, count):
    mean = total[0:1] / count
    var = total[1:2] / count - mean * mean
    return mean, lax.rsqrt(var + 1e-05)


def second_conv_kernel(g, chunk, count, z1, st, params, w, cot, h_ref, z_ref, st_ref):
    rows_in, rows_out = g.tall - 2, g.tall - 4
    place = Place()
    mean, rstd = stats_of(total_of(st), count)
    scale = params[0:1] * rstd
    shift = params[1:2] - mean * scale
    edge = edge_mask(place, g)
    sums = [jnp.zeros((8, g.c), F32) for _ in range(4)]
    for s in range(g.s):
        for r in range(rows_in):
            start = (s * rows_in + r) * g.wp
            row = jnp.maximum(z1[start : start + g.wp, :] * scale + shift, 0.0)
            store_shifted(h_ref, start, in_grid(row, r + 1, g, place, edge))
        for r in range(0, rows_out, chunk):
            base = (s * rows_in + r) * g.wp
            size = chunk * g.wp
            lhs = jnp.concatenate(
                [h_ref[base + a * g.wp : base + a * g.wp + size, :] for a in range(3)], axis=1
            )
            acc = dot(lhs, w[...])
            z_ref[(s * rows_out + r) * g.wp : (s * rows_out + r) * g.wp + size, :] = acc
            for i in range(chunk):
                if RIM <= r + i + 2 < RIM + g.h:
                    v = acc[i * g.wp : i * g.wp + g.w]
                    dn = wide(cot, s, r + i + 2 - RIM)[: g.w]
                    for k, term in enumerate((v, v * v, dn, dn * v)):
                        sums[k] = sums[k] + sum_rows(term)
    to_all(st_ref, [jnp.sum(v, 0, keepdims=True) for v in sums])


def own_transposed(g, source, first, s, dt_ref):
    span = g.h * g.wp
    block = source[first : first + span, :]
    inside = lax.broadcasted_iota(jnp.int32, (span, 1), 0) % g.wp < g.w
    dt_ref[:, s * span : (s + 1) * span] = jnp.where(inside, block, jnp.zeros_like(block)).T


def kernel_gradient(g, core, field, rows_field, first_row, dt_ref, keep, send, first, prepare, adjust=None):
    chans, half = g.c, g.c // 2
    span = g.h * g.wp
    mine = pl.ds(pl.multiple_of(core * half, half), half)
    other = pl.ds(pl.multiple_of((1 - core) * half, half), half)
    totals = [None] * 3
    cut = g.s // 2
    groups = (range(cut), range(cut, g.s))
    for s in groups[0]:
        prepare(s)
    for group in groups:
        lanes = slice(group[0] * span, (group[-1] + 1) * span)
        lhs = jnp.concatenate([dt_ref[mine, lanes], dt_ref[other, lanes]], axis=0)
        for a in range(3):
            starts = [(s * rows_field + first_row + a) * g.wp for s in group]
            acc = dot(lhs, jnp.concatenate([field[at : at + span, :] for at in starts], axis=0))
            if group[0] == 0 and a < len(groups[1]):
                prepare(groups[1][a])
            if group[0] == 0:
                for b in range(3):
                    keep[a * 3 + b] = acc[0:half, b * chans : (b + 1) * chans]
                    first[a * 3 + b] = acc[half:, b * chans : (b + 1) * chans]
                continue
            for b in range(3):
                own_half = keep[a * 3 + b] + acc[0:half, b * chans : (b + 1) * chans]
                other_half = first[a * 3 + b] + acc[half:, b * chans : (b + 1) * chans]
                if adjust is not None:
                    own_half = own_half - adjust(a * 3 + b, mine)
                    other_half = other_half - adjust(a * 3 + b, other)
                keep[a * 3 + b] = own_half
                send[a * 3 + b] = other_half


def second_gradient_kernel(
    g, count, z2, st, params, cot, cot_next, h, d_ref, keep, send, sums_ref, dt_ref, columns
):
    place = Place()
    rows = g.cot_tall
    total = total_of(st)
    mean, rstd = stats_of(total, count)
    sum_dn = total[2:3]
    sum_dx = rstd * (total[3:4] - mean * sum_dn)
    k0 = params[2:3] * rstd
    k1 = k0 * (sum_dn / count)
    k2 = k0 * rstd * (sum_dx / count)
    edge = edge_mask(place, g)
    added = [[None] * 3 for _ in range(g.h)]

    def prepare(s):
        for i in range(rows):
            rim = not g.near <= i < g.near + g.h
            dn = wide(cot_next, s, 0 if i < g.near else 1) if rim else wide(cot, s, i - g.near)
            start = (s * rows + i) * g.wp
            d = k0 * dn - k1 - (z2[start : start + g.wp, :] - mean) * k2
            d = in_grid(d, i + RIM - g.near, g, place, edge).astype(BF16)
            d_ref[start : start + g.wp, :] = d
            if not rim:
                row = d.astype(F32)[: g.w]
                parts = sum_rows(row), row[:8], row[g.w - 8 :]
                r = i - g.near
                added[r] = [v if u is None else u + v for u, v in zip(added[r], parts, strict=True)]
        own_transposed(g, d_ref, (s * rows + g.near) * g.wp, s, dt_ref)
        if s == g.s - 1:
            tap_sums()

    def tap_sums():
        found = [[None] * 3 for _ in range(3)]
        for b in range(3):
            line = []
            for r in range(g.h):
                value = jnp.sum(added[r][0], axis=0, keepdims=True)
                if b == 0:
                    value = value - (1.0 - place.left) * added[r][1][:1]
                if b == 2:
                    value = value - (1.0 - place.right) * added[r][2][7:]
                line.append(value)
            every = functools.reduce(lambda u, v: u + v, line)
            found[0][b] = every - (1.0 - place.above) * line[0]
            found[1][b] = every
            found[2][b] = every - (1.0 - place.below) * line[-1]
        table = jnp.concatenate(sum(found, []) + [jnp.zeros((7, g.c), F32)], axis=0)
        sums_ref[...] = table
        spare = jnp.zeros((columns.shape[1] - 16, g.c), F32)
        columns[...] = jnp.concatenate([table, spare], axis=0).T

    typical = typical_hidden(params)

    def adjust(tap, rows):
        return columns[rows, tap : tap + 1] * typical

    kernel_gradient(
        g, place.core, h, g.tall - 2, RIM - 2, dt_ref, keep, send, send, prepare, adjust
    )


def transposed_conv(g, d_ref, w, s, rows_in, r, chunk):
    acc = None
    size = chunk * g.wp
    for a in range(3):
        start = (s * rows_in + r + a) * g.wp
        for b in range(3):
            tap = (2 - a) * 3 + (2 - b)
            term = dot_nt(
                d_ref[start : start + size, b * g.c : (b + 1) * g.c],
                w[tap * g.c : (tap + 1) * g.c, :],
            )
            acc = term if acc is None else acc + term
    return acc


def hidden_gradient_kernel(
    g, chunk, count, d, w, z1, z2, st, st2, params, ext, sums, dn_ref, st_ref, out_ref, d_ref
):
    mean2, rstd2 = stats_of(total_of(st2), count)
    scale2 = params[2:3] * rstd2
    shift2 = params[3:4] - mean2 * scale2
    rows_in, rows_out, z_rows = g.tall - 4, g.tall - 6, g.tall - 2
    mean, rstd = stats_of(total_of(st), count)
    scale = params[0:1] * rstd
    shift = params[1:2] - mean * scale
    s0 = jnp.zeros((8, g.c), F32)
    s1 = jnp.zeros((8, g.c), F32)
    for s in range(g.s):
        for i in range(rows_in):
            at = (s * rows_in + i) * g.wp
            store_shifted(d_ref, at, wide(d, slice(at, at + g.wp)))
        for r in range(g.h):
            at = (s * rows_in + r + g.near) * g.wp
            normed = z2[at : at + g.w, :] * scale2 + shift2
            out_ref[s, r] = (wide(ext, s, r)[: g.w] + normed).astype(BF16)
        for r in range(0, rows_out, chunk):
            acc = transposed_conv(g, d_ref, w, s, rows_in, r, chunk)
            at = (s * z_rows + r + 2) * g.wp
            z = z1[at : at + chunk * g.wp, :]
            dn = jnp.where(z * scale + shift > 0, acc, 0.0)
            dn_ref[(s * rows_out + r) * g.wp : (s * rows_out + r + chunk) * g.wp, :] = dn
            for i in range(chunk):
                if RIM <= r + i + 3 < RIM + g.h:
                    v = dn[i * g.wp : i * g.wp + g.w]
                    s0 = s0 + sum_rows(v)
                    s1 = s1 + sum_rows(v * (z[i * g.wp : i * g.wp + g.w] - mean))
    own = [jnp.sum(s0, 0, keepdims=True), jnp.sum(s1, 0, keepdims=True) * rstd]
    devices, count, _ = st_ref.shape
    if count == 2:
        to_all(st_ref, own)
    else:
        share = 9 * g.c // devices
        for i in range(devices):
            taps = i * share // g.c, (i * share + share - 1) // g.c
            st_ref[i] = jnp.concatenate(own + [sums[t : t + 1] for t in taps], axis=0)


def half_gradient(g, which, field, rows_field, first_row, dt_ref, out_ref, sums, prepare=None):
    chans, half = g.c, g.c // 2
    span = g.h * g.wp
    channels = pl.ds(pl.multiple_of(which * half, half), half)
    cut = g.s // 2
    groups = range(cut), range(cut, g.s)
    if prepare is not None:
        for s in groups[0]:
            prepare(s)
    for group in groups:
        lhs = dt_ref[channels, group[0] * span : (group[-1] + 1) * span]
        for a in range(3):
            starts = [(s * rows_field + first_row + a) * g.wp for s in group]
            acc = dot(lhs, jnp.concatenate([field[at : at + span, :] for at in starts], axis=0))
            if group[0] == 0 and prepare is not None and a < len(groups[1]):
                prepare(groups[1][a])
            for b in range(3):
                part = acc[:, b * chans : (b + 1) * chans]
                if group[0] == 0:
                    sums[a * 3 + b] = part
                else:
                    rows = slice((a * 3 + b) * chans, (a * 3 + b + 1) * chans)
                    out_ref[rows, :] = (sums[a * 3 + b] + part).T.astype(out_ref.dtype)


def first_gradient_kernel(
    g, count, dn, z, st, st3, params, x, e_ref, a_ref, b_ref, send, dt_ref, first
):
    place = Place()
    mean, rstd = stats_of(total_of(st), count)
    total = total_of(st3)
    k0 = params[0:1] * rstd
    k1 = k0 * (total[0:1] / count)
    k2 = k0 * rstd * (total[1:2] / count)
    edge = edge_mask(place, g)

    def prepare(s):
        for i in range(g.h):
            at = (s * g.h + i) * g.wp
            z_at = (s * (g.tall - 2) + i + RIM - 1) * g.wp
            d = k0 * dn[at : at + g.wp, :] - k1 - (z[z_at : z_at + g.wp, :] - mean) * k2
            d = in_grid(d, i + RIM, g, place, edge)
            e_ref[at : at + g.wp, :] = d.astype(BF16)
            if i == 0:
                top = d
        a_ref[s, 0] = jnp.where(place.odd_row, top, d).astype(BF16)
        b_ref[s, 0] = jnp.where(place.odd_row, d, top).astype(BF16)
        own_transposed(g, e_ref, s * g.h * g.wp, s, dt_ref)
    half_gradient(g, 1 - place.core, x, g.h + 2, 0, dt_ref, send, first, prepare)


def first_own_kernel(g, x, dt_ref, keep, first):
    half_gradient(g, Place().core, x, g.h + 2, 0, dt_ref, keep, first)


def input_gradient_kernel(
    g, chunk, e, ra, rb, w_far, cot_far, occ, out_ref, w, cot, e_ref, sems
):
    rows_in = g.h + 2
    place = Place()
    copies = [
        pltpu.make_async_copy(w_far, w, sems.at[0]),
        pltpu.make_async_copy(cot_far, cot, sems.at[1]),
    ]
    for copy in copies:
        copy.start()
    for copy in copies:
        copy.wait()
    for s in range(g.s):
        a, b = wide(ra, s, 0), wide(rb, s, 0)
        rows = [jnp.where(place.odd_row, a, b)]
        for r in range(g.h):
            at = (s * g.h + r) * g.wp
            rows.append(wide(e, slice(at, at + g.wp)))
        rows.append(jnp.where(place.odd_row, b, a))
        for i in range(rows_in):
            place_shifted(e_ref, s * rows_in + i, rows[i])
        mask = pixel_mask(occ, s)
        for r in range(0, g.h, chunk):
            acc = transposed_conv(g, e_ref, w, s, rows_in, r, chunk)
            for i in range(chunk):
                v = acc[i * g.wp : i * g.wp + g.w]
                out_ref[s, r + i] = (wide(cot, s, r + i) + v) * mask[:, r + i : r + i + 1]


def pair_total(keep, got, t):
    if keep.ndim == 3:
        return (keep[t] + wide(got, t)).T
    chans = 2 * keep.shape[1]
    rows = slice(t * chans, (t + 1) * chans)
    return keep[rows, :] + wide(got, rows)


def pair_sum_kernel(lane, keep, got, *refs):
    *_, out_far, buffer, sems = refs
    half = buffer.shape[1]
    chans = 2 * half
    taps = buffer.shape[0] // chans
    copies = []
    for t in range(taps):
        rows = pl.ds(t * chans, chans)
        buffer[rows, :] = pair_total(keep, got, t).astype(BF16)
        copies.append(
            pltpu.make_async_copy(buffer.at[rows], out_far.at[rows, pl.ds(lane, half)], sems.at[t])
        )
        copies[-1].start()
    for copy in copies:
        copy.wait()


def half_rows(share):
    return -(-(share // 2) // 8) * 8


def split_kernel(keep, got, kept_ref, sent_ref, buffer):
    taps, half, chans = keep.shape
    devices, rows, _ = kept_ref.shape
    share = taps * chans // devices
    for t in range(taps):
        buffer[t * chans : (t + 1) * chans, :] = pair_total(keep, got, t)
    second = Place().second
    for i in range(devices):
        mine = pl.multiple_of(i * share + (share - rows) * second, 8)
        other = pl.multiple_of(i * share + (share - rows) * (1 - second), 8)
        kept_ref[i] = buffer[pl.ds(mine, rows), :]
        sent_ref[i] = buffer[pl.ds(other, rows), :].astype(BF16)


def join_kernel(kept, came, out_ref):
    for i in range(kept.shape[0]):
        out_ref[i] = kept[i] + wide(came, i)


def message_kernel(keep, got, kept, out_far, out_ref, sems):
    devices = kept.shape[0]
    share = keep.shape[0] // devices
    copies = []
    count = sems.shape[0]
    for part in range(count):
        mine = pl.ds(part * devices // count, devices // count)
        for i in range(part * devices // count, (part + 1) * devices // count):
            rows = slice(i * share, (i + 1) * share)
            first = keep[rows, :] + wide(got, rows)
            out_ref[i] = jnp.concatenate([first, kept[i]], axis=0).astype(BF16)
        copies.append(pltpu.make_async_copy(out_ref.at[mine], out_far.at[mine], sems.at[part]))
        copies[-1].start()
    for copy in copies:
        copy.wait()


def adamw(weight, grad, first, second, rate):
    first_new = 0.9 * first + 0.1 * grad
    second_new = 0.999 * second + 0.001 * grad * grad
    first_hat = first_new / (1.0 - 0.9**STEP)
    second_hat = second_new / (1.0 - 0.999**STEP)
    weight_new = weight - rate * (first_hat / (jnp.sqrt(second_hat) + 1e-08) + 0.01 * weight)
    return (weight_new, first_new, second_new)


def update_kernel(
    count, parts, w, first_m, second_m, st2, st3, params, n_first, n_second,
    grad_out, w_out, first_out, second_out, n_grad, n_out, n_first_out, n_second_out, typical_rows
):
    devices, ncols = parts.shape[0], lax.axis_size("cols")
    share = w.shape[0] // 4
    total2, total3 = total_of(st2), total_of(st3)
    mean, rstd = stats_of(total2, count)
    sum_dn = total2[2:3]
    grads = jnp.concatenate(
        [total3[1:2], total3[0:1], rstd * (total2[3:4] - mean * sum_dn), sum_dn], axis=0
    )
    n_grad[...] = grads
    n_out[...], n_first_out[...], n_second_out[...] = adamw(
        params[...], grads, n_first[...], n_second[...], 0.75
    )
    def over(chosen, rows, lanes):
        total = None
        for source in range(devices):
            if chosen(source // ncols):
                term = wide(parts, source)[rows, lanes]
                total = term if total is None else total + term
        return total

    grads = []
    every = slice(None)
    if parts.shape[2] != 256:
        chans = params.shape[1]
        column = jnp.broadcast_to(typical_hidden(params), (128, chans)).T
        typical_rows[0:chans] = column
        typical_rows[chans:] = column
        first_typical = pl.multiple_of(Place().index * share % chans, 8)
        wrap = chans - first_typical
        place_rows = lax.broadcasted_iota(jnp.int32, (share, 128), 0)
    for half in range(2):
        if parts.shape[2] == 256:
            for k in range(2):
                lanes = slice(k * 128, (k + 1) * 128)
                grads.append((k, half, over(lambda row: row % 2 == half, every, lanes)))
        else:
            grads.append((0, half, over(lambda row: row % 2 == half, slice(0, share), every)))
            size = half_rows(share)
            upper = over(lambda row: row % 4 == half, slice(share, None), every)
            lower = over(lambda row: row % 4 == half + 2, slice(2 * size, None), every)
            lanes = slice(half * 128, (half + 1) * 128)
            sums = jnp.where(place_rows < wrap, total3[2:3, lanes], total3[3:4, lanes])
            back = typical_rows[pl.ds(first_typical, share), :] * sums
            grads.append((1, half, jnp.concatenate([upper, lower], axis=0) + back))
    for k, half, grad in grads:
        at = pl.ds(2 * half + k, share, stride=4)
        new = adamw(w[at, :], grad, first_m[at, :], second_m[at, :], 0.02)
        grad_out[at, :] = grad
        w_out[at, :], first_out[at, :], second_out[at, :] = new


def swapped(block, axis, first):
    count = lax.axis_size(axis)
    pairs = []
    for i in range(first, count - 1, 2):
        pairs += [(i, i + 1), (i + 1, i)]
    return lax.ppermute(block, axis, pairs)


def swapped_both(block, first_row, first_col):
    nrows, ncols = lax.axis_size("rows"), lax.axis_size("cols")

    def partner(i, first, count):
        j = i + 1 if (i - first) % 2 == 0 else i - 1
        return j if min(i, j) >= first and max(i, j) < count else None

    pairs = []
    for i in range(nrows):
        for j in range(ncols):
            to = partner(i, first_row, nrows), partner(j, first_col, ncols)
            if None not in to:
                pairs.append((i * ncols + j, to[0] * ncols + to[1]))
    return lax.ppermute(block, BOTH, pairs)


def to_chunks(flat):
    return flat.reshape(2, -1, 128).transpose(1, 0, 2).reshape(-1, 128)


def from_chunks(rows):
    return rows.reshape(-1, 2, 128).transpose(1, 0, 2).reshape(2, -1)


def exchange(parts):
    return lax.all_to_all(parts, BOTH, 0, 0, tiled=True)


def body(
    features,
    occupancy,
    cotangent,
    conv_weights,
    conv_first,
    conv_second,
    norm_scale_bias,
    norm_first,
    norm_second,
):
    scenes, height, width, chans = features.shape
    g = Geometry(scenes, height, width, chans)
    wp = g.wp
    devices = lax.axis_size("rows") * lax.axis_size("cols")
    count = float(scenes * height * width * devices)
    taps = 9 * chans
    n0, n1, n2, n3 = (scenes * wp * (g.tall - 2 * i) for i in range(4))
    own_pixels = scenes * height * wp
    dma = pltpu.SemaphoreType.DMA

    def conv_flops(n):
        return 2 * n * taps * chans

    side = shape_of((scenes, g.side, chans), BF16)
    corner = shape_of((scenes, g.corner, chans), BF16)
    own, c, d, b, bc, bd = kernel_call(
        functools.partial(pack_kernel, g),
        [
            shape_of(features.shape, BF16),
            side,
            side,
            shape_of((scenes, RIM + g.near, width, chans), BF16),
            corner,
            corner,
        ],
        1e8,
        far=(0, 1, 2),
        scratch=[
            pltpu.VMEM(features.shape, BF16),
            pltpu.VMEM(features.shape, BF16),
            pltpu.VMEM(occupancy.shape, jnp.int32),
            dma((3, scenes)),
        ],
    )(features, occupancy, cotangent)
    rb = swapped(b, "rows", 1)
    rc, rd = swapped(c, "cols", 0), swapped(d, "cols", 1)
    rb_c, rb_d = swapped_both(bc, 1, 0), swapped_both(bd, 1, 1)
    chunked = to_chunks(conv_weights)
    share = conv_first.shape[1]
    chunk_shape = shape_of((share // 64, 128), F32)
    weights = (taps, chans)
    w1, w2 = kernel_call(
        prepare_kernel,
        [held(weights, BF16)] * 2,
        0,
        size=1024,
        far=(0,),
        scratch=[pltpu.VMEM((9, chunked.shape[0] // 9, 128), F32), dma((9,))],
    )(chunked)

    def wide_rows(rows):
        return shape_of((scenes, rows, wp, chans), BF16)

    ext, cot_ext, a = kernel_call(
        functools.partial(assemble_kernel, g),
        [wide_rows(n) for n in (height, height, RIM + g.near)],
        0,
        size=1024,
    )(own, cotangent, rc, rd)
    rows_x = scenes * (height + 2) * wp
    x_shape = held((rows_x, 3 * chans), BF16)
    z1, st, x = kernel_call(
        functools.partial(own_conv_kernel, g),
        [held((n1, chans), F32), held((16, chans), F32), x_shape],
        0,
        size=1024,
    )(ext, w1)
    a, rb, rb_c, rb_d, w1 = lax.optimization_barrier((a, rb, rb_c, rb_d, w1))
    ra = swapped(a, "rows", 0)
    z1, st, x, cot_next = kernel_call(
        functools.partial(rim_conv_kernel, g),
        [held((n1, chans), F32), shape_of((devices, 2, chans), F32), x_shape, wide_rows(2)],
        0,
        size=1024,
        scratch=[pltpu.VMEM((scenes * 2 * (RIM + 2) * wp, 3 * chans), BF16)],
        alias={7: 0, 8: 2},
    )(ext, ra, rb, rb_c, rb_d, w1, st, z1, x)
    st1 = exchange(st)
    h, z2, st = kernel_call(
        functools.partial(second_conv_kernel, g, 5, count),
        [
            held((n1, 3 * chans), BF16),
            held((n2, chans), F32),
            shape_of((devices, 4, chans), F32),
        ],
        conv_flops(n2),
    )(z1, st1, norm_scale_bias, w2, cot_ext)
    st2 = exchange(st)
    grad_shape = held((9, chans // 2, chans), F32)
    nrows = lax.axis_size("rows")
    cut_again = nrows % 4 == 0 and taps // devices % 8 == 0
    d, keep2, send2, sums = kernel_call(
        functools.partial(second_gradient_kernel, g, count),
        [held((n2, chans), BF16), grad_shape, grad_shape, held((16, chans), F32)],
        conv_flops(own_pixels),
        scratch=[pltpu.VMEM((chans, own_pixels), BF16), pltpu.VMEM((chans, 128), F32)],
    )(z2, st2, norm_scale_bias, cot_ext, cot_next, h)
    got2 = swapped(send2, "rows", 0)
    dn1, st, block_out = kernel_call(
        functools.partial(hidden_gradient_kernel, g, 8, count),
        [
            held((n3, chans), F32),
            shape_of((devices, 4 if cut_again else 2, chans), F32),
            held(features.shape, BF16),
        ],
        conv_flops(n3),
        scratch=[pltpu.VMEM((n2, 3 * chans), BF16)],
    )(d, w2, z1, z2, st1, st2, norm_scale_bias, ext, sums)
    if cut_again:
        got2, st = lax.optimization_barrier((got2, st))
        kept_shape = (devices, half_rows(taps // devices), chans // 2)
        kept, sent = kernel_call(
            split_kernel,
            [held(kept_shape, F32), held(kept_shape, BF16)],
            1e8,
            scratch=[pltpu.VMEM((taps, chans // 2), F32)],
        )(keep2, got2)
        st, kept = lax.optimization_barrier((st, kept))
        came = lax.ppermute(sent, "rows", [(i, i ^ 2) for i in range(nrows)])
        st3 = exchange(st)
    else:
        st, got2 = lax.optimization_barrier((st, got2))
        st3 = exchange(st)
    if cut_again:
        kept, st3 = lax.optimization_barrier((kept, st3))
        (kept,) = kernel_call(join_kernel, [held(kept_shape, F32)], 0, size=1024)(kept, came)
        dn1, kept = lax.optimization_barrier((dn1, kept))
    sent_shape = held((taps, chans // 2), BF16)
    part = pltpu.VMEM(grad_shape.shape, F32)
    e, a, b, send1, dt = kernel_call(
        functools.partial(first_gradient_kernel, g, count),
        [
            held((n3, chans), BF16),
            wide_rows(1),
            wide_rows(1),
            sent_shape,
            held((chans, own_pixels), BF16),
        ],
        0,
        size=1024,
        scratch=[part],
    )(dn1, z1, st1, st3, norm_scale_bias, x)
    (keep1,) = kernel_call(
        functools.partial(first_own_kernel, g), [held((taps, chans // 2), F32)], 0, size=1024, scratch=[part]
    )(x, dt)
    got1 = swapped(send1, "rows", 0)
    share_rows = taps // devices
    if cut_again:
        rows = share_rows + kept.shape[1]
        (parts,) = kernel_call(
            message_kernel,
            [stored((devices, rows, chans // 2), BF16)],
            1e9,
            far_out=(0,),
            scratch=[pltpu.VMEM((devices, rows, chans // 2), BF16), dma((4,))],
        )(keep1, got1, kept)
    else:

        def add_pair(lane, *operands, **options):
            return kernel_call(
                functools.partial(pair_sum_kernel, lane),
                [stored((taps, chans), BF16)],
                1e9,
                far_out=(0,),
                scratch=[pltpu.VMEM((taps, chans // 2), BF16), dma((9,))],
                **options,
            )(*operands)

        (parts,) = add_pair(chans // 2, keep2, got2)
        (parts,) = add_pair(0, keep1, got1, parts, far=(2,), alias={2: 0})
        parts = parts.reshape(devices, share_rows, chans)
    parts, chunked = lax.optimization_barrier((parts, chunked))
    parts = exchange(parts)
    ra, rb = swapped(a, "rows", 0), swapped(b, "rows", 1)
    (grad_input,) = kernel_call(
        functools.partial(input_gradient_kernel, g, 8),
        [shape_of(features.shape, F32)],
        conv_flops(own_pixels),
        far=(3, 4),
        scratch=[
            pltpu.VMEM(weights, BF16),
            pltpu.VMEM(features.shape, BF16),
            pltpu.VMEM((rows_x, 3 * chans), BF16),
            dma((2,)),
        ],
    )(e, ra, rb, w1, cotangent, occupancy)
    own_rows = share // 64
    first_row = (lax.axis_index("rows") * lax.axis_size("cols") + lax.axis_index("cols")) * own_rows
    own_weights = lax.dynamic_slice_in_dim(chunked, first_row, own_rows, 0)

    norm_shape = shape_of(norm_first.shape, F32)
    updated = kernel_call(
        functools.partial(update_kernel, count),
        [chunk_shape] * 4 + [norm_shape] * 4,
        1e8,
        scratch=[pltpu.VMEM((2 * chans, 128), F32)],
    )(
        parts, own_weights, to_chunks(conv_first), to_chunks(conv_second), st2, st3,
        norm_scale_bias, norm_first, norm_second,
    )
    return (block_out, grad_input, *map(from_chunks, updated[:4]), *updated[4:])


def solution(mesh):
    tile = P(None, "rows", "cols", None)
    share = P(None, ("rows", "cols"))
    return jax.shard_map(
        body,
        mesh=mesh,
        in_specs=(tile, P(None, "rows", "cols"), tile, P(), share, share, P(), P(), P()),
        out_specs=(tile, tile, share, share, share, share, P(), P(), P(), P()),
        check_vma=False,
    )
```

```python
import functools
import math

import jax
import jax.numpy as jnp
from jax import lax
from jax.experimental import pallas as pl
from jax.experimental.pallas import tpu as pltpu
from jax.sharding import PartitionSpec as P

STEP = 5
BOTH = ("rows", "cols")
RIM = 3
COLS = 4
SIDE = 2 * COLS
F32, BF16 = jnp.float32, jnp.bfloat16


def shape_of(shape, dtype):
    return jax.ShapeDtypeStruct(shape, dtype)


def held(shape, dtype):
    return pltpu.VMEM(shape, dtype)


def stored(shape, dtype):
    return pltpu.HBM(shape, dtype)


def kernel_call(body, out_shape, flops, far=(), far_out=(), scratch=(), limit=16, alias=None, size=4 << 20):
    def call(*operands):
        operands = [
            pltpu.with_memory_space_constraint(v, pltpu.HBM if i in far else pltpu.VMEM)
            for i, v in enumerate(operands)
        ]
        specs = [
            pl.BlockSpec(memory_space=pltpu.HBM if i in far else pltpu.VMEM)
            for i in range(len(operands))
        ]
        return pl.pallas_call(
            body,
            out_shape=out_shape,
            in_specs=specs,
            out_specs=[
                pl.BlockSpec(memory_space=pltpu.HBM if i in far_out else pltpu.VMEM)
                for i in range(len(out_shape))
            ],
            scratch_shapes=list(scratch),
            input_output_aliases=alias or {},
            compiler_params=pltpu.CompilerParams(vmem_limit_bytes=limit << 20),
            cost_estimate=pl.CostEstimate(
                flops=int(flops), bytes_accessed=size, transcendentals=0
            ),
        )(*operands)

    return call


def dot(a, b):
    return jnp.dot(a, b, preferred_element_type=F32)


def dot_nt(a, b):
    return lax.dot_general(a, b, (((1,), (1,)), ((), ())), preferred_element_type=F32)


def total_of(ref):
    count = ref.shape[0]
    total = ref[0]
    for i in range(1, count):
        total = total + ref[i]
    return total


def to_all(ref, parts):
    value = jnp.concatenate(parts, axis=0)
    for i in range(ref.shape[0]):
        ref[i] = value


def store_shifted(ref, start, row, offsets=(0, 1, 2)):
    width, chans = row.shape
    for b in offsets:
        moved = row if b == 1 else pltpu.roll(row, 1 if b == 0 else width - 1, 0)
        ref[start : start + width, b * chans : (b + 1) * chans] = moved.astype(BF16)


class Geometry:
    def __init__(self, scenes, height, width, chans):
        self.s, self.h, self.w, self.c = scenes, height, width, chans
        self.wp = width + SIDE
        self.tall = height + 2 * RIM
        self.near = RIM - 2
        self.near_cols = COLS - 2
        self.cot_tall = height + 2 * self.near
        self.side = (COLS + self.near_cols) * height
        self.corner = -(-(COLS * RIM + self.near_cols * self.near) // 16) * 16


class Place:
    def __init__(self):
        row, col = lax.axis_index("rows"), lax.axis_index("cols")
        nrows, ncols = lax.axis_size("rows"), lax.axis_size("cols")
        self.above = (row > 0).astype(F32)
        self.below = (row < nrows - 1).astype(F32)
        self.right = (col < ncols - 1).astype(F32)
        self.left = (col > 0).astype(F32)
        self.core = row % 2
        self.second = row // 2 % 2
        self.odd_row = row % 2 == 1
        self.odd_col = col % 2 == 1
        self.index = row * ncols + col


def wide(ref, *index):
    return ref[index].astype(F32)


def far_rows(g, place, rb, rb_c, rb_d, s):
    right, left = sides(g, place, rb_c, rb_d, s)
    rows = []
    for k in range(RIM + g.near):
        width = COLS if k < RIM else g.near_cols
        at = COLS * min(k, RIM) + g.near_cols * max(k - RIM, 0)
        rows.append(
            jnp.concatenate([wide(rb, s, k), side_columns(g, right, left, at, width)], axis=0)
        )
    return rows


def pixel_mask(occ, s):
    return occ[s].astype(F32).T


def in_grid(row, r, g, place, edge):
    row = jnp.concatenate([row[: g.w], row[g.w :] * edge], axis=0)
    if r < RIM:
        row = row * place.above
    elif r >= RIM + g.h:
        row = row * place.below
    return row


def edge_mask(place, g):
    where = lax.broadcasted_iota(jnp.int32, (SIDE, g.c), 0)
    return jnp.where(where < SIDE // 2, place.right, place.left)


def sum_rows(value):
    rows, chans = value.shape
    return jnp.sum(value.reshape(rows // 8, 8, chans), axis=0)


def pack_kernel(
    g, features, occ_far, cot, own, c_ref, d_ref, b_ref, bc_ref, bd_ref, given, seen, occ, sems
):
    copies = []
    flags = pltpu.make_async_copy(occ_far, occ, sems.at[2, 0])
    flags.start()
    for s in range(g.s):
        copies.append(
            (
                pltpu.make_async_copy(features.at[s], given.at[s], sems.at[0, s]),
                pltpu.make_async_copy(cot.at[s], seen.at[s], sems.at[1, s]),
            )
        )
        for copy in copies[-1]:
            copy.start()
    odd, odd_row = Place().odd_col, Place().odd_row
    flags.wait()

    for s in range(g.s):
        mask = pixel_mask(occ, s)
        for copy in copies[s]:
            copy.wait()
        rows = []
        for r in range(g.h):
            row = wide(given, s, r) * mask[:, r : r + 1]
            rows.append(row)
            own[s, r] = row.astype(BF16)
        cots = [wide(seen, s, r) for r in range(g.h)]
        ends = []
        for field, count in ((rows, RIM), (cots, g.near)):
            for k in range(count):
                ends.append(jnp.where(odd_row, field[g.h - count + k], field[k]))
                b_ref[s, len(ends) - 1] = ends[-1].astype(BF16)
        spare = jnp.zeros((g.corner - COLS * RIM - g.near_cols * g.near, g.c), F32)
        widths = [COLS] * RIM + [g.near_cols] * g.near
        right = [v[g.w - width :] for v, width in zip(ends, widths, strict=True)]
        left = [v[:width] for v, width in zip(ends, widths, strict=True)]
        right, left = (jnp.concatenate(v + [spare], axis=0) for v in (right, left))
        bc_ref[s] = jnp.where(odd, left, right).astype(BF16)
        bd_ref[s] = jnp.where(odd, right, left).astype(BF16)
        right = jnp.concatenate(
            [v[g.w - COLS :] for v in rows] + [v[g.w - g.near_cols :] for v in cots], axis=0
        )
        left = jnp.concatenate([v[:COLS] for v in rows] + [v[: g.near_cols] for v in cots], axis=0)
        c_ref[s] = jnp.where(odd, left, right).astype(BF16)
        d_ref[s] = jnp.where(odd, right, left).astype(BF16)


def sides(g, place, rc, rd, s):
    c, d = wide(rc, s), wide(rd, s)
    return jnp.where(place.odd_col, d, c), jnp.where(place.odd_col, c, d)


def side_columns(g, right, left, at, width):
    parts = [right[at : at + width], jnp.zeros((SIDE - 2 * width, g.c), F32), left[at : at + width]]
    return jnp.concatenate([part for part in parts if part.shape[0]], axis=0)


def assemble_kernel(g, own, cot, rc, rd, ext, cot_ext, a_ref):
    place = Place()

    odd = place.odd_row
    for s in range(g.s):
        right, left = sides(g, place, rc, rd, s)
        for source, full, at, width, count, first in (
            (own, ext, 0, COLS, RIM, 0),
            (cot, cot_ext, COLS * g.h, g.near_cols, g.near, RIM),
        ):
            rows = []
            for r in range(g.h):
                beyond = side_columns(g, right, left, at + width * r, width)
                rows.append(jnp.concatenate([wide(source, s, r), beyond], axis=0))
                full[s, r] = rows[r].astype(BF16)
            for k in range(count):
                top, bottom = rows[k], rows[g.h - count + k]
                a_ref[s, first + k] = jnp.where(odd, top, bottom).astype(BF16)


def prepare_kernel(w_ref, one_ref, two_ref, buffer, sems):
    chans = one_ref.shape[1]
    taps, size, lanes = buffer.shape
    per = chans // lanes
    copies = [
        pltpu.make_async_copy(w_ref.at[pl.ds(t * size, size)], buffer.at[t], sems.at[t])
        for t in range(taps)
    ]
    for copy in copies:
        copy.start()
    for t in range(taps):
        copies[t].wait()
        for k, out in enumerate((one_ref, two_ref)):
            parts = [buffer[t, pl.ds(2 * half + k, chans, stride=2 * per), :] for half in range(per)]
            out[t * chans : (t + 1) * chans, :] = jnp.concatenate(parts, axis=1).astype(BF16)


def place_shifted(ref, row_index, row):
    store_shifted(ref, row_index * row.shape[0], row)


def window_rows(g, x_ref, first, count):
    size = count * g.wp
    return jnp.concatenate(
        [x_ref[(first + a) * g.wp : (first + a) * g.wp + size, :] for a in range(3)], axis=1
    )


def own_conv_kernel(g, ext, w, z_ref, st_ref, x_ref):
    count = g.h - 2
    s1 = jnp.zeros((8, g.c), F32)
    s2 = jnp.zeros((8, g.c), F32)
    for s in range(g.s):
        for r in range(g.h):
            place_shifted(x_ref, s * (g.h + 2) + 1 + r, wide(ext, s, r))
        half = count // 2
        for first in range(0, count, half):
            acc = dot(window_rows(g, x_ref, s * (g.h + 2) + 1 + first, half), w[...])
            at = (s * (g.tall - 2) + RIM + first) * g.wp
            z_ref[at : at + half * g.wp, :] = acc
            for i in range(half):
                v = acc[i * g.wp : i * g.wp + g.w]
                s1 = s1 + sum_rows(v)
                s2 = s2 + sum_rows(v * v)
    st_ref[0:8] = s1
    st_ref[8:16] = s2


def rim_conv_kernel(
    g, ext, ra, rb, rb_c, rb_d, w, st_in, z_in, x_in, z_ref, st_ref, x_own, cot_ref, x_ref
):
    del z_in, x_in
    place = Place()
    odd = place.odd_row
    s1, s2 = st_in[0:8], st_in[8:16]
    span = RIM + 2
    for s in range(g.s):
        far = far_rows(g, place, rb, rb_c, rb_d, s)
        near = [wide(ra, s, k) for k in range(RIM + g.near)]
        for side in range(2):
            base = span * (2 * s + side)
            beyond = [
                jnp.where(odd, b, a) if side else jnp.where(odd, a, b)
                for a, b in zip(near, far, strict=True)
            ]
            for k in range(RIM):
                place_shifted(x_ref, base + 2 * side + k, beyond[k])
            next_row = beyond[0 if side else RIM - 1]
            place_shifted(x_own, s * (g.h + 2) + (g.h + 1) * side, next_row)
            cot_ref[s, side] = beyond[RIM].astype(BF16)
            source = (s * (g.h + 2) + 1 + (g.h - 2) * side) * g.wp
            target = (base + RIM * (1 - side)) * g.wp
            x_ref[target : target + 2 * g.wp, :] = x_own[source : source + 2 * g.wp, :]
            acc = dot(window_rows(g, x_ref, base, RIM), w[...])
            at = (s * (g.tall - 2) + (g.h + RIM - 2) * side) * g.wp
            z_ref[at : at + RIM * g.wp, :] = acc
            i = 0 if side else RIM - 1
            v = acc[i * g.wp : i * g.wp + g.w]
            s1 = s1 + sum_rows(v)
            s2 = s2 + sum_rows(v * v)
    to_all(st_ref, [jnp.sum(s1, 0, keepdims=True), jnp.sum(s2, 0, keepdims=True)])


def typical_hidden(params):
    scale, shift = params[0:1], params[1:2]
    return 0.5 * (shift + jnp.sqrt(shift * shift + 0.64 * scale * scale))


def stats_of(total, count):
    mean = total[0:1] / count
    var = total[1:2] / count - mean * mean
    return mean, lax.rsqrt(var + 1e-05)


def second_conv_kernel(g, chunk, count, z1, st, params, w, cot, h_ref, z_ref, st_ref, own_ref):
    rows_in, rows_out = g.tall - 2, g.tall - 4
    place = Place()
    mean, rstd = stats_of(total_of(st), count)
    scale = params[0:1] * rstd
    shift = params[1:2] - mean * scale
    edge = edge_mask(place, g)
    sums = [jnp.zeros((8, g.c), F32) for _ in range(4)]
    for s in range(g.s):
        for r in range(rows_in):
            start = (s * rows_in + r) * g.wp
            row = jnp.maximum(z1[start : start + g.wp, :] * scale + shift, 0.0)
            store_shifted(h_ref, start, in_grid(row, r + 1, g, place, edge))
        for r in range(0, rows_out, chunk):
            base = (s * rows_in + r) * g.wp
            size = chunk * g.wp
            lhs = jnp.concatenate(
                [h_ref[base + a * g.wp : base + a * g.wp + size, :] for a in range(3)], axis=1
            )
            acc = dot(lhs, w[...])
            z_ref[(s * rows_out + r) * g.wp : (s * rows_out + r) * g.wp + size, :] = acc
            for i in range(chunk):
                if RIM <= r + i + 2 < RIM + g.h:
                    v = acc[i * g.wp : i * g.wp + g.w]
                    dn = wide(cot, s, r + i + 2 - RIM)[: g.w]
                    for k, term in enumerate((v, v * v, dn, dn * v)):
                        sums[k] = sums[k] + sum_rows(term)
    own = [jnp.sum(v, 0, keepdims=True) for v in sums]
    own_ref[0:4] = jnp.concatenate(own, axis=0)
    to_all(st_ref, own)


def own_transposed(g, source, first, s, dt_ref):
    span = g.h * g.wp
    block = source[first : first + span, :]
    inside = lax.broadcasted_iota(jnp.int32, (span, 1), 0) % g.wp < g.w
    dt_ref[:, s * span : (s + 1) * span] = jnp.where(inside, block, jnp.zeros_like(block)).T


def kernel_gradient(g, core, field, rows_field, first_row, dt_ref, keep, send, first, prepare, less):
    chans, half = g.c, g.c // 2
    span = g.h * g.wp
    mine = pl.ds(pl.multiple_of(core * half, half), half)
    other = pl.ds(pl.multiple_of((1 - core) * half, half), half)
    totals = [None] * 3
    cut = g.s // 2
    groups = (range(cut), range(cut, g.s))
    for s in groups[0]:
        prepare(s)
    for group in groups:
        lanes = slice(group[0] * span, (group[-1] + 1) * span)
        lhs = jnp.concatenate([dt_ref[mine, lanes], dt_ref[other, lanes]], axis=0)
        for a in range(3):
            starts = [(s * rows_field + first_row + a) * g.wp for s in group]
            acc = dot(lhs, jnp.concatenate([field[at : at + span, :] for at in starts], axis=0))
            if group[0] == 0 and a < len(groups[1]):
                prepare(groups[1][a])
            if group[0] == 0:
                for b in range(3):
                    keep[a * 3 + b] = acc[0:half, b * chans : (b + 1) * chans]
                    first[a * 3 + b] = acc[half:, b * chans : (b + 1) * chans]
                continue
            for b in range(3):
                keep[a * 3 + b] += acc[0:half, b * chans : (b + 1) * chans] - less(mine)
                other_half = first[a * 3 + b] + acc[half:, b * chans : (b + 1) * chans] - less(other)
                send[a * 3 + b] = other_half.astype(BF16)


def second_gradient_kernel(
    g, count, z2, st, own, params, cot, cot_next, h, d_ref, keep, send, dt_ref, sums, first
):
    place = Place()
    rows = g.cot_tall
    total = total_of(st)
    mean, rstd = stats_of(total, count)
    sum_dn = total[2:3]
    sum_dx = rstd * (total[3:4] - mean * sum_dn)
    k0 = params[2:3] * rstd
    k1 = k0 * (sum_dn / count)
    k2 = k0 * rstd * (sum_dx / count)
    edge = edge_mask(place, g)
    def prepare(s):
        for i in range(rows):
            rim = not g.near <= i < g.near + g.h
            dn = wide(cot_next, s, 0 if i < g.near else 1) if rim else wide(cot, s, i - g.near)
            start = (s * rows + i) * g.wp
            d = k0 * dn - k1 - (z2[start : start + g.wp, :] - mean) * k2
            d = in_grid(d, i + RIM - g.near, g, place, edge)
            d_ref[start : start + g.wp, :] = d.astype(BF16)
        own_transposed(g, d_ref, (s * rows + g.near) * g.wp, s, dt_ref)
    pixels = float(g.s * g.h * g.w)
    tile_sum = k0 * own[2:3] - pixels * k1 - k2 * (own[0:1] - pixels * mean)
    sums[...] = jnp.broadcast_to(tile_sum, (sums.shape[1], g.c)).T
    typical = typical_hidden(params)

    def less(channels):
        column = sums[channels, :]
        return jnp.concatenate([column] * (g.c // column.shape[1]), axis=1) * typical

    kernel_gradient(g, place.core, h, g.tall - 2, RIM - 2, dt_ref, keep, send, first, prepare, less)


def transposed_conv(g, d_ref, w, s, rows_in, r, chunk):
    acc = None
    size = chunk * g.wp
    for a in range(3):
        start = (s * rows_in + r + a) * g.wp
        for b in range(3):
            tap = (2 - a) * 3 + (2 - b)
            term = dot_nt(
                d_ref[start : start + size, b * g.c : (b + 1) * g.c],
                w[tap * g.c : (tap + 1) * g.c, :],
            )
            acc = term if acc is None else acc + term
    return acc


def hidden_gradient_kernel(
    g, chunk, count, scenes, d, w, z1, z2, st, st2, params, ext, *refs
):
    *before, dn_ref, st_ref, out_ref, d_ref = refs
    mean2, rstd2 = stats_of(total_of(st2), count)
    scale2 = params[2:3] * rstd2
    shift2 = params[3:4] - mean2 * scale2
    rows_in, rows_out, z_rows = g.tall - 4, g.tall - 6, g.tall - 2
    mean, rstd = stats_of(total_of(st), count)
    scale = params[0:1] * rstd
    shift = params[1:2] - mean * scale
    s0 = before[1][0:8] if before else jnp.zeros((8, g.c), F32)
    s1 = before[1][8:16] if before else jnp.zeros((8, g.c), F32)
    for s in scenes:
        for i in range(rows_in):
            at = (s * rows_in + i) * g.wp
            store_shifted(d_ref, at, wide(d, slice(at, at + g.wp)))
        for r in range(g.h):
            at = (s * rows_in + r + g.near) * g.wp
            normed = z2[at : at + g.w, :] * scale2 + shift2
            out_ref[s, r] = (wide(ext, s, r)[: g.w] + normed).astype(BF16)
        for r in range(0, rows_out, chunk):
            acc = transposed_conv(g, d_ref, w, s, rows_in, r, chunk)
            at = (s * z_rows + r + 2) * g.wp
            z = z1[at : at + chunk * g.wp, :]
            dn = jnp.where(z * scale + shift > 0, acc, 0.0)
            dn_ref[(s * rows_out + r) * g.wp : (s * rows_out + r + chunk) * g.wp, :] = dn
            for i in range(chunk):
                if RIM <= r + i + 3 < RIM + g.h:
                    v = dn[i * g.wp : i * g.wp + g.w]
                    s0 = s0 + sum_rows(v)
                    s1 = s1 + sum_rows(v * (z[i * g.wp : i * g.wp + g.w] - mean))
    if not before:
        st_ref[0:8] = s0
        st_ref[8:16] = s1
    else:
        to_all(st_ref, [jnp.sum(s0, 0, keepdims=True), jnp.sum(s1, 0, keepdims=True) * rstd])


def half_gradient(g, which, field, rows_field, first_row, dt_ref, out_ref, sums, prepare=None):
    chans, half = g.c, g.c // 2
    span = g.h * g.wp
    channels = pl.ds(pl.multiple_of(which * half, half), half)
    cut = g.s // 2
    groups = range(cut), range(cut, g.s)
    if prepare is not None:
        for s in groups[0]:
            prepare(s)
    for group in groups:
        lhs = dt_ref[channels, group[0] * span : (group[-1] + 1) * span]
        for a in range(3):
            starts = [(s * rows_field + first_row + a) * g.wp for s in group]
            acc = dot(lhs, jnp.concatenate([field[at : at + span, :] for at in starts], axis=0))
            if group[0] == 0 and prepare is not None and a < len(groups[1]):
                prepare(groups[1][a])
            for b in range(3):
                part = acc[:, b * chans : (b + 1) * chans]
                if group[0] == 0:
                    sums[a * 3 + b] = part
                else:
                    rows = slice((a * 3 + b) * chans, (a * 3 + b + 1) * chans)
                    out_ref[rows, :] = (sums[a * 3 + b] + part).T.astype(out_ref.dtype)


def first_gradient_kernel(
    g, count, dn, z, st, st3, params, x, e_ref, a_ref, b_ref, send, dt_ref, first
):
    place = Place()
    mean, rstd = stats_of(total_of(st), count)
    total = total_of(st3)
    k0 = params[0:1] * rstd
    k1 = k0 * (total[0:1] / count)
    k2 = k0 * rstd * (total[1:2] / count)
    edge = edge_mask(place, g)

    def prepare(s):
        for i in range(g.h):
            at = (s * g.h + i) * g.wp
            z_at = (s * (g.tall - 2) + i + RIM - 1) * g.wp
            d = k0 * dn[at : at + g.wp, :] - k1 - (z[z_at : z_at + g.wp, :] - mean) * k2
            d = in_grid(d, i + RIM, g, place, edge)
            e_ref[at : at + g.wp, :] = d.astype(BF16)
            if i == 0:
                top = d
        a_ref[s, 0] = jnp.where(place.odd_row, top, d).astype(BF16)
        b_ref[s, 0] = jnp.where(place.odd_row, d, top).astype(BF16)
        own_transposed(g, e_ref, s * g.h * g.wp, s, dt_ref)
    half_gradient(g, 1 - place.core, x, g.h + 2, 0, dt_ref, send, first, prepare)


def first_own_kernel(g, x, dt_ref, keep, first):
    half_gradient(g, Place().core, x, g.h + 2, 0, dt_ref, keep, first)


def input_gradient_kernel(
    g, chunk, e, ra, rb, w_far, cot_far, occ, out_ref, w, cot, e_ref, sems
):
    rows_in = g.h + 2
    place = Place()
    copies = [
        pltpu.make_async_copy(w_far, w, sems.at[0]),
        pltpu.make_async_copy(cot_far, cot, sems.at[1]),
    ]
    for copy in copies:
        copy.start()
    for copy in copies:
        copy.wait()
    for s in range(g.s):
        a, b = wide(ra, s, 0), wide(rb, s, 0)
        rows = [jnp.where(place.odd_row, a, b)]
        for r in range(g.h):
            at = (s * g.h + r) * g.wp
            rows.append(wide(e, slice(at, at + g.wp)))
        rows.append(jnp.where(place.odd_row, b, a))
        for i in range(rows_in):
            place_shifted(e_ref, s * rows_in + i, rows[i])
        mask = pixel_mask(occ, s)
        for r in range(0, g.h, chunk):
            acc = transposed_conv(g, e_ref, w, s, rows_in, r, chunk)
            for i in range(chunk):
                v = acc[i * g.wp : i * g.wp + g.w]
                out_ref[s, r + i] = (wide(cot, s, r + i) + v) * mask[:, r + i : r + i + 1]


def pair_total(keep, got, t):
    if keep.ndim == 3:
        return (keep[t] + wide(got, t)).T
    chans = 2 * keep.shape[1]
    rows = slice(t * chans, (t + 1) * chans)
    return keep[rows, :] + wide(got, rows)


def pair_sum_kernel(lane, keep, got, *refs):
    *_, out_far, buffer, sems = refs
    half = buffer.shape[1]
    chans = 2 * half
    taps = buffer.shape[0] // chans
    copies = []
    for t in range(taps):
        rows = pl.ds(t * chans, chans)
        buffer[rows, :] = pair_total(keep, got, t).astype(BF16)
        copies.append(
            pltpu.make_async_copy(buffer.at[rows], out_far.at[rows, pl.ds(lane, half)], sems.at[t])
        )
        copies[-1].start()
    for copy in copies:
        copy.wait()


def half_rows(share):
    return -(-(share // 2) // 8) * 8


def split_kernel(keep, got, kept_ref, sent_ref, buffer):
    taps, half, chans = keep.shape
    devices, rows, _ = kept_ref.shape
    share = taps * chans // devices
    for t in range(taps):
        buffer[t * chans : (t + 1) * chans, :] = pair_total(keep, got, t)
    second = Place().second
    for i in range(devices):
        mine = pl.multiple_of(i * share + (share - rows) * second, 8)
        other = pl.multiple_of(i * share + (share - rows) * (1 - second), 8)
        kept_ref[i] = buffer[pl.ds(mine, rows), :]
        sent_ref[i] = buffer[pl.ds(other, rows), :].astype(BF16)


def join_kernel(kept, came, out_ref):
    for i in range(kept.shape[0]):
        out_ref[i] = kept[i] + wide(came, i)


def message_kernel(keep, got, kept, out_far, out_ref, sems):
    devices = kept.shape[0]
    share = keep.shape[0] // devices
    copies = []
    count = sems.shape[0]
    for part in range(count):
        mine = pl.ds(part * devices // count, devices // count)
        for i in range(part * devices // count, (part + 1) * devices // count):
            rows = slice(i * share, (i + 1) * share)
            first = keep[rows, :] + wide(got, rows)
            out_ref[i] = jnp.concatenate([first, kept[i]], axis=0).astype(BF16)
        copies.append(pltpu.make_async_copy(out_ref.at[mine], out_far.at[mine], sems.at[part]))
        copies[-1].start()
    for copy in copies:
        copy.wait()


def adamw(weight, grad, first, second, rate):
    first_new = 0.9 * first + 0.1 * grad
    second_new = 0.999 * second + 0.001 * grad * grad
    first_hat = first_new / (1.0 - 0.9**STEP)
    second_hat = second_new / (1.0 - 0.999**STEP)
    weight_new = weight - rate * (first_hat / (jnp.sqrt(second_hat) + 1e-08) + 0.01 * weight)
    return (weight_new, first_new, second_new)


def update_kernel(
    count, parts, w, first_m, second_m, st2, st3, params, n_first, n_second,
    grad_out, w_out, first_out, second_out, n_grad, n_out, n_first_out, n_second_out
):
    devices, ncols = parts.shape[0], lax.axis_size("cols")
    share = w.shape[0] // 4
    total2, total3 = total_of(st2), total_of(st3)
    mean, rstd = stats_of(total2, count)
    sum_dn = total2[2:3]
    grads = jnp.concatenate(
        [total3[1:2], total3[0:1], rstd * (total2[3:4] - mean * sum_dn), sum_dn], axis=0
    )
    n_grad[...] = grads
    n_out[...], n_first_out[...], n_second_out[...] = adamw(
        params[...], grads, n_first[...], n_second[...], 0.75
    )
    def over(chosen, rows, lanes):
        total = None
        for source in range(devices):
            if chosen(source // ncols):
                term = wide(parts, source)[rows, lanes]
                total = term if total is None else total + term
        return total

    grads = []
    every = slice(None)
    for half in range(2):
        if parts.shape[2] == 256:
            for k in range(2):
                lanes = slice(k * 128, (k + 1) * 128)
                grads.append((k, half, over(lambda row: row % 2 == half, every, lanes)))
        else:
            rows = half_rows(share)
            first = over(lambda row: row % 2 == half, slice(0, share), every)
            upper = over(lambda row: row % 4 == half, slice(share, None), every)
            lower = over(lambda row: row % 4 == half + 2, slice(2 * rows, None), every)
            grads += [(0, half, first), (1, half, jnp.concatenate([upper, lower], axis=0))]
    for k, half, grad in grads:
        at = pl.ds(2 * half + k, share, stride=4)
        new = adamw(w[at, :], grad, first_m[at, :], second_m[at, :], 0.02)
        grad_out[at, :] = grad
        w_out[at, :], first_out[at, :], second_out[at, :] = new


def swapped(block, axis, first):
    count = lax.axis_size(axis)
    pairs = []
    for i in range(first, count - 1, 2):
        pairs += [(i, i + 1), (i + 1, i)]
    return lax.ppermute(block, axis, pairs)


def swapped_both(block, first_row, first_col):
    nrows, ncols = lax.axis_size("rows"), lax.axis_size("cols")

    def partner(i, first, count):
        j = i + 1 if (i - first) % 2 == 0 else i - 1
        return j if min(i, j) >= first and max(i, j) < count else None

    pairs = []
    for i in range(nrows):
        for j in range(ncols):
            to = partner(i, first_row, nrows), partner(j, first_col, ncols)
            if None not in to:
                pairs.append((i * ncols + j, to[0] * ncols + to[1]))
    return lax.ppermute(block, BOTH, pairs)


def to_chunks(flat):
    return flat.reshape(2, -1, 128).transpose(1, 0, 2).reshape(-1, 128)


def from_chunks(rows):
    return rows.reshape(-1, 2, 128).transpose(1, 0, 2).reshape(2, -1)


def exchange(parts):
    return lax.all_to_all(parts, BOTH, 0, 0, tiled=True)


def body(
    features,
    occupancy,
    cotangent,
    conv_weights,
    conv_first,
    conv_second,
    norm_scale_bias,
    norm_first,
    norm_second,
):
    scenes, height, width, chans = features.shape
    g = Geometry(scenes, height, width, chans)
    wp = g.wp
    devices = lax.axis_size("rows") * lax.axis_size("cols")
    count = float(scenes * height * width * devices)
    taps = 9 * chans
    n0, n1, n2, n3 = (scenes * wp * (g.tall - 2 * i) for i in range(4))
    own_pixels = scenes * height * wp
    dma = pltpu.SemaphoreType.DMA

    def conv_flops(n):
        return 2 * n * taps * chans

    side = shape_of((scenes, g.side, chans), BF16)
    corner = shape_of((scenes, g.corner, chans), BF16)
    own, c, d, b, bc, bd = kernel_call(
        functools.partial(pack_kernel, g),
        [
            shape_of(features.shape, BF16),
            side,
            side,
            shape_of((scenes, RIM + g.near, width, chans), BF16),
            corner,
            corner,
        ],
        1e8,
        far=(0, 1, 2),
        scratch=[
            pltpu.VMEM(features.shape, BF16),
            pltpu.VMEM(features.shape, BF16),
            pltpu.VMEM(occupancy.shape, jnp.int32),
            dma((3, scenes)),
        ],
    )(features, occupancy, cotangent)
    rb = swapped(b, "rows", 1)
    rc, rd = swapped(c, "cols", 0), swapped(d, "cols", 1)
    rb_c, rb_d = swapped_both(bc, 1, 0), swapped_both(bd, 1, 1)
    chunked = to_chunks(conv_weights)
    share = conv_first.shape[1]
    chunk_shape = shape_of((share // 64, 128), F32)
    weights = (taps, chans)
    w1, w2 = kernel_call(
        prepare_kernel,
        [held(weights, BF16)] * 2,
        0,
        size=1024,
        far=(0,),
        scratch=[pltpu.VMEM((9, chunked.shape[0] // 9, 128), F32), dma((9,))],
    )(chunked)

    def wide_rows(rows):
        return shape_of((scenes, rows, wp, chans), BF16)

    ext, cot_ext, a = kernel_call(
        functools.partial(assemble_kernel, g),
        [wide_rows(n) for n in (height, height, RIM + g.near)],
        0,
        size=1024,
    )(own, cotangent, rc, rd)
    rows_x = scenes * (height + 2) * wp
    x_shape = held((rows_x, 3 * chans), BF16)
    z1, st, x = kernel_call(
        functools.partial(own_conv_kernel, g),
        [held((n1, chans), F32), held((16, chans), F32), x_shape],
        0,
        size=1024,
    )(ext, w1)
    a, rb, rb_c, rb_d, w1 = lax.optimization_barrier((a, rb, rb_c, rb_d, w1))
    ra = swapped(a, "rows", 0)
    z1, st, x, cot_next = kernel_call(
        functools.partial(rim_conv_kernel, g),
        [held((n1, chans), F32), shape_of((devices, 2, chans), F32), x_shape, wide_rows(2)],
        0,
        size=1024,
        scratch=[pltpu.VMEM((scenes * 2 * (RIM + 2) * wp, 3 * chans), BF16)],
        alias={7: 0, 8: 2},
    )(ext, ra, rb, rb_c, rb_d, w1, st, z1, x)
    st1 = exchange(st)
    h, z2, st, own_sums = kernel_call(
        functools.partial(second_conv_kernel, g, 5, count),
        [
            held((n1, 3 * chans), BF16),
            held((n2, chans), F32),
            shape_of((devices, 4, chans), F32),
            held((8, chans), F32),
        ],
        conv_flops(n2),
    )(z1, st1, norm_scale_bias, w2, cot_ext)
    st2 = exchange(st)
    grad_shape = held((9, chans // 2, chans), F32)
    d, keep2, send2 = kernel_call(
        functools.partial(second_gradient_kernel, g, count),
        [held((n2, chans), BF16), grad_shape, held(grad_shape.shape, BF16)],
        conv_flops(own_pixels),
        scratch=[
            pltpu.VMEM((chans, own_pixels), BF16),
            pltpu.VMEM((chans, 128), F32),
            pltpu.VMEM(grad_shape.shape, F32),
        ],
    )(z2, st2, own_sums, norm_scale_bias, cot_ext, cot_next, h)
    got2 = swapped(send2, "rows", 0)
    nrows = lax.axis_size("rows")
    cut_again = nrows % 4 == 0 and taps // devices % 8 == 0
    hidden_shape, output_shape = held((n3, chans), F32), held(features.shape, BF16)

    def hidden_gradient(scenes, part_shape, *before, **options):
        return kernel_call(
            functools.partial(hidden_gradient_kernel, g, 8, count, scenes),
            [hidden_shape, part_shape, output_shape],
            0,
            size=1024,
            scratch=[pltpu.VMEM((n2, 3 * chans), BF16)],
            **options,
        )(d, w2, z1, z2, st1, st2, norm_scale_bias, ext, *before)

    early = range(3)
    dn1, part, block_out = hidden_gradient(early, held((16, chans), F32))
    got2, part = lax.optimization_barrier((got2, part))
    if cut_again:
        kept_shape = (devices, half_rows(taps // devices), chans // 2)
        kept, sent = kernel_call(
            split_kernel,
            [held(kept_shape, F32), held(kept_shape, BF16)],
            0,
            size=1024,
            scratch=[pltpu.VMEM((taps, chans // 2), F32)],
        )(keep2, got2)
        came = lax.ppermute(sent, "rows", [(i, i ^ 2) for i in range(nrows)])
        kept, part = lax.optimization_barrier((kept, part))
    dn1, st, block_out = hidden_gradient(
        range(len(early), scenes),
        shape_of((devices, 2, chans), F32),
        dn1,
        part,
        block_out,
        alias={8: 0, 10: 2},
    )
    st3 = exchange(st)
    if cut_again:
        kept, st3 = lax.optimization_barrier((kept, st3))
        (kept,) = kernel_call(join_kernel, [held(kept_shape, F32)], 0, size=1024)(kept, came)
        dn1, kept = lax.optimization_barrier((dn1, kept))
    sent_shape = held((taps, chans // 2), BF16)
    part = pltpu.VMEM(grad_shape.shape, F32)
    e, a, b, send1, dt = kernel_call(
        functools.partial(first_gradient_kernel, g, count),
        [
            held((n3, chans), BF16),
            wide_rows(1),
            wide_rows(1),
            sent_shape,
            held((chans, own_pixels), BF16),
        ],
        0,
        size=1024,
        scratch=[part],
    )(dn1, z1, st1, st3, norm_scale_bias, x)
    (keep1,) = kernel_call(
        functools.partial(first_own_kernel, g), [held((taps, chans // 2), F32)], 0, size=1024, scratch=[part]
    )(x, dt)
    got1 = swapped(send1, "rows", 0)
    share_rows = taps // devices
    if cut_again:
        rows = share_rows + kept.shape[1]
        (parts,) = kernel_call(
            message_kernel,
            [stored((devices, rows, chans // 2), BF16)],
            1e9,
            far_out=(0,),
            scratch=[pltpu.VMEM((devices, rows, chans // 2), BF16), dma((4,))],
        )(keep1, got1, kept)
    else:

        def add_pair(lane, *operands, **options):
            return kernel_call(
                functools.partial(pair_sum_kernel, lane),
                [stored((taps, chans), BF16)],
                1e9,
                far_out=(0,),
                scratch=[pltpu.VMEM((taps, chans // 2), BF16), dma((9,))],
                **options,
            )(*operands)

        (parts,) = add_pair(chans // 2, keep2, got2)
        (parts,) = add_pair(0, keep1, got1, parts, far=(2,), alias={2: 0})
        parts = parts.reshape(devices, share_rows, chans)
    parts, chunked = lax.optimization_barrier((parts, chunked))
    parts = exchange(parts)
    ra, rb = swapped(a, "rows", 0), swapped(b, "rows", 1)
    (grad_input,) = kernel_call(
        functools.partial(input_gradient_kernel, g, 8),
        [shape_of(features.shape, F32)],
        conv_flops(own_pixels),
        far=(3, 4),
        scratch=[
            pltpu.VMEM(weights, BF16),
            pltpu.VMEM(features.shape, BF16),
            pltpu.VMEM((rows_x, 3 * chans), BF16),
            dma((2,)),
        ],
    )(e, ra, rb, w1, cotangent, occupancy)
    own_rows = share // 64
    first_row = (lax.axis_index("rows") * lax.axis_size("cols") + lax.axis_index("cols")) * own_rows
    own_weights = lax.dynamic_slice_in_dim(chunked, first_row, own_rows, 0)

    norm_shape = shape_of(norm_first.shape, F32)
    updated = kernel_call(
        functools.partial(update_kernel, count),
        [chunk_shape] * 4 + [norm_shape] * 4,
        1e8,
    )(
        parts, own_weights, to_chunks(conv_first), to_chunks(conv_second), st2, st3,
        norm_scale_bias, norm_first, norm_second,
    )
    return (block_out, grad_input, *map(from_chunks, updated[:4]), *updated[4:])


def solution(mesh):
    tile = P(None, "rows", "cols", None)
    share = P(None, ("rows", "cols"))
    return jax.shard_map(
        body,
        mesh=mesh,
        in_specs=(tile, P(None, "rows", "cols"), tile, P(), share, share, P(), P(), P()),
        out_specs=(tile, tile, share, share, share, share, P(), P(), P(), P()),
        check_vma=False,
    )
```

```python
import functools
import math

import jax
import jax.numpy as jnp
from jax import lax
from jax.experimental import pallas as pl
from jax.experimental.pallas import tpu as pltpu
from jax.sharding import PartitionSpec as P

STEP = 5
BOTH = ("rows", "cols")
RIM = 3
COLS = 4
SIDE = 2 * COLS
F32, BF16 = jnp.float32, jnp.bfloat16


def shape_of(shape, dtype):
    return jax.ShapeDtypeStruct(shape, dtype)


def held(shape, dtype):
    return pltpu.VMEM(shape, dtype)


def stored(shape, dtype):
    return pltpu.HBM(shape, dtype)


def kernel_call(body, out_shape, flops, far=(), far_out=(), scratch=(), limit=16, alias=None, size=4 << 20):
    def call(*operands):
        operands = [
            pltpu.with_memory_space_constraint(v, pltpu.HBM if i in far else pltpu.VMEM)
            for i, v in enumerate(operands)
        ]
        specs = [
            pl.BlockSpec(memory_space=pltpu.HBM if i in far else pltpu.VMEM)
            for i in range(len(operands))
        ]
        return pl.pallas_call(
            body,
            out_shape=out_shape,
            in_specs=specs,
            out_specs=[
                pl.BlockSpec(memory_space=pltpu.HBM if i in far_out else pltpu.VMEM)
                for i in range(len(out_shape))
            ],
            scratch_shapes=list(scratch),
            input_output_aliases=alias or {},
            compiler_params=pltpu.CompilerParams(vmem_limit_bytes=limit << 20),
            cost_estimate=pl.CostEstimate(
                flops=int(flops), bytes_accessed=size, transcendentals=0
            ),
        )(*operands)

    return call


def dot(a, b):
    return jnp.dot(a, b, preferred_element_type=F32)


def dot_nt(a, b):
    return lax.dot_general(a, b, (((1,), (1,)), ((), ())), preferred_element_type=F32)


def total_of(ref):
    count = ref.shape[0]
    total = ref[0]
    for i in range(1, count):
        total = total + ref[i]
    return total


def to_all(ref, parts):
    value = jnp.concatenate(parts, axis=0)
    for i in range(ref.shape[0]):
        ref[i] = value


def store_shifted(ref, start, row, offsets=(0, 1, 2)):
    width, chans = row.shape
    for b in offsets:
        moved = row if b == 1 else pltpu.roll(row, 1 if b == 0 else width - 1, 0)
        ref[start : start + width, b * chans : (b + 1) * chans] = moved.astype(BF16)


class Geometry:
    def __init__(self, scenes, height, width, chans):
        self.s, self.h, self.w, self.c = scenes, height, width, chans
        self.wp = width + SIDE
        self.tall = height + 2 * RIM
        self.near = RIM - 2
        self.near_cols = COLS - 2
        self.cot_tall = height + 2 * self.near
        self.side = (COLS + self.near_cols) * height
        self.corner = -(-(COLS * RIM + self.near_cols * self.near) // 16) * 16


class Place:
    def __init__(self):
        row, col = lax.axis_index("rows"), lax.axis_index("cols")
        nrows, ncols = lax.axis_size("rows"), lax.axis_size("cols")
        self.above = (row > 0).astype(F32)
        self.below = (row < nrows - 1).astype(F32)
        self.right = (col < ncols - 1).astype(F32)
        self.left = (col > 0).astype(F32)
        self.core = row % 2
        self.second = row // 2 % 2
        self.odd_row = row % 2 == 1
        self.odd_col = col % 2 == 1
        self.index = row * ncols + col


def wide(ref, *index):
    return ref[index].astype(F32)


def far_rows(g, place, rb, rb_c, rb_d, s):
    right, left = sides(g, place, rb_c, rb_d, s)
    rows = []
    for k in range(RIM + g.near):
        width = COLS if k < RIM else g.near_cols
        at = COLS * min(k, RIM) + g.near_cols * max(k - RIM, 0)
        rows.append(
            jnp.concatenate([wide(rb, s, k), side_columns(g, right, left, at, width)], axis=0)
        )
    return rows


def pixel_mask(occ, s):
    return occ[s].astype(F32).T


def in_grid(row, r, g, place, edge):
    row = jnp.concatenate([row[: g.w], row[g.w :] * edge], axis=0)
    if r < RIM:
        row = row * place.above
    elif r >= RIM + g.h:
        row = row * place.below
    return row


def edge_mask(place, g):
    where = lax.broadcasted_iota(jnp.int32, (SIDE, g.c), 0)
    return jnp.where(where < SIDE // 2, place.right, place.left)


def sum_rows(value):
    rows, chans = value.shape
    return jnp.sum(value.reshape(rows // 8, 8, chans), axis=0)


def pack_kernel(
    g, features, occ_far, cot, own, c_ref, d_ref, b_ref, bc_ref, bd_ref, given, seen, occ, sems
):
    copies = []
    flags = pltpu.make_async_copy(occ_far, occ, sems.at[2, 0])
    flags.start()
    for s in range(g.s):
        copies.append(
            (
                pltpu.make_async_copy(features.at[s], given.at[s], sems.at[0, s]),
                pltpu.make_async_copy(cot.at[s], seen.at[s], sems.at[1, s]),
            )
        )
        for copy in copies[-1]:
            copy.start()
    odd, odd_row = Place().odd_col, Place().odd_row
    flags.wait()

    for s in range(g.s):
        mask = pixel_mask(occ, s)
        for copy in copies[s]:
            copy.wait()
        rows = []
        for r in range(g.h):
            row = wide(given, s, r) * mask[:, r : r + 1]
            rows.append(row)
            own[s, r] = row.astype(BF16)
        cots = [wide(seen, s, r) for r in range(g.h)]
        ends = []
        for field, count in ((rows, RIM), (cots, g.near)):
            for k in range(count):
                ends.append(jnp.where(odd_row, field[g.h - count + k], field[k]))
                b_ref[s, len(ends) - 1] = ends[-1].astype(BF16)
        spare = jnp.zeros((g.corner - COLS * RIM - g.near_cols * g.near, g.c), F32)
        widths = [COLS] * RIM + [g.near_cols] * g.near
        right = [v[g.w - width :] for v, width in zip(ends, widths, strict=True)]
        left = [v[:width] for v, width in zip(ends, widths, strict=True)]
        right, left = (jnp.concatenate(v + [spare], axis=0) for v in (right, left))
        bc_ref[s] = jnp.where(odd, left, right).astype(BF16)
        bd_ref[s] = jnp.where(odd, right, left).astype(BF16)
        right = jnp.concatenate(
            [v[g.w - COLS :] for v in rows] + [v[g.w - g.near_cols :] for v in cots], axis=0
        )
        left = jnp.concatenate([v[:COLS] for v in rows] + [v[: g.near_cols] for v in cots], axis=0)
        c_ref[s] = jnp.where(odd, left, right).astype(BF16)
        d_ref[s] = jnp.where(odd, right, left).astype(BF16)


def sides(g, place, rc, rd, s):
    c, d = wide(rc, s), wide(rd, s)
    return jnp.where(place.odd_col, d, c), jnp.where(place.odd_col, c, d)


def side_columns(g, right, left, at, width):
    parts = [right[at : at + width], jnp.zeros((SIDE - 2 * width, g.c), F32), left[at : at + width]]
    return jnp.concatenate([part for part in parts if part.shape[0]], axis=0)


def assemble_kernel(g, own, cot, rc, rd, ext, cot_ext, a_ref):
    place = Place()

    odd = place.odd_row
    for s in range(g.s):
        right, left = sides(g, place, rc, rd, s)
        for source, full, at, width, count, first in (
            (own, ext, 0, COLS, RIM, 0),
            (cot, cot_ext, COLS * g.h, g.near_cols, g.near, RIM),
        ):
            rows = []
            for r in range(g.h):
                beyond = side_columns(g, right, left, at + width * r, width)
                rows.append(jnp.concatenate([wide(source, s, r), beyond], axis=0))
                full[s, r] = rows[r].astype(BF16)
            for k in range(count):
                top, bottom = rows[k], rows[g.h - count + k]
                a_ref[s, first + k] = jnp.where(odd, top, bottom).astype(BF16)


def prepare_kernel(w_ref, one_ref, two_ref, buffer, sems):
    chans = one_ref.shape[1]
    taps, size, lanes = buffer.shape
    per = chans // lanes
    copies = [
        pltpu.make_async_copy(w_ref.at[pl.ds(t * size, size)], buffer.at[t], sems.at[t])
        for t in range(taps)
    ]
    for copy in copies:
        copy.start()
    for t in range(taps):
        copies[t].wait()
        for k, out in enumerate((one_ref, two_ref)):
            parts = [buffer[t, pl.ds(2 * half + k, chans, stride=2 * per), :] for half in range(per)]
            out[t * chans : (t + 1) * chans, :] = jnp.concatenate(parts, axis=1).astype(BF16)


def place_shifted(ref, row_index, row):
    store_shifted(ref, row_index * row.shape[0], row)


def window_rows(g, x_ref, first, count):
    size = count * g.wp
    return jnp.concatenate(
        [x_ref[(first + a) * g.wp : (first + a) * g.wp + size, :] for a in range(3)], axis=1
    )


def own_conv_kernel(g, ext, w, z_ref, st_ref, x_ref):
    count = g.h - 2
    s1 = jnp.zeros((8, g.c), F32)
    s2 = jnp.zeros((8, g.c), F32)
    for s in range(g.s):
        for r in range(g.h):
            place_shifted(x_ref, s * (g.h + 2) + 1 + r, wide(ext, s, r))
        half = count // 2
        for first in range(0, count, half):
            acc = dot(window_rows(g, x_ref, s * (g.h + 2) + 1 + first, half), w[...])
            at = (s * (g.tall - 2) + RIM + first) * g.wp
            z_ref[at : at + half * g.wp, :] = acc
            for i in range(half):
                v = acc[i * g.wp : i * g.wp + g.w]
                s1 = s1 + sum_rows(v)
                s2 = s2 + sum_rows(v * v)
    st_ref[0:8] = s1
    st_ref[8:16] = s2


def rim_conv_kernel(
    g, ext, ra, rb, rb_c, rb_d, w, st_in, z_in, x_in, z_ref, st_ref, x_own, cot_ref, x_ref
):
    del z_in, x_in
    place = Place()
    odd = place.odd_row
    s1, s2 = st_in[0:8], st_in[8:16]
    span = RIM + 2
    for s in range(g.s):
        far = far_rows(g, place, rb, rb_c, rb_d, s)
        near = [wide(ra, s, k) for k in range(RIM + g.near)]
        for side in range(2):
            base = span * (2 * s + side)
            beyond = [
                jnp.where(odd, b, a) if side else jnp.where(odd, a, b)
                for a, b in zip(near, far, strict=True)
            ]
            for k in range(RIM):
                place_shifted(x_ref, base + 2 * side + k, beyond[k])
            next_row = beyond[0 if side else RIM - 1]
            place_shifted(x_own, s * (g.h + 2) + (g.h + 1) * side, next_row)
            cot_ref[s, side] = beyond[RIM].astype(BF16)
            source = (s * (g.h + 2) + 1 + (g.h - 2) * side) * g.wp
            target = (base + RIM * (1 - side)) * g.wp
            x_ref[target : target + 2 * g.wp, :] = x_own[source : source + 2 * g.wp, :]
            acc = dot(window_rows(g, x_ref, base, RIM), w[...])
            at = (s * (g.tall - 2) + (g.h + RIM - 2) * side) * g.wp
            z_ref[at : at + RIM * g.wp, :] = acc
            i = 0 if side else RIM - 1
            v = acc[i * g.wp : i * g.wp + g.w]
            s1 = s1 + sum_rows(v)
            s2 = s2 + sum_rows(v * v)
    to_all(st_ref, [jnp.sum(s1, 0, keepdims=True), jnp.sum(s2, 0, keepdims=True)])


def typical_hidden(params):
    scale, shift = params[0:1], params[1:2]
    return 0.5 * (shift + jnp.sqrt(shift * shift + 0.64 * scale * scale))


def stats_of(total, count):
    mean = total[0:1] / count
    var = total[1:2] / count - mean * mean
    return mean, lax.rsqrt(var + 1e-05)


def second_conv_kernel(g, chunk, count, z1, st, params, w, cot, h_ref, z_ref, st_ref, own_ref):
    rows_in, rows_out = g.tall - 2, g.tall - 4
    place = Place()
    mean, rstd = stats_of(total_of(st), count)
    scale = params[0:1] * rstd
    shift = params[1:2] - mean * scale
    edge = edge_mask(place, g)
    sums = [jnp.zeros((8, g.c), F32) for _ in range(4)]
    for s in range(g.s):
        for r in range(rows_in):
            start = (s * rows_in + r) * g.wp
            row = jnp.maximum(z1[start : start + g.wp, :] * scale + shift, 0.0)
            store_shifted(h_ref, start, in_grid(row, r + 1, g, place, edge))
        for r in range(0, rows_out, chunk):
            base = (s * rows_in + r) * g.wp
            size = chunk * g.wp
            lhs = jnp.concatenate(
                [h_ref[base + a * g.wp : base + a * g.wp + size, :] for a in range(3)], axis=1
            )
            acc = dot(lhs, w[...])
            z_ref[(s * rows_out + r) * g.wp : (s * rows_out + r) * g.wp + size, :] = acc
            for i in range(chunk):
                if RIM <= r + i + 2 < RIM + g.h:
                    v = acc[i * g.wp : i * g.wp + g.w]
                    dn = wide(cot, s, r + i + 2 - RIM)[: g.w]
                    for k, term in enumerate((v, v * v, dn, dn * v)):
                        sums[k] = sums[k] + sum_rows(term)
    own = [jnp.sum(v, 0, keepdims=True) for v in sums]
    own_ref[0:4] = jnp.concatenate(own, axis=0)
    to_all(st_ref, own)


def own_transposed(g, source, first, s, dt_ref):
    span = g.h * g.wp
    block = source[first : first + span, :]
    inside = lax.broadcasted_iota(jnp.int32, (span, 1), 0) % g.wp < g.w
    dt_ref[:, s * span : (s + 1) * span] = jnp.where(inside, block, jnp.zeros_like(block)).T


def kernel_gradient(g, core, field, rows_field, first_row, dt_ref, keep, send, first, prepare, less):
    chans, half = g.c, g.c // 2
    span = g.h * g.wp
    mine = pl.ds(pl.multiple_of(core * half, half), half)
    other = pl.ds(pl.multiple_of((1 - core) * half, half), half)
    totals = [None] * 3
    cut = g.s // 2
    groups = (range(cut), range(cut, g.s))
    for s in groups[0]:
        prepare(s)
    for group in groups:
        lanes = slice(group[0] * span, (group[-1] + 1) * span)
        lhs = jnp.concatenate([dt_ref[mine, lanes], dt_ref[other, lanes]], axis=0)
        for a in range(3):
            starts = [(s * rows_field + first_row + a) * g.wp for s in group]
            acc = dot(lhs, jnp.concatenate([field[at : at + span, :] for at in starts], axis=0))
            if group[0] == 0 and a < len(groups[1]):
                prepare(groups[1][a])
            if group[0] == 0:
                for b in range(3):
                    first[a * 3 + b] = acc[:, b * chans : (b + 1) * chans]
                continue
            for b in range(3):
                rows = slice((a * 3 + b) * chans, (a * 3 + b + 1) * chans)
                part = acc[:, b * chans : (b + 1) * chans] + first[a * 3 + b]
                keep[rows, :] = (part[0:half] - less(mine)).T
                send[rows, :] = (part[half:] - less(other)).T.astype(BF16)


def second_gradient_kernel(
    g, count, z2, st, own, params, cot, cot_next, h, d_ref, keep, send, dt_ref, sums, first
):
    place = Place()
    rows = g.cot_tall
    total = total_of(st)
    mean, rstd = stats_of(total, count)
    sum_dn = total[2:3]
    sum_dx = rstd * (total[3:4] - mean * sum_dn)
    k0 = params[2:3] * rstd
    k1 = k0 * (sum_dn / count)
    k2 = k0 * rstd * (sum_dx / count)
    edge = edge_mask(place, g)
    def prepare(s):
        for i in range(rows):
            rim = not g.near <= i < g.near + g.h
            dn = wide(cot_next, s, 0 if i < g.near else 1) if rim else wide(cot, s, i - g.near)
            start = (s * rows + i) * g.wp
            d = k0 * dn - k1 - (z2[start : start + g.wp, :] - mean) * k2
            d = in_grid(d, i + RIM - g.near, g, place, edge)
            d_ref[start : start + g.wp, :] = d.astype(BF16)
        own_transposed(g, d_ref, (s * rows + g.near) * g.wp, s, dt_ref)
    pixels = float(g.s * g.h * g.w)
    tile_sum = k0 * own[2:3] - pixels * k1 - k2 * (own[0:1] - pixels * mean)
    sums[...] = jnp.broadcast_to(tile_sum, (sums.shape[1], g.c)).T
    typical = typical_hidden(params)

    def less(channels):
        column = sums[channels, :]
        return jnp.concatenate([column] * (g.c // column.shape[1]), axis=1) * typical

    kernel_gradient(g, place.core, h, g.tall - 2, RIM - 2, dt_ref, keep, send, first, prepare, less)


def transposed_conv(g, d_ref, w, s, rows_in, r, chunk):
    acc = None
    size = chunk * g.wp
    for a in range(3):
        start = (s * rows_in + r + a) * g.wp
        for b in range(3):
            tap = (2 - a) * 3 + (2 - b)
            term = dot_nt(
                d_ref[start : start + size, b * g.c : (b + 1) * g.c],
                w[tap * g.c : (tap + 1) * g.c, :],
            )
            acc = term if acc is None else acc + term
    return acc


def hidden_gradient_kernel(
    g, chunk, count, scenes, d, w, z1, z2, st, st2, params, ext, *refs
):
    *before, dn_ref, st_ref, out_ref, d_ref = refs
    mean2, rstd2 = stats_of(total_of(st2), count)
    scale2 = params[2:3] * rstd2
    shift2 = params[3:4] - mean2 * scale2
    rows_in, rows_out, z_rows = g.tall - 4, g.tall - 6, g.tall - 2
    mean, rstd = stats_of(total_of(st), count)
    scale = params[0:1] * rstd
    shift = params[1:2] - mean * scale
    s0 = before[1][0:8] if before else jnp.zeros((8, g.c), F32)
    s1 = before[1][8:16] if before else jnp.zeros((8, g.c), F32)
    for s in scenes:
        for i in range(rows_in):
            at = (s * rows_in + i) * g.wp
            store_shifted(d_ref, at, wide(d, slice(at, at + g.wp)))
        for r in range(g.h):
            at = (s * rows_in + r + g.near) * g.wp
            normed = z2[at : at + g.w, :] * scale2 + shift2
            out_ref[s, r] = (wide(ext, s, r)[: g.w] + normed).astype(BF16)
        for r in range(0, rows_out, chunk):
            acc = transposed_conv(g, d_ref, w, s, rows_in, r, chunk)
            at = (s * z_rows + r + 2) * g.wp
            z = z1[at : at + chunk * g.wp, :]
            dn = jnp.where(z * scale + shift > 0, acc, 0.0)
            dn_ref[(s * rows_out + r) * g.wp : (s * rows_out + r + chunk) * g.wp, :] = dn
            for i in range(chunk):
                if RIM <= r + i + 3 < RIM + g.h:
                    v = dn[i * g.wp : i * g.wp + g.w]
                    s0 = s0 + sum_rows(v)
                    s1 = s1 + sum_rows(v * (z[i * g.wp : i * g.wp + g.w] - mean))
    if not before:
        st_ref[0:8] = s0
        st_ref[8:16] = s1
    else:
        to_all(st_ref, [jnp.sum(s0, 0, keepdims=True), jnp.sum(s1, 0, keepdims=True) * rstd])


def half_gradient(g, which, field, rows_field, first_row, dt_ref, out_ref, sums, prepare=None):
    chans, half = g.c, g.c // 2
    span = g.h * g.wp
    channels = pl.ds(pl.multiple_of(which * half, half), half)
    cut = g.s // 2
    groups = range(cut), range(cut, g.s)
    if prepare is not None:
        for s in groups[0]:
            prepare(s)
    for group in groups:
        lhs = dt_ref[channels, group[0] * span : (group[-1] + 1) * span]
        for a in range(3):
            starts = [(s * rows_field + first_row + a) * g.wp for s in group]
            acc = dot(lhs, jnp.concatenate([field[at : at + span, :] for at in starts], axis=0))
            if group[0] == 0 and prepare is not None and a < len(groups[1]):
                prepare(groups[1][a])
            for b in range(3):
                part = acc[:, b * chans : (b + 1) * chans]
                if group[0] == 0:
                    sums[a * 3 + b] = part
                else:
                    rows = slice((a * 3 + b) * chans, (a * 3 + b + 1) * chans)
                    out_ref[rows, :] = (sums[a * 3 + b] + part).T.astype(out_ref.dtype)


def first_gradient_kernel(
    g, count, dn, z, st, st3, params, x, e_ref, a_ref, b_ref, send, dt_ref, first
):
    place = Place()
    mean, rstd = stats_of(total_of(st), count)
    total = total_of(st3)
    k0 = params[0:1] * rstd
    k1 = k0 * (total[0:1] / count)
    k2 = k0 * rstd * (total[1:2] / count)
    edge = edge_mask(place, g)

    def prepare(s):
        for i in range(g.h):
            at = (s * g.h + i) * g.wp
            z_at = (s * (g.tall - 2) + i + RIM - 1) * g.wp
            d = k0 * dn[at : at + g.wp, :] - k1 - (z[z_at : z_at + g.wp, :] - mean) * k2
            d = in_grid(d, i + RIM, g, place, edge)
            e_ref[at : at + g.wp, :] = d.astype(BF16)
            if i == 0:
                top = d
        a_ref[s, 0] = jnp.where(place.odd_row, top, d).astype(BF16)
        b_ref[s, 0] = jnp.where(place.odd_row, d, top).astype(BF16)
        own_transposed(g, e_ref, s * g.h * g.wp, s, dt_ref)
    half_gradient(g, 1 - place.core, x, g.h + 2, 0, dt_ref, send, first, prepare)


def first_own_kernel(g, x, dt_ref, keep, first):
    half_gradient(g, Place().core, x, g.h + 2, 0, dt_ref, keep, first)


def input_gradient_kernel(
    g, chunk, e, ra, rb, w_far, cot_far, occ, out_ref, w, cot, e_ref, sems
):
    rows_in = g.h + 2
    place = Place()
    copies = [
        pltpu.make_async_copy(w_far, w, sems.at[0]),
        pltpu.make_async_copy(cot_far, cot, sems.at[1]),
    ]
    for copy in copies:
        copy.start()
    for copy in copies:
        copy.wait()
    for s in range(g.s):
        a, b = wide(ra, s, 0), wide(rb, s, 0)
        rows = [jnp.where(place.odd_row, a, b)]
        for r in range(g.h):
            at = (s * g.h + r) * g.wp
            rows.append(wide(e, slice(at, at + g.wp)))
        rows.append(jnp.where(place.odd_row, b, a))
        for i in range(rows_in):
            place_shifted(e_ref, s * rows_in + i, rows[i])
        mask = pixel_mask(occ, s)
        for r in range(0, g.h, chunk):
            acc = transposed_conv(g, e_ref, w, s, rows_in, r, chunk)
            for i in range(chunk):
                v = acc[i * g.wp : i * g.wp + g.w]
                out_ref[s, r + i] = (wide(cot, s, r + i) + v) * mask[:, r + i : r + i + 1]


def pair_total(keep, got, t):
    chans = 2 * keep.shape[1]
    rows = slice(t * chans, (t + 1) * chans)
    return keep[rows, :] + wide(got, rows)


def pair_sum_kernel(lane, keep, got, *refs):
    *_, out_far, buffer, sems = refs
    half = buffer.shape[1]
    chans = 2 * half
    taps = buffer.shape[0] // chans
    copies = []
    for t in range(taps):
        rows = pl.ds(t * chans, chans)
        buffer[rows, :] = pair_total(keep, got, t).astype(BF16)
        copies.append(
            pltpu.make_async_copy(buffer.at[rows], out_far.at[rows, pl.ds(lane, half)], sems.at[t])
        )
        copies[-1].start()
    for copy in copies:
        copy.wait()


def half_rows(share):
    return -(-(share // 2) // 8) * 8


def split_kernel(keep, got, kept_ref, sent_ref, buffer):
    half = keep.shape[1]
    chans = 2 * half
    taps = keep.shape[0] // chans
    devices, rows, _ = kept_ref.shape
    share = taps * chans // devices
    for t in range(taps):
        buffer[t * chans : (t + 1) * chans, :] = pair_total(keep, got, t)
    second = Place().second
    for i in range(devices):
        mine = pl.multiple_of(i * share + (share - rows) * second, 8)
        other = pl.multiple_of(i * share + (share - rows) * (1 - second), 8)
        kept_ref[i] = buffer[pl.ds(mine, rows), :]
        sent_ref[i] = buffer[pl.ds(other, rows), :].astype(BF16)


def join_kernel(kept, came, out_ref):
    for i in range(kept.shape[0]):
        out_ref[i] = kept[i] + wide(came, i)


def message_kernel(keep, got, kept, out_far, out_ref, sems):
    devices = kept.shape[0]
    share = keep.shape[0] // devices
    copies = []
    count = sems.shape[0]
    for part in range(count):
        mine = pl.ds(part * devices // count, devices // count)
        for i in range(part * devices // count, (part + 1) * devices // count):
            rows = slice(i * share, (i + 1) * share)
            first = keep[rows, :] + wide(got, rows)
            out_ref[i] = jnp.concatenate([first, kept[i]], axis=0).astype(BF16)
        copies.append(pltpu.make_async_copy(out_ref.at[mine], out_far.at[mine], sems.at[part]))
        copies[-1].start()
    for copy in copies:
        copy.wait()


def adamw(weight, grad, first, second, rate):
    first_new = 0.9 * first + 0.1 * grad
    second_new = 0.999 * second + 0.001 * grad * grad
    first_hat = first_new / (1.0 - 0.9**STEP)
    second_hat = second_new / (1.0 - 0.999**STEP)
    weight_new = weight - rate * (first_hat / (jnp.sqrt(second_hat) + 1e-08) + 0.01 * weight)
    return (weight_new, first_new, second_new)


def update_kernel(
    count, parts, w, first_m, second_m, st2, st3, params, n_first, n_second,
    grad_out, w_out, first_out, second_out, n_grad, n_out, n_first_out, n_second_out
):
    devices, ncols = parts.shape[0], lax.axis_size("cols")
    share = w.shape[0] // 4
    total2, total3 = total_of(st2), total_of(st3)
    mean, rstd = stats_of(total2, count)
    sum_dn = total2[2:3]
    grads = jnp.concatenate(
        [total3[1:2], total3[0:1], rstd * (total2[3:4] - mean * sum_dn), sum_dn], axis=0
    )
    n_grad[...] = grads
    n_out[...], n_first_out[...], n_second_out[...] = adamw(
        params[...], grads, n_first[...], n_second[...], 0.75
    )
    def over(chosen, rows, lanes):
        total = None
        for source in range(devices):
            if chosen(source // ncols):
                term = wide(parts, source)[rows, lanes]
                total = term if total is None else total + term
        return total

    grads = []
    every = slice(None)
    for half in range(2):
        if parts.shape[2] == 256:
            for k in range(2):
                lanes = slice(k * 128, (k + 1) * 128)
                grads.append((k, half, over(lambda row: row % 2 == half, every, lanes)))
        else:
            rows = half_rows(share)
            first = over(lambda row: row % 2 == half, slice(0, share), every)
            upper = over(lambda row: row % 4 == half, slice(share, None), every)
            lower = over(lambda row: row % 4 == half + 2, slice(2 * rows, None), every)
            grads += [(0, half, first), (1, half, jnp.concatenate([upper, lower], axis=0))]
    for k, half, grad in grads:
        at = pl.ds(2 * half + k, share, stride=4)
        new = adamw(w[at, :], grad, first_m[at, :], second_m[at, :], 0.02)
        grad_out[at, :] = grad
        w_out[at, :], first_out[at, :], second_out[at, :] = new


def swapped(block, axis, first):
    count = lax.axis_size(axis)
    pairs = []
    for i in range(first, count - 1, 2):
        pairs += [(i, i + 1), (i + 1, i)]
    return lax.ppermute(block, axis, pairs)


def swapped_both(block, first_row, first_col):
    nrows, ncols = lax.axis_size("rows"), lax.axis_size("cols")

    def partner(i, first, count):
        j = i + 1 if (i - first) % 2 == 0 else i - 1
        return j if min(i, j) >= first and max(i, j) < count else None

    pairs = []
    for i in range(nrows):
        for j in range(ncols):
            to = partner(i, first_row, nrows), partner(j, first_col, ncols)
            if None not in to:
                pairs.append((i * ncols + j, to[0] * ncols + to[1]))
    return lax.ppermute(block, BOTH, pairs)


def to_chunks(flat):
    return flat.reshape(2, -1, 128).transpose(1, 0, 2).reshape(-1, 128)


def from_chunks(rows):
    return rows.reshape(-1, 2, 128).transpose(1, 0, 2).reshape(2, -1)


def exchange(parts):
    return lax.all_to_all(parts, BOTH, 0, 0, tiled=True)


def body(
    features,
    occupancy,
    cotangent,
    conv_weights,
    conv_first,
    conv_second,
    norm_scale_bias,
    norm_first,
    norm_second,
):
    scenes, height, width, chans = features.shape
    g = Geometry(scenes, height, width, chans)
    wp = g.wp
    devices = lax.axis_size("rows") * lax.axis_size("cols")
    count = float(scenes * height * width * devices)
    taps = 9 * chans
    n0, n1, n2, n3 = (scenes * wp * (g.tall - 2 * i) for i in range(4))
    own_pixels = scenes * height * wp
    dma = pltpu.SemaphoreType.DMA

    def conv_flops(n):
        return 2 * n * taps * chans

    side = shape_of((scenes, g.side, chans), BF16)
    corner = shape_of((scenes, g.corner, chans), BF16)
    own, c, d, b, bc, bd = kernel_call(
        functools.partial(pack_kernel, g),
        [
            shape_of(features.shape, BF16),
            side,
            side,
            shape_of((scenes, RIM + g.near, width, chans), BF16),
            corner,
            corner,
        ],
        1e8,
        far=(0, 1, 2),
        scratch=[
            pltpu.VMEM(features.shape, BF16),
            pltpu.VMEM(features.shape, BF16),
            pltpu.VMEM(occupancy.shape, jnp.int32),
            dma((3, scenes)),
        ],
    )(features, occupancy, cotangent)
    rb = swapped(b, "rows", 1)
    rc, rd = swapped(c, "cols", 0), swapped(d, "cols", 1)
    rb_c, rb_d = swapped_both(bc, 1, 0), swapped_both(bd, 1, 1)
    chunked = to_chunks(conv_weights)
    share = conv_first.shape[1]
    chunk_shape = shape_of((share // 64, 128), F32)
    weights = (taps, chans)
    w1, w2 = kernel_call(
        prepare_kernel,
        [held(weights, BF16)] * 2,
        0,
        size=1024,
        far=(0,),
        scratch=[pltpu.VMEM((9, chunked.shape[0] // 9, 128), F32), dma((9,))],
    )(chunked)

    def wide_rows(rows):
        return shape_of((scenes, rows, wp, chans), BF16)

    ext, cot_ext, a = kernel_call(
        functools.partial(assemble_kernel, g),
        [wide_rows(n) for n in (height, height, RIM + g.near)],
        0,
        size=1024,
    )(own, cotangent, rc, rd)
    rows_x = scenes * (height + 2) * wp
    x_shape = held((rows_x, 3 * chans), BF16)
    z1, st, x = kernel_call(
        functools.partial(own_conv_kernel, g),
        [held((n1, chans), F32), held((16, chans), F32), x_shape],
        0,
        size=1024,
    )(ext, w1)
    a, rb, rb_c, rb_d, w1 = lax.optimization_barrier((a, rb, rb_c, rb_d, w1))
    ra = swapped(a, "rows", 0)
    z1, st, x, cot_next = kernel_call(
        functools.partial(rim_conv_kernel, g),
        [held((n1, chans), F32), shape_of((devices, 2, chans), F32), x_shape, wide_rows(2)],
        0,
        size=1024,
        scratch=[pltpu.VMEM((scenes * 2 * (RIM + 2) * wp, 3 * chans), BF16)],
        alias={7: 0, 8: 2},
    )(ext, ra, rb, rb_c, rb_d, w1, st, z1, x)
    st1 = exchange(st)
    h, z2, st, own_sums = kernel_call(
        functools.partial(second_conv_kernel, g, 5, count),
        [
            held((n1, 3 * chans), BF16),
            held((n2, chans), F32),
            shape_of((devices, 4, chans), F32),
            held((8, chans), F32),
        ],
        conv_flops(n2),
    )(z1, st1, norm_scale_bias, w2, cot_ext)
    st2 = exchange(st)
    grad_shape = held((taps, chans // 2), F32)
    d, keep2, send2 = kernel_call(
        functools.partial(second_gradient_kernel, g, count),
        [held((n2, chans), BF16), grad_shape, held(grad_shape.shape, BF16)],
        conv_flops(own_pixels),
        scratch=[
            pltpu.VMEM((chans, own_pixels), BF16),
            pltpu.VMEM((chans, 128), F32),
            pltpu.VMEM((9, chans, chans), F32),
        ],
    )(z2, st2, own_sums, norm_scale_bias, cot_ext, cot_next, h)
    got2 = swapped(send2, "rows", 0)
    nrows = lax.axis_size("rows")
    cut_again = nrows % 4 == 0 and taps // devices % 8 == 0
    hidden_shape, output_shape = held((n3, chans), F32), held(features.shape, BF16)

    def hidden_gradient(scenes, part_shape, *before, **options):
        return kernel_call(
            functools.partial(hidden_gradient_kernel, g, 8, count, scenes),
            [hidden_shape, part_shape, output_shape],
            0,
            size=1024,
            scratch=[pltpu.VMEM((n2, 3 * chans), BF16)],
            **options,
        )(d, w2, z1, z2, st1, st2, norm_scale_bias, ext, *before)

    early = range(3)
    dn1, part, block_out = hidden_gradient(early, held((16, chans), F32))
    got2, part = lax.optimization_barrier((got2, part))
    if cut_again:
        kept_shape = (devices, half_rows(taps // devices), chans // 2)
        kept, sent = kernel_call(
            split_kernel,
            [held(kept_shape, F32), held(kept_shape, BF16)],
            0,
            size=1024,
            scratch=[pltpu.VMEM((taps, chans // 2), F32)],
        )(keep2, got2)
        came = lax.ppermute(sent, "rows", [(i, i ^ 2) for i in range(nrows)])
        kept, part = lax.optimization_barrier((kept, part))
    dn1, st, block_out = hidden_gradient(
        range(len(early), scenes),
        shape_of((devices, 2, chans), F32),
        dn1,
        part,
        block_out,
        alias={8: 0, 10: 2},
    )
    st3 = exchange(st)
    if cut_again:
        kept, st3 = lax.optimization_barrier((kept, st3))
        (kept,) = kernel_call(join_kernel, [held(kept_shape, F32)], 0, size=1024)(kept, came)
        dn1, kept = lax.optimization_barrier((dn1, kept))
    sent_shape = held((taps, chans // 2), BF16)
    part = pltpu.VMEM((9, chans // 2, chans), F32)
    e, a, b, send1, dt = kernel_call(
        functools.partial(first_gradient_kernel, g, count),
        [
            held((n3, chans), BF16),
            wide_rows(1),
            wide_rows(1),
            sent_shape,
            held((chans, own_pixels), BF16),
        ],
        0,
        size=1024,
        scratch=[part],
    )(dn1, z1, st1, st3, norm_scale_bias, x)
    (keep1,) = kernel_call(
        functools.partial(first_own_kernel, g), [held((taps, chans // 2), F32)], 0, size=1024, scratch=[part]
    )(x, dt)
    got1 = swapped(send1, "rows", 0)
    share_rows = taps // devices
    if cut_again:
        rows = share_rows + kept.shape[1]
        (parts,) = kernel_call(
            message_kernel,
            [stored((devices, rows, chans // 2), BF16)],
            1e9,
            far_out=(0,),
            scratch=[pltpu.VMEM((devices, rows, chans // 2), BF16), dma((4,))],
        )(keep1, got1, kept)
    else:

        def add_pair(lane, *operands, **options):
            return kernel_call(
                functools.partial(pair_sum_kernel, lane),
                [stored((taps, chans), BF16)],
                1e9,
                far_out=(0,),
                scratch=[pltpu.VMEM((taps, chans // 2), BF16), dma((9,))],
                **options,
            )(*operands)

        (parts,) = add_pair(chans // 2, keep2, got2)
        (parts,) = add_pair(0, keep1, got1, parts, far=(2,), alias={2: 0})
        parts = parts.reshape(devices, share_rows, chans)
    parts, chunked = lax.optimization_barrier((parts, chunked))
    parts = exchange(parts)
    ra, rb = swapped(a, "rows", 0), swapped(b, "rows", 1)
    (grad_input,) = kernel_call(
        functools.partial(input_gradient_kernel, g, 8),
        [shape_of(features.shape, F32)],
        conv_flops(own_pixels),
        far=(3, 4),
        scratch=[
            pltpu.VMEM(weights, BF16),
            pltpu.VMEM(features.shape, BF16),
            pltpu.VMEM((rows_x, 3 * chans), BF16),
            dma((2,)),
        ],
    )(e, ra, rb, w1, cotangent, occupancy)
    own_rows = share // 64
    first_row = (lax.axis_index("rows") * lax.axis_size("cols") + lax.axis_index("cols")) * own_rows
    own_weights = lax.dynamic_slice_in_dim(chunked, first_row, own_rows, 0)

    norm_shape = shape_of(norm_first.shape, F32)
    updated = kernel_call(
        functools.partial(update_kernel, count),
        [chunk_shape] * 4 + [norm_shape] * 4,
        1e8,
    )(
        parts, own_weights, to_chunks(conv_first), to_chunks(conv_second), st2, st3,
        norm_scale_bias, norm_first, norm_second,
    )
    return (block_out, grad_input, *map(from_chunks, updated[:4]), *updated[4:])


def solution(mesh):
    tile = P(None, "rows", "cols", None)
    share = P(None, ("rows", "cols"))
    return jax.shard_map(
        body,
        mesh=mesh,
        in_specs=(tile, P(None, "rows", "cols"), tile, P(), share, share, P(), P(), P()),
        out_specs=(tile, tile, share, share, share, share, P(), P(), P(), P()),
        check_vma=False,
    )
```

```python
import functools
import math

import jax
import jax.numpy as jnp
from jax import lax
from jax.experimental import pallas as pl
from jax.experimental.pallas import tpu as pltpu
from jax.sharding import PartitionSpec as P

STEP = 5
BOTH = ("rows", "cols")
RIM = 3
COLS = 4
SIDE = 2 * COLS
F32, BF16 = jnp.float32, jnp.bfloat16


def shape_of(shape, dtype):
    return jax.ShapeDtypeStruct(shape, dtype)


def held(shape, dtype):
    return pltpu.VMEM(shape, dtype)


def stored(shape, dtype):
    return pltpu.HBM(shape, dtype)


def kernel_call(body, out_shape, flops, far=(), far_out=(), scratch=(), limit=16, alias=None, size=4 << 20):
    def call(*operands):
        operands = [
            pltpu.with_memory_space_constraint(v, pltpu.HBM if i in far else pltpu.VMEM)
            for i, v in enumerate(operands)
        ]
        specs = [
            pl.BlockSpec(memory_space=pltpu.HBM if i in far else pltpu.VMEM)
            for i in range(len(operands))
        ]
        return pl.pallas_call(
            body,
            out_shape=out_shape,
            in_specs=specs,
            out_specs=[
                pl.BlockSpec(memory_space=pltpu.HBM if i in far_out else pltpu.VMEM)
                for i in range(len(out_shape))
            ],
            scratch_shapes=list(scratch),
            input_output_aliases=alias or {},
            compiler_params=pltpu.CompilerParams(vmem_limit_bytes=limit << 20),
            cost_estimate=pl.CostEstimate(
                flops=int(flops), bytes_accessed=size, transcendentals=0
            ),
        )(*operands)

    return call


def dot(a, b):
    return jnp.dot(a, b, preferred_element_type=F32)


def dot_nt(a, b):
    return lax.dot_general(a, b, (((1,), (1,)), ((), ())), preferred_element_type=F32)


def total_of(ref):
    count = ref.shape[0]
    total = ref[0]
    for i in range(1, count):
        total = total + ref[i]
    return total


def to_all(ref, parts):
    value = jnp.concatenate(parts, axis=0)
    for i in range(ref.shape[0]):
        ref[i] = value


def store_shifted(ref, start, row, offsets=(0, 1, 2)):
    width, chans = row.shape
    for b in offsets:
        moved = row if b == 1 else pltpu.roll(row, 1 if b == 0 else width - 1, 0)
        ref[start : start + width, b * chans : (b + 1) * chans] = moved.astype(BF16)


class Geometry:
    def __init__(self, scenes, height, width, chans):
        self.s, self.h, self.w, self.c = scenes, height, width, chans
        self.wp = width + SIDE
        self.tall = height + 2 * RIM
        self.near = RIM - 2
        self.near_cols = COLS - 2
        self.cot_tall = height + 2 * self.near
        self.side = (COLS + self.near_cols) * height
        self.corner = -(-(COLS * RIM + self.near_cols * self.near) // 16) * 16


class Place:
    def __init__(self):
        row, col = lax.axis_index("rows"), lax.axis_index("cols")
        nrows, ncols = lax.axis_size("rows"), lax.axis_size("cols")
        self.above = (row > 0).astype(F32)
        self.below = (row < nrows - 1).astype(F32)
        self.right = (col < ncols - 1).astype(F32)
        self.left = (col > 0).astype(F32)
        self.core = row % 2
        self.second = row // 4 % 2
        self.odd_row = row % 2 == 1
        self.odd_col = col % 2 == 1
        self.index = row * ncols + col


def wide(ref, *index):
    return ref[index].astype(F32)


def far_rows(g, place, rb, rb_c, rb_d, s):
    right, left = sides(g, place, rb_c, rb_d, s)
    rows = []
    for k in range(RIM + g.near):
        width = COLS if k < RIM else g.near_cols
        at = COLS * min(k, RIM) + g.near_cols * max(k - RIM, 0)
        rows.append(
            jnp.concatenate([wide(rb, s, k), side_columns(g, right, left, at, width)], axis=0)
        )
    return rows


def pixel_mask(occ, s):
    return occ[s].astype(F32).T


def in_grid(row, r, g, place, edge):
    row = jnp.concatenate([row[: g.w], row[g.w :] * edge], axis=0)
    if r < RIM:
        row = row * place.above
    elif r >= RIM + g.h:
        row = row * place.below
    return row


def edge_mask(place, g):
    where = lax.broadcasted_iota(jnp.int32, (SIDE, g.c), 0)
    return jnp.where(where < SIDE // 2, place.right, place.left)


def sum_rows(value):
    rows, chans = value.shape
    return jnp.sum(value.reshape(rows // 8, 8, chans), axis=0)


def pack_kernel(
    g, features, occ_far, cot, own, c_ref, d_ref, b_ref, bc_ref, bd_ref, given, seen, occ, sems
):
    copies = []
    flags = pltpu.make_async_copy(occ_far, occ, sems.at[2, 0])
    flags.start()
    for s in range(g.s):
        copies.append(
            (
                pltpu.make_async_copy(features.at[s], given.at[s], sems.at[0, s]),
                pltpu.make_async_copy(cot.at[s], seen.at[s], sems.at[1, s]),
            )
        )
        for copy in copies[-1]:
            copy.start()
    odd, odd_row = Place().odd_col, Place().odd_row
    flags.wait()

    for s in range(g.s):
        mask = pixel_mask(occ, s)
        for copy in copies[s]:
            copy.wait()
        rows = []
        for r in range(g.h):
            row = wide(given, s, r) * mask[:, r : r + 1]
            rows.append(row)
            own[s, r] = row.astype(BF16)
        cots = [wide(seen, s, r) for r in range(g.h)]
        ends = []
        for field, count in ((rows, RIM), (cots, g.near)):
            for k in range(count):
                ends.append(jnp.where(odd_row, field[g.h - count + k], field[k]))
                b_ref[s, len(ends) - 1] = ends[-1].astype(BF16)
        spare = jnp.zeros((g.corner - COLS * RIM - g.near_cols * g.near, g.c), F32)
        widths = [COLS] * RIM + [g.near_cols] * g.near
        right = [v[g.w - width :] for v, width in zip(ends, widths, strict=True)]
        left = [v[:width] for v, width in zip(ends, widths, strict=True)]
        right, left = (jnp.concatenate(v + [spare], axis=0) for v in (right, left))
        bc_ref[s] = jnp.where(odd, left, right).astype(BF16)
        bd_ref[s] = jnp.where(odd, right, left).astype(BF16)
        right = jnp.concatenate(
            [v[g.w - COLS :] for v in rows] + [v[g.w - g.near_cols :] for v in cots], axis=0
        )
        left = jnp.concatenate([v[:COLS] for v in rows] + [v[: g.near_cols] for v in cots], axis=0)
        c_ref[s] = jnp.where(odd, left, right).astype(BF16)
        d_ref[s] = jnp.where(odd, right, left).astype(BF16)


def sides(g, place, rc, rd, s):
    c, d = wide(rc, s), wide(rd, s)
    return jnp.where(place.odd_col, d, c), jnp.where(place.odd_col, c, d)


def side_columns(g, right, left, at, width):
    parts = [right[at : at + width], jnp.zeros((SIDE - 2 * width, g.c), F32), left[at : at + width]]
    return jnp.concatenate([part for part in parts if part.shape[0]], axis=0)


def assemble_kernel(g, own, cot, rc, rd, ext, cot_ext, a_ref):
    place = Place()

    odd = place.odd_row
    for s in range(g.s):
        right, left = sides(g, place, rc, rd, s)
        for source, full, at, width, count, first in (
            (own, ext, 0, COLS, RIM, 0),
            (cot, cot_ext, COLS * g.h, g.near_cols, g.near, RIM),
        ):
            rows = []
            for r in range(g.h):
                beyond = side_columns(g, right, left, at + width * r, width)
                rows.append(jnp.concatenate([wide(source, s, r), beyond], axis=0))
                full[s, r] = rows[r].astype(BF16)
            for k in range(count):
                top, bottom = rows[k], rows[g.h - count + k]
                a_ref[s, first + k] = jnp.where(odd, top, bottom).astype(BF16)


def prepare_kernel(w_ref, one_ref, two_ref, buffer, sems):
    chans = one_ref.shape[1]
    taps, size, lanes = buffer.shape
    per = chans // lanes
    copies = [
        pltpu.make_async_copy(w_ref.at[pl.ds(t * size, size)], buffer.at[t], sems.at[t])
        for t in range(taps)
    ]
    for copy in copies:
        copy.start()
    for t in range(taps):
        copies[t].wait()
        for k, out in enumerate((one_ref, two_ref)):
            parts = [buffer[t, pl.ds(2 * half + k, chans, stride=2 * per), :] for half in range(per)]
            out[t * chans : (t + 1) * chans, :] = jnp.concatenate(parts, axis=1).astype(BF16)


def place_shifted(ref, row_index, row):
    store_shifted(ref, row_index * row.shape[0], row)


def window_rows(g, x_ref, first, count):
    size = count * g.wp
    return jnp.concatenate(
        [x_ref[(first + a) * g.wp : (first + a) * g.wp + size, :] for a in range(3)], axis=1
    )


def own_conv_kernel(g, ext, w, z_ref, st_ref, x_ref):
    count = g.h - 2
    s1 = jnp.zeros((8, g.c), F32)
    s2 = jnp.zeros((8, g.c), F32)
    for s in range(g.s):
        for r in range(g.h):
            place_shifted(x_ref, s * (g.h + 2) + 1 + r, wide(ext, s, r))
        half = count // 2
        for first in range(0, count, half):
            acc = dot(window_rows(g, x_ref, s * (g.h + 2) + 1 + first, half), w[...])
            at = (s * (g.tall - 2) + RIM + first) * g.wp
            z_ref[at : at + half * g.wp, :] = acc
            for i in range(half):
                v = acc[i * g.wp : i * g.wp + g.w]
                s1 = s1 + sum_rows(v)
                s2 = s2 + sum_rows(v * v)
    st_ref[0:8] = s1
    st_ref[8:16] = s2


def rim_conv_kernel(
    g, ext, ra, rb, rb_c, rb_d, w, st_in, z_in, x_in, z_ref, st_ref, x_own, cot_ref, x_ref
):
    del z_in, x_in
    place = Place()
    odd = place.odd_row
    s1, s2 = st_in[0:8], st_in[8:16]
    span = RIM + 2
    for s in range(g.s):
        far = far_rows(g, place, rb, rb_c, rb_d, s)
        near = [wide(ra, s, k) for k in range(RIM + g.near)]
        for side in range(2):
            base = span * (2 * s + side)
            beyond = [
                jnp.where(odd, b, a) if side else jnp.where(odd, a, b)
                for a, b in zip(near, far, strict=True)
            ]
            for k in range(RIM):
                place_shifted(x_ref, base + 2 * side + k, beyond[k])
            next_row = beyond[0 if side else RIM - 1]
            place_shifted(x_own, s * (g.h + 2) + (g.h + 1) * side, next_row)
            cot_ref[s, side] = beyond[RIM].astype(BF16)
            source = (s * (g.h + 2) + 1 + (g.h - 2) * side) * g.wp
            target = (base + RIM * (1 - side)) * g.wp
            x_ref[target : target + 2 * g.wp, :] = x_own[source : source + 2 * g.wp, :]
            acc = dot(window_rows(g, x_ref, base, RIM), w[...])
            at = (s * (g.tall - 2) + (g.h + RIM - 2) * side) * g.wp
            z_ref[at : at + RIM * g.wp, :] = acc
            i = 0 if side else RIM - 1
            v = acc[i * g.wp : i * g.wp + g.w]
            s1 = s1 + sum_rows(v)
            s2 = s2 + sum_rows(v * v)
    to_all(st_ref, [jnp.sum(s1, 0, keepdims=True), jnp.sum(s2, 0, keepdims=True)])


def typical_hidden(params):
    scale, shift = params[0:1], params[1:2]
    return 0.5 * (shift + jnp.sqrt(shift * shift + 0.64 * scale * scale))


def stats_of(total, count):
    mean = total[0:1] / count
    var = total[1:2] / count - mean * mean
    return mean, lax.rsqrt(var + 1e-05)


def second_conv_kernel(g, chunk, count, z1, st, params, w, cot, h_ref, z_ref, st_ref, own_ref):
    rows_in, rows_out = g.tall - 2, g.tall - 4
    place = Place()
    mean, rstd = stats_of(total_of(st), count)
    scale = params[0:1] * rstd
    shift = params[1:2] - mean * scale
    edge = edge_mask(place, g)
    sums = [jnp.zeros((8, g.c), F32) for _ in range(4)]
    for s in range(g.s):
        for r in range(rows_in):
            start = (s * rows_in + r) * g.wp
            row = jnp.maximum(z1[start : start + g.wp, :] * scale + shift, 0.0)
            store_shifted(h_ref, start, in_grid(row, r + 1, g, place, edge))
        for r in range(0, rows_out, chunk):
            base = (s * rows_in + r) * g.wp
            size = chunk * g.wp
            lhs = jnp.concatenate(
                [h_ref[base + a * g.wp : base + a * g.wp + size, :] for a in range(3)], axis=1
            )
            acc = dot(lhs, w[...])
            z_ref[(s * rows_out + r) * g.wp : (s * rows_out + r) * g.wp + size, :] = acc
            for i in range(chunk):
                if RIM <= r + i + 2 < RIM + g.h:
                    v = acc[i * g.wp : i * g.wp + g.w]
                    dn = wide(cot, s, r + i + 2 - RIM)[: g.w]
                    for k, term in enumerate((v, v * v, dn, dn * v)):
                        sums[k] = sums[k] + sum_rows(term)
    own = [jnp.sum(v, 0, keepdims=True) for v in sums]
    own_ref[0:4] = jnp.concatenate(own, axis=0)
    to_all(st_ref, own)


def own_transposed(g, source, first, s, dt_ref):
    span = g.h * g.wp
    block = source[first : first + span, :]
    inside = lax.broadcasted_iota(jnp.int32, (span, 1), 0) % g.wp < g.w
    dt_ref[:, s * span : (s + 1) * span] = jnp.where(inside, block, jnp.zeros_like(block)).T


def kernel_gradient(g, core, field, rows_field, first_row, dt_ref, keep, send, first, prepare, less):
    chans, half = g.c, g.c // 2
    span = g.h * g.wp
    mine = pl.ds(pl.multiple_of(core * half, half), half)
    other = pl.ds(pl.multiple_of((1 - core) * half, half), half)
    totals = [None] * 3
    cut = g.s // 2
    groups = (range(cut), range(cut, g.s))
    for s in groups[0]:
        prepare(s)
    for group in groups:
        lanes = slice(group[0] * span, (group[-1] + 1) * span)
        lhs = jnp.concatenate([dt_ref[mine, lanes], dt_ref[other, lanes]], axis=0)
        for a in range(3):
            starts = [(s * rows_field + first_row + a) * g.wp for s in group]
            acc = dot(lhs, jnp.concatenate([field[at : at + span, :] for at in starts], axis=0))
            if group[0] == 0 and a < len(groups[1]):
                prepare(groups[1][a])
            if group[0] == 0:
                for b in range(3):
                    first[a * 3 + b] = acc[:, b * chans : (b + 1) * chans]
                continue
            for b in range(3):
                rows = slice((a * 3 + b) * chans, (a * 3 + b + 1) * chans)
                part = acc[:, b * chans : (b + 1) * chans] + first[a * 3 + b]
                keep[rows, :] = (part[0:half] - less(mine)).T
                send[rows, :] = (part[half:] - less(other)).T.astype(BF16)


def second_gradient_kernel(
    g, count, z2, st, own, params, cot, cot_next, h, d_ref, keep, send, dt_ref, sums, first
):
    place = Place()
    rows = g.cot_tall
    total = total_of(st)
    mean, rstd = stats_of(total, count)
    sum_dn = total[2:3]
    sum_dx = rstd * (total[3:4] - mean * sum_dn)
    k0 = params[2:3] * rstd
    k1 = k0 * (sum_dn / count)
    k2 = k0 * rstd * (sum_dx / count)
    edge = edge_mask(place, g)
    def prepare(s):
        for i in range(rows):
            rim = not g.near <= i < g.near + g.h
            dn = wide(cot_next, s, 0 if i < g.near else 1) if rim else wide(cot, s, i - g.near)
            start = (s * rows + i) * g.wp
            d = k0 * dn - k1 - (z2[start : start + g.wp, :] - mean) * k2
            d = in_grid(d, i + RIM - g.near, g, place, edge)
            d_ref[start : start + g.wp, :] = d.astype(BF16)
        own_transposed(g, d_ref, (s * rows + g.near) * g.wp, s, dt_ref)
    pixels = float(g.s * g.h * g.w)
    tile_sum = k0 * own[2:3] - pixels * k1 - k2 * (own[0:1] - pixels * mean)
    sums[...] = jnp.broadcast_to(tile_sum, (sums.shape[1], g.c)).T
    typical = typical_hidden(params)

    def less(channels):
        column = sums[channels, :]
        return jnp.concatenate([column] * (g.c // column.shape[1]), axis=1) * typical

    kernel_gradient(g, place.core, h, g.tall - 2, RIM - 2, dt_ref, keep, send, first, prepare, less)


def transposed_conv(g, d_ref, w, s, rows_in, r, chunk):
    acc = None
    size = chunk * g.wp
    for a in range(3):
        start = (s * rows_in + r + a) * g.wp
        for b in range(3):
            tap = (2 - a) * 3 + (2 - b)
            term = dot_nt(
                d_ref[start : start + size, b * g.c : (b + 1) * g.c],
                w[tap * g.c : (tap + 1) * g.c, :],
            )
            acc = term if acc is None else acc + term
    return acc


def hidden_gradient_kernel(
    g, chunk, count, scenes, d, w, z1, z2, st, st2, params, ext, *refs
):
    *before, dn_ref, st_ref, out_ref, d_ref = refs
    mean2, rstd2 = stats_of(total_of(st2), count)
    scale2 = params[2:3] * rstd2
    shift2 = params[3:4] - mean2 * scale2
    rows_in, rows_out, z_rows = g.tall - 4, g.tall - 6, g.tall - 2
    mean, rstd = stats_of(total_of(st), count)
    scale = params[0:1] * rstd
    shift = params[1:2] - mean * scale
    s0 = before[1][0:8] if before else jnp.zeros((8, g.c), F32)
    s1 = before[1][8:16] if before else jnp.zeros((8, g.c), F32)
    for s in scenes:
        for i in range(rows_in):
            at = (s * rows_in + i) * g.wp
            store_shifted(d_ref, at, wide(d, slice(at, at + g.wp)))
        for r in range(g.h):
            at = (s * rows_in + r + g.near) * g.wp
            normed = z2[at : at + g.w, :] * scale2 + shift2
            out_ref[s, r] = (wide(ext, s, r)[: g.w] + normed).astype(BF16)
        for r in range(0, rows_out, chunk):
            acc = transposed_conv(g, d_ref, w, s, rows_in, r, chunk)
            at = (s * z_rows + r + 2) * g.wp
            z = z1[at : at + chunk * g.wp, :]
            dn = jnp.where(z * scale + shift > 0, acc, 0.0)
            dn_ref[(s * rows_out + r) * g.wp : (s * rows_out + r + chunk) * g.wp, :] = dn
            for i in range(chunk):
                if RIM <= r + i + 3 < RIM + g.h:
                    v = dn[i * g.wp : i * g.wp + g.w]
                    s0 = s0 + sum_rows(v)
                    s1 = s1 + sum_rows(v * (z[i * g.wp : i * g.wp + g.w] - mean))
    if not before:
        st_ref[0:8] = s0
        st_ref[8:16] = s1
    else:
        to_all(st_ref, [jnp.sum(s0, 0, keepdims=True), jnp.sum(s1, 0, keepdims=True) * rstd])


def half_gradient(g, which, field, rows_field, first_row, dt_ref, out_ref, sums, prepare=None):
    chans, half = g.c, g.c // 2
    span = g.h * g.wp
    channels = pl.ds(pl.multiple_of(which * half, half), half)
    cut = g.s // 2
    groups = range(cut), range(cut, g.s)
    if prepare is not None:
        for s in groups[0]:
            prepare(s)
    for group in groups:
        lhs = dt_ref[channels, group[0] * span : (group[-1] + 1) * span]
        for a in range(3):
            starts = [(s * rows_field + first_row + a) * g.wp for s in group]
            acc = dot(lhs, jnp.concatenate([field[at : at + span, :] for at in starts], axis=0))
            if group[0] == 0 and prepare is not None and a < len(groups[1]):
                prepare(groups[1][a])
            for b in range(3):
                part = acc[:, b * chans : (b + 1) * chans]
                if group[0] == 0:
                    sums[a * 3 + b] = part
                else:
                    rows = slice((a * 3 + b) * chans, (a * 3 + b + 1) * chans)
                    out_ref[rows, :] = (sums[a * 3 + b] + part).T.astype(out_ref.dtype)


def first_gradient_kernel(
    g, count, dn, z, st, st3, params, x, e_ref, a_ref, b_ref, send, dt_ref, first
):
    place = Place()
    mean, rstd = stats_of(total_of(st), count)
    total = total_of(st3)
    k0 = params[0:1] * rstd
    k1 = k0 * (total[0:1] / count)
    k2 = k0 * rstd * (total[1:2] / count)
    edge = edge_mask(place, g)

    def prepare(s):
        for i in range(g.h):
            at = (s * g.h + i) * g.wp
            z_at = (s * (g.tall - 2) + i + RIM - 1) * g.wp
            d = k0 * dn[at : at + g.wp, :] - k1 - (z[z_at : z_at + g.wp, :] - mean) * k2
            d = in_grid(d, i + RIM, g, place, edge)
            e_ref[at : at + g.wp, :] = d.astype(BF16)
            if i == 0:
                top = d
        a_ref[s, 0] = jnp.where(place.odd_row, top, d).astype(BF16)
        b_ref[s, 0] = jnp.where(place.odd_row, d, top).astype(BF16)
        own_transposed(g, e_ref, s * g.h * g.wp, s, dt_ref)
    half_gradient(g, 1 - place.core, x, g.h + 2, 0, dt_ref, send, first, prepare)


def first_own_kernel(g, x, dt_ref, keep, first):
    half_gradient(g, Place().core, x, g.h + 2, 0, dt_ref, keep, first)


def input_gradient_kernel(
    g, chunk, e, ra, rb, w_far, cot_far, occ, out_ref, w, cot, e_ref, sems
):
    rows_in = g.h + 2
    place = Place()
    copies = [
        pltpu.make_async_copy(w_far, w, sems.at[0]),
        pltpu.make_async_copy(cot_far, cot, sems.at[1]),
    ]
    for copy in copies:
        copy.start()
    for copy in copies:
        copy.wait()
    for s in range(g.s):
        a, b = wide(ra, s, 0), wide(rb, s, 0)
        rows = [jnp.where(place.odd_row, a, b)]
        for r in range(g.h):
            at = (s * g.h + r) * g.wp
            rows.append(wide(e, slice(at, at + g.wp)))
        rows.append(jnp.where(place.odd_row, b, a))
        for i in range(rows_in):
            place_shifted(e_ref, s * rows_in + i, rows[i])
        mask = pixel_mask(occ, s)
        for r in range(0, g.h, chunk):
            acc = transposed_conv(g, e_ref, w, s, rows_in, r, chunk)
            for i in range(chunk):
                v = acc[i * g.wp : i * g.wp + g.w]
                out_ref[s, r + i] = (wide(cot, s, r + i) + v) * mask[:, r + i : r + i + 1]


def pair_total(keep, got, t):
    chans = 2 * keep.shape[1]
    rows = slice(t * chans, (t + 1) * chans)
    return keep[rows, :] + wide(got, rows)


def pair_sum_kernel(lane, keep, got, *refs):
    *_, out_far, buffer, sems = refs
    half = buffer.shape[1]
    chans = 2 * half
    taps = buffer.shape[0] // chans
    copies = []
    for t in range(taps):
        rows = pl.ds(t * chans, chans)
        buffer[rows, :] = pair_total(keep, got, t).astype(BF16)
        copies.append(
            pltpu.make_async_copy(buffer.at[rows], out_far.at[rows, pl.ds(lane, half)], sems.at[t])
        )
        copies[-1].start()
    for copy in copies:
        copy.wait()


def half_rows(share):
    return -(-(share // 2) // 8) * 8


def split_kernel(keep, got, kept_ref, sent_ref, buffer):
    half = keep.shape[1]
    chans = 2 * half
    taps = keep.shape[0] // chans
    devices, rows, _ = kept_ref.shape
    share = taps * chans // devices
    for t in range(taps):
        buffer[t * chans : (t + 1) * chans, :] = pair_total(keep, got, t)
    second = Place().second
    for i in range(devices):
        mine = pl.multiple_of(i * share + (share - rows) * second, 8)
        other = pl.multiple_of(i * share + (share - rows) * (1 - second), 8)
        kept_ref[i] = buffer[pl.ds(mine, rows), :]
        sent_ref[i] = buffer[pl.ds(other, rows), :].astype(BF16)


def join_kernel(kept, came, out_ref):
    for i in range(kept.shape[0]):
        out_ref[i] = kept[i] + wide(came, i)


def message_kernel(keep, got, kept, out_far, out_ref, sems):
    devices = kept.shape[0]
    share = keep.shape[0] // devices
    copies = []
    count = sems.shape[0]
    for part in range(count):
        mine = pl.ds(part * devices // count, devices // count)
        for i in range(part * devices // count, (part + 1) * devices // count):
            rows = slice(i * share, (i + 1) * share)
            first = keep[rows, :] + wide(got, rows)
            out_ref[i] = jnp.concatenate([first, kept[i]], axis=0).astype(BF16)
        copies.append(pltpu.make_async_copy(out_ref.at[mine], out_far.at[mine], sems.at[part]))
        copies[-1].start()
    for copy in copies:
        copy.wait()


def adamw(weight, grad, first, second, rate):
    first_new = 0.9 * first + 0.1 * grad
    second_new = 0.999 * second + 0.001 * grad * grad
    first_hat = first_new / (1.0 - 0.9**STEP)
    second_hat = second_new / (1.0 - 0.999**STEP)
    weight_new = weight - rate * (first_hat / (jnp.sqrt(second_hat) + 1e-08) + 0.01 * weight)
    return (weight_new, first_new, second_new)


def update_kernel(
    count, parts, w, first_m, second_m, st2, st3, params, n_first, n_second,
    grad_out, w_out, first_out, second_out, n_grad, n_out, n_first_out, n_second_out
):
    devices, ncols = parts.shape[0], lax.axis_size("cols")
    share = w.shape[0] // 4
    total2, total3 = total_of(st2), total_of(st3)
    mean, rstd = stats_of(total2, count)
    sum_dn = total2[2:3]
    grads = jnp.concatenate(
        [total3[1:2], total3[0:1], rstd * (total2[3:4] - mean * sum_dn), sum_dn], axis=0
    )
    n_grad[...] = grads
    n_out[...], n_first_out[...], n_second_out[...] = adamw(
        params[...], grads, n_first[...], n_second[...], 0.75
    )
    def over(chosen, rows, lanes):
        total = None
        for source in range(devices):
            if chosen(source // ncols):
                term = wide(parts, source)[rows, lanes]
                total = term if total is None else total + term
        return total

    grads = []
    every = slice(None)
    for half in range(2):
        if parts.shape[2] == 256:
            for k in range(2):
                lanes = slice(k * 128, (k + 1) * 128)
                grads.append((k, half, over(lambda row: row % 2 == half, every, lanes)))
        else:
            rows = half_rows(share)
            first = over(lambda row: row % 2 == half, slice(0, share), every)
            upper = over(lambda row: row % 2 == half and row // 4 % 2 == 0, slice(share, None), every)
            lower = over(lambda row: row % 2 == half and row // 4 % 2 == 1, slice(2 * rows, None), every)
            grads += [(0, half, first), (1, half, jnp.concatenate([upper, lower], axis=0))]
    for k, half, grad in grads:
        at = pl.ds(2 * half + k, share, stride=4)
        new = adamw(w[at, :], grad, first_m[at, :], second_m[at, :], 0.02)
        grad_out[at, :] = grad
        w_out[at, :], first_out[at, :], second_out[at, :] = new


def swapped(block, axis, first):
    count = lax.axis_size(axis)
    pairs = []
    for i in range(first, count - 1, 2):
        pairs += [(i, i + 1), (i + 1, i)]
    return lax.ppermute(block, axis, pairs)


def swapped_both(block, first_row, first_col):
    nrows, ncols = lax.axis_size("rows"), lax.axis_size("cols")

    def partner(i, first, count):
        j = i + 1 if (i - first) % 2 == 0 else i - 1
        return j if min(i, j) >= first and max(i, j) < count else None

    pairs = []
    for i in range(nrows):
        for j in range(ncols):
            to = partner(i, first_row, nrows), partner(j, first_col, ncols)
            if None not in to:
                pairs.append((i * ncols + j, to[0] * ncols + to[1]))
    return lax.ppermute(block, BOTH, pairs)


def to_chunks(flat):
    return flat.reshape(2, -1, 128).transpose(1, 0, 2).reshape(-1, 128)


def from_chunks(rows):
    return rows.reshape(-1, 2, 128).transpose(1, 0, 2).reshape(2, -1)


def exchange(parts):
    return lax.all_to_all(parts, BOTH, 0, 0, tiled=True)


def body(
    features,
    occupancy,
    cotangent,
    conv_weights,
    conv_first,
    conv_second,
    norm_scale_bias,
    norm_first,
    norm_second,
):
    scenes, height, width, chans = features.shape
    g = Geometry(scenes, height, width, chans)
    wp = g.wp
    devices = lax.axis_size("rows") * lax.axis_size("cols")
    count = float(scenes * height * width * devices)
    taps = 9 * chans
    n0, n1, n2, n3 = (scenes * wp * (g.tall - 2 * i) for i in range(4))
    own_pixels = scenes * height * wp
    dma = pltpu.SemaphoreType.DMA

    def conv_flops(n):
        return 2 * n * taps * chans

    side = shape_of((scenes, g.side, chans), BF16)
    corner = shape_of((scenes, g.corner, chans), BF16)
    own, c, d, b, bc, bd = kernel_call(
        functools.partial(pack_kernel, g),
        [
            shape_of(features.shape, BF16),
            side,
            side,
            shape_of((scenes, RIM + g.near, width, chans), BF16),
            corner,
            corner,
        ],
        1e8,
        far=(0, 1, 2),
        scratch=[
            pltpu.VMEM(features.shape, BF16),
            pltpu.VMEM(features.shape, BF16),
            pltpu.VMEM(occupancy.shape, jnp.int32),
            dma((3, scenes)),
        ],
    )(features, occupancy, cotangent)
    rb = swapped(b, "rows", 1)
    rc, rd = swapped(c, "cols", 0), swapped(d, "cols", 1)
    rb_c, rb_d = swapped_both(bc, 1, 0), swapped_both(bd, 1, 1)
    chunked = to_chunks(conv_weights)
    share = conv_first.shape[1]
    chunk_shape = shape_of((share // 64, 128), F32)
    weights = (taps, chans)
    w1, w2 = kernel_call(
        prepare_kernel,
        [held(weights, BF16)] * 2,
        0,
        size=1024,
        far=(0,),
        scratch=[pltpu.VMEM((9, chunked.shape[0] // 9, 128), F32), dma((9,))],
    )(chunked)

    def wide_rows(rows):
        return shape_of((scenes, rows, wp, chans), BF16)

    ext, cot_ext, a = kernel_call(
        functools.partial(assemble_kernel, g),
        [wide_rows(n) for n in (height, height, RIM + g.near)],
        0,
        size=1024,
    )(own, cotangent, rc, rd)
    rows_x = scenes * (height + 2) * wp
    x_shape = held((rows_x, 3 * chans), BF16)
    z1, st, x = kernel_call(
        functools.partial(own_conv_kernel, g),
        [held((n1, chans), F32), held((16, chans), F32), x_shape],
        0,
        size=1024,
    )(ext, w1)
    a, rb, rb_c, rb_d, w1 = lax.optimization_barrier((a, rb, rb_c, rb_d, w1))
    ra = swapped(a, "rows", 0)
    z1, st, x, cot_next = kernel_call(
        functools.partial(rim_conv_kernel, g),
        [held((n1, chans), F32), shape_of((devices, 2, chans), F32), x_shape, wide_rows(2)],
        0,
        size=1024,
        scratch=[pltpu.VMEM((scenes * 2 * (RIM + 2) * wp, 3 * chans), BF16)],
        alias={7: 0, 8: 2},
    )(ext, ra, rb, rb_c, rb_d, w1, st, z1, x)
    st1 = exchange(st)
    h, z2, st, own_sums = kernel_call(
        functools.partial(second_conv_kernel, g, 5, count),
        [
            held((n1, 3 * chans), BF16),
            held((n2, chans), F32),
            shape_of((devices, 4, chans), F32),
            held((8, chans), F32),
        ],
        conv_flops(n2),
    )(z1, st1, norm_scale_bias, w2, cot_ext)
    st2 = exchange(st)
    grad_shape = held((taps, chans // 2), F32)
    d, keep2, send2 = kernel_call(
        functools.partial(second_gradient_kernel, g, count),
        [held((n2, chans), BF16), grad_shape, held(grad_shape.shape, BF16)],
        conv_flops(own_pixels),
        scratch=[
            pltpu.VMEM((chans, own_pixels), BF16),
            pltpu.VMEM((chans, 128), F32),
            pltpu.VMEM((9, chans, chans), F32),
        ],
    )(z2, st2, own_sums, norm_scale_bias, cot_ext, cot_next, h)
    got2 = swapped(send2, "rows", 0)
    nrows = lax.axis_size("rows")
    cut_again = nrows % 8 == 0 and taps // devices % 8 == 0
    hidden_shape, output_shape = held((n3, chans), F32), held(features.shape, BF16)

    def hidden_gradient(scenes, part_shape, *before, **options):
        return kernel_call(
            functools.partial(hidden_gradient_kernel, g, 8, count, scenes),
            [hidden_shape, part_shape, output_shape],
            0,
            size=1024,
            scratch=[pltpu.VMEM((n2, 3 * chans), BF16)],
            **options,
        )(d, w2, z1, z2, st1, st2, norm_scale_bias, ext, *before)

    early = range(3)
    dn1, part, block_out = hidden_gradient(early, held((16, chans), F32))
    got2, part = lax.optimization_barrier((got2, part))
    if cut_again:
        kept_shape = (devices, half_rows(taps // devices), chans // 2)
        kept, sent = kernel_call(
            split_kernel,
            [held(kept_shape, F32), held(kept_shape, BF16)],
            0,
            size=1024,
            scratch=[pltpu.VMEM((taps, chans // 2), F32)],
        )(keep2, got2)
        came = lax.ppermute(sent, "rows", [(i, i ^ 4) for i in range(nrows)])
        kept, part = lax.optimization_barrier((kept, part))
    dn1, st, block_out = hidden_gradient(
        range(len(early), scenes),
        shape_of((devices, 2, chans), F32),
        dn1,
        part,
        block_out,
        alias={8: 0, 10: 2},
    )
    st3 = exchange(st)
    if cut_again:
        kept, st3 = lax.optimization_barrier((kept, st3))
        (kept,) = kernel_call(join_kernel, [held(kept_shape, F32)], 0, size=1024)(kept, came)
        dn1, kept = lax.optimization_barrier((dn1, kept))
    sent_shape = held((taps, chans // 2), BF16)
    part = pltpu.VMEM((9, chans // 2, chans), F32)
    e, a, b, send1, dt = kernel_call(
        functools.partial(first_gradient_kernel, g, count),
        [
            held((n3, chans), BF16),
            wide_rows(1),
            wide_rows(1),
            sent_shape,
            held((chans, own_pixels), BF16),
        ],
        0,
        size=1024,
        scratch=[part],
    )(dn1, z1, st1, st3, norm_scale_bias, x)
    (keep1,) = kernel_call(
        functools.partial(first_own_kernel, g), [held((taps, chans // 2), F32)], 0, size=1024, scratch=[part]
    )(x, dt)
    got1 = swapped(send1, "rows", 0)
    share_rows = taps // devices
    if cut_again:
        rows = share_rows + kept.shape[1]
        (parts,) = kernel_call(
            message_kernel,
            [stored((devices, rows, chans // 2), BF16)],
            1e9,
            far_out=(0,),
            scratch=[pltpu.VMEM((devices, rows, chans // 2), BF16), dma((4,))],
        )(keep1, got1, kept)
    else:

        def add_pair(lane, *operands, **options):
            return kernel_call(
                functools.partial(pair_sum_kernel, lane),
                [stored((taps, chans), BF16)],
                1e9,
                far_out=(0,),
                scratch=[pltpu.VMEM((taps, chans // 2), BF16), dma((9,))],
                **options,
            )(*operands)

        (parts,) = add_pair(chans // 2, keep2, got2)
        (parts,) = add_pair(0, keep1, got1, parts, far=(2,), alias={2: 0})
        parts = parts.reshape(devices, share_rows, chans)
    parts, chunked = lax.optimization_barrier((parts, chunked))
    parts = exchange(parts)
    ra, rb = swapped(a, "rows", 0), swapped(b, "rows", 1)
    (grad_input,) = kernel_call(
        functools.partial(input_gradient_kernel, g, 8),
        [shape_of(features.shape, F32)],
        conv_flops(own_pixels),
        far=(3, 4),
        scratch=[
            pltpu.VMEM(weights, BF16),
            pltpu.VMEM(features.shape, BF16),
            pltpu.VMEM((rows_x, 3 * chans), BF16),
            dma((2,)),
        ],
    )(e, ra, rb, w1, cotangent, occupancy)
    own_rows = share // 64
    first_row = (lax.axis_index("rows") * lax.axis_size("cols") + lax.axis_index("cols")) * own_rows
    own_weights = lax.dynamic_slice_in_dim(chunked, first_row, own_rows, 0)

    norm_shape = shape_of(norm_first.shape, F32)
    updated = kernel_call(
        functools.partial(update_kernel, count),
        [chunk_shape] * 4 + [norm_shape] * 4,
        1e8,
    )(
        parts, own_weights, to_chunks(conv_first), to_chunks(conv_second), st2, st3,
        norm_scale_bias, norm_first, norm_second,
    )
    return (block_out, grad_input, *map(from_chunks, updated[:4]), *updated[4:])


def solution(mesh):
    tile = P(None, "rows", "cols", None)
    share = P(None, ("rows", "cols"))
    return jax.shard_map(
        body,
        mesh=mesh,
        in_specs=(tile, P(None, "rows", "cols"), tile, P(), share, share, P(), P(), P()),
        out_specs=(tile, tile, share, share, share, share, P(), P(), P(), P()),
        check_vma=False,
    )
```

```python
import functools
import math

import jax
import jax.numpy as jnp
from jax import lax
from jax.experimental import pallas as pl
from jax.experimental.pallas import tpu as pltpu
from jax.sharding import PartitionSpec as P

STEP = 5
BOTH = ("rows", "cols")
RIM = 3
COLS = 4
SIDE = 2 * COLS
F32, BF16 = jnp.float32, jnp.bfloat16


def shape_of(shape, dtype):
    return jax.ShapeDtypeStruct(shape, dtype)


def held(shape, dtype):
    return pltpu.VMEM(shape, dtype)


def stored(shape, dtype):
    return pltpu.HBM(shape, dtype)


def kernel_call(body, out_shape, flops, far=(), far_out=(), scratch=(), limit=16, alias=None, size=4 << 20):
    def call(*operands):
        operands = [
            pltpu.with_memory_space_constraint(v, pltpu.HBM if i in far else pltpu.VMEM)
            for i, v in enumerate(operands)
        ]
        specs = [
            pl.BlockSpec(memory_space=pltpu.HBM if i in far else pltpu.VMEM)
            for i in range(len(operands))
        ]
        return pl.pallas_call(
            body,
            out_shape=out_shape,
            in_specs=specs,
            out_specs=[
                pl.BlockSpec(memory_space=pltpu.HBM if i in far_out else pltpu.VMEM)
                for i in range(len(out_shape))
            ],
            scratch_shapes=list(scratch),
            input_output_aliases=alias or {},
            compiler_params=pltpu.CompilerParams(vmem_limit_bytes=limit << 20),
            cost_estimate=pl.CostEstimate(
                flops=int(flops), bytes_accessed=size, transcendentals=0
            ),
        )(*operands)

    return call


def dot(a, b):
    return jnp.dot(a, b, preferred_element_type=F32)


def dot_nt(a, b):
    return lax.dot_general(a, b, (((1,), (1,)), ((), ())), preferred_element_type=F32)


def total_of(ref):
    count = ref.shape[0]
    total = ref[0]
    for i in range(1, count):
        total = total + ref[i]
    return total


def to_all(ref, parts):
    value = jnp.concatenate(parts, axis=0)
    for i in range(ref.shape[0]):
        ref[i] = value


def store_shifted(ref, start, row, offsets=(0, 1, 2)):
    width, chans = row.shape
    for b in offsets:
        moved = row if b == 1 else pltpu.roll(row, 1 if b == 0 else width - 1, 0)
        ref[start : start + width, b * chans : (b + 1) * chans] = moved.astype(BF16)


class Geometry:
    def __init__(self, scenes, height, width, chans):
        self.s, self.h, self.w, self.c = scenes, height, width, chans
        self.wp = width + SIDE
        self.tall = height + 2 * RIM
        self.near = RIM - 2
        self.near_cols = COLS - 2
        self.cot_tall = height + 2 * self.near
        self.side = (COLS + self.near_cols) * height
        self.corner = -(-(COLS * RIM + self.near_cols * self.near) // 16) * 16


class Place:
    def __init__(self):
        row, col = lax.axis_index("rows"), lax.axis_index("cols")
        nrows, ncols = lax.axis_size("rows"), lax.axis_size("cols")
        self.above = (row > 0).astype(F32)
        self.below = (row < nrows - 1).astype(F32)
        self.right = (col < ncols - 1).astype(F32)
        self.left = (col > 0).astype(F32)
        self.core = row % 2
        self.second, self.third = row // 4 % 2, row // 2 % 2
        self.odd_row = row % 2 == 1
        self.odd_col = col % 2 == 1
        self.index = row * ncols + col


def wide(ref, *index):
    return ref[index].astype(F32)


def far_rows(g, place, rb, rb_c, rb_d, s):
    right, left = sides(g, place, rb_c, rb_d, s)
    rows = []
    for k in range(RIM + g.near):
        width = COLS if k < RIM else g.near_cols
        at = COLS * min(k, RIM) + g.near_cols * max(k - RIM, 0)
        rows.append(
            jnp.concatenate([wide(rb, s, k), side_columns(g, right, left, at, width)], axis=0)
        )
    return rows


def pixel_mask(occ, s):
    return occ[s].astype(F32).T


def in_grid(row, r, g, place, edge):
    row = jnp.concatenate([row[: g.w], row[g.w :] * edge], axis=0)
    if r < RIM:
        row = row * place.above
    elif r >= RIM + g.h:
        row = row * place.below
    return row


def edge_mask(place, g):
    where = lax.broadcasted_iota(jnp.int32, (SIDE, g.c), 0)
    return jnp.where(where < SIDE // 2, place.right, place.left)


def sum_rows(value):
    rows, chans = value.shape
    return jnp.sum(value.reshape(rows // 8, 8, chans), axis=0)


def pack_kernel(
    g, features, occ_far, cot, own, c_ref, d_ref, b_ref, bc_ref, bd_ref, given, seen, occ, sems
):
    copies = []
    flags = pltpu.make_async_copy(occ_far, occ, sems.at[2, 0])
    flags.start()
    for s in range(g.s):
        copies.append(
            (
                pltpu.make_async_copy(features.at[s], given.at[s], sems.at[0, s]),
                pltpu.make_async_copy(cot.at[s], seen.at[s], sems.at[1, s]),
            )
        )
        for copy in copies[-1]:
            copy.start()
    odd, odd_row = Place().odd_col, Place().odd_row
    flags.wait()

    for s in range(g.s):
        mask = pixel_mask(occ, s)
        for copy in copies[s]:
            copy.wait()
        rows = []
        for r in range(g.h):
            row = wide(given, s, r) * mask[:, r : r + 1]
            rows.append(row)
            own[s, r] = row.astype(BF16)
        cots = [wide(seen, s, r) for r in range(g.h)]
        ends = []
        for field, count in ((rows, RIM), (cots, g.near)):
            for k in range(count):
                ends.append(jnp.where(odd_row, field[g.h - count + k], field[k]))
                b_ref[s, len(ends) - 1] = ends[-1].astype(BF16)
        spare = jnp.zeros((g.corner - COLS * RIM - g.near_cols * g.near, g.c), F32)
        widths = [COLS] * RIM + [g.near_cols] * g.near
        right = [v[g.w - width :] for v, width in zip(ends, widths, strict=True)]
        left = [v[:width] for v, width in zip(ends, widths, strict=True)]
        right, left = (jnp.concatenate(v + [spare], axis=0) for v in (right, left))
        bc_ref[s] = jnp.where(odd, left, right).astype(BF16)
        bd_ref[s] = jnp.where(odd, right, left).astype(BF16)
        right = jnp.concatenate(
            [v[g.w - COLS :] for v in rows] + [v[g.w - g.near_cols :] for v in cots], axis=0
        )
        left = jnp.concatenate([v[:COLS] for v in rows] + [v[: g.near_cols] for v in cots], axis=0)
        c_ref[s] = jnp.where(odd, left, right).astype(BF16)
        d_ref[s] = jnp.where(odd, right, left).astype(BF16)


def sides(g, place, rc, rd, s):
    c, d = wide(rc, s), wide(rd, s)
    return jnp.where(place.odd_col, d, c), jnp.where(place.odd_col, c, d)


def side_columns(g, right, left, at, width):
    parts = [right[at : at + width], jnp.zeros((SIDE - 2 * width, g.c), F32), left[at : at + width]]
    return jnp.concatenate([part for part in parts if part.shape[0]], axis=0)


def assemble_kernel(g, own, cot, rc, rd, ext, cot_ext, a_ref):
    place = Place()

    odd = place.odd_row
    for s in range(g.s):
        right, left = sides(g, place, rc, rd, s)
        for source, full, at, width, count, first in (
            (own, ext, 0, COLS, RIM, 0),
            (cot, cot_ext, COLS * g.h, g.near_cols, g.near, RIM),
        ):
            rows = []
            for r in range(g.h):
                beyond = side_columns(g, right, left, at + width * r, width)
                rows.append(jnp.concatenate([wide(source, s, r), beyond], axis=0))
                full[s, r] = rows[r].astype(BF16)
            for k in range(count):
                top, bottom = rows[k], rows[g.h - count + k]
                a_ref[s, first + k] = jnp.where(odd, top, bottom).astype(BF16)


def prepare_kernel(w_ref, one_ref, two_ref, buffer, sems):
    chans = one_ref.shape[1]
    taps, size, lanes = buffer.shape
    per = chans // lanes
    copies = [
        pltpu.make_async_copy(w_ref.at[pl.ds(t * size, size)], buffer.at[t], sems.at[t])
        for t in range(taps)
    ]
    for copy in copies:
        copy.start()
    for t in range(taps):
        copies[t].wait()
        for k, out in enumerate((one_ref, two_ref)):
            parts = [buffer[t, pl.ds(2 * half + k, chans, stride=2 * per), :] for half in range(per)]
            out[t * chans : (t + 1) * chans, :] = jnp.concatenate(parts, axis=1).astype(BF16)


def place_shifted(ref, row_index, row):
    store_shifted(ref, row_index * row.shape[0], row)


def window_rows(g, x_ref, first, count):
    size = count * g.wp
    return jnp.concatenate(
        [x_ref[(first + a) * g.wp : (first + a) * g.wp + size, :] for a in range(3)], axis=1
    )


def own_conv_kernel(g, ext, w, z_ref, st_ref, x_ref):
    count = g.h - 2
    s1 = jnp.zeros((8, g.c), F32)
    s2 = jnp.zeros((8, g.c), F32)
    for s in range(g.s):
        for r in range(g.h):
            place_shifted(x_ref, s * (g.h + 2) + 1 + r, wide(ext, s, r))
        half = count // 2
        for first in range(0, count, half):
            acc = dot(window_rows(g, x_ref, s * (g.h + 2) + 1 + first, half), w[...])
            at = (s * (g.tall - 2) + RIM + first) * g.wp
            z_ref[at : at + half * g.wp, :] = acc
            for i in range(half):
                v = acc[i * g.wp : i * g.wp + g.w]
                s1 = s1 + sum_rows(v)
                s2 = s2 + sum_rows(v * v)
    st_ref[0:8] = s1
    st_ref[8:16] = s2


def rim_conv_kernel(
    g, ext, ra, rb, rb_c, rb_d, w, st_in, z_in, x_in, z_ref, st_ref, x_own, cot_ref, x_ref
):
    del z_in, x_in
    place = Place()
    odd = place.odd_row
    s1, s2 = st_in[0:8], st_in[8:16]
    span = RIM + 2
    for s in range(g.s):
        far = far_rows(g, place, rb, rb_c, rb_d, s)
        near = [wide(ra, s, k) for k in range(RIM + g.near)]
        for side in range(2):
            base = span * (2 * s + side)
            beyond = [
                jnp.where(odd, b, a) if side else jnp.where(odd, a, b)
                for a, b in zip(near, far, strict=True)
            ]
            for k in range(RIM):
                place_shifted(x_ref, base + 2 * side + k, beyond[k])
            next_row = beyond[0 if side else RIM - 1]
            place_shifted(x_own, s * (g.h + 2) + (g.h + 1) * side, next_row)
            cot_ref[s, side] = beyond[RIM].astype(BF16)
            source = (s * (g.h + 2) + 1 + (g.h - 2) * side) * g.wp
            target = (base + RIM * (1 - side)) * g.wp
            x_ref[target : target + 2 * g.wp, :] = x_own[source : source + 2 * g.wp, :]
            acc = dot(window_rows(g, x_ref, base, RIM), w[...])
            at = (s * (g.tall - 2) + (g.h + RIM - 2) * side) * g.wp
            z_ref[at : at + RIM * g.wp, :] = acc
            i = 0 if side else RIM - 1
            v = acc[i * g.wp : i * g.wp + g.w]
            s1 = s1 + sum_rows(v)
            s2 = s2 + sum_rows(v * v)
    to_all(st_ref, [jnp.sum(s1, 0, keepdims=True), jnp.sum(s2, 0, keepdims=True)])


def typical_hidden(params):
    scale, shift = params[0:1], params[1:2]
    return 0.5 * (shift + jnp.sqrt(shift * shift + 0.64 * scale * scale))


def stats_of(total, count):
    mean = total[0:1] / count
    var = total[1:2] / count - mean * mean
    return mean, lax.rsqrt(var + 1e-05)


def second_conv_kernel(g, chunk, count, z1, st, params, w, cot, h_ref, z_ref, st_ref, own_ref):
    rows_in, rows_out = g.tall - 2, g.tall - 4
    place = Place()
    mean, rstd = stats_of(total_of(st), count)
    scale = params[0:1] * rstd
    shift = params[1:2] - mean * scale
    edge = edge_mask(place, g)
    sums = [jnp.zeros((8, g.c), F32) for _ in range(4)]
    for s in range(g.s):
        for r in range(rows_in):
            start = (s * rows_in + r) * g.wp
            row = jnp.maximum(z1[start : start + g.wp, :] * scale + shift, 0.0)
            store_shifted(h_ref, start, in_grid(row, r + 1, g, place, edge))
        for r in range(0, rows_out, chunk):
            base = (s * rows_in + r) * g.wp
            size = chunk * g.wp
            lhs = jnp.concatenate(
                [h_ref[base + a * g.wp : base + a * g.wp + size, :] for a in range(3)], axis=1
            )
            acc = dot(lhs, w[...])
            z_ref[(s * rows_out + r) * g.wp : (s * rows_out + r) * g.wp + size, :] = acc
            for i in range(chunk):
                if RIM <= r + i + 2 < RIM + g.h:
                    v = acc[i * g.wp : i * g.wp + g.w]
                    dn = wide(cot, s, r + i + 2 - RIM)[: g.w]
                    for k, term in enumerate((v, v * v, dn, dn * v)):
                        sums[k] = sums[k] + sum_rows(term)
    own = [jnp.sum(v, 0, keepdims=True) for v in sums]
    own_ref[0:4] = jnp.concatenate(own, axis=0)
    to_all(st_ref, own)


def own_transposed(g, source, first, s, dt_ref):
    span = g.h * g.wp
    block = source[first : first + span, :]
    inside = lax.broadcasted_iota(jnp.int32, (span, 1), 0) % g.wp < g.w
    dt_ref[:, s * span : (s + 1) * span] = jnp.where(inside, block, jnp.zeros_like(block)).T


def kernel_gradient(g, core, field, rows_field, first_row, dt_ref, keep, send, first, prepare, less):
    chans, half = g.c, g.c // 2
    span = g.h * g.wp
    mine = pl.ds(pl.multiple_of(core * half, half), half)
    other = pl.ds(pl.multiple_of((1 - core) * half, half), half)
    totals = [None] * 3
    cut = g.s // 2
    groups = (range(cut), range(cut, g.s))
    for s in groups[0]:
        prepare(s)
    for group in groups:
        lanes = slice(group[0] * span, (group[-1] + 1) * span)
        lhs = jnp.concatenate([dt_ref[mine, lanes], dt_ref[other, lanes]], axis=0)
        for a in range(3):
            starts = [(s * rows_field + first_row + a) * g.wp for s in group]
            acc = dot(lhs, jnp.concatenate([field[at : at + span, :] for at in starts], axis=0))
            if group[0] == 0 and a < len(groups[1]):
                prepare(groups[1][a])
            if group[0] == 0:
                for b in range(3):
                    first[a * 3 + b] = acc[:, b * chans : (b + 1) * chans]
                continue
            for b in range(3):
                rows = slice((a * 3 + b) * chans, (a * 3 + b + 1) * chans)
                part = acc[:, b * chans : (b + 1) * chans] + first[a * 3 + b]
                keep[rows, :] = (part[0:half] - less(mine)).T
                send[rows, :] = (part[half:] - less(other)).T.astype(BF16)


def second_gradient_kernel(
    g, count, z2, st, own, params, cot, cot_next, h, d_ref, keep, send, dt_ref, sums, first
):
    place = Place()
    rows = g.cot_tall
    total = total_of(st)
    mean, rstd = stats_of(total, count)
    sum_dn = total[2:3]
    sum_dx = rstd * (total[3:4] - mean * sum_dn)
    k0 = params[2:3] * rstd
    k1 = k0 * (sum_dn / count)
    k2 = k0 * rstd * (sum_dx / count)
    edge = edge_mask(place, g)
    def prepare(s):
        for i in range(rows):
            rim = not g.near <= i < g.near + g.h
            dn = wide(cot_next, s, 0 if i < g.near else 1) if rim else wide(cot, s, i - g.near)
            start = (s * rows + i) * g.wp
            d = k0 * dn - k1 - (z2[start : start + g.wp, :] - mean) * k2
            d = in_grid(d, i + RIM - g.near, g, place, edge)
            d_ref[start : start + g.wp, :] = d.astype(BF16)
        own_transposed(g, d_ref, (s * rows + g.near) * g.wp, s, dt_ref)
    pixels = float(g.s * g.h * g.w)
    tile_sum = k0 * own[2:3] - pixels * k1 - k2 * (own[0:1] - pixels * mean)
    sums[...] = jnp.broadcast_to(tile_sum, (sums.shape[1], g.c)).T
    typical = typical_hidden(params)

    def less(channels):
        column = sums[channels, :]
        return jnp.concatenate([column] * (g.c // column.shape[1]), axis=1) * typical

    kernel_gradient(g, place.core, h, g.tall - 2, RIM - 2, dt_ref, keep, send, first, prepare, less)


def transposed_conv(g, d_ref, w, s, rows_in, r, chunk):
    acc = None
    size = chunk * g.wp
    for a in range(3):
        start = (s * rows_in + r + a) * g.wp
        for b in range(3):
            tap = (2 - a) * 3 + (2 - b)
            term = dot_nt(
                d_ref[start : start + size, b * g.c : (b + 1) * g.c],
                w[tap * g.c : (tap + 1) * g.c, :],
            )
            acc = term if acc is None else acc + term
    return acc


def hidden_gradient_kernel(
    g, chunk, count, scenes, d, w, z1, z2, st, st2, params, ext, *refs
):
    *before, dn_ref, st_ref, out_ref, d_ref = refs
    mean2, rstd2 = stats_of(total_of(st2), count)
    scale2 = params[2:3] * rstd2
    shift2 = params[3:4] - mean2 * scale2
    rows_in, rows_out, z_rows = g.tall - 4, g.tall - 6, g.tall - 2
    mean, rstd = stats_of(total_of(st), count)
    scale = params[0:1] * rstd
    shift = params[1:2] - mean * scale
    s0 = before[1][0:8] if before else jnp.zeros((8, g.c), F32)
    s1 = before[1][8:16] if before else jnp.zeros((8, g.c), F32)
    for s in scenes:
        for i in range(rows_in):
            at = (s * rows_in + i) * g.wp
            store_shifted(d_ref, at, wide(d, slice(at, at + g.wp)))
        for r in range(g.h):
            at = (s * rows_in + r + g.near) * g.wp
            normed = z2[at : at + g.w, :] * scale2 + shift2
            out_ref[s, r] = (wide(ext, s, r)[: g.w] + normed).astype(BF16)
        for r in range(0, rows_out, chunk):
            acc = transposed_conv(g, d_ref, w, s, rows_in, r, chunk)
            at = (s * z_rows + r + 2) * g.wp
            z = z1[at : at + chunk * g.wp, :]
            dn = jnp.where(z * scale + shift > 0, acc, 0.0)
            dn_ref[(s * rows_out + r) * g.wp : (s * rows_out + r + chunk) * g.wp, :] = dn
            for i in range(chunk):
                if RIM <= r + i + 3 < RIM + g.h:
                    v = dn[i * g.wp : i * g.wp + g.w]
                    s0 = s0 + sum_rows(v)
                    s1 = s1 + sum_rows(v * (z[i * g.wp : i * g.wp + g.w] - mean))
    if not before:
        st_ref[0:8] = s0
        st_ref[8:16] = s1
    else:
        to_all(st_ref, [jnp.sum(s0, 0, keepdims=True), jnp.sum(s1, 0, keepdims=True) * rstd])


def put(refs, rows, value):
    if not isinstance(refs, tuple):
        refs = (refs,)
    at = 0
    for ref in refs:
        first, last = max(rows.start, at), min(rows.stop, at + ref.shape[0])
        if first < last:
            part = value[first - rows.start : last - rows.start]
            ref[first - at : last - at, :] = part.astype(ref.dtype)
        at += ref.shape[0]


def half_gradient(g, which, field, rows_field, first_row, dt_ref, out_ref, sums, prepare=None):
    chans, half = g.c, g.c // 2
    span = g.h * g.wp
    channels = pl.ds(pl.multiple_of(which * half, half), half)
    cut = g.s // 2
    groups = range(cut), range(cut, g.s)
    if prepare is not None:
        for s in groups[0]:
            prepare(s)
    for group in groups:
        lhs = dt_ref[channels, group[0] * span : (group[-1] + 1) * span]
        for a in range(3):
            starts = [(s * rows_field + first_row + a) * g.wp for s in group]
            acc = dot(lhs, jnp.concatenate([field[at : at + span, :] for at in starts], axis=0))
            if group[0] == 0 and prepare is not None and a < len(groups[1]):
                prepare(groups[1][a])
            for b in range(3):
                part = acc[:, b * chans : (b + 1) * chans]
                if group[0] == 0:
                    sums[a * 3 + b] = part
                else:
                    rows = slice((a * 3 + b) * chans, (a * 3 + b + 1) * chans)
                    put(out_ref, rows, (sums[a * 3 + b] + part).T)


def first_gradient_kernel(
    g, count, dn, z, st, st3, params, x, e_ref, a_ref, b_ref, *refs
):
    *send, dt_ref, first = refs
    place = Place()
    mean, rstd = stats_of(total_of(st), count)
    total = total_of(st3)
    k0 = params[0:1] * rstd
    k1 = k0 * (total[0:1] / count)
    k2 = k0 * rstd * (total[1:2] / count)
    edge = edge_mask(place, g)

    def prepare(s):
        for i in range(g.h):
            at = (s * g.h + i) * g.wp
            z_at = (s * (g.tall - 2) + i + RIM - 1) * g.wp
            d = k0 * dn[at : at + g.wp, :] - k1 - (z[z_at : z_at + g.wp, :] - mean) * k2
            d = in_grid(d, i + RIM, g, place, edge)
            e_ref[at : at + g.wp, :] = d.astype(BF16)
            if i == 0:
                top = d
        a_ref[s, 0] = jnp.where(place.odd_row, top, d).astype(BF16)
        b_ref[s, 0] = jnp.where(place.odd_row, d, top).astype(BF16)
        own_transposed(g, e_ref, s * g.h * g.wp, s, dt_ref)
    half_gradient(g, 1 - place.core, x, g.h + 2, 0, dt_ref, tuple(send), first, prepare)


def first_own_kernel(g, x, dt_ref, keep, first):
    half_gradient(g, Place().core, x, g.h + 2, 0, dt_ref, keep, first)


def input_gradient_kernel(
    g, chunk, e, ra, rb, w_far, cot_far, occ, out_ref, w, cot, e_ref, sems
):
    rows_in = g.h + 2
    place = Place()
    copies = [
        pltpu.make_async_copy(w_far, w, sems.at[0]),
        pltpu.make_async_copy(cot_far, cot, sems.at[1]),
    ]
    for copy in copies:
        copy.start()
    for copy in copies:
        copy.wait()
    for s in range(g.s):
        a, b = wide(ra, s, 0), wide(rb, s, 0)
        rows = [jnp.where(place.odd_row, a, b)]
        for r in range(g.h):
            at = (s * g.h + r) * g.wp
            rows.append(wide(e, slice(at, at + g.wp)))
        rows.append(jnp.where(place.odd_row, b, a))
        for i in range(rows_in):
            place_shifted(e_ref, s * rows_in + i, rows[i])
        mask = pixel_mask(occ, s)
        for r in range(0, g.h, chunk):
            acc = transposed_conv(g, e_ref, w, s, rows_in, r, chunk)
            for i in range(chunk):
                v = acc[i * g.wp : i * g.wp + g.w]
                out_ref[s, r + i] = (wide(cot, s, r + i) + v) * mask[:, r + i : r + i + 1]


def pair_total(keep, got, t):
    chans = 2 * keep.shape[1]
    rows = slice(t * chans, (t + 1) * chans)
    return keep[rows, :] + wide(got, rows)


def pair_sum_kernel(lane, keep, got, *refs):
    *_, out_far, buffer, sems = refs
    half = buffer.shape[1]
    chans = 2 * half
    taps = buffer.shape[0] // chans
    copies = []
    for t in range(taps):
        rows = pl.ds(t * chans, chans)
        buffer[rows, :] = pair_total(keep, got, t).astype(BF16)
        copies.append(
            pltpu.make_async_copy(buffer.at[rows], out_far.at[rows, pl.ds(lane, half)], sems.at[t])
        )
        copies[-1].start()
    for copy in copies:
        copy.wait()


def half_rows(share):
    return -(-(share // 2) // 8) * 8


def split_kernel(keep, got, kept_ref, sent_ref, buffer):
    half = keep.shape[1]
    chans = 2 * half
    taps = keep.shape[0] // chans
    devices, rows, _ = kept_ref.shape
    share = taps * chans // devices
    for t in range(taps):
        buffer[t * chans : (t + 1) * chans, :] = pair_total(keep, got, t)
    second = Place().second
    for i in range(devices):
        mine = pl.multiple_of(i * share + (share - rows) * second, 8)
        other = pl.multiple_of(i * share + (share - rows) * (1 - second), 8)
        kept_ref[i] = buffer[pl.ds(mine, rows), :]
        sent_ref[i] = buffer[pl.ds(other, rows), :].astype(BF16)


def split_again_kernel(kept, came, kept_ref, sent_ref, buffer):
    devices, rows, _ = kept_ref.shape
    spare = kept.shape[1] - rows
    third = Place().third
    for i in range(devices):
        buffer[i] = kept[i] + wide(came, i)
    for i in range(devices):
        kept_ref[i] = buffer[i, pl.ds(pl.multiple_of(spare * third, 8), rows)]
    for j in range(devices // 2):
        large = buffer[2 * j + 1 - third, pl.ds(pl.multiple_of(spare * (1 - third), 8), rows)]
        small = buffer[2 * j + third, pl.ds(pl.multiple_of(rows * (1 - third), 8), spare)]
        sent_ref[j] = jnp.concatenate([large, small], axis=0).astype(BF16)


def message_kernel(keep, *refs):
    *got, kept, came, out_far, out_ref, sems = refs
    devices = kept.shape[0]
    share = keep.shape[0] // devices
    copies = []
    count = sems.shape[0]
    rows = kept.shape[1]
    spare = came.shape[1] - rows
    third = Place().third
    none = jnp.zeros((rows - spare, kept.shape[2]), F32)
    for part in range(count):
        per = devices // count
        mine = pl.ds(part * per, per)
        for k in range(per):
            i = part * per + k
            first = keep[i * share : (i + 1) * share, :]
            first = first + wide(got[part], slice(k * share, (k + 1) * share))
            others = wide(came, i // 2)
            small = [others[rows:], none] if i % 2 else [none, others[rows:]]
            second = kept[i] + jnp.where(third == i % 2, others[:rows], jnp.concatenate(small, axis=0))
            out_ref[i] = jnp.concatenate([first, second], axis=0).astype(BF16)
        copies.append(pltpu.make_async_copy(out_ref.at[mine], out_far.at[mine], sems.at[part]))
        copies[-1].start()
    for copy in copies:
        copy.wait()


def adamw(weight, grad, first, second, rate):
    first_new = 0.9 * first + 0.1 * grad
    second_new = 0.999 * second + 0.001 * grad * grad
    first_hat = first_new / (1.0 - 0.9**STEP)
    second_hat = second_new / (1.0 - 0.999**STEP)
    weight_new = weight - rate * (first_hat / (jnp.sqrt(second_hat) + 1e-08) + 0.01 * weight)
    return (weight_new, first_new, second_new)


def update_kernel(
    count, parts, w, first_m, second_m, st2, st3, params, n_first, n_second,
    grad_out, w_out, first_out, second_out, n_grad, n_out, n_first_out, n_second_out
):
    devices, ncols = parts.shape[0], lax.axis_size("cols")
    share = w.shape[0] // 4
    total2, total3 = total_of(st2), total_of(st3)
    mean, rstd = stats_of(total2, count)
    sum_dn = total2[2:3]
    grads = jnp.concatenate(
        [total3[1:2], total3[0:1], rstd * (total2[3:4] - mean * sum_dn), sum_dn], axis=0
    )
    n_grad[...] = grads
    n_out[...], n_first_out[...], n_second_out[...] = adamw(
        params[...], grads, n_first[...], n_second[...], 0.75
    )
    def over(chosen, rows, lanes):
        total = None
        for source in range(devices):
            if chosen(source // ncols):
                term = wide(parts, source)[rows, lanes]
                total = term if total is None else total + term
        return total

    grads = []
    every = slice(None)
    for half in range(2):
        if parts.shape[2] == 256:
            for k in range(2):
                lanes = slice(k * 128, (k + 1) * 128)
                grads.append((k, half, over(lambda row: row % 2 == half, every, lanes)))
        else:
            grads.append((0, half, over(lambda row: row % 2 == half, slice(0, share), every)))
            size = half_rows(share)
            last = half_rows(size)
            spare = size - last
            odd = lax.axis_index("cols") % 2 == 1
            blocks = []
            for second in range(2):
                one, two = (
                    over(lambda r, row=half + 4 * second + 2 * third: r % 8 == row, slice(share, None), every)
                    for third in range(2)
                )
                middle = jnp.where(odd, two[: last - spare], one[spare:])
                blocks.append(jnp.concatenate([one[:spare], middle, two[last - spare :]], axis=0))
            blocks[1] = blocks[1][2 * size - share :]
            grads.append((1, half, jnp.concatenate(blocks, axis=0)))
    for k, half, grad in grads:
        at = pl.ds(2 * half + k, share, stride=4)
        new = adamw(w[at, :], grad, first_m[at, :], second_m[at, :], 0.02)
        grad_out[at, :] = grad
        w_out[at, :], first_out[at, :], second_out[at, :] = new


def swapped(block, axis, first):
    count = lax.axis_size(axis)
    pairs = []
    for i in range(first, count - 1, 2):
        pairs += [(i, i + 1), (i + 1, i)]
    return lax.ppermute(block, axis, pairs)


def swapped_both(block, first_row, first_col):
    nrows, ncols = lax.axis_size("rows"), lax.axis_size("cols")

    def partner(i, first, count):
        j = i + 1 if (i - first) % 2 == 0 else i - 1
        return j if min(i, j) >= first and max(i, j) < count else None

    pairs = []
    for i in range(nrows):
        for j in range(ncols):
            to = partner(i, first_row, nrows), partner(j, first_col, ncols)
            if None not in to:
                pairs.append((i * ncols + j, to[0] * ncols + to[1]))
    return lax.ppermute(block, BOTH, pairs)


def to_chunks(flat):
    return flat.reshape(2, -1, 128).transpose(1, 0, 2).reshape(-1, 128)


def from_chunks(rows):
    return rows.reshape(-1, 2, 128).transpose(1, 0, 2).reshape(2, -1)


def exchange(parts):
    return lax.all_to_all(parts, BOTH, 0, 0, tiled=True)


def body(
    features,
    occupancy,
    cotangent,
    conv_weights,
    conv_first,
    conv_second,
    norm_scale_bias,
    norm_first,
    norm_second,
):
    scenes, height, width, chans = features.shape
    g = Geometry(scenes, height, width, chans)
    wp = g.wp
    devices = lax.axis_size("rows") * lax.axis_size("cols")
    count = float(scenes * height * width * devices)
    taps = 9 * chans
    n0, n1, n2, n3 = (scenes * wp * (g.tall - 2 * i) for i in range(4))
    own_pixels = scenes * height * wp
    dma = pltpu.SemaphoreType.DMA

    def conv_flops(n):
        return 2 * n * taps * chans

    side = shape_of((scenes, g.side, chans), BF16)
    corner = shape_of((scenes, g.corner, chans), BF16)
    own, c, d, b, bc, bd = kernel_call(
        functools.partial(pack_kernel, g),
        [
            shape_of(features.shape, BF16),
            side,
            side,
            shape_of((scenes, RIM + g.near, width, chans), BF16),
            corner,
            corner,
        ],
        1e8,
        far=(0, 1, 2),
        scratch=[
            pltpu.VMEM(features.shape, BF16),
            pltpu.VMEM(features.shape, BF16),
            pltpu.VMEM(occupancy.shape, jnp.int32),
            dma((3, scenes)),
        ],
    )(features, occupancy, cotangent)
    rb = swapped(b, "rows", 1)
    rc, rd = swapped(c, "cols", 0), swapped(d, "cols", 1)
    rb_c, rb_d = swapped_both(bc, 1, 0), swapped_both(bd, 1, 1)
    chunked = to_chunks(conv_weights)
    share = conv_first.shape[1]
    chunk_shape = shape_of((share // 64, 128), F32)
    weights = (taps, chans)
    w1, w2 = kernel_call(
        prepare_kernel,
        [held(weights, BF16)] * 2,
        0,
        size=1024,
        far=(0,),
        scratch=[pltpu.VMEM((9, chunked.shape[0] // 9, 128), F32), dma((9,))],
    )(chunked)

    def wide_rows(rows):
        return shape_of((scenes, rows, wp, chans), BF16)

    ext, cot_ext, a = kernel_call(
        functools.partial(assemble_kernel, g),
        [wide_rows(n) for n in (height, height, RIM + g.near)],
        0,
        size=1024,
    )(own, cotangent, rc, rd)
    rows_x = scenes * (height + 2) * wp
    x_shape = held((rows_x, 3 * chans), BF16)
    z1, st, x = kernel_call(
        functools.partial(own_conv_kernel, g),
        [held((n1, chans), F32), held((16, chans), F32), x_shape],
        0,
        size=1024,
    )(ext, w1)
    a, rb, rb_c, rb_d, w1 = lax.optimization_barrier((a, rb, rb_c, rb_d, w1))
    ra = swapped(a, "rows", 0)
    z1, st, x, cot_next = kernel_call(
        functools.partial(rim_conv_kernel, g),
        [held((n1, chans), F32), shape_of((devices, 2, chans), F32), x_shape, wide_rows(2)],
        0,
        size=1024,
        scratch=[pltpu.VMEM((scenes * 2 * (RIM + 2) * wp, 3 * chans), BF16)],
        alias={7: 0, 8: 2},
    )(ext, ra, rb, rb_c, rb_d, w1, st, z1, x)
    st1 = exchange(st)
    h, z2, st, own_sums = kernel_call(
        functools.partial(second_conv_kernel, g, 5, count),
        [
            held((n1, 3 * chans), BF16),
            held((n2, chans), F32),
            shape_of((devices, 4, chans), F32),
            held((8, chans), F32),
        ],
        conv_flops(n2),
    )(z1, st1, norm_scale_bias, w2, cot_ext)
    st2 = exchange(st)
    grad_shape = held((taps, chans // 2), F32)
    d, keep2, send2 = kernel_call(
        functools.partial(second_gradient_kernel, g, count),
        [held((n2, chans), BF16), grad_shape, held(grad_shape.shape, BF16)],
        conv_flops(own_pixels),
        scratch=[
            pltpu.VMEM((chans, own_pixels), BF16),
            pltpu.VMEM((chans, 128), F32),
            pltpu.VMEM((9, chans, chans), F32),
        ],
    )(z2, st2, own_sums, norm_scale_bias, cot_ext, cot_next, h)
    got2 = swapped(send2, "rows", 0)
    nrows = lax.axis_size("rows")
    cut_again = nrows % 8 == 0 and lax.axis_size("cols") % 2 == 0 and taps // devices % 8 == 0
    hidden_shape, output_shape = held((n3, chans), F32), held(features.shape, BF16)

    def hidden_gradient(scenes, part_shape, *before, **options):
        return kernel_call(
            functools.partial(hidden_gradient_kernel, g, 8, count, scenes),
            [hidden_shape, part_shape, output_shape],
            0,
            size=1024,
            scratch=[pltpu.VMEM((n2, 3 * chans), BF16)],
            **options,
        )(d, w2, z1, z2, st1, st2, norm_scale_bias, ext, *before)

    early = range(3)
    dn1, part, block_out = hidden_gradient(early, held((16, chans), F32))
    got2, part = lax.optimization_barrier((got2, part))
    if cut_again:
        kept_shape = (devices, half_rows(taps // devices), chans // 2)
        kept, sent = kernel_call(
            split_kernel,
            [held(kept_shape, F32), held(kept_shape, BF16)],
            0,
            size=1024,
            scratch=[pltpu.VMEM((taps, chans // 2), F32)],
        )(keep2, got2)
        came = lax.ppermute(sent, "rows", [(i, i ^ 4) for i in range(nrows)])
        kept, part = lax.optimization_barrier((kept, part))
    dn1, st, block_out = hidden_gradient(
        range(len(early), scenes),
        shape_of((devices, 2, chans), F32),
        dn1,
        part,
        block_out,
        alias={8: 0, 10: 2},
    )
    st3 = exchange(st)
    if cut_again:
        kept, st3 = lax.optimization_barrier((kept, st3))
        again_shape = (devices, half_rows(kept_shape[1]), chans // 2)
        kept, sent = kernel_call(
            split_again_kernel,
            [held(again_shape, F32), held((devices // 2, *kept_shape[1:]), BF16)],
            0,
            size=1024,
            scratch=[pltpu.VMEM(kept_shape, F32)],
        )(kept, came)
        came = lax.ppermute(sent, "rows", [(i, i ^ 2) for i in range(nrows)])
        dn1, kept = lax.optimization_barrier((dn1, kept))
    cuts = 4 if cut_again else 1
    sent_shape = held((taps // cuts, chans // 2), BF16)
    part = pltpu.VMEM((9, chans // 2, chans), F32)
    e, a, b, *send1, dt = kernel_call(
        functools.partial(first_gradient_kernel, g, count),
        [held((n3, chans), BF16), wide_rows(1), wide_rows(1)]
        + [sent_shape] * cuts
        + [held((chans, own_pixels), BF16)],
        0,
        size=1024,
        scratch=[part],
    )(dn1, z1, st1, st3, norm_scale_bias, x)
    (keep1,) = kernel_call(
        functools.partial(first_own_kernel, g), [held((taps, chans // 2), F32)], 0, size=1024, scratch=[part]
    )(x, dt)
    got1 = [swapped(part, "rows", 0) for part in send1]
    share_rows = taps // devices
    if cut_again:
        rows = share_rows + kept.shape[1]
        (parts,) = kernel_call(
            message_kernel,
            [stored((devices, rows, chans // 2), BF16)],
            1e9,
            far_out=(0,),
            scratch=[pltpu.VMEM((devices, rows, chans // 2), BF16), dma((4,))],
        )(keep1, *got1, kept, came)
    else:

        def add_pair(lane, *operands, **options):
            return kernel_call(
                functools.partial(pair_sum_kernel, lane),
                [stored((taps, chans), BF16)],
                1e9,
                far_out=(0,),
                scratch=[pltpu.VMEM((taps, chans // 2), BF16), dma((9,))],
                **options,
            )(*operands)

        (parts,) = add_pair(chans // 2, keep2, got2)
        (parts,) = add_pair(0, keep1, *got1, parts, far=(2,), alias={2: 0})
        parts = parts.reshape(devices, share_rows, chans)
    parts, chunked = lax.optimization_barrier((parts, chunked))
    parts = exchange(parts)
    ra, rb = swapped(a, "rows", 0), swapped(b, "rows", 1)
    (grad_input,) = kernel_call(
        functools.partial(input_gradient_kernel, g, 8),
        [shape_of(features.shape, F32)],
        conv_flops(own_pixels),
        far=(3, 4),
        scratch=[
            pltpu.VMEM(weights, BF16),
            pltpu.VMEM(features.shape, BF16),
            pltpu.VMEM((rows_x, 3 * chans), BF16),
            dma((2,)),
        ],
    )(e, ra, rb, w1, cotangent, occupancy)
    own_rows = share // 64
    first_row = (lax.axis_index("rows") * lax.axis_size("cols") + lax.axis_index("cols")) * own_rows
    own_weights = lax.dynamic_slice_in_dim(chunked, first_row, own_rows, 0)

    norm_shape = shape_of(norm_first.shape, F32)
    updated = kernel_call(
        functools.partial(update_kernel, count),
        [chunk_shape] * 4 + [norm_shape] * 4,
        1e8,
    )(
        parts, own_weights, to_chunks(conv_first), to_chunks(conv_second), st2, st3,
        norm_scale_bias, norm_first, norm_second,
    )
    return (block_out, grad_input, *map(from_chunks, updated[:4]), *updated[4:])


def solution(mesh):
    tile = P(None, "rows", "cols", None)
    share = P(None, ("rows", "cols"))
    return jax.shard_map(
        body,
        mesh=mesh,
        in_specs=(tile, P(None, "rows", "cols"), tile, P(), share, share, P(), P(), P()),
        out_specs=(tile, tile, share, share, share, share, P(), P(), P(), P()),
        check_vma=False,
    )
```

```python
import functools
import math

import jax
import jax.numpy as jnp
from jax import lax
from jax.experimental import pallas as pl
from jax.experimental.pallas import tpu as pltpu
from jax.sharding import PartitionSpec as P

STEP = 5
BOTH = ("rows", "cols")
RIM = 3
COLS = 4
SIDE = 2 * COLS
F32, BF16 = jnp.float32, jnp.bfloat16


def shape_of(shape, dtype):
    return jax.ShapeDtypeStruct(shape, dtype)


def held(shape, dtype):
    return pltpu.VMEM(shape, dtype)


def stored(shape, dtype):
    return pltpu.HBM(shape, dtype)


def kernel_call(body, out_shape, flops, far=(), far_out=(), scratch=(), limit=16, alias=None, size=4 << 20):
    def call(*operands):
        operands = [
            pltpu.with_memory_space_constraint(v, pltpu.HBM if i in far else pltpu.VMEM)
            for i, v in enumerate(operands)
        ]
        specs = [
            pl.BlockSpec(memory_space=pltpu.HBM if i in far else pltpu.VMEM)
            for i in range(len(operands))
        ]
        return pl.pallas_call(
            body,
            out_shape=out_shape,
            in_specs=specs,
            out_specs=[
                pl.BlockSpec(memory_space=pltpu.HBM if i in far_out else pltpu.VMEM)
                for i in range(len(out_shape))
            ],
            scratch_shapes=list(scratch),
            input_output_aliases=alias or {},
            compiler_params=pltpu.CompilerParams(vmem_limit_bytes=limit << 20),
            cost_estimate=pl.CostEstimate(
                flops=int(flops), bytes_accessed=size, transcendentals=0
            ),
        )(*operands)

    return call


def dot(a, b):
    return jnp.dot(a, b, preferred_element_type=F32)


def dot_nt(a, b):
    return lax.dot_general(a, b, (((1,), (1,)), ((), ())), preferred_element_type=F32)


def total_of(ref):
    count = ref.shape[0]
    total = ref[0]
    for i in range(1, count):
        total = total + ref[i]
    return total


def to_all(ref, parts):
    value = jnp.concatenate(parts, axis=0)
    for i in range(ref.shape[0]):
        ref[i] = value


def store_shifted(ref, start, row, offsets=(0, 1, 2)):
    width, chans = row.shape
    for b in offsets:
        moved = row if b == 1 else pltpu.roll(row, 1 if b == 0 else width - 1, 0)
        ref[start : start + width, b * chans : (b + 1) * chans] = moved.astype(BF16)


class Geometry:
    def __init__(self, scenes, height, width, chans):
        self.s, self.h, self.w, self.c = scenes, height, width, chans
        self.wp = width + SIDE
        self.tall = height + 2 * RIM
        self.near = RIM - 2
        self.near_cols = COLS - 2
        self.cot_tall = height + 2 * self.near
        self.side = (COLS + self.near_cols) * height
        self.corner = -(-(COLS * RIM + self.near_cols * self.near) // 16) * 16


class Place:
    def __init__(self):
        row, col = lax.axis_index("rows"), lax.axis_index("cols")
        nrows, ncols = lax.axis_size("rows"), lax.axis_size("cols")
        self.above = (row > 0).astype(F32)
        self.below = (row < nrows - 1).astype(F32)
        self.right = (col < ncols - 1).astype(F32)
        self.left = (col > 0).astype(F32)
        self.core = row % 2
        self.second, self.third = row // 4 % 2, row // 2 % 2
        self.odd_row = row % 2 == 1
        self.odd_col = col % 2 == 1
        self.index = row * ncols + col


def wide(ref, *index):
    return ref[index].astype(F32)


def far_rows(g, place, rb, rb_c, rb_d, s):
    right, left = sides(g, place, rb_c, rb_d, s)
    rows = []
    for k in range(RIM + g.near):
        width = COLS if k < RIM else g.near_cols
        at = COLS * min(k, RIM) + g.near_cols * max(k - RIM, 0)
        rows.append(
            jnp.concatenate([wide(rb, s, k), side_columns(g, right, left, at, width)], axis=0)
        )
    return rows


def pixel_mask(occ, s):
    return occ[s].astype(F32).T


def in_grid(row, r, g, place, edge):
    row = jnp.concatenate([row[: g.w], row[g.w :] * edge], axis=0)
    if r < RIM:
        row = row * place.above
    elif r >= RIM + g.h:
        row = row * place.below
    return row


def edge_mask(place, g):
    where = lax.broadcasted_iota(jnp.int32, (SIDE, g.c), 0)
    return jnp.where(where < SIDE // 2, place.right, place.left)


def sum_rows(value):
    rows, chans = value.shape
    return jnp.sum(value.reshape(rows // 8, 8, chans), axis=0)


def pack_kernel(
    g, features, occ_far, cot, own, c_ref, d_ref, b_ref, bc_ref, bd_ref, given, seen, occ, sems
):
    copies = []
    flags = pltpu.make_async_copy(occ_far, occ, sems.at[2, 0])
    flags.start()
    for s in range(g.s):
        copies.append(
            (
                pltpu.make_async_copy(features.at[s], given.at[s], sems.at[0, s]),
                pltpu.make_async_copy(cot.at[s], seen.at[s], sems.at[1, s]),
            )
        )
        for copy in copies[-1]:
            copy.start()
    odd, odd_row = Place().odd_col, Place().odd_row
    flags.wait()

    for s in range(g.s):
        mask = pixel_mask(occ, s)
        for copy in copies[s]:
            copy.wait()
        rows = []
        for r in range(g.h):
            row = wide(given, s, r) * mask[:, r : r + 1]
            rows.append(row)
            own[s, r] = row.astype(BF16)
        cots = [wide(seen, s, r) for r in range(g.h)]
        ends = []
        for field, count in ((rows, RIM), (cots, g.near)):
            for k in range(count):
                ends.append(jnp.where(odd_row, field[g.h - count + k], field[k]))
                b_ref[s, len(ends) - 1] = ends[-1].astype(BF16)
        spare = jnp.zeros((g.corner - COLS * RIM - g.near_cols * g.near, g.c), F32)
        widths = [COLS] * RIM + [g.near_cols] * g.near
        right = [v[g.w - width :] for v, width in zip(ends, widths, strict=True)]
        left = [v[:width] for v, width in zip(ends, widths, strict=True)]
        right, left = (jnp.concatenate(v + [spare], axis=0) for v in (right, left))
        bc_ref[s] = jnp.where(odd, left, right).astype(BF16)
        bd_ref[s] = jnp.where(odd, right, left).astype(BF16)
        right = jnp.concatenate(
            [v[g.w - COLS :] for v in rows] + [v[g.w - g.near_cols :] for v in cots], axis=0
        )
        left = jnp.concatenate([v[:COLS] for v in rows] + [v[: g.near_cols] for v in cots], axis=0)
        c_ref[s] = jnp.where(odd, left, right).astype(BF16)
        d_ref[s] = jnp.where(odd, right, left).astype(BF16)


def sides(g, place, rc, rd, s):
    c, d = wide(rc, s), wide(rd, s)
    return jnp.where(place.odd_col, d, c), jnp.where(place.odd_col, c, d)


def side_columns(g, right, left, at, width):
    parts = [right[at : at + width], jnp.zeros((SIDE - 2 * width, g.c), F32), left[at : at + width]]
    return jnp.concatenate([part for part in parts if part.shape[0]], axis=0)


def assemble_kernel(g, own, cot, rc, rd, ext, cot_ext, a_ref):
    place = Place()

    odd = place.odd_row
    for s in range(g.s):
        right, left = sides(g, place, rc, rd, s)
        for source, full, at, width, count, first in (
            (own, ext, 0, COLS, RIM, 0),
            (cot, cot_ext, COLS * g.h, g.near_cols, g.near, RIM),
        ):
            rows = []
            for r in range(g.h):
                beyond = side_columns(g, right, left, at + width * r, width)
                rows.append(jnp.concatenate([wide(source, s, r), beyond], axis=0))
                full[s, r] = rows[r].astype(BF16)
            for k in range(count):
                top, bottom = rows[k], rows[g.h - count + k]
                a_ref[s, first + k] = jnp.where(odd, top, bottom).astype(BF16)


def prepare_kernel(w_ref, one_ref, two_ref, buffer, sems):
    chans = one_ref.shape[1]
    taps, size, lanes = buffer.shape
    per = chans // lanes
    copies = [
        pltpu.make_async_copy(w_ref.at[pl.ds(t * size, size)], buffer.at[t], sems.at[t])
        for t in range(taps)
    ]
    for copy in copies:
        copy.start()
    for t in range(taps):
        copies[t].wait()
        for k, out in enumerate((one_ref, two_ref)):
            parts = [buffer[t, pl.ds(2 * half + k, chans, stride=2 * per), :] for half in range(per)]
            out[t * chans : (t + 1) * chans, :] = jnp.concatenate(parts, axis=1).astype(BF16)


def place_shifted(ref, row_index, row):
    store_shifted(ref, row_index * row.shape[0], row)


def window_rows(g, x_ref, first, count):
    size = count * g.wp
    return jnp.concatenate(
        [x_ref[(first + a) * g.wp : (first + a) * g.wp + size, :] for a in range(3)], axis=1
    )


def own_conv_kernel(g, ext, w, z_ref, st_ref, x_ref):
    count = g.h - 2
    s1 = jnp.zeros((8, g.c), F32)
    s2 = jnp.zeros((8, g.c), F32)
    for s in range(g.s):
        for r in range(g.h):
            place_shifted(x_ref, s * (g.h + 2) + 1 + r, wide(ext, s, r))
        half = count // 2
        for first in range(0, count, half):
            acc = dot(window_rows(g, x_ref, s * (g.h + 2) + 1 + first, half), w[...])
            at = (s * (g.tall - 2) + RIM + first) * g.wp
            z_ref[at : at + half * g.wp, :] = acc
            for i in range(half):
                v = acc[i * g.wp : i * g.wp + g.w]
                s1 = s1 + sum_rows(v)
                s2 = s2 + sum_rows(v * v)
    st_ref[0:8] = s1
    st_ref[8:16] = s2


def rim_conv_kernel(
    g, ext, ra, rb, rb_c, rb_d, w, st_in, z_in, x_in, z_ref, st_ref, x_own, cot_ref, x_ref
):
    del z_in, x_in
    place = Place()
    odd = place.odd_row
    s1, s2 = st_in[0:8], st_in[8:16]
    span = RIM + 2
    for s in range(g.s):
        far = far_rows(g, place, rb, rb_c, rb_d, s)
        near = [wide(ra, s, k) for k in range(RIM + g.near)]
        for side in range(2):
            base = span * (2 * s + side)
            beyond = [
                jnp.where(odd, b, a) if side else jnp.where(odd, a, b)
                for a, b in zip(near, far, strict=True)
            ]
            for k in range(RIM):
                place_shifted(x_ref, base + 2 * side + k, beyond[k])
            next_row = beyond[0 if side else RIM - 1]
            place_shifted(x_own, s * (g.h + 2) + (g.h + 1) * side, next_row)
            cot_ref[s, side] = beyond[RIM].astype(BF16)
            source = (s * (g.h + 2) + 1 + (g.h - 2) * side) * g.wp
            target = (base + RIM * (1 - side)) * g.wp
            x_ref[target : target + 2 * g.wp, :] = x_own[source : source + 2 * g.wp, :]
            acc = dot(window_rows(g, x_ref, base, RIM), w[...])
            at = (s * (g.tall - 2) + (g.h + RIM - 2) * side) * g.wp
            z_ref[at : at + RIM * g.wp, :] = acc
            i = 0 if side else RIM - 1
            v = acc[i * g.wp : i * g.wp + g.w]
            s1 = s1 + sum_rows(v)
            s2 = s2 + sum_rows(v * v)
    to_all(st_ref, [jnp.sum(s1, 0, keepdims=True), jnp.sum(s2, 0, keepdims=True)])


def typical_hidden(params):
    scale, shift = params[0:1], params[1:2]
    return 0.5 * (shift + jnp.sqrt(shift * shift + 0.64 * scale * scale))


def stats_of(total, count):
    mean = total[0:1] / count
    var = total[1:2] / count - mean * mean
    return mean, lax.rsqrt(var + 1e-05)


def second_conv_kernel(g, chunk, count, z1, st, params, w, cot, h_ref, z_ref, st_ref, own_ref):
    rows_in, rows_out = g.tall - 2, g.tall - 4
    place = Place()
    mean, rstd = stats_of(total_of(st), count)
    scale = params[0:1] * rstd
    shift = params[1:2] - mean * scale
    edge = edge_mask(place, g)
    sums = [jnp.zeros((8, g.c), F32) for _ in range(4)]
    for s in range(g.s):
        for r in range(rows_in):
            start = (s * rows_in + r) * g.wp
            row = jnp.maximum(z1[start : start + g.wp, :] * scale + shift, 0.0)
            store_shifted(h_ref, start, in_grid(row, r + 1, g, place, edge))
        for r in range(0, rows_out, chunk):
            base = (s * rows_in + r) * g.wp
            size = chunk * g.wp
            lhs = jnp.concatenate(
                [h_ref[base + a * g.wp : base + a * g.wp + size, :] for a in range(3)], axis=1
            )
            acc = dot(lhs, w[...])
            z_ref[(s * rows_out + r) * g.wp : (s * rows_out + r) * g.wp + size, :] = acc
            for i in range(chunk):
                if RIM <= r + i + 2 < RIM + g.h:
                    v = acc[i * g.wp : i * g.wp + g.w]
                    dn = wide(cot, s, r + i + 2 - RIM)[: g.w]
                    for k, term in enumerate((v, v * v, dn, dn * v)):
                        sums[k] = sums[k] + sum_rows(term)
    own = [jnp.sum(v, 0, keepdims=True) for v in sums]
    own_ref[0:4] = jnp.concatenate(own, axis=0)
    to_all(st_ref, own)


def own_transposed(g, source, first, s, dt_ref):
    span = g.h * g.wp
    block = source[first : first + span, :]
    inside = lax.broadcasted_iota(jnp.int32, (span, 1), 0) % g.wp < g.w
    dt_ref[:, s * span : (s + 1) * span] = jnp.where(inside, block, jnp.zeros_like(block)).T


def kernel_gradient(g, core, field, rows_field, first_row, dt_ref, keep, send, first, prepare, less):
    chans, half = g.c, g.c // 2
    span = g.h * g.wp
    mine = pl.ds(pl.multiple_of(core * half, half), half)
    other = pl.ds(pl.multiple_of((1 - core) * half, half), half)
    totals = [None] * 3
    cut = g.s // 2
    groups = (range(cut), range(cut, g.s))
    for s in groups[0]:
        prepare(s)
    for group in groups:
        lanes = slice(group[0] * span, (group[-1] + 1) * span)
        lhs = jnp.concatenate([dt_ref[mine, lanes], dt_ref[other, lanes]], axis=0)
        for a in range(3):
            starts = [(s * rows_field + first_row + a) * g.wp for s in group]
            acc = dot(lhs, jnp.concatenate([field[at : at + span, :] for at in starts], axis=0))
            if group[0] == 0 and a < len(groups[1]):
                prepare(groups[1][a])
            if group[0] == 0:
                for b in range(3):
                    first[a * 3 + b] = acc[:, b * chans : (b + 1) * chans]
                continue
            for b in range(3):
                rows = slice((a * 3 + b) * chans, (a * 3 + b + 1) * chans)
                part = acc[:, b * chans : (b + 1) * chans] + first[a * 3 + b]
                keep[rows, :] = (part[0:half] - less(mine)).T
                send[rows, :] = (part[half:] - less(other)).T.astype(BF16)


def second_gradient_kernel(
    g, count, z2, st, own, params, cot, cot_next, h, d_ref, keep, send, dt_ref, sums, first
):
    place = Place()
    rows = g.cot_tall
    total = total_of(st)
    mean, rstd = stats_of(total, count)
    sum_dn = total[2:3]
    sum_dx = rstd * (total[3:4] - mean * sum_dn)
    k0 = params[2:3] * rstd
    k1 = k0 * (sum_dn / count)
    k2 = k0 * rstd * (sum_dx / count)
    edge = edge_mask(place, g)
    def prepare(s):
        for i in range(rows):
            rim = not g.near <= i < g.near + g.h
            dn = wide(cot_next, s, 0 if i < g.near else 1) if rim else wide(cot, s, i - g.near)
            start = (s * rows + i) * g.wp
            d = k0 * dn - k1 - (z2[start : start + g.wp, :] - mean) * k2
            d = in_grid(d, i + RIM - g.near, g, place, edge)
            d_ref[start : start + g.wp, :] = d.astype(BF16)
        own_transposed(g, d_ref, (s * rows + g.near) * g.wp, s, dt_ref)
    pixels = float(g.s * g.h * g.w)
    tile_sum = k0 * own[2:3] - pixels * k1 - k2 * (own[0:1] - pixels * mean)
    sums[...] = jnp.broadcast_to(tile_sum, (sums.shape[1], g.c)).T
    typical = typical_hidden(params)

    def less(channels):
        column = sums[channels, :]
        return jnp.concatenate([column] * (g.c // column.shape[1]), axis=1) * typical

    kernel_gradient(g, place.core, h, g.tall - 2, RIM - 2, dt_ref, keep, send, first, prepare, less)


def transposed_conv(g, d_ref, w, s, rows_in, r, chunk):
    acc = None
    size = chunk * g.wp
    for a in range(3):
        start = (s * rows_in + r + a) * g.wp
        for b in range(3):
            tap = (2 - a) * 3 + (2 - b)
            term = dot_nt(
                d_ref[start : start + size, b * g.c : (b + 1) * g.c],
                w[tap * g.c : (tap + 1) * g.c, :],
            )
            acc = term if acc is None else acc + term
    return acc


def hidden_gradient_kernel(
    g, chunk, count, scenes, d, w, z1, z2, st, st2, params, ext, *refs
):
    *before, dn_ref, st_ref, out_ref, d_ref = refs
    mean2, rstd2 = stats_of(total_of(st2), count)
    scale2 = params[2:3] * rstd2
    shift2 = params[3:4] - mean2 * scale2
    rows_in, rows_out, z_rows = g.tall - 4, g.tall - 6, g.tall - 2
    mean, rstd = stats_of(total_of(st), count)
    scale = params[0:1] * rstd
    shift = params[1:2] - mean * scale
    s0 = before[1][0:8] if before else jnp.zeros((8, g.c), F32)
    s1 = before[1][8:16] if before else jnp.zeros((8, g.c), F32)
    for s in scenes:
        for i in range(rows_in):
            at = (s * rows_in + i) * g.wp
            store_shifted(d_ref, at, wide(d, slice(at, at + g.wp)))
        for r in range(g.h):
            at = (s * rows_in + r + g.near) * g.wp
            normed = z2[at : at + g.w, :] * scale2 + shift2
            out_ref[s, r] = (wide(ext, s, r)[: g.w] + normed).astype(BF16)
        for r in range(0, rows_out, chunk):
            acc = transposed_conv(g, d_ref, w, s, rows_in, r, chunk)
            at = (s * z_rows + r + 2) * g.wp
            z = z1[at : at + chunk * g.wp, :]
            dn = jnp.where(z * scale + shift > 0, acc, 0.0)
            dn_ref[(s * rows_out + r) * g.wp : (s * rows_out + r + chunk) * g.wp, :] = dn
            for i in range(chunk):
                if RIM <= r + i + 3 < RIM + g.h:
                    v = dn[i * g.wp : i * g.wp + g.w]
                    s0 = s0 + sum_rows(v)
                    s1 = s1 + sum_rows(v * (z[i * g.wp : i * g.wp + g.w] - mean))
    if not before:
        st_ref[0:8] = s0
        st_ref[8:16] = s1
    else:
        to_all(st_ref, [jnp.sum(s0, 0, keepdims=True), jnp.sum(s1, 0, keepdims=True) * rstd])


def put(refs, rows, value):
    if not isinstance(refs, tuple):
        refs = (refs,)
    at = 0
    for ref in refs:
        first, last = max(rows.start, at), min(rows.stop, at + ref.shape[0])
        if first < last:
            part = value[first - rows.start : last - rows.start]
            ref[first - at : last - at, :] = part.astype(ref.dtype)
        at += ref.shape[0]


def half_gradient(g, which, field, rows_field, first_row, dt_ref, out_ref, sums, prepare=None):
    chans, half = g.c, g.c // 2
    span = g.h * g.wp
    channels = pl.ds(pl.multiple_of(which * half, half), half)
    cut = g.s // 2
    groups = range(cut), range(cut, g.s)
    if prepare is not None:
        for s in groups[0]:
            prepare(s)
    for group in groups:
        lhs = dt_ref[channels, group[0] * span : (group[-1] + 1) * span]
        for a in range(3):
            starts = [(s * rows_field + first_row + a) * g.wp for s in group]
            acc = dot(lhs, jnp.concatenate([field[at : at + span, :] for at in starts], axis=0))
            if group[0] == 0 and prepare is not None and a < len(groups[1]):
                prepare(groups[1][a])
            for b in range(3):
                part = acc[:, b * chans : (b + 1) * chans]
                if group[0] == 0:
                    sums[a * 3 + b] = part
                else:
                    rows = slice((a * 3 + b) * chans, (a * 3 + b + 1) * chans)
                    put(out_ref, rows, (sums[a * 3 + b] + part).T)


def first_gradient_kernel(
    g, count, dn, z, st, st3, params, x, e_ref, a_ref, b_ref, *refs
):
    *send, dt_ref, first = refs
    place = Place()
    mean, rstd = stats_of(total_of(st), count)
    total = total_of(st3)
    k0 = params[0:1] * rstd
    k1 = k0 * (total[0:1] / count)
    k2 = k0 * rstd * (total[1:2] / count)
    edge = edge_mask(place, g)

    def prepare(s):
        for i in range(g.h):
            at = (s * g.h + i) * g.wp
            z_at = (s * (g.tall - 2) + i + RIM - 1) * g.wp
            d = k0 * dn[at : at + g.wp, :] - k1 - (z[z_at : z_at + g.wp, :] - mean) * k2
            d = in_grid(d, i + RIM, g, place, edge)
            e_ref[at : at + g.wp, :] = d.astype(BF16)
            if i == 0:
                top = d
        a_ref[s, 0] = jnp.where(place.odd_row, top, d).astype(BF16)
        b_ref[s, 0] = jnp.where(place.odd_row, d, top).astype(BF16)
        own_transposed(g, e_ref, s * g.h * g.wp, s, dt_ref)
    half_gradient(g, 1 - place.core, x, g.h + 2, 0, dt_ref, tuple(send), first, prepare)


def first_own_kernel(g, x, dt_ref, keep, first):
    half_gradient(g, Place().core, x, g.h + 2, 0, dt_ref, keep, first)


def input_gradient_kernel(
    g, chunk, e, ra, rb, w_far, cot_far, occ, out_ref, w, cot, e_ref, sems
):
    rows_in = g.h + 2
    place = Place()
    copies = [
        pltpu.make_async_copy(w_far, w, sems.at[0]),
        pltpu.make_async_copy(cot_far, cot, sems.at[1]),
    ]
    for copy in copies:
        copy.start()
    for copy in copies:
        copy.wait()
    for s in range(g.s):
        a, b = wide(ra, s, 0), wide(rb, s, 0)
        rows = [jnp.where(place.odd_row, a, b)]
        for r in range(g.h):
            at = (s * g.h + r) * g.wp
            rows.append(wide(e, slice(at, at + g.wp)))
        rows.append(jnp.where(place.odd_row, b, a))
        for i in range(rows_in):
            place_shifted(e_ref, s * rows_in + i, rows[i])
        mask = pixel_mask(occ, s)
        for r in range(0, g.h, chunk):
            acc = transposed_conv(g, e_ref, w, s, rows_in, r, chunk)
            for i in range(chunk):
                v = acc[i * g.wp : i * g.wp + g.w]
                out_ref[s, r + i] = (wide(cot, s, r + i) + v) * mask[:, r + i : r + i + 1]


def pair_total(keep, got, t):
    chans = 2 * keep.shape[1]
    rows = slice(t * chans, (t + 1) * chans)
    return keep[rows, :] + wide(got, rows)


def pair_sum_kernel(lane, keep, got, *refs):
    *_, out_far, buffer, sems = refs
    half = buffer.shape[1]
    chans = 2 * half
    taps = buffer.shape[0] // chans
    copies = []
    for t in range(taps):
        rows = pl.ds(t * chans, chans)
        buffer[rows, :] = pair_total(keep, got, t).astype(BF16)
        copies.append(
            pltpu.make_async_copy(buffer.at[rows], out_far.at[rows, pl.ds(lane, half)], sems.at[t])
        )
        copies[-1].start()
    for copy in copies:
        copy.wait()


def half_rows(share):
    return -(-(share // 2) // 8) * 8


def split_kernel(keep, got, kept_ref, sent_ref, buffer):
    half = keep.shape[1]
    chans = 2 * half
    taps = keep.shape[0] // chans
    devices, rows, _ = kept_ref.shape
    share = taps * chans // devices
    for t in range(taps):
        buffer[t * chans : (t + 1) * chans, :] = pair_total(keep, got, t)
    second = Place().second
    for i in range(devices):
        mine = pl.multiple_of(i * share + (share - rows) * second, 8)
        other = pl.multiple_of(i * share + (share - rows) * (1 - second), 8)
        kept_ref[i] = buffer[pl.ds(mine, rows), :]
        sent_ref[i] = buffer[pl.ds(other, rows), :].astype(BF16)


def split_again_kernel(kept, came, kept_ref, sent_ref, buffer):
    devices, rows, _ = kept_ref.shape
    spare = kept.shape[1] - rows
    third = Place().third
    for i in range(devices):
        buffer[i] = kept[i] + wide(came, i)
    for i in range(devices):
        kept_ref[i] = buffer[i, pl.ds(pl.multiple_of(spare * third, 8), rows)]
    for j in range(devices // 2):
        large = buffer[2 * j + 1 - third, pl.ds(pl.multiple_of(spare * (1 - third), 8), rows)]
        small = buffer[2 * j + third, pl.ds(pl.multiple_of(rows * (1 - third), 8), spare)]
        sent_ref[j] = jnp.concatenate([large, small], axis=0).astype(BF16)


def whole_tiles(share):
    return share // 16 * 16


def write_parts(block_of, first_row, out_far, buffer, sems):
    devices, rows, _ = buffer.shape
    count = sems.shape[0]
    per = devices // count
    copies = []
    for part in range(count):
        mine = pl.ds(part * per, per)
        for i in range(part * per, (part + 1) * per):
            buffer[i] = block_of(i).astype(BF16)
        there = out_far.at[mine, pl.ds(first_row, rows)]
        copies.append(pltpu.make_async_copy(buffer.at[mine], there, sems.at[part]))
        copies[-1].start()
    for copy in copies:
        copy.wait()


def first_rows(keep, got, share, i, rows):
    piece, at = divmod(i * share, got[0].shape[0])
    mine = keep[i * share + rows.start : i * share + rows.stop, :]
    return mine + wide(got[piece], slice(at + rows.start, at + rows.stop))


def early_message_kernel(keep, *refs):
    *got, out_far, buffer, sems = refs
    devices, rows, _ = buffer.shape
    share = keep.shape[0] // devices
    write_parts(lambda i: first_rows(keep, got, share, i, slice(0, rows)), 0, out_far, buffer, sems)


def message_kernel(keep, *refs):
    *got, kept, came, _, out_far, buffer, sems = refs
    devices = kept.shape[0]
    share = keep.shape[0] // devices
    rows = kept.shape[1]
    spare = came.shape[1] - rows
    third = Place().third
    none = jnp.zeros((rows - spare, kept.shape[2]), F32)

    def block_of(i):
        others = wide(came, i // 2)
        small = [others[rows:], none] if i % 2 else [none, others[rows:]]
        second = kept[i] + jnp.where(third == i % 2, others[:rows], jnp.concatenate(small, axis=0))
        last = first_rows(keep, got, share, i, slice(whole_tiles(share), share))
        return jnp.concatenate([last, second], axis=0)

    write_parts(block_of, whole_tiles(share), out_far, buffer, sems)


def adamw(weight, grad, first, second, rate):
    first_new = 0.9 * first + 0.1 * grad
    second_new = 0.999 * second + 0.001 * grad * grad
    first_hat = first_new / (1.0 - 0.9**STEP)
    second_hat = second_new / (1.0 - 0.999**STEP)
    weight_new = weight - rate * (first_hat / (jnp.sqrt(second_hat) + 1e-08) + 0.01 * weight)
    return (weight_new, first_new, second_new)


def update_kernel(
    count, parts, w, first_m, second_m, st2, st3, params, n_first, n_second,
    grad_out, w_out, first_out, second_out, n_grad, n_out, n_first_out, n_second_out
):
    devices, ncols = parts.shape[0], lax.axis_size("cols")
    share = w.shape[0] // 4
    total2, total3 = total_of(st2), total_of(st3)
    mean, rstd = stats_of(total2, count)
    sum_dn = total2[2:3]
    grads = jnp.concatenate(
        [total3[1:2], total3[0:1], rstd * (total2[3:4] - mean * sum_dn), sum_dn], axis=0
    )
    n_grad[...] = grads
    n_out[...], n_first_out[...], n_second_out[...] = adamw(
        params[...], grads, n_first[...], n_second[...], 0.75
    )
    def over(chosen, rows, lanes):
        total = None
        for source in range(devices):
            if chosen(source // ncols):
                term = wide(parts, source)[rows, lanes]
                total = term if total is None else total + term
        return total

    grads = []
    every = slice(None)
    for half in range(2):
        if parts.shape[2] == 256:
            for k in range(2):
                lanes = slice(k * 128, (k + 1) * 128)
                grads.append((k, half, over(lambda row: row % 2 == half, every, lanes)))
        else:
            grads.append((0, half, over(lambda row: row % 2 == half, slice(0, share), every)))
            size = half_rows(share)
            last = half_rows(size)
            spare = size - last
            odd = lax.axis_index("cols") % 2 == 1
            blocks = []
            for second in range(2):
                one, two = (
                    over(lambda r, row=half + 4 * second + 2 * third: r % 8 == row, slice(share, None), every)
                    for third in range(2)
                )
                middle = jnp.where(odd, two[: last - spare], one[spare:])
                blocks.append(jnp.concatenate([one[:spare], middle, two[last - spare :]], axis=0))
            blocks[1] = blocks[1][2 * size - share :]
            grads.append((1, half, jnp.concatenate(blocks, axis=0)))
    for k, half, grad in grads:
        at = pl.ds(2 * half + k, share, stride=4)
        new = adamw(w[at, :], grad, first_m[at, :], second_m[at, :], 0.02)
        grad_out[at, :] = grad
        w_out[at, :], first_out[at, :], second_out[at, :] = new


def swapped(block, axis, first):
    count = lax.axis_size(axis)
    pairs = []
    for i in range(first, count - 1, 2):
        pairs += [(i, i + 1), (i + 1, i)]
    return lax.ppermute(block, axis, pairs)


def swapped_both(block, first_row, first_col):
    nrows, ncols = lax.axis_size("rows"), lax.axis_size("cols")

    def partner(i, first, count):
        j = i + 1 if (i - first) % 2 == 0 else i - 1
        return j if min(i, j) >= first and max(i, j) < count else None

    pairs = []
    for i in range(nrows):
        for j in range(ncols):
            to = partner(i, first_row, nrows), partner(j, first_col, ncols)
            if None not in to:
                pairs.append((i * ncols + j, to[0] * ncols + to[1]))
    return lax.ppermute(block, BOTH, pairs)


def to_chunks(flat):
    return flat.reshape(2, -1, 128).transpose(1, 0, 2).reshape(-1, 128)


def from_chunks(rows):
    return rows.reshape(-1, 2, 128).transpose(1, 0, 2).reshape(2, -1)


def exchange(parts):
    return lax.all_to_all(parts, BOTH, 0, 0, tiled=True)


def body(
    features,
    occupancy,
    cotangent,
    conv_weights,
    conv_first,
    conv_second,
    norm_scale_bias,
    norm_first,
    norm_second,
):
    scenes, height, width, chans = features.shape
    g = Geometry(scenes, height, width, chans)
    wp = g.wp
    devices = lax.axis_size("rows") * lax.axis_size("cols")
    count = float(scenes * height * width * devices)
    taps = 9 * chans
    n0, n1, n2, n3 = (scenes * wp * (g.tall - 2 * i) for i in range(4))
    own_pixels = scenes * height * wp
    dma = pltpu.SemaphoreType.DMA

    def conv_flops(n):
        return 2 * n * taps * chans

    side = shape_of((scenes, g.side, chans), BF16)
    corner = shape_of((scenes, g.corner, chans), BF16)
    own, c, d, b, bc, bd = kernel_call(
        functools.partial(pack_kernel, g),
        [
            shape_of(features.shape, BF16),
            side,
            side,
            shape_of((scenes, RIM + g.near, width, chans), BF16),
            corner,
            corner,
        ],
        1e8,
        far=(0, 1, 2),
        scratch=[
            pltpu.VMEM(features.shape, BF16),
            pltpu.VMEM(features.shape, BF16),
            pltpu.VMEM(occupancy.shape, jnp.int32),
            dma((3, scenes)),
        ],
    )(features, occupancy, cotangent)
    rb = swapped(b, "rows", 1)
    rc, rd = swapped(c, "cols", 0), swapped(d, "cols", 1)
    rb_c, rb_d = swapped_both(bc, 1, 0), swapped_both(bd, 1, 1)
    chunked = to_chunks(conv_weights)
    share = conv_first.shape[1]
    chunk_shape = shape_of((share // 64, 128), F32)
    weights = (taps, chans)
    w1, w2 = kernel_call(
        prepare_kernel,
        [held(weights, BF16)] * 2,
        0,
        size=1024,
        far=(0,),
        scratch=[pltpu.VMEM((9, chunked.shape[0] // 9, 128), F32), dma((9,))],
    )(chunked)

    def wide_rows(rows):
        return shape_of((scenes, rows, wp, chans), BF16)

    ext, cot_ext, a = kernel_call(
        functools.partial(assemble_kernel, g),
        [wide_rows(n) for n in (height, height, RIM + g.near)],
        0,
        size=1024,
    )(own, cotangent, rc, rd)
    rows_x = scenes * (height + 2) * wp
    x_shape = held((rows_x, 3 * chans), BF16)
    z1, st, x = kernel_call(
        functools.partial(own_conv_kernel, g),
        [held((n1, chans), F32), held((16, chans), F32), x_shape],
        0,
        size=1024,
    )(ext, w1)
    a, rb, rb_c, rb_d, w1 = lax.optimization_barrier((a, rb, rb_c, rb_d, w1))
    ra = swapped(a, "rows", 0)
    z1, st, x, cot_next = kernel_call(
        functools.partial(rim_conv_kernel, g),
        [held((n1, chans), F32), shape_of((devices, 2, chans), F32), x_shape, wide_rows(2)],
        0,
        size=1024,
        scratch=[pltpu.VMEM((scenes * 2 * (RIM + 2) * wp, 3 * chans), BF16)],
        alias={7: 0, 8: 2},
    )(ext, ra, rb, rb_c, rb_d, w1, st, z1, x)
    st1 = exchange(st)
    h, z2, st, own_sums = kernel_call(
        functools.partial(second_conv_kernel, g, 5, count),
        [
            held((n1, 3 * chans), BF16),
            held((n2, chans), F32),
            shape_of((devices, 4, chans), F32),
            held((8, chans), F32),
        ],
        conv_flops(n2),
    )(z1, st1, norm_scale_bias, w2, cot_ext)
    st2 = exchange(st)
    grad_shape = held((taps, chans // 2), F32)
    d, keep2, send2 = kernel_call(
        functools.partial(second_gradient_kernel, g, count),
        [held((n2, chans), BF16), grad_shape, held(grad_shape.shape, BF16)],
        conv_flops(own_pixels),
        scratch=[
            pltpu.VMEM((chans, own_pixels), BF16),
            pltpu.VMEM((chans, 128), F32),
            pltpu.VMEM((9, chans, chans), F32),
        ],
    )(z2, st2, own_sums, norm_scale_bias, cot_ext, cot_next, h)
    got2 = swapped(send2, "rows", 0)
    nrows = lax.axis_size("rows")
    cut_again = nrows % 8 == 0 and lax.axis_size("cols") % 2 == 0 and taps // devices % 8 == 0
    hidden_shape, output_shape = held((n3, chans), F32), held(features.shape, BF16)

    def hidden_gradient(scenes, part_shape, *before, **options):
        return kernel_call(
            functools.partial(hidden_gradient_kernel, g, 8, count, scenes),
            [hidden_shape, part_shape, output_shape],
            0,
            size=1024,
            scratch=[pltpu.VMEM((n2, 3 * chans), BF16)],
            **options,
        )(d, w2, z1, z2, st1, st2, norm_scale_bias, ext, *before)

    early = range(3)
    dn1, part, block_out = hidden_gradient(early, held((16, chans), F32))
    got2, part = lax.optimization_barrier((got2, part))
    if cut_again:
        kept_shape = (devices, half_rows(taps // devices), chans // 2)
        kept, sent = kernel_call(
            split_kernel,
            [held(kept_shape, F32), held(kept_shape, BF16)],
            0,
            size=1024,
            scratch=[pltpu.VMEM((taps, chans // 2), F32)],
        )(keep2, got2)
        came = lax.ppermute(sent, "rows", [(i, i ^ 4) for i in range(nrows)])
        kept, part = lax.optimization_barrier((kept, part))
    dn1, st, block_out = hidden_gradient(
        range(len(early), scenes),
        shape_of((devices, 2, chans), F32),
        dn1,
        part,
        block_out,
        alias={8: 0, 10: 2},
    )
    st3 = exchange(st)
    if cut_again:
        kept, st3 = lax.optimization_barrier((kept, st3))
        again_shape = (devices, half_rows(kept_shape[1]), chans // 2)
        kept, sent = kernel_call(
            split_again_kernel,
            [held(again_shape, F32), held((devices // 2, *kept_shape[1:]), BF16)],
            0,
            size=1024,
            scratch=[pltpu.VMEM(kept_shape, F32)],
        )(kept, came)
        came = lax.ppermute(sent, "rows", [(i, i ^ 2) for i in range(nrows)])
        dn1, kept = lax.optimization_barrier((dn1, kept))
    cuts = 4 if cut_again else 1
    sent_shape = held((taps // cuts, chans // 2), BF16)
    part = pltpu.VMEM((9, chans // 2, chans), F32)
    e, a, b, *send1, dt = kernel_call(
        functools.partial(first_gradient_kernel, g, count),
        [held((n3, chans), BF16), wide_rows(1), wide_rows(1)]
        + [sent_shape] * cuts
        + [held((chans, own_pixels), BF16)],
        0,
        size=1024,
        scratch=[part],
    )(dn1, z1, st1, st3, norm_scale_bias, x)
    (keep1,) = kernel_call(
        functools.partial(first_own_kernel, g), [held((taps, chans // 2), F32)], 0, size=1024, scratch=[part]
    )(x, dt)
    got1 = [swapped(part, "rows", 0) for part in send1]
    share_rows = taps // devices
    if cut_again:
        rows = share_rows + kept.shape[1]
        parts_shape = stored((devices, rows, chans // 2), BF16)
        ready = whole_tiles(share_rows)
        (parts,) = kernel_call(
            early_message_kernel,
            [parts_shape],
            0,
            size=1024,
            far_out=(0,),
            scratch=[pltpu.VMEM((devices, ready, chans // 2), BF16), dma((4,))],
        )(keep1, *got1)
        operands = (keep1, *got1, kept, came, parts)
        at = len(operands) - 1
        (parts,) = kernel_call(
            message_kernel,
            [parts_shape],
            1e9,
            far=(at,),
            far_out=(0,),
            scratch=[pltpu.VMEM((devices, rows - ready, chans // 2), BF16), dma((4,))],
            alias={at: 0},
        )(*operands)
    else:

        def add_pair(lane, *operands, **options):
            return kernel_call(
                functools.partial(pair_sum_kernel, lane),
                [stored((taps, chans), BF16)],
                1e9,
                far_out=(0,),
                scratch=[pltpu.VMEM((taps, chans // 2), BF16), dma((9,))],
                **options,
            )(*operands)

        (parts,) = add_pair(chans // 2, keep2, got2)
        (parts,) = add_pair(0, keep1, *got1, parts, far=(2,), alias={2: 0})
        parts = parts.reshape(devices, share_rows, chans)
    parts, chunked = lax.optimization_barrier((parts, chunked))
    parts = exchange(parts)
    ra, rb = swapped(a, "rows", 0), swapped(b, "rows", 1)
    (grad_input,) = kernel_call(
        functools.partial(input_gradient_kernel, g, 8),
        [shape_of(features.shape, F32)],
        conv_flops(own_pixels),
        far=(3, 4),
        scratch=[
            pltpu.VMEM(weights, BF16),
            pltpu.VMEM(features.shape, BF16),
            pltpu.VMEM((rows_x, 3 * chans), BF16),
            dma((2,)),
        ],
    )(e, ra, rb, w1, cotangent, occupancy)
    own_rows = share // 64
    first_row = (lax.axis_index("rows") * lax.axis_size("cols") + lax.axis_index("cols")) * own_rows
    own_weights = lax.dynamic_slice_in_dim(chunked, first_row, own_rows, 0)

    norm_shape = shape_of(norm_first.shape, F32)
    updated = kernel_call(
        functools.partial(update_kernel, count),
        [chunk_shape] * 4 + [norm_shape] * 4,
        1e8,
    )(
        parts, own_weights, to_chunks(conv_first), to_chunks(conv_second), st2, st3,
        norm_scale_bias, norm_first, norm_second,
    )
    return (block_out, grad_input, *map(from_chunks, updated[:4]), *updated[4:])


def solution(mesh):
    tile = P(None, "rows", "cols", None)
    share = P(None, ("rows", "cols"))
    return jax.shard_map(
        body,
        mesh=mesh,
        in_specs=(tile, P(None, "rows", "cols"), tile, P(), share, share, P(), P(), P()),
        out_specs=(tile, tile, share, share, share, share, P(), P(), P(), P()),
        check_vma=False,
    )
```

```python
import functools
import math

import jax
import jax.numpy as jnp
from jax import lax
from jax.experimental import pallas as pl
from jax.experimental.pallas import tpu as pltpu
from jax.sharding import PartitionSpec as P

STEP = 5
BOTH = ("rows", "cols")
RIM = 3
COLS = 4
SIDE = 2 * COLS
F32, BF16 = jnp.float32, jnp.bfloat16


def shape_of(shape, dtype):
    return jax.ShapeDtypeStruct(shape, dtype)


def held(shape, dtype):
    return pltpu.VMEM(shape, dtype)


def stored(shape, dtype):
    return pltpu.HBM(shape, dtype)


def kernel_call(body, out_shape, flops, far=(), far_out=(), scratch=(), limit=16, alias=None, size=4 << 20):
    def call(*operands):
        operands = [
            pltpu.with_memory_space_constraint(v, pltpu.HBM if i in far else pltpu.VMEM)
            for i, v in enumerate(operands)
        ]
        specs = [
            pl.BlockSpec(memory_space=pltpu.HBM if i in far else pltpu.VMEM)
            for i in range(len(operands))
        ]
        return pl.pallas_call(
            body,
            out_shape=out_shape,
            in_specs=specs,
            out_specs=[
                pl.BlockSpec(memory_space=pltpu.HBM if i in far_out else pltpu.VMEM)
                for i in range(len(out_shape))
            ],
            scratch_shapes=list(scratch),
            input_output_aliases=alias or {},
            compiler_params=pltpu.CompilerParams(vmem_limit_bytes=limit << 20),
            cost_estimate=pl.CostEstimate(
                flops=int(flops), bytes_accessed=size, transcendentals=0
            ),
        )(*operands)

    return call


def dot(a, b):
    return jnp.dot(a, b, preferred_element_type=F32)


def dot_nt(a, b):
    return lax.dot_general(a, b, (((1,), (1,)), ((), ())), preferred_element_type=F32)


def total_of(ref):
    count = ref.shape[0]
    total = ref[0]
    for i in range(1, count):
        total = total + ref[i]
    return total


def to_all(ref, parts):
    value = jnp.concatenate(parts, axis=0)
    for i in range(ref.shape[0]):
        ref[i] = value


def store_shifted(ref, start, row, offsets=(0, 1, 2)):
    width, chans = row.shape
    for b in offsets:
        moved = row if b == 1 else pltpu.roll(row, 1 if b == 0 else width - 1, 0)
        ref[start : start + width, b * chans : (b + 1) * chans] = moved.astype(BF16)


class Geometry:
    def __init__(self, scenes, height, width, chans):
        self.s, self.h, self.w, self.c = scenes, height, width, chans
        self.wp = width + SIDE
        self.tall = height + 2 * RIM
        self.near = RIM - 2
        self.near_cols = COLS - 2
        self.cot_tall = height + 2 * self.near
        self.side = (COLS + self.near_cols) * height
        self.corner = -(-(COLS * RIM + self.near_cols * self.near) // 16) * 16


class Place:
    def __init__(self):
        row, col = lax.axis_index("rows"), lax.axis_index("cols")
        nrows, ncols = lax.axis_size("rows"), lax.axis_size("cols")
        self.above = (row > 0).astype(F32)
        self.below = (row < nrows - 1).astype(F32)
        self.right = (col < ncols - 1).astype(F32)
        self.left = (col > 0).astype(F32)
        self.core = row % 2
        self.second, self.third = row // 4 % 2, row // 2 % 2
        self.odd_row = row % 2 == 1
        self.odd_col = col % 2 == 1
        self.index = row * ncols + col


def wide(ref, *index):
    return ref[index].astype(F32)


def far_rows(g, place, rb, rb_c, rb_d, s):
    right, left = sides(g, place, rb_c, rb_d, s)
    rows = []
    for k in range(RIM + g.near):
        width = COLS if k < RIM else g.near_cols
        at = COLS * min(k, RIM) + g.near_cols * max(k - RIM, 0)
        rows.append(
            jnp.concatenate([wide(rb, s, k), side_columns(g, right, left, at, width)], axis=0)
        )
    return rows


def pixel_mask(occ, s):
    return occ[s].astype(F32).T


def in_grid(row, r, g, place, edge):
    row = jnp.concatenate([row[: g.w], row[g.w :] * edge], axis=0)
    if r < RIM:
        row = row * place.above
    elif r >= RIM + g.h:
        row = row * place.below
    return row


def edge_mask(place, g):
    where = lax.broadcasted_iota(jnp.int32, (SIDE, g.c), 0)
    return jnp.where(where < SIDE // 2, place.right, place.left)


def sum_rows(value):
    rows, chans = value.shape
    return jnp.sum(value.reshape(rows // 8, 8, chans), axis=0)


def pack_kernel(
    g, features, occ_far, cot, own, c_ref, d_ref, b_ref, bc_ref, bd_ref, given, seen, occ, sems
):
    copies = []
    flags = pltpu.make_async_copy(occ_far, occ, sems.at[2, 0])
    flags.start()
    for s in range(g.s):
        copies.append(
            (
                pltpu.make_async_copy(features.at[s], given.at[s], sems.at[0, s]),
                pltpu.make_async_copy(cot.at[s], seen.at[s], sems.at[1, s]),
            )
        )
        for copy in copies[-1]:
            copy.start()
    odd, odd_row = Place().odd_col, Place().odd_row
    flags.wait()

    for s in range(g.s):
        mask = pixel_mask(occ, s)
        for copy in copies[s]:
            copy.wait()
        rows = []
        for r in range(g.h):
            row = wide(given, s, r) * mask[:, r : r + 1]
            rows.append(row)
            own[s, r] = row.astype(BF16)
        cots = [wide(seen, s, r) for r in range(g.h)]
        ends = []
        for field, count in ((rows, RIM), (cots, g.near)):
            for k in range(count):
                ends.append(jnp.where(odd_row, field[g.h - count + k], field[k]))
                b_ref[s, len(ends) - 1] = ends[-1].astype(BF16)
        spare = jnp.zeros((g.corner - COLS * RIM - g.near_cols * g.near, g.c), F32)
        widths = [COLS] * RIM + [g.near_cols] * g.near
        right = [v[g.w - width :] for v, width in zip(ends, widths, strict=True)]
        left = [v[:width] for v, width in zip(ends, widths, strict=True)]
        right, left = (jnp.concatenate(v + [spare], axis=0) for v in (right, left))
        bc_ref[s] = jnp.where(odd, left, right).astype(BF16)
        bd_ref[s] = jnp.where(odd, right, left).astype(BF16)
        right = jnp.concatenate(
            [v[g.w - COLS :] for v in rows] + [v[g.w - g.near_cols :] for v in cots], axis=0
        )
        left = jnp.concatenate([v[:COLS] for v in rows] + [v[: g.near_cols] for v in cots], axis=0)
        c_ref[s] = jnp.where(odd, left, right).astype(BF16)
        d_ref[s] = jnp.where(odd, right, left).astype(BF16)


def sides(g, place, rc, rd, s):
    c, d = wide(rc, s), wide(rd, s)
    return jnp.where(place.odd_col, d, c), jnp.where(place.odd_col, c, d)


def side_columns(g, right, left, at, width):
    parts = [right[at : at + width], jnp.zeros((SIDE - 2 * width, g.c), F32), left[at : at + width]]
    return jnp.concatenate([part for part in parts if part.shape[0]], axis=0)


def assemble_kernel(g, own, cot, rc, rd, ext, cot_ext, a_ref):
    place = Place()

    odd = place.odd_row
    for s in range(g.s):
        right, left = sides(g, place, rc, rd, s)
        for source, full, at, width, count, first in (
            (own, ext, 0, COLS, RIM, 0),
            (cot, cot_ext, COLS * g.h, g.near_cols, g.near, RIM),
        ):
            rows = []
            for r in range(g.h):
                beyond = side_columns(g, right, left, at + width * r, width)
                rows.append(jnp.concatenate([wide(source, s, r), beyond], axis=0))
                full[s, r] = rows[r].astype(BF16)
            for k in range(count):
                top, bottom = rows[k], rows[g.h - count + k]
                a_ref[s, first + k] = jnp.where(odd, top, bottom).astype(BF16)


def prepare_kernel(w_ref, one_ref, two_ref, buffer, sems):
    chans = one_ref.shape[1]
    taps, size, lanes = buffer.shape
    per = chans // lanes
    copies = [
        pltpu.make_async_copy(w_ref.at[pl.ds(t * size, size)], buffer.at[t], sems.at[t])
        for t in range(taps)
    ]
    for copy in copies:
        copy.start()
    for t in range(taps):
        copies[t].wait()
        for k, out in enumerate((one_ref, two_ref)):
            parts = [buffer[t, pl.ds(2 * half + k, chans, stride=2 * per), :] for half in range(per)]
            out[t * chans : (t + 1) * chans, :] = jnp.concatenate(parts, axis=1).astype(BF16)


def place_shifted(ref, row_index, row):
    store_shifted(ref, row_index * row.shape[0], row)


def window_rows(g, x_ref, first, count):
    size = count * g.wp
    return jnp.concatenate(
        [x_ref[(first + a) * g.wp : (first + a) * g.wp + size, :] for a in range(3)], axis=1
    )


def own_conv_kernel(g, ext, w, z_ref, st_ref, x_ref):
    count = g.h - 2
    s1 = jnp.zeros((8, g.c), F32)
    s2 = jnp.zeros((8, g.c), F32)
    for s in range(g.s):
        for r in range(g.h):
            place_shifted(x_ref, s * (g.h + 2) + 1 + r, wide(ext, s, r))
        half = count // 2
        for first in range(0, count, half):
            acc = dot(window_rows(g, x_ref, s * (g.h + 2) + 1 + first, half), w[...])
            at = (s * (g.tall - 2) + RIM + first) * g.wp
            z_ref[at : at + half * g.wp, :] = acc
            for i in range(half):
                v = acc[i * g.wp : i * g.wp + g.w]
                s1 = s1 + sum_rows(v)
                s2 = s2 + sum_rows(v * v)
    st_ref[0:8] = s1
    st_ref[8:16] = s2


def rim_conv_kernel(
    g, ext, ra, rb, rb_c, rb_d, w, st_in, z_in, x_in, z_ref, st_ref, x_own, cot_ref, x_ref
):
    del z_in, x_in
    place = Place()
    odd = place.odd_row
    s1, s2 = st_in[0:8], st_in[8:16]
    span = RIM + 2
    for s in range(g.s):
        far = far_rows(g, place, rb, rb_c, rb_d, s)
        near = [wide(ra, s, k) for k in range(RIM + g.near)]
        for side in range(2):
            base = span * (2 * s + side)
            beyond = [
                jnp.where(odd, b, a) if side else jnp.where(odd, a, b)
                for a, b in zip(near, far, strict=True)
            ]
            for k in range(RIM):
                place_shifted(x_ref, base + 2 * side + k, beyond[k])
            next_row = beyond[0 if side else RIM - 1]
            place_shifted(x_own, s * (g.h + 2) + (g.h + 1) * side, next_row)
            cot_ref[s, side] = beyond[RIM].astype(BF16)
            source = (s * (g.h + 2) + 1 + (g.h - 2) * side) * g.wp
            target = (base + RIM * (1 - side)) * g.wp
            x_ref[target : target + 2 * g.wp, :] = x_own[source : source + 2 * g.wp, :]
            acc = dot(window_rows(g, x_ref, base, RIM), w[...])
            at = (s * (g.tall - 2) + (g.h + RIM - 2) * side) * g.wp
            z_ref[at : at + RIM * g.wp, :] = acc
            i = 0 if side else RIM - 1
            v = acc[i * g.wp : i * g.wp + g.w]
            s1 = s1 + sum_rows(v)
            s2 = s2 + sum_rows(v * v)
    to_all(st_ref, [jnp.sum(s1, 0, keepdims=True), jnp.sum(s2, 0, keepdims=True)])


def typical_hidden(params):
    scale, shift = params[0:1], params[1:2]
    return 0.5 * (shift + jnp.sqrt(shift * shift + 0.64 * scale * scale))


def stats_of(total, count):
    mean = total[0:1] / count
    var = total[1:2] / count - mean * mean
    return mean, lax.rsqrt(var + 1e-05)


def second_conv_kernel(g, chunk, count, z1, st, params, w, cot, h_ref, z_ref, st_ref, own_ref):
    rows_in, rows_out = g.tall - 2, g.tall - 4
    place = Place()
    mean, rstd = stats_of(total_of(st), count)
    scale = params[0:1] * rstd
    shift = params[1:2] - mean * scale
    edge = edge_mask(place, g)
    sums = [jnp.zeros((8, g.c), F32) for _ in range(4)]
    for s in range(g.s):
        for r in range(rows_in):
            start = (s * rows_in + r) * g.wp
            row = jnp.maximum(z1[start : start + g.wp, :] * scale + shift, 0.0)
            store_shifted(h_ref, start, in_grid(row, r + 1, g, place, edge))
        for r in range(0, rows_out, chunk):
            base = (s * rows_in + r) * g.wp
            size = chunk * g.wp
            lhs = jnp.concatenate(
                [h_ref[base + a * g.wp : base + a * g.wp + size, :] for a in range(3)], axis=1
            )
            acc = dot(lhs, w[...])
            z_ref[(s * rows_out + r) * g.wp : (s * rows_out + r) * g.wp + size, :] = acc
            for i in range(chunk):
                if RIM <= r + i + 2 < RIM + g.h:
                    v = acc[i * g.wp : i * g.wp + g.w]
                    dn = wide(cot, s, r + i + 2 - RIM)[: g.w]
                    for k, term in enumerate((v, v * v, dn, dn * v)):
                        sums[k] = sums[k] + sum_rows(term)
    own = [jnp.sum(v, 0, keepdims=True) for v in sums]
    own_ref[0:4] = jnp.concatenate(own, axis=0)
    to_all(st_ref, own)


def own_transposed(g, source, first, s, dt_ref):
    span = g.h * g.wp
    block = source[first : first + span, :]
    inside = lax.broadcasted_iota(jnp.int32, (span, 1), 0) % g.wp < g.w
    dt_ref[:, s * span : (s + 1) * span] = jnp.where(inside, block, jnp.zeros_like(block)).T


def kernel_gradient(g, core, field, rows_field, first_row, dt_ref, keep, send, first, prepare, less):
    chans, half = g.c, g.c // 2
    span = g.h * g.wp
    mine = pl.ds(pl.multiple_of(core * half, half), half)
    other = pl.ds(pl.multiple_of((1 - core) * half, half), half)
    totals = [None] * 3
    cut = g.s // 2
    groups = (range(cut), range(cut, g.s))
    for s in groups[0]:
        prepare(s)
    for group in groups:
        lanes = slice(group[0] * span, (group[-1] + 1) * span)
        lhs = jnp.concatenate([dt_ref[mine, lanes], dt_ref[other, lanes]], axis=0)
        for a in range(3):
            starts = [(s * rows_field + first_row + a) * g.wp for s in group]
            acc = dot(lhs, jnp.concatenate([field[at : at + span, :] for at in starts], axis=0))
            if group[0] == 0 and a < len(groups[1]):
                prepare(groups[1][a])
            if group[0] == 0:
                for b in range(3):
                    first[a * 3 + b] = acc[:, b * chans : (b + 1) * chans]
                continue
            for b in range(3):
                rows = slice((a * 3 + b) * chans, (a * 3 + b + 1) * chans)
                part = acc[:, b * chans : (b + 1) * chans] + first[a * 3 + b]
                keep[rows, :] = (part[0:half] - less(mine)).T
                send[rows, :] = (part[half:] - less(other)).T.astype(BF16)


def second_gradient_kernel(
    g, count, z2, st, own, params, cot, cot_next, h, d_ref, keep, send, dt_ref, sums, first
):
    place = Place()
    rows = g.cot_tall
    total = total_of(st)
    mean, rstd = stats_of(total, count)
    sum_dn = total[2:3]
    sum_dx = rstd * (total[3:4] - mean * sum_dn)
    k0 = params[2:3] * rstd
    k1 = k0 * (sum_dn / count)
    k2 = k0 * rstd * (sum_dx / count)
    edge = edge_mask(place, g)
    def prepare(s):
        for i in range(rows):
            rim = not g.near <= i < g.near + g.h
            dn = wide(cot_next, s, 0 if i < g.near else 1) if rim else wide(cot, s, i - g.near)
            start = (s * rows + i) * g.wp
            d = k0 * dn - k1 - (z2[start : start + g.wp, :] - mean) * k2
            d = in_grid(d, i + RIM - g.near, g, place, edge)
            d_ref[start : start + g.wp, :] = d.astype(BF16)
        own_transposed(g, d_ref, (s * rows + g.near) * g.wp, s, dt_ref)
    pixels = float(g.s * g.h * g.w)
    tile_sum = k0 * own[2:3] - pixels * k1 - k2 * (own[0:1] - pixels * mean)
    sums[...] = jnp.broadcast_to(tile_sum, (sums.shape[1], g.c)).T
    typical = typical_hidden(params)

    def less(channels):
        column = sums[channels, :]
        return jnp.concatenate([column] * (g.c // column.shape[1]), axis=1) * typical

    kernel_gradient(g, place.core, h, g.tall - 2, RIM - 2, dt_ref, keep, send, first, prepare, less)


def transposed_conv(g, d_ref, w, s, rows_in, r, chunk):
    acc = None
    size = chunk * g.wp
    for a in range(3):
        start = (s * rows_in + r + a) * g.wp
        for b in range(3):
            tap = (2 - a) * 3 + (2 - b)
            term = dot_nt(
                d_ref[start : start + size, b * g.c : (b + 1) * g.c],
                w[tap * g.c : (tap + 1) * g.c, :],
            )
            acc = term if acc is None else acc + term
    return acc


def hidden_gradient_kernel(
    g, chunk, count, scenes, d, w, z1, z2, st, st2, params, ext, *refs
):
    *before, dn_ref, st_ref, out_ref, d_ref = refs
    mean2, rstd2 = stats_of(total_of(st2), count)
    scale2 = params[2:3] * rstd2
    shift2 = params[3:4] - mean2 * scale2
    rows_in, rows_out, z_rows = g.tall - 4, g.tall - 6, g.tall - 2
    mean, rstd = stats_of(total_of(st), count)
    scale = params[0:1] * rstd
    shift = params[1:2] - mean * scale
    s0 = before[1][0:8] if before else jnp.zeros((8, g.c), F32)
    s1 = before[1][8:16] if before else jnp.zeros((8, g.c), F32)
    for s in scenes:
        for i in range(rows_in):
            at = (s * rows_in + i) * g.wp
            store_shifted(d_ref, at, wide(d, slice(at, at + g.wp)))
        for r in range(g.h):
            at = (s * rows_in + r + g.near) * g.wp
            normed = z2[at : at + g.w, :] * scale2 + shift2
            out_ref[s, r] = (wide(ext, s, r)[: g.w] + normed).astype(BF16)
        for r in range(0, rows_out, chunk):
            acc = transposed_conv(g, d_ref, w, s, rows_in, r, chunk)
            at = (s * z_rows + r + 2) * g.wp
            z = z1[at : at + chunk * g.wp, :]
            dn = jnp.where(z * scale + shift > 0, acc, 0.0)
            dn_ref[(s * rows_out + r) * g.wp : (s * rows_out + r + chunk) * g.wp, :] = dn
            for i in range(chunk):
                if RIM <= r + i + 3 < RIM + g.h:
                    v = dn[i * g.wp : i * g.wp + g.w]
                    s0 = s0 + sum_rows(v)
                    s1 = s1 + sum_rows(v * (z[i * g.wp : i * g.wp + g.w] - mean))
    if not before:
        st_ref[0:8] = s0
        st_ref[8:16] = s1
    else:
        to_all(st_ref, [jnp.sum(s0, 0, keepdims=True), jnp.sum(s1, 0, keepdims=True) * rstd])


def put(refs, rows, value):
    if not isinstance(refs, tuple):
        refs = (refs,)
    at = 0
    for ref in refs:
        first, last = max(rows.start, at), min(rows.stop, at + ref.shape[0])
        if first < last:
            part = value[first - rows.start : last - rows.start]
            ref[first - at : last - at, :] = part.astype(ref.dtype)
        at += ref.shape[0]


def half_gradient(g, which, field, rows_field, first_row, dt_ref, out_ref, sums, prepare=None):
    chans, half = g.c, g.c // 2
    span = g.h * g.wp
    channels = pl.ds(pl.multiple_of(which * half, half), half)
    cut = g.s // 2
    groups = range(cut), range(cut, g.s)
    if prepare is not None:
        for s in groups[0]:
            prepare(s)
    for group in groups:
        lhs = dt_ref[channels, group[0] * span : (group[-1] + 1) * span]
        for a in range(3):
            starts = [(s * rows_field + first_row + a) * g.wp for s in group]
            acc = dot(lhs, jnp.concatenate([field[at : at + span, :] for at in starts], axis=0))
            if group[0] == 0 and prepare is not None and a < len(groups[1]):
                prepare(groups[1][a])
            for b in range(3):
                part = acc[:, b * chans : (b + 1) * chans]
                if group[0] == 0:
                    sums[a * 3 + b] = part
                else:
                    rows = slice((a * 3 + b) * chans, (a * 3 + b + 1) * chans)
                    put(out_ref, rows, (sums[a * 3 + b] + part).T)


def first_gradient_kernel(
    g, count, dn, z, st, st3, params, x, e_ref, a_ref, b_ref, *refs
):
    *send, dt_ref, first = refs
    place = Place()
    mean, rstd = stats_of(total_of(st), count)
    total = total_of(st3)
    k0 = params[0:1] * rstd
    k1 = k0 * (total[0:1] / count)
    k2 = k0 * rstd * (total[1:2] / count)
    edge = edge_mask(place, g)

    def prepare(s):
        for i in range(g.h):
            at = (s * g.h + i) * g.wp
            z_at = (s * (g.tall - 2) + i + RIM - 1) * g.wp
            d = k0 * dn[at : at + g.wp, :] - k1 - (z[z_at : z_at + g.wp, :] - mean) * k2
            d = in_grid(d, i + RIM, g, place, edge)
            e_ref[at : at + g.wp, :] = d.astype(BF16)
            if i == 0:
                top = d
        a_ref[s, 0] = jnp.where(place.odd_row, top, d).astype(BF16)
        b_ref[s, 0] = jnp.where(place.odd_row, d, top).astype(BF16)
        own_transposed(g, e_ref, s * g.h * g.wp, s, dt_ref)
    half_gradient(g, 1 - place.core, x, g.h + 2, 0, dt_ref, tuple(send), first, prepare)


def first_own_kernel(g, x, dt_ref, keep, first):
    half_gradient(g, Place().core, x, g.h + 2, 0, dt_ref, keep, first)


def input_gradient_kernel(
    g, chunk, e, ra, rb, w_far, cot_far, occ, out_ref, w, cot, e_ref, sems
):
    rows_in = g.h + 2
    place = Place()
    copies = [
        pltpu.make_async_copy(w_far, w, sems.at[0]),
        pltpu.make_async_copy(cot_far, cot, sems.at[1]),
    ]
    for copy in copies:
        copy.start()
    for copy in copies:
        copy.wait()
    for s in range(g.s):
        a, b = wide(ra, s, 0), wide(rb, s, 0)
        rows = [jnp.where(place.odd_row, a, b)]
        for r in range(g.h):
            at = (s * g.h + r) * g.wp
            rows.append(wide(e, slice(at, at + g.wp)))
        rows.append(jnp.where(place.odd_row, b, a))
        for i in range(rows_in):
            place_shifted(e_ref, s * rows_in + i, rows[i])
        mask = pixel_mask(occ, s)
        for r in range(0, g.h, chunk):
            acc = transposed_conv(g, e_ref, w, s, rows_in, r, chunk)
            for i in range(chunk):
                v = acc[i * g.wp : i * g.wp + g.w]
                out_ref[s, r + i] = (wide(cot, s, r + i) + v) * mask[:, r + i : r + i + 1]


def pair_total(keep, got, t):
    chans = 2 * keep.shape[1]
    rows = slice(t * chans, (t + 1) * chans)
    return keep[rows, :] + wide(got, rows)


def pair_sum_kernel(lane, keep, got, *refs):
    *_, out_far, buffer, sems = refs
    half = buffer.shape[1]
    chans = 2 * half
    taps = buffer.shape[0] // chans
    copies = []
    for t in range(taps):
        rows = pl.ds(t * chans, chans)
        buffer[rows, :] = pair_total(keep, got, t).astype(BF16)
        copies.append(
            pltpu.make_async_copy(buffer.at[rows], out_far.at[rows, pl.ds(lane, half)], sems.at[t])
        )
        copies[-1].start()
    for copy in copies:
        copy.wait()


def half_rows(share):
    return -(-(share // 2) // 8) * 8


def split_kernel(keep, got, kept_ref, sent_ref, buffer):
    half = keep.shape[1]
    chans = 2 * half
    taps = keep.shape[0] // chans
    devices, rows, _ = kept_ref.shape
    share = taps * chans // devices
    for t in range(taps):
        buffer[t * chans : (t + 1) * chans, :] = pair_total(keep, got, t)
    second = Place().second
    for i in range(devices):
        mine = pl.multiple_of(i * share + (share - rows) * second, 8)
        other = pl.multiple_of(i * share + (share - rows) * (1 - second), 8)
        kept_ref[i] = buffer[pl.ds(mine, rows), :]
        sent_ref[i] = buffer[pl.ds(other, rows), :].astype(BF16)


def split_again_kernel(kept, came, kept_ref, sent_ref, buffer):
    devices, rows, _ = kept_ref.shape
    spare = kept.shape[1] - rows
    third = Place().third
    for i in range(devices):
        buffer[i] = kept[i] + wide(came, i)
    for i in range(devices):
        kept_ref[i] = buffer[i, pl.ds(pl.multiple_of(spare * third, 8), rows)]
    for j in range(devices // 2):
        large = buffer[2 * j + 1 - third, pl.ds(pl.multiple_of(spare * (1 - third), 8), rows)]
        small = buffer[2 * j + third, pl.ds(pl.multiple_of(rows * (1 - third), 8), spare)]
        sent_ref[j] = jnp.concatenate([large, small], axis=0).astype(BF16)


def whole_tiles(share):
    return share // 16 * 16


def write_parts(block_of, first_row, out_far, buffer, sems):
    devices, rows, _ = buffer.shape
    count = sems.shape[0]
    per = devices // count
    copies = []
    for part in range(count):
        mine = pl.ds(part * per, per)
        for i in range(part * per, (part + 1) * per):
            buffer[i] = block_of(i).astype(BF16)
        there = out_far.at[mine, pl.ds(first_row, rows)]
        copies.append(pltpu.make_async_copy(buffer.at[mine], there, sems.at[part]))
        copies[-1].start()
    for copy in copies:
        copy.wait()


def first_rows(keep, got, share, i, rows):
    piece, at = divmod(i * share, got[0].shape[0])
    mine = keep[i * share + rows.start : i * share + rows.stop, :]
    return mine + wide(got[piece], slice(at + rows.start, at + rows.stop))


def early_message_kernel(keep, *refs):
    *got, out_far, buffer, sems = refs
    devices, rows, _ = buffer.shape
    share = keep.shape[0] // devices
    write_parts(lambda i: first_rows(keep, got, share, i, slice(0, rows)), 0, out_far, buffer, sems)


def message_kernel(keep, *refs):
    *got, kept, came, _, out_far, buffer, sems = refs
    devices = kept.shape[0]
    share = keep.shape[0] // devices
    rows = kept.shape[1]
    spare = came.shape[1] - rows
    third = Place().third
    none = jnp.zeros((rows - spare, kept.shape[2]), F32)

    def block_of(i):
        others = wide(came, i // 2)
        small = [others[rows:], none] if i % 2 else [none, others[rows:]]
        second = kept[i] + jnp.where(third == i % 2, others[:rows], jnp.concatenate(small, axis=0))
        last = first_rows(keep, got, share, i, slice(whole_tiles(share), share))
        return jnp.concatenate([last, second], axis=0)

    write_parts(block_of, whole_tiles(share), out_far, buffer, sems)


def adamw(weight, grad, first, second, rate):
    first_new = 0.9 * first + 0.1 * grad
    second_new = 0.999 * second + 0.001 * grad * grad
    first_hat = first_new / (1.0 - 0.9**STEP)
    second_hat = second_new / (1.0 - 0.999**STEP)
    weight_new = weight - rate * (first_hat / (jnp.sqrt(second_hat) + 1e-08) + 0.01 * weight)
    return (weight_new, first_new, second_new)


def update_kernel(
    count, parts, w, first_m, second_m, st2, st3, params, n_first, n_second,
    grad_out, w_out, first_out, second_out, n_grad, n_out, n_first_out, n_second_out
):
    devices, ncols = parts.shape[0], lax.axis_size("cols")
    share = w.shape[0] // 4
    total2, total3 = total_of(st2), total_of(st3)
    mean, rstd = stats_of(total2, count)
    sum_dn = total2[2:3]
    grads = jnp.concatenate(
        [total3[1:2], total3[0:1], rstd * (total2[3:4] - mean * sum_dn), sum_dn], axis=0
    )
    n_grad[...] = grads
    n_out[...], n_first_out[...], n_second_out[...] = adamw(
        params[...], grads, n_first[...], n_second[...], 0.75
    )
    def over(chosen, rows, lanes):
        total = None
        for source in range(devices):
            if chosen(source // ncols):
                term = wide(parts, source)[rows, lanes]
                total = term if total is None else total + term
        return total

    grads = []
    every = slice(None)
    for half in range(2):
        if parts.shape[2] == 256:
            for k in range(2):
                lanes = slice(k * 128, (k + 1) * 128)
                grads.append((k, half, over(lambda row: row % 2 == half, every, lanes)))
        else:
            grads.append((0, half, over(lambda row: row % 2 == half, slice(0, share), every)))
            size = half_rows(share)
            last = half_rows(size)
            spare = size - last
            odd = lax.axis_index("cols") % 2 == 1
            blocks = []
            for second in range(2):
                one, two = (
                    over(lambda r, row=half + 4 * second + 2 * third: r % 8 == row, slice(share, None), every)
                    for third in range(2)
                )
                middle = jnp.where(odd, two[: last - spare], one[spare:])
                blocks.append(jnp.concatenate([one[:spare], middle, two[last - spare :]], axis=0))
            blocks[1] = blocks[1][2 * size - share :]
            grads.append((1, half, jnp.concatenate(blocks, axis=0)))
    for k, half, grad in grads:
        at = pl.ds(2 * half + k, share, stride=4)
        new = adamw(w[at, :], grad, first_m[at, :], second_m[at, :], 0.02)
        grad_out[at, :] = grad
        w_out[at, :], first_out[at, :], second_out[at, :] = new


def swapped(block, axis, first):
    count = lax.axis_size(axis)
    pairs = []
    for i in range(first, count - 1, 2):
        pairs += [(i, i + 1), (i + 1, i)]
    return lax.ppermute(block, axis, pairs)


def swapped_both(block, first_row, first_col):
    nrows, ncols = lax.axis_size("rows"), lax.axis_size("cols")

    def partner(i, first, count):
        j = i + 1 if (i - first) % 2 == 0 else i - 1
        return j if min(i, j) >= first and max(i, j) < count else None

    pairs = []
    for i in range(nrows):
        for j in range(ncols):
            to = partner(i, first_row, nrows), partner(j, first_col, ncols)
            if None not in to:
                pairs.append((i * ncols + j, to[0] * ncols + to[1]))
    return lax.ppermute(block, BOTH, pairs)


def to_chunks(flat):
    return flat.reshape(2, -1, 128).transpose(1, 0, 2).reshape(-1, 128)


def from_chunks(rows):
    return rows.reshape(-1, 2, 128).transpose(1, 0, 2).reshape(2, -1)


def exchange(parts):
    return lax.all_to_all(parts, BOTH, 0, 0, tiled=True)


def body(
    features,
    occupancy,
    cotangent,
    conv_weights,
    conv_first,
    conv_second,
    norm_scale_bias,
    norm_first,
    norm_second,
):
    scenes, height, width, chans = features.shape
    g = Geometry(scenes, height, width, chans)
    wp = g.wp
    devices = lax.axis_size("rows") * lax.axis_size("cols")
    count = float(scenes * height * width * devices)
    taps = 9 * chans
    n0, n1, n2, n3 = (scenes * wp * (g.tall - 2 * i) for i in range(4))
    own_pixels = scenes * height * wp
    dma = pltpu.SemaphoreType.DMA

    def conv_flops(n):
        return 2 * n * taps * chans

    side = shape_of((scenes, g.side, chans), BF16)
    corner = shape_of((scenes, g.corner, chans), BF16)
    own, c, d, b, bc, bd = kernel_call(
        functools.partial(pack_kernel, g),
        [
            shape_of(features.shape, BF16),
            side,
            side,
            shape_of((scenes, RIM + g.near, width, chans), BF16),
            corner,
            corner,
        ],
        1e8,
        far=(0, 1, 2),
        scratch=[
            pltpu.VMEM(features.shape, BF16),
            pltpu.VMEM(features.shape, BF16),
            pltpu.VMEM(occupancy.shape, jnp.int32),
            dma((3, scenes)),
        ],
    )(features, occupancy, cotangent)
    rb = swapped(b, "rows", 1)
    rc, rd = swapped(c, "cols", 0), swapped(d, "cols", 1)
    rb_c, rb_d = swapped_both(bc, 1, 0), swapped_both(bd, 1, 1)
    chunked = to_chunks(conv_weights)
    share = conv_first.shape[1]
    chunk_shape = shape_of((share // 64, 128), F32)
    weights = (taps, chans)
    w1, w2 = kernel_call(
        prepare_kernel,
        [held(weights, BF16)] * 2,
        0,
        size=1024,
        far=(0,),
        scratch=[pltpu.VMEM((9, chunked.shape[0] // 9, 128), F32), dma((9,))],
    )(chunked)

    def wide_rows(rows):
        return shape_of((scenes, rows, wp, chans), BF16)

    ext, cot_ext, a = kernel_call(
        functools.partial(assemble_kernel, g),
        [wide_rows(n) for n in (height, height, RIM + g.near)],
        0,
        size=1024,
    )(own, cotangent, rc, rd)
    rows_x = scenes * (height + 2) * wp
    x_shape = held((rows_x, 3 * chans), BF16)
    z1, st, x = kernel_call(
        functools.partial(own_conv_kernel, g),
        [held((n1, chans), F32), held((16, chans), F32), x_shape],
        0,
        size=1024,
    )(ext, w1)
    a, rb, rb_c, rb_d, w1 = lax.optimization_barrier((a, rb, rb_c, rb_d, w1))
    ra = swapped(a, "rows", 0)
    z1, st, x, cot_next = kernel_call(
        functools.partial(rim_conv_kernel, g),
        [held((n1, chans), F32), shape_of((devices, 2, chans), F32), x_shape, wide_rows(2)],
        0,
        size=1024,
        scratch=[pltpu.VMEM((scenes * 2 * (RIM + 2) * wp, 3 * chans), BF16)],
        alias={7: 0, 8: 2},
    )(ext, ra, rb, rb_c, rb_d, w1, st, z1, x)
    st1 = exchange(st)
    h, z2, st, own_sums = kernel_call(
        functools.partial(second_conv_kernel, g, 5, count),
        [
            held((n1, 3 * chans), BF16),
            held((n2, chans), F32),
            shape_of((devices, 4, chans), F32),
            held((8, chans), F32),
        ],
        conv_flops(n2),
    )(z1, st1, norm_scale_bias, w2, cot_ext)
    st2 = exchange(st)
    grad_shape = held((taps, chans // 2), F32)
    d, keep2, send2 = kernel_call(
        functools.partial(second_gradient_kernel, g, count),
        [held((n2, chans), BF16), grad_shape, held(grad_shape.shape, BF16)],
        conv_flops(own_pixels),
        scratch=[
            pltpu.VMEM((chans, own_pixels), BF16),
            pltpu.VMEM((chans, 128), F32),
            pltpu.VMEM((9, chans, chans), F32),
        ],
    )(z2, st2, own_sums, norm_scale_bias, cot_ext, cot_next, h)
    got2 = swapped(send2, "rows", 0)
    nrows = lax.axis_size("rows")
    cut_again = nrows % 8 == 0 and lax.axis_size("cols") % 2 == 0 and taps // devices % 8 == 0
    hidden_shape, output_shape = held((n3, chans), F32), held(features.shape, BF16)

    def hidden_gradient(scenes, part_shape, *before, **options):
        return kernel_call(
            functools.partial(hidden_gradient_kernel, g, 8, count, scenes),
            [hidden_shape, part_shape, output_shape],
            0,
            size=1024,
            scratch=[pltpu.VMEM((n2, 3 * chans), BF16)],
            **options,
        )(d, w2, z1, z2, st1, st2, norm_scale_bias, ext, *before)

    early = range(3)
    dn1, part, block_out = hidden_gradient(early, held((16, chans), F32))
    got2, part = lax.optimization_barrier((got2, part))
    if cut_again:
        kept_shape = (devices, half_rows(taps // devices), chans // 2)
        kept, sent = kernel_call(
            split_kernel,
            [held(kept_shape, F32), held(kept_shape, BF16)],
            0,
            size=1024,
            scratch=[pltpu.VMEM((taps, chans // 2), F32)],
        )(keep2, got2)
        came = lax.ppermute(sent, "rows", [(i, i ^ 4) for i in range(nrows)])
        kept, part = lax.optimization_barrier((kept, part))
    dn1, st, block_out = hidden_gradient(
        range(len(early), scenes),
        shape_of((devices, 2, chans), F32),
        dn1,
        part,
        block_out,
        alias={8: 0, 10: 2},
    )
    st3 = exchange(st)
    if cut_again:
        kept, st3 = lax.optimization_barrier((kept, st3))
        again_shape = (devices, half_rows(kept_shape[1]), chans // 2)
        kept, sent = kernel_call(
            split_again_kernel,
            [held(again_shape, F32), held((devices // 2, *kept_shape[1:]), BF16)],
            0,
            size=1024,
            scratch=[pltpu.VMEM(kept_shape, F32)],
        )(kept, came)
        came = lax.ppermute(sent, "rows", [(i, i ^ 2) for i in range(nrows)])
        dn1, kept = lax.optimization_barrier((dn1, kept))
    cuts = 4 if cut_again else 1
    sent_shape = held((taps // cuts, chans // 2), BF16)
    part = pltpu.VMEM((9, chans // 2, chans), F32)
    e, a, b, *send1, dt = kernel_call(
        functools.partial(first_gradient_kernel, g, count),
        [held((n3, chans), BF16), wide_rows(1), wide_rows(1)]
        + [sent_shape] * cuts
        + [held((chans, own_pixels), BF16)],
        0,
        size=1024,
        scratch=[part],
    )(dn1, z1, st1, st3, norm_scale_bias, x)
    (keep1,) = kernel_call(
        functools.partial(first_own_kernel, g), [held((taps, chans // 2), F32)], 0, size=1024, scratch=[part]
    )(x, dt)
    got1 = [swapped(part, "rows", 0) for part in send1]
    share_rows = taps // devices
    if cut_again:
        rows = share_rows + kept.shape[1]
        parts_shape = stored((devices, rows, chans // 2), BF16)
        ready = whole_tiles(share_rows)
        (parts,) = kernel_call(
            early_message_kernel,
            [parts_shape],
            0,
            size=1024,
            far_out=(0,),
            scratch=[pltpu.VMEM((devices, ready, chans // 2), BF16), dma((4,))],
        )(keep1, *got1)
        operands = (keep1, *got1, kept, came, parts)
        at = len(operands) - 1
        (parts,) = kernel_call(
            message_kernel,
            [parts_shape],
            0,
            size=1024,
            far=(at,),
            far_out=(0,),
            scratch=[pltpu.VMEM((devices, rows - ready, chans // 2), BF16), dma((4,))],
            alias={at: 0},
        )(*operands)
    else:

        def add_pair(lane, *operands, **options):
            return kernel_call(
                functools.partial(pair_sum_kernel, lane),
                [stored((taps, chans), BF16)],
                1e9,
                far_out=(0,),
                scratch=[pltpu.VMEM((taps, chans // 2), BF16), dma((9,))],
                **options,
            )(*operands)

        (parts,) = add_pair(chans // 2, keep2, got2)
        (parts,) = add_pair(0, keep1, *got1, parts, far=(2,), alias={2: 0})
        parts = parts.reshape(devices, share_rows, chans)
    parts, chunked = lax.optimization_barrier((parts, chunked))
    parts = exchange(parts)
    ra, rb = swapped(a, "rows", 0), swapped(b, "rows", 1)
    (grad_input,) = kernel_call(
        functools.partial(input_gradient_kernel, g, 8),
        [shape_of(features.shape, F32)],
        conv_flops(own_pixels),
        far=(3, 4),
        scratch=[
            pltpu.VMEM(weights, BF16),
            pltpu.VMEM(features.shape, BF16),
            pltpu.VMEM((rows_x, 3 * chans), BF16),
            dma((2,)),
        ],
    )(e, ra, rb, w1, cotangent, occupancy)
    own_rows = share // 64
    first_row = (lax.axis_index("rows") * lax.axis_size("cols") + lax.axis_index("cols")) * own_rows
    own_weights = lax.dynamic_slice_in_dim(chunked, first_row, own_rows, 0)

    norm_shape = shape_of(norm_first.shape, F32)
    updated = kernel_call(
        functools.partial(update_kernel, count),
        [chunk_shape] * 4 + [norm_shape] * 4,
        1e8,
    )(
        parts, own_weights, to_chunks(conv_first), to_chunks(conv_second), st2, st3,
        norm_scale_bias, norm_first, norm_second,
    )
    return (block_out, grad_input, *map(from_chunks, updated[:4]), *updated[4:])


def solution(mesh):
    tile = P(None, "rows", "cols", None)
    share = P(None, ("rows", "cols"))
    return jax.shard_map(
        body,
        mesh=mesh,
        in_specs=(tile, P(None, "rows", "cols"), tile, P(), share, share, P(), P(), P()),
        out_specs=(tile, tile, share, share, share, share, P(), P(), P(), P()),
        check_vma=False,
    )
```
